32 devices in a mesh: seq: 8 (over y, x, core), heads: 4 (over z).
Axes of the slice: x: 2, y: 2, z: 4, core: 2. Of those that a mesh axis runs over, the one named last changes fastest.
Arguments:
- tokens: bfloat16 [2, 2048, 2048], P(None, 'seq'), may hold values from -6 to 6
- attn_gain: float32 [2048], replicated, may hold values from 0.5 to 1.5
- base_qkv: bfloat16 [3, 2048, 2048], P(None, None, 'heads'), may hold values from -0.125 to 0.125
- adapt_a_qkv: bfloat16 [3, 2048, 16], replicated, may hold values from -0.125 to 0.125
- adapt_b_qkv: bfloat16 [3, 16, 2048], P(None, None, 'heads'), may hold values from -0.375 to 0.375
- magnitude_qkv: float32 [3, 2048], P(None, 'heads'), may hold values from 0.7 to 1.8
- base_out: bfloat16 [2048, 2048], P('heads'), may hold values from -0.125 to 0.125
- adapt_a_out: bfloat16 [2048, 16], P('heads'), may hold values from -0.125 to 0.125
- adapt_b_out: bfloat16 [16, 2048], replicated, may hold values from -0.375 to 0.375
- magnitude_out: float32 [2048], replicated, may hold values from 4 to 16
- ffn_gain: float32 [2048], replicated, may hold values from 0.5 to 1.5
- base_gu: bfloat16 [2, 2048, 5632], P(None, None, 'heads'), may hold values from -0.125 to 0.125
- adapt_a_gu: bfloat16 [2, 2048, 16], replicated, may hold values from -0.125 to 0.125
- adapt_b_gu: bfloat16 [2, 16, 5632], P(None, None, 'heads'), may hold values from -0.375 to 0.375
- magnitude_gu: float32 [2, 5632], P(None, 'heads'), may hold values from 0.5 to 2
- base_down: bfloat16 [5632, 2048], P('heads'), may hold values from -0.078125 to 0.078125
- adapt_a_down: bfloat16 [5632, 16], P('heads'), may hold values from -0.078125 to 0.078125
- adapt_b_down: bfloat16 [16, 2048], replicated, may hold values from -0.375 to 0.375
- magnitude_down: float32 [2048], replicated, may hold values from 1 to 4
- doc_lengths: int32 [2, 8], replicated, may hold values from 1 to 1536, 2048 in all within a row
- cotangent: bfloat16 [2, 2048, 2048], P(None, 'seq'), may hold values from -6 to 6
Outputs:
- mixed: bfloat16 [2, 2048, 2048], P(None, 'seq')
- grad_tokens: float32 [2, 2048, 2048], P(None, 'seq')
- grad_attn_gain: float32 [2048], replicated
- grad_a_qkv: float32 [3, 2048, 16], replicated
- grad_b_qkv: float32 [3, 16, 2048], P(None, None, 'heads')
- grad_m_qkv: float32 [3, 2048], P(None, 'heads')
- grad_a_out: float32 [2048, 16], P('heads')
- grad_b_out: float32 [16, 2048], replicated
- grad_m_out: float32 [2048], replicated
- grad_ffn_gain: float32 [2048], replicated
- grad_a_gu: float32 [2, 2048, 16], replicated
- grad_b_gu: float32 [2, 16, 5632], P(None, None, 'heads')
- grad_m_gu: float32 [2, 5632], P(None, 'heads')
- grad_a_down: float32 [5632, 16], P('heads')
- grad_b_down: float32 [16, 2048], replicated
- grad_m_down: float32 [2048], replicated
The draws below stay inside these ranges and needn't reach their ends.
Inputs may be any that keep to these rules, and one draw needn't show every extreme that they name: `doc_lengths`: each row's 8 lengths sum to 2048, and the longest of each row is exactly 1536.
All inputs are finite; a program needn't handle non-finite values.
Results may differ from the reference program's by a relative error of at most 0.029.
Values may be sent and summed in bfloat16 or wider, within the bound.
A program may use at most 448 MiB of HBM per device.

```python
import math
import jax
import jax.numpy as jnp
import numpy as np
from jax import lax

D = 2048
HEAD_COUNT = 16
HD = 128
FF = 5632
R = 16
DOCS = 8
ROWS = 2
L = 2048


def steps_of(rng, dims, pieces, least, high):
    loudness, own = 1.0, jax.random.fold_in(rng, 6)
    for dim, shards_of in pieces:
        heights = jnp.exp(jax.random.uniform(jax.random.fold_in(own, dim), (shards_of,), jnp.float32, least / len(pieces), high / len(pieces)))
        loudness = loudness * jnp.repeat(heights, dims[dim] // shards_of).reshape([-1 if axis == dim else 1 for axis in range(len(dims))])
    return loudness


def profile(amount, total, most, skew):
    weights = [(1 << 20) // math.isqrt(grade ** skew) + 1 for grade in range(2, amount + 1)]
    spare, holding = total - most - (amount - 1), [1] * (amount - 1)
    while spare > 0:
        candidates = [i for i in range(amount - 1) if holding[i] < most]
        whole, budget = sum([weights[i] for i in candidates]), spare
        for i in candidates:
            extra = min(most - holding[i], max(1, budget * weights[i] // whole), spare)
            holding[i] = holding[i] + extra
            spare = spare - extra
    return np.array([most] + holding)


def uneven(own_key, count, total, reach, lean):
    if count == 2:
        one = jax.random.randint(own_key, (), max(1, total - reach), min(reach, total - 1) + 1)
        return jnp.stack([one, total - one])
    lengths = jnp.asarray(profile(count, total, reach, lean), jnp.int32)
    twos = (count - 1) // 2
    giver, sink = lengths[1:1 + 2 * twos:2], lengths[2:2 + 2 * twos:2]
    slack = jnp.minimum(giver - 1, reach - sink)
    moved = jax.random.randint(jax.random.fold_in(own_key, 1), (twos,), 0, 1 << 20) % (slack + 1)
    lengths = lengths.at[1:1 + 2 * twos:2].set(giver - moved).at[2:2 + 2 * twos:2].set(sink + moved)
    return lengths[jax.random.permutation(jax.random.fold_in(own_key, 2), count)]


def noise(key, extent, spread, most, split=(), kind=jnp.bfloat16):
    array = jax.random.normal(key, extent, jnp.float32) * spread
    if len(split) > 0:
        array = steps_of(key, extent, split, -0.22, 0.18) * array
    return jnp.clip(array, min=-most, max=most).astype(kind)


def setup_inputs(seed: int = 0) -> dict:
    seeds = jax.random.split(jax.random.key(seed), 22)
    tokens = noise(seeds[0], (ROWS, L, D), 1.0, 6.0, ((1, 8),))
    attn_gain = jnp.clip(1.0 + 0.1 * jax.random.normal(seeds[1], (D,), jnp.float32), 0.5, 1.5)
    base_qkv = noise(seeds[2], (3, D, D), D ** -0.5, 0.125, ((2, 4),))
    adapt_a_qkv = noise(seeds[3], (3, D, R), D ** -0.5, 0.125)
    adapt_b_qkv = noise(seeds[4], (3, R, D), (16 * R) ** -0.5, 0.375, ((2, 4),))
    magnitude_qkv = jnp.clip(jnp.exp(math.log(1.8) - 0.9444616 * jax.random.uniform(seeds[5], (3, D), jnp.float32) ** steps_of(seeds[5], (3, D), ((1, 4),), -0.2, 0.2)), 0.7, 1.8)
    base_out = noise(seeds[6], (D, D), D ** -0.5, 0.125, ((0, 4),))
    adapt_a_out = noise(seeds[7], (D, R), D ** -0.5, 0.125, ((0, 4),))
    adapt_b_out = noise(seeds[8], (R, D), (16 * R) ** -0.5, 0.375)
    magnitude_out = jnp.clip(jnp.exp(jax.random.uniform(seeds[9], (D,), jnp.float32, math.log(4.0), math.log(16.0))), 4.0, 16.0)
    ffn_gain = jnp.clip(1.0 + 0.1 * jax.random.normal(seeds[10], (D,), jnp.float32), 0.5, 1.5)
    base_gu = noise(seeds[11], (2, D, FF), D ** -0.5, 0.125, ((2, 4),))
    adapt_a_gu = noise(seeds[12], (2, D, R), D ** -0.5, 0.125)
    adapt_b_gu = noise(seeds[13], (2, R, FF), (16 * R) ** -0.5, 0.375, ((2, 4),))
    magnitude_gu = jnp.clip(jnp.exp(math.log(2.0) - 1.3862944 * jax.random.uniform(seeds[14], (2, FF), jnp.float32) ** steps_of(seeds[14], (2, FF), ((1, 4),), -0.2, 0.2)), 0.5, 2.0)
    base_down = noise(seeds[15], (FF, D), FF ** -0.5, 0.078125, ((0, 4),))
    adapt_a_down = noise(seeds[16], (FF, R), FF ** -0.5, 0.078125, ((0, 4),))
    adapt_b_down = noise(seeds[17], (R, D), (16 * R) ** -0.5, 0.375)
    magnitude_down = jnp.clip(jnp.exp(jax.random.uniform(seeds[18], (D,), jnp.float32, math.log(1.0), math.log(4.0))), 1.0, 4.0)
    doc_lengths = jax.vmap(lambda own: uneven(own, DOCS, L, 3 * L // 4, 2))(jax.random.split(seeds[19], ROWS)).reshape((ROWS, DOCS)).astype(jnp.int32)
    cotangent = noise(seeds[20], (ROWS, L, D), 1.0, 6.0, ((1, 8),))
    return dict(tokens=tokens, attn_gain=attn_gain, base_qkv=base_qkv, adapt_a_qkv=adapt_a_qkv, adapt_b_qkv=adapt_b_qkv, magnitude_qkv=magnitude_qkv, base_out=base_out, adapt_a_out=adapt_a_out, adapt_b_out=adapt_b_out, magnitude_out=magnitude_out, ffn_gain=ffn_gain, base_gu=base_gu, adapt_a_gu=adapt_a_gu, adapt_b_gu=adapt_b_gu, magnitude_gu=magnitude_gu, base_down=base_down, adapt_a_down=adapt_a_down, adapt_b_down=adapt_b_down, magnitude_down=magnitude_down, doc_lengths=doc_lengths, cotangent=cotangent)


ADAPT_SCALE = 2.0
NORM_EPS = 1e-05
COLUMN_EPS = 1e-06
ROPE_BASE = 10000.0
NEG_LARGE = -1e+30
FULL_PRECISION = lax.Precision.HIGHEST
WIDE_TYPE = jnp.float32
NARROW_TYPE = jnp.bfloat16

@jax.custom_vjp
def low(v):
    return lax.optimization_barrier(v.astype(jnp.bfloat16)).astype(jnp.float32)

@jax.custom_vjp
def low_back(v):
    return v

def low_keep(v):
    return (low(v), None)

def low_pass(kept, grad):
    return (grad,)

def back_keep(v):
    return (v, None)

def back_low(kept, grad):
    return (low(grad),)
low.defvjp(low_keep, low_pass)
low_back.defvjp(back_keep, back_low)

def doc_layout(doc_lengths, start_at, span_rows):
    doc_ends = jnp.cumsum(doc_lengths, axis=1).astype(jnp.int32)
    starts = doc_ends - doc_lengths
    places = start_at + jnp.arange(span_rows, dtype=jnp.int32)
    passed = places[None, :, None] >= doc_ends[:, None, :]
    segment = lax.optimization_barrier(jnp.sum(passed.astype(jnp.int32), axis=2)).astype(jnp.int32)
    inside = jnp.logical_and(places[None, :, None] >= starts[:, None, :], jnp.logical_not(passed))
    offsets = lax.optimization_barrier(jnp.sum(jnp.where(inside, starts[:, None, :], 0), axis=2)).astype(jnp.int32)
    row_places = jnp.broadcast_to(places[None, :], segment.shape)
    return (segment, row_places - offsets, row_places)

def rope_tables(positions, head_size):
    half_size = head_size // 2
    frequency = ROPE_BASE ** (jnp.arange(half_size, dtype=WIDE_TYPE) * (-2.0 / head_size))
    angles = positions.astype(WIDE_TYPE)[..., None] * frequency
    return (jnp.cos(angles)[:, :, None, :], jnp.sin(angles)[:, :, None, :])

def rotate(values, cosine, sine_t):
    half_size = values.shape[-1] // 2
    first_half = values[..., :half_size]
    second_half = values[..., half_size:]
    return jnp.concatenate([first_half * cosine - second_half * sine_t, second_half * cosine + first_half * sine_t], axis=-1)

def rms_norm(values, gain_vec):
    return values * lax.rsqrt(lax.optimization_barrier(jnp.mean(values * values, axis=-1, keepdims=True)) + NORM_EPS) * gain_vec

def dora_project(inputs, base_w, adapt_a, adapt_b, magnitude):
    full_weight = base_w + ADAPT_SCALE * jnp.dot(adapt_a, adapt_b, precision=FULL_PRECISION)
    col_norm = jnp.sqrt(lax.optimization_barrier(jnp.sum(full_weight * full_weight, axis=0)) + COLUMN_EPS)
    low_rank = low(jnp.dot(inputs, adapt_a, precision=FULL_PRECISION))
    pre_act = low_back(jnp.dot(inputs, base_w, precision=FULL_PRECISION) + ADAPT_SCALE * jnp.dot(low_rank, adapt_b, precision=FULL_PRECISION))
    return pre_act * (magnitude / col_norm)

def attend(queries, key_set, values, segment, places):
    rows_n, row_len = segment.shape
    q_block = min(512, row_len)
    per_row = row_len // q_block

    def query_block(block_index):
        row_at = block_index // per_row
        start_at = block_index % per_row * q_block
        q_row = lax.dynamic_index_in_dim(queries, row_at, 0, keepdims=False)
        k_row = lax.dynamic_index_in_dim(key_set, row_at, 0, keepdims=False)
        v_row = lax.dynamic_index_in_dim(values, row_at, 0, keepdims=False)
        seg_row = lax.dynamic_index_in_dim(segment, row_at, 0, keepdims=False)
        place_row = lax.dynamic_index_in_dim(places, row_at, 0, keepdims=False)
        q_part = lax.dynamic_slice_in_dim(q_row, start_at, q_block, 0)
        seg_q = lax.dynamic_slice_in_dim(seg_row, start_at, q_block, 0)
        place_q = lax.dynamic_slice_in_dim(place_row, start_at, q_block, 0)
        scores = low_back(jnp.einsum('qhd,khd->hqk', q_part, k_row, precision=FULL_PRECISION) * HD ** (-0.5))
        visible = jnp.logical_and(seg_q[:, None] == seg_row[None, :], place_row[None, :] <= place_q[:, None])
        masked = jnp.where(visible[None], scores, NEG_LARGE)
        shifted = jnp.exp(masked - lax.optimization_barrier(jnp.max(masked, axis=-1, keepdims=True)))
        probs = low(shifted / lax.optimization_barrier(jnp.sum(shifted, axis=-1, keepdims=True)))
        return jnp.einsum('hqk,khd->qhd', probs, v_row, precision=FULL_PRECISION)
    blocks_out = lax.map(jax.checkpoint(query_block), jnp.arange(rows_n * per_row, dtype=jnp.int32))
    return blocks_out.reshape(rows_n, row_len, queries.shape[2], queries.shape[3])

def reference(tokens, attn_gain, base_qkv, adapt_a_qkv, adapt_b_qkv, magnitude_qkv, base_out, adapt_a_out, adapt_b_out, magnitude_out, ffn_gain, base_gu, adapt_a_gu, adapt_b_gu, magnitude_gu, base_down, adapt_a_down, adapt_b_down, magnitude_down, doc_lengths, cotangent):
    segment, position, places = doc_layout(doc_lengths, 0, L)
    cosine, sine_t = rope_tables(position, HD)
    w_qkv = base_qkv.astype(WIDE_TYPE)
    w_out = base_out.astype(WIDE_TYPE)
    w_gu = base_gu.astype(WIDE_TYPE)
    w_down = base_down.astype(WIDE_TYPE)

    def forward(inputs, gain_first, a_qkv, b_qkv, m_qkv, a_out, b_out, m_out, gain_second, a_gu, b_gu, m_gu, a_down, b_down, m_down):
        flat_in = inputs.reshape(ROWS * L, D)
        normed = low(rms_norm(flat_in, gain_first))
        shaped = [dora_project(normed, w_qkv[slot_at], a_qkv[slot_at], b_qkv[slot_at], m_qkv[slot_at]).reshape(ROWS, L, HEAD_COUNT, HD) for slot_at in range(3)]
        queries = low(rotate(shaped[0], cosine, sine_t))
        key_set = low(rotate(shaped[1], cosine, sine_t))
        values = low(shaped[2])
        attended = low(low_back(attend(queries, key_set, values, segment, places)))
        residual = flat_in + dora_project(attended.reshape(ROWS * L, D), w_out, a_out, b_out, m_out)
        normed_two = low(rms_norm(residual, gain_second))
        gate_out = dora_project(normed_two, w_gu[0], a_gu[0], b_gu[0], m_gu[0])
        up_out = dora_project(normed_two, w_gu[1], a_gu[1], b_gu[1], m_gu[1])
        hidden = low(jax.nn.silu(gate_out) * up_out)
        result = residual + dora_project(hidden, w_down, a_down, b_down, m_down)
        return result.reshape(ROWS, L, D)
    result, pullback = jax.vjp(forward, tokens.astype(WIDE_TYPE), attn_gain, adapt_a_qkv.astype(WIDE_TYPE), adapt_b_qkv.astype(WIDE_TYPE), magnitude_qkv, adapt_a_out.astype(WIDE_TYPE), adapt_b_out.astype(WIDE_TYPE), magnitude_out, ffn_gain, adapt_a_gu.astype(WIDE_TYPE), adapt_b_gu.astype(WIDE_TYPE), magnitude_gu, adapt_a_down.astype(WIDE_TYPE), adapt_b_down.astype(WIDE_TYPE), magnitude_down)
    gradients = pullback(cotangent.astype(WIDE_TYPE))
    return (result.astype(NARROW_TYPE), gradients[0], gradients[1], gradients[2], gradients[3], gradients[4], gradients[5], gradients[6], gradients[7], gradients[8], gradients[9], gradients[10], gradients[11], gradients[12], gradients[13], gradients[14])
```

```python
import functools

import jax
import jax.numpy as jnp
from jax import lax
from jax.experimental import pallas as pl
from jax.experimental.pallas import tpu as pltpu
from jax.sharding import PartitionSpec as P

HD = 128
ADAPT_SCALE = 2.0
NORM_EPS = 1e-05
COLUMN_EPS = 1e-06
ROPE_BASE = 10000.0
NEG_LARGE = -1e30
F32 = jnp.float32
BF16 = jnp.bfloat16
MESH = pl.DeviceIdType.MESH
VMEM_LIMIT = 56 * 2**20
NN = (((1,), (0,)), ((), ()))
NT = (((1,), (1,)), ((), ()))
TN = (((0,), (0,)), ((), ()))


def dot(a, b, dims=NN):
    return lax.dot_general(a.astype(BF16), b.astype(BF16), dims, preferred_element_type=F32)


def exchange_plan(kind, me, seq_n, pairs):
    fan = seq_n // pairs
    if kind == "queries":
        return [(p * fan + lax.rem(me, fan), p, me // fan) for p in range(pairs)], seq_n // fan
    if kind == "keys":
        return [(e, e // fan, me) for e in range(seq_n)], seq_n
    if kind == "queries_back":
        return [(lax.rem(me, fan) + fan * i, i, me // fan) for i in range(seq_n // fan)], pairs
    return [(e, e, me) for e in range(seq_n)], seq_n


def exchange_kernel(kinds, seq_n, pairs, *refs):
    n = len(kinds)
    ins, outs, sems = refs[:n], refs[n : 2 * n], refs[2 * n :]
    me = lax.axis_index("seq")
    barrier = pltpu.get_barrier_semaphore()
    for d in range(1, seq_n):
        pl.semaphore_signal(
            barrier, inc=1, device_id={"seq": lax.rem(me + d, seq_n)}, device_id_type=MESH
        )
    pl.semaphore_wait(barrier, seq_n - 1)
    sent, landed = [], []
    for a, kind in enumerate(kinds):
        plan, slots = exchange_plan(kind, me, seq_n, pairs)
        send_sem, recv_sem = sems[2 * a], sems[2 * a + 1]
        for j, (target, block, slot) in enumerate(plan):
            far = pltpu.make_async_remote_copy(
                src_ref=ins[a].at[block],
                dst_ref=outs[a].at[slot],
                send_sem=send_sem.at[j],
                recv_sem=recv_sem.at[slot],
                device_id={"seq": target},
                device_id_type=MESH,
            )
            near = pltpu.make_async_copy(ins[a].at[block], outs[a].at[slot], recv_sem.at[slot])

            @pl.when(target != me)
            def _(far=far):
                far.start()

            @pl.when(target == me)
            def _(near=near):
                near.start()

            sent.append((target, far))
        for slot in range(slots):
            landed.append(
                pltpu.make_async_copy(ins[a].at[0], outs[a].at[slot], recv_sem.at[slot])
            )
    for target, far in sent:

        @pl.when(target != me)
        def _(far=far):
            far.wait_send()

    for near in landed:
        near.wait()


def exchange(kinds, arrays, pairs, collective_id):
    seq_n = lax.axis_size("seq")
    out_shape, scratch = [], []
    for kind, array in zip(kinds, arrays):
        plan, slots = exchange_plan(kind, 0, seq_n, pairs)
        out_shape.append(jax.ShapeDtypeStruct((slots,) + array.shape[1:], array.dtype))
        scratch += [pltpu.SemaphoreType.DMA((len(plan),)), pltpu.SemaphoreType.DMA((slots,))]
    return pl.pallas_call(
        functools.partial(exchange_kernel, kinds, seq_n, pairs),
        out_shape=out_shape,
        in_specs=[pl.BlockSpec(memory_space=pltpu.VMEM)] * len(arrays),
        out_specs=[pl.BlockSpec(memory_space=pltpu.VMEM)] * len(arrays),
        scratch_shapes=scratch,
        compiler_params=pltpu.CompilerParams(
            collective_id=collective_id, has_side_effects=True, vmem_limit_bytes=VMEM_LIMIT
        ),
    )(*arrays)


def line_sum_kernel(depth, chunks, rows, x_ref, out_ref, got, held, *sems):
    up_send, up_recv, down_send, down_recv = sems
    h = lax.axis_index("heads")
    barrier = pltpu.get_barrier_semaphore()
    for step in (-1, 1):

        @pl.when((h + step >= 0) & (h + step < depth))
        def _(step=step):
            pl.semaphore_signal(barrier, inc=1, device_id={"heads": h + step}, device_id_type=MESH)

    pl.semaphore_wait(barrier, jnp.where((h == 0) | (h == depth - 1), 1, 2))

    half = chunks * rows

    def place(stream, c):
        return pl.ds(pl.multiple_of((1 - stream) * half + c * rows, rows), rows)

    def up_copy(stream, c, src, to):
        return pltpu.make_async_remote_copy(
            src_ref=src,
            dst_ref=got.at[stream, c],
            send_sem=up_send.at[stream, c],
            recv_sem=up_recv.at[stream, c],
            device_id={"heads": to},
            device_id_type=MESH,
        )

    def down_copy(stream, c, to):
        return pltpu.make_async_remote_copy(
            src_ref=out_ref.at[place(stream, c)],
            dst_ref=out_ref.at[place(stream, c)],
            send_sem=down_send.at[stream, c],
            recv_sem=down_recv.at[stream, c],
            device_id={"heads": to},
            device_id_type=MESH,
        )

    def step(t, carry):
        for stream in range(2):
            pos = h if stream == 0 else depth - 1 - h
            ahead = h + 1 if stream == 0 else h - 1
            behind = h - 1 if stream == 0 else h + 1
            c = t - pos
            live = (c >= 0) & (c < chunks)

            @pl.when(live & (pos == 0))
            def _():
                up_copy(stream, c, x_ref.at[place(stream, c)], ahead).start()

            @pl.when(live & (pos > 0))
            def _():
                up_copy(stream, c, held.at[stream, c], h).wait_recv()
                total = got[stream, c].astype(F32) + x_ref[place(stream, c), :].astype(F32)

                @pl.when(pos < depth - 1)
                def _():
                    held[stream, c] = total.astype(BF16)
                    up_copy(stream, c, held.at[stream, c], ahead).start()

                @pl.when(pos == depth - 1)
                def _():
                    out_ref[place(stream, c), :] = total.astype(BF16)
                    down_copy(stream, c, behind).start()

            b = t - (2 * (depth - 1) - pos)

            @pl.when((b >= 0) & (b < chunks) & (pos < depth - 1))
            def _():
                down_copy(stream, b, h).wait_recv()

                @pl.when(pos > 0)
                def _():
                    down_copy(stream, b, behind).start()

        return carry

    lax.fori_loop(0, chunks + 2 * (depth - 1), step, 0)

    def drain(c, carry):
        for stream in range(2):
            pos = h if stream == 0 else depth - 1 - h

            @pl.when(pos < depth - 1)
            def _():
                up_copy(stream, c, held.at[stream, c], h).wait_send()

            @pl.when(pos > 0)
            def _():
                down_copy(stream, c, h).wait_send()

        return carry

    lax.fori_loop(0, chunks, drain, 0)


def line_sum(x, collective_id, rows=16):
    depth = lax.axis_size("heads")
    tokens, width = x.shape
    chunks = tokens // (2 * rows)
    sem = pltpu.SemaphoreType.DMA((2, chunks))
    return pl.pallas_call(
        functools.partial(line_sum_kernel, depth, chunks, rows),
        out_shape=jax.ShapeDtypeStruct(x.shape, BF16),
        in_specs=[pl.BlockSpec(memory_space=pltpu.VMEM)],
        out_specs=pl.BlockSpec(memory_space=pltpu.VMEM),
        scratch_shapes=[
            pltpu.VMEM((2, chunks, rows, width), BF16),
            pltpu.VMEM((2, chunks, rows, width), BF16),
            sem,
            sem,
            sem,
            sem,
        ],
        compiler_params=pltpu.CompilerParams(
            collective_id=collective_id, has_side_effects=True, vmem_limit_bytes=VMEM_LIMIT
        ),
    )(x)


def attend_kernel(block, low_ref, high_ref, q_ref, k_ref, v_ref, start_ref, place_ref, o_ref, lse_ref, vt):
    scale = HD**-0.5
    vt[...] = v_ref[...].T

    def per_query(i, carry):
        at = pl.ds(pl.multiple_of(i * block, block), block)
        q = q_ref[at, :]
        start, place = start_ref[:, at], place_ref[:, at]

        def per_key(j, state):
            top, total, acc = state
            over = pl.ds(pl.multiple_of(j * block, block), block)
            s = dot(k_ref[over, :], q, NT) * scale
            key = j * block + lax.broadcasted_iota(jnp.int32, (block, block), 0)
            s = jnp.where((key >= start) & (key <= place), s, NEG_LARGE)
            new_top = jnp.maximum(top, jnp.max(s, axis=0, keepdims=True))
            p = jnp.exp(s - new_top)
            fade = jnp.exp(top - new_top)
            total = total * fade + jnp.sum(p, axis=0, keepdims=True)
            acc = acc * fade + dot(vt[:, over], p)
            return new_top, total, acc

        begin = (
            jnp.full((1, block), -1e29, F32),
            jnp.zeros((1, block), F32),
            jnp.zeros((HD, block), F32),
        )
        top, total, acc = lax.fori_loop(low_ref[i], high_ref[i] + 1, per_key, begin)
        o_ref[at, :] = (acc / total).T.astype(BF16)
        lse_ref[:, at] = top + jnp.log(total)
        return carry

    lax.fori_loop(0, q_ref.shape[0] // block, per_query, 0)


def attend(q, k, v, low, high, start, place, block):
    smem, vmem = pl.BlockSpec(memory_space=pltpu.SMEM), pl.BlockSpec(memory_space=pltpu.VMEM)
    return pl.pallas_call(
        functools.partial(attend_kernel, block),
        out_shape=[
            jax.ShapeDtypeStruct(q.shape, BF16),
            jax.ShapeDtypeStruct((1, q.shape[0]), F32),
        ],
        in_specs=[smem, smem, vmem, vmem, vmem, vmem, vmem],
        out_specs=[vmem, vmem],
        scratch_shapes=[pltpu.VMEM((HD, k.shape[0]), BF16)],
        compiler_params=pltpu.CompilerParams(vmem_limit_bytes=VMEM_LIMIT),
    )(low, high, q, k, v, start, place)


def attend_back_kernel(
    block, low_ref, high_ref, q_ref, k_ref, v_ref, o_ref, do_ref, lse_ref, start_ref, place_ref,
    dq_ref, dk_ref, dv_ref, kt, dk_acc, dv_acc,
):
    scale = HD**-0.5
    kt[...] = k_ref[...].T
    dk_acc[...] = jnp.zeros_like(dk_acc)
    dv_acc[...] = jnp.zeros_like(dv_acc)

    def per_query(i, carry):
        at = pl.ds(pl.multiple_of(i * block, block), block)
        q, do = q_ref[at, :], do_ref[at, :]
        start, place, lse = start_ref[:, at], place_ref[:, at], lse_ref[:, at]
        delta = jnp.sum((do.astype(F32) * o_ref[at, :].astype(F32)).T, axis=0, keepdims=True)

        def per_key(j, acc):
            over = pl.ds(pl.multiple_of(j * block, block), block)
            k = k_ref[over, :]
            s = dot(k, q, NT) * scale
            key = j * block + lax.broadcasted_iota(jnp.int32, (block, block), 0)
            p = jnp.exp(jnp.where((key >= start) & (key <= place), s - lse, NEG_LARGE))
            dp = dot(v_ref[over, :], do, NT)
            ds = (p * (dp - delta)).astype(BF16)
            dv_acc[over, :] += dot(p, do)
            dk_acc[over, :] += dot(ds, q)
            return acc + dot(kt[:, over], ds)

        acc = lax.fori_loop(low_ref[i], high_ref[i] + 1, per_key, jnp.zeros((HD, block), F32))
        dq_ref[at, :] = (acc * scale).T.astype(BF16)
        return carry

    lax.fori_loop(0, q_ref.shape[0] // block, per_query, 0)
    dk_ref[...] = (dk_acc[...] * scale).astype(BF16)
    dv_ref[...] = dv_acc[...].astype(BF16)


def attend_back(q, k, v, o, do, lse, low, high, start, place, block):
    smem, vmem = pl.BlockSpec(memory_space=pltpu.SMEM), pl.BlockSpec(memory_space=pltpu.VMEM)
    return pl.pallas_call(
        functools.partial(attend_back_kernel, block),
        out_shape=[jax.ShapeDtypeStruct(a.shape, BF16) for a in (q, k, v)],
        in_specs=[smem, smem] + [vmem] * 8,
        out_specs=[vmem] * 3,
        scratch_shapes=[
            pltpu.VMEM((HD, k.shape[0]), BF16),
            pltpu.VMEM(k.shape, F32),
            pltpu.VMEM(v.shape, F32),
        ],
        compiler_params=pltpu.CompilerParams(vmem_limit_bytes=VMEM_LIMIT),
    )(low, high, q, k, v, o, do, lse, start, place)


def rope_tables(positions):
    half = HD // 2
    frequency = ROPE_BASE ** (jnp.arange(half, dtype=F32) * (-2.0 / HD))
    angles = positions.astype(F32)[..., None] * frequency
    return jnp.cos(angles)[:, :, None, :], jnp.sin(angles)[:, :, None, :]


def rotate(values, cosine, sine):
    first, second = values[..., : HD // 2], values[..., HD // 2 :]
    return jnp.concatenate([first * cosine - second * sine, second * cosine + first * sine], axis=-1)


def column_stats(w, a, b):
    aw = dot(a, w, TN)
    bf = b.astype(F32)
    ab = dot(dot(a, a, TN), b)
    wf = w.astype(F32)
    squares = jnp.sum(wf * wf, axis=0) + 2.0 * ADAPT_SCALE * jnp.sum(bf * aw, axis=0)
    squares = squares + ADAPT_SCALE * ADAPT_SCALE * jnp.sum(bf * ab, axis=0)
    return squares, aw + ADAPT_SCALE * ab


def back(e, pre, scale, magnitude, norm, h, low, w, a, b, at_v):
    sums = jnp.sum(e * pre, axis=0)
    dpre = (e * scale).astype(BF16)
    turn = magnitude * sums / (norm * norm * norm)
    tb = (turn[None, :] * b.astype(F32)).astype(BF16)
    dlow = (ADAPT_SCALE * dot(dpre, b, NT)).astype(BF16)
    dh = dot(dpre, w, NT) + dot(dlow, a, NT)
    grad_b = ADAPT_SCALE * (dot(low, dpre, TN) - at_v * turn[None, :])
    v_tb = dot(tb, w, NT) + ADAPT_SCALE * dot(dot(tb, b, NT), a, NT)
    grad_a = dot(dlow, h, TN) - ADAPT_SCALE * v_tb
    return dh, grad_a, grad_b, sums / norm


def per_device(
    tokens, attn_gain, base_qkv, adapt_a_qkv, adapt_b_qkv, magnitude_qkv, base_out, adapt_a_out,
    adapt_b_out, magnitude_out, ffn_gain, base_gu, adapt_a_gu, adapt_b_gu, magnitude_gu, base_down,
    adapt_a_down, adapt_b_down, magnitude_down, doc_lengths, cotangent,
):
    rows_n, group, width = tokens.shape
    count = rows_n * group
    local = base_qkv.shape[2]
    heads = local // HD
    pairs = rows_n * heads
    seq_n = lax.axis_size("seq")
    fan = seq_n // pairs
    length = group * seq_n
    me = lax.axis_index("seq")

    order = jnp.arange(doc_lengths.shape[1])
    doc_ends = jnp.sum(
        jnp.where(order[None, :, None] <= order[None, None, :], doc_lengths[:, :, None], 0), axis=1
    )
    doc_starts = doc_ends - doc_lengths

    def starts_of(places, ends, starts):
        inside = (places[..., None] >= starts) & (places[..., None] < ends)
        return jnp.sum(jnp.where(inside, starts, 0), axis=-1)

    mine = me * group + jnp.arange(group, dtype=jnp.int32)
    position = mine[None, :] - starts_of(
        jnp.broadcast_to(mine[None, :], (rows_n, group)), doc_ends[:, None], doc_starts[:, None]
    )
    cosine, sine = rope_tables(position)
    pair = me // fan
    row = pair // heads
    block_at = lax.rem(me, fan) + fan * jnp.arange(seq_n // fan, dtype=jnp.int32)
    place = (block_at[:, None] * group + jnp.arange(group, dtype=jnp.int32)[None, :]).reshape(-1)
    pick = (jnp.arange(rows_n) == row)[:, None]
    row_ends = jnp.sum(jnp.where(pick, doc_ends, 0), axis=0)
    row_starts = jnp.sum(jnp.where(pick, doc_starts, 0), axis=0)
    start = starts_of(place, row_ends, row_starts)
    low_block = start.reshape(-1, group)[:, 0] // group
    place, start = place[None, :], start[None, :]

    qkv_stats = [column_stats(base_qkv[i], adapt_a_qkv[i], adapt_b_qkv[i]) for i in range(3)]
    gu_stats = [column_stats(base_gu[i], adapt_a_gu[i], adapt_b_gu[i]) for i in range(2)]
    out_squares, out_at_v = column_stats(base_out, adapt_a_out, adapt_b_out)
    down_squares, down_at_v = column_stats(base_down, adapt_a_down, adapt_b_down)
    out_squares, down_squares = lax.psum((out_squares, down_squares), "heads")
    qkv_norm = [jnp.sqrt(s + COLUMN_EPS) for s, _ in qkv_stats]
    gu_norm = [jnp.sqrt(s + COLUMN_EPS) for s, _ in gu_stats]
    out_norm, down_norm = jnp.sqrt(out_squares + COLUMN_EPS), jnp.sqrt(down_squares + COLUMN_EPS)
    qkv_scale = [magnitude_qkv[i] / qkv_norm[i] for i in range(3)]
    gu_scale = [magnitude_gu[i] / gu_norm[i] for i in range(2)]
    out_scale, down_scale = magnitude_out / out_norm, magnitude_down / down_norm

    x = tokens.astype(F32).reshape(count, width)
    inverse_one = lax.rsqrt(jnp.mean(x * x, axis=-1, keepdims=True) + NORM_EPS)
    h1 = (x * inverse_one * attn_gain).astype(BF16)
    qkv_low = [dot(h1, adapt_a_qkv[i]).astype(BF16) for i in range(3)]
    qkv_pre = [
        dot(h1, base_qkv[i]) + ADAPT_SCALE * dot(qkv_low[i], adapt_b_qkv[i]) for i in range(3)
    ]
    shaped = [
        (qkv_pre[i] * qkv_scale[i]).reshape(rows_n, group, heads, HD) for i in range(3)
    ]
    shaped = [rotate(shaped[0], cosine, sine), rotate(shaped[1], cosine, sine), shaped[2]]
    q, k, v = exchange(
        ("queries", "keys", "keys"),
        [s.transpose(0, 2, 1, 3).reshape(pairs, group, HD).astype(BF16) for s in shaped],
        pairs,
        1,
    )
    q, k, v = q.reshape(-1, HD), k.reshape(length, HD), v.reshape(length, HD)
    o, lse = attend(q, k, v, low_block, block_at, start, place, group)
    [attn] = exchange(("queries_back",), [o.reshape(-1, group, HD)], pairs, 2)
    attn = attn.reshape(rows_n, heads, group, HD).transpose(0, 2, 1, 3).reshape(count, local)

    out_low = dot(attn, adapt_a_out).astype(BF16)
    out_pre = line_sum(
        (dot(attn, base_out) + ADAPT_SCALE * dot(out_low, adapt_b_out)).astype(BF16), 3
    ).astype(F32)
    x2 = x + out_pre * out_scale
    inverse_two = lax.rsqrt(jnp.mean(x2 * x2, axis=-1, keepdims=True) + NORM_EPS)
    h2 = (x2 * inverse_two * ffn_gain).astype(BF16)

    gu_low = [dot(h2, adapt_a_gu[i]).astype(BF16) for i in range(2)]
    gu_pre = [dot(h2, base_gu[i]) + ADAPT_SCALE * dot(gu_low[i], adapt_b_gu[i]) for i in range(2)]
    gate, up = gu_pre[0] * gu_scale[0], gu_pre[1] * gu_scale[1]
    sigma = jax.nn.sigmoid(gate)
    z = (gate * sigma * up).astype(BF16)
    down_low = dot(z, adapt_a_down).astype(BF16)
    down_part = (dot(z, base_down) + ADAPT_SCALE * dot(down_low, adapt_b_down)).astype(BF16)
    dy = cotangent.astype(F32).reshape(count, width)
    down_dpre = (dy * down_scale).astype(BF16)
    down_dlow = (ADAPT_SCALE * dot(down_dpre, adapt_b_down, NT)).astype(BF16)
    dz = dot(down_dpre, base_down, NT) + dot(down_dlow, adapt_a_down, NT)
    dgate = dz * up * sigma * (1.0 + gate * (1.0 - sigma))
    dup = dz * gate * sigma
    gu_back = [
        back(
            e, gu_pre[i], gu_scale[i], magnitude_gu[i], gu_norm[i], h2, gu_low[i], base_gu[i],
            adapt_a_gu[i], adapt_b_gu[i], gu_stats[i][1],
        )
        for i, e in enumerate((dgate, dup))
    ]
    dh2 = line_sum((gu_back[0][0] + gu_back[1][0]).astype(BF16), 4).astype(F32)
    down_pre = lax.psum(down_part, "heads").astype(F32)
    mixed = (x2 + down_pre * down_scale).astype(BF16)
    down_sums = jnp.sum(dy * down_pre, axis=0)
    down_turn = magnitude_down * down_sums / (down_norm * down_norm * down_norm)
    down_tb = (down_turn[None, :] * adapt_b_down.astype(F32)).astype(BF16)
    down_v_tb = dot(down_tb, base_down, NT) + ADAPT_SCALE * dot(
        dot(down_tb, adapt_b_down, NT), adapt_a_down, NT
    )
    grad_a_down = dot(down_dlow, z, TN) - ADAPT_SCALE * down_v_tb
    grad_b_down = ADAPT_SCALE * (dot(down_low, down_dpre, TN) - down_at_v * down_turn[None, :])

    scaled = dh2 * ffn_gain
    dx2 = dy + inverse_two * scaled - x2 * inverse_two**3 * jnp.mean(scaled * x2, axis=-1, keepdims=True)
    grad_ffn_gain = jnp.sum(dh2 * x2 * inverse_two, axis=0)

    dattn, grad_a_out, grad_b_out, grad_m_out = back(
        dx2, out_pre, out_scale, magnitude_out, out_norm, attn, out_low, base_out, adapt_a_out,
        adapt_b_out, out_at_v,
    )
    dattn = dattn.astype(BF16).reshape(rows_n, group, heads, HD).transpose(0, 2, 1, 3)
    [do] = exchange(("queries",), [dattn.reshape(pairs, group, HD)], pairs, 5)
    dq, dk, dv = attend_back(
        q, k, v, o, do.reshape(-1, HD), lse, low_block, block_at, start, place, group
    )
    dq, dk, dv = exchange(
        ("queries_back", "keys_back", "keys_back"),
        [dq.reshape(-1, group, HD), dk.reshape(-1, group, HD), dv.reshape(-1, group, HD)],
        pairs,
        6,
    )
    dk, dv = [jnp.sum(a.reshape(pairs, fan, group, HD).astype(F32), axis=1) for a in (dk, dv)]
    dq, dk, dv = [
        a.astype(F32).reshape(rows_n, heads, group, HD).transpose(0, 2, 1, 3) for a in (dq, dk, dv)
    ]
    grads = [
        a.reshape(count, local) for a in (rotate(dq, cosine, -sine), rotate(dk, cosine, -sine), dv)
    ]
    qkv_back = [
        back(
            grads[i], qkv_pre[i], qkv_scale[i], magnitude_qkv[i], qkv_norm[i], h1, qkv_low[i],
            base_qkv[i], adapt_a_qkv[i], adapt_b_qkv[i], qkv_stats[i][1],
        )
        for i in range(3)
    ]
    dh1 = line_sum((qkv_back[0][0] + qkv_back[1][0] + qkv_back[2][0]).astype(BF16), 7).astype(F32)
    scaled = dh1 * attn_gain
    dx = dx2 + inverse_one * scaled - x * inverse_one**3 * jnp.mean(scaled * x, axis=-1, keepdims=True)
    grad_attn_gain = jnp.sum(dh1 * x * inverse_one, axis=0)

    both = [
        jnp.stack([qkv_back[i][1] for i in range(3)]),
        jnp.stack([gu_back[i][1] for i in range(2)]),
        grad_b_out,
        grad_b_down,
    ]
    both = lax.psum([a.astype(BF16) for a in both], ("seq", "heads"))
    over_seq = [
        jnp.stack([qkv_back[i][2] for i in range(3)]),
        jnp.stack([qkv_back[i][3] for i in range(3)]),
        grad_a_out,
        grad_m_out,
        jnp.stack([gu_back[i][2] for i in range(2)]),
        jnp.stack([gu_back[i][3] for i in range(2)]),
        grad_a_down,
        down_sums / down_norm,
        grad_ffn_gain,
        grad_attn_gain,
    ]
    over_seq = lax.psum([a.astype(BF16) for a in over_seq], "seq")
    both = [a.astype(F32) for a in both]
    over_seq = [a.astype(F32) for a in over_seq]
    return (
        mixed.reshape(rows_n, group, width),
        dx.reshape(rows_n, group, width),
        over_seq[9],
        both[0].transpose(0, 2, 1),
        over_seq[0],
        over_seq[1],
        over_seq[2].T,
        both[2],
        over_seq[3],
        over_seq[8],
        both[1].transpose(0, 2, 1),
        over_seq[4],
        over_seq[5],
        over_seq[6].T,
        both[3],
        over_seq[7],
    )


def solution(mesh):
    in_specs = (
        P(None, "seq", None), P(), P(None, None, "heads"), P(), P(None, None, "heads"), P(None, "heads"),
        P("heads", None), P("heads", None), P(), P(), P(), P(None, None, "heads"), P(),
        P(None, None, "heads"), P(None, "heads"), P("heads", None), P("heads", None), P(), P(), P(),
        P(None, "seq", None),
    )
    out_specs = (
        P(None, "seq", None), P(None, "seq", None), P(), P(), P(None, None, "heads"), P(None, "heads"),
        P("heads", None), P(), P(), P(), P(), P(None, None, "heads"), P(None, "heads"),
        P("heads", None), P(), P(),
    )
    return jax.shard_map(
        per_device, mesh=mesh, in_specs=in_specs, out_specs=out_specs, check_vma=False
    )
```

```python
import functools

import jax
import jax.numpy as jnp
from jax import lax
from jax.experimental import pallas as pl
from jax.experimental.pallas import tpu as pltpu
from jax.sharding import PartitionSpec as P

HD = 128
RANK = 16
ADAPT_SCALE = 2.0
NORM_EPS = 1e-05
COLUMN_EPS = 1e-06
ROPE_BASE = 10000.0
NEG_LARGE = -1e30
F32 = jnp.float32
BF16 = jnp.bfloat16
MESH = pl.DeviceIdType.MESH
NN = (((1,), (0,)), ((), ()))
NT = (((1,), (1,)), ((), ()))
TN = (((0,), (0,)), ((), ()))
OWNERS = 8
IN_VMEM = pl.BlockSpec(memory_space=pltpu.VMEM)
IN_SMEM = pl.BlockSpec(memory_space=pltpu.SMEM)
ANYWHERE = pl.BlockSpec(memory_space=pl.ANY)


def dot(a, b, dims=NN):
    return lax.dot_general(a.astype(BF16), b.astype(BF16), dims, preferred_element_type=F32)


def shape(*dims, dtype=BF16):
    return jax.ShapeDtypeStruct(dims, dtype)


def dma(*dims):
    return pltpu.SemaphoreType.DMA(dims)


def params(mib, collective_id=None):
    more = {} if collective_id is None else {"collective_id": collective_id, "has_side_effects": True}
    return pltpu.CompilerParams(vmem_limit_bytes=mib * 2**20, **more)


def tiles(count, size, body):
    whole = count // size
    if whole:

        def step(t, carry):
            body(pl.ds(pl.multiple_of(t * size, 128), size), t)
            return carry

        lax.fori_loop(0, whole, step, 0)
    if count - whole * size:
        body(pl.ds(whole * size, count - whole * size), whole)


def row_loop(count, size, body, init=0):
    def step(t, carry):
        return body(pl.ds(pl.multiple_of(t * size, size), size), carry)

    return lax.fori_loop(0, count // size, step, init)


def fold(v):
    return jnp.sum(v.reshape(v.shape[0] // 8, 8, v.shape[1]), axis=0)


def total(v):
    return jnp.sum(v, axis=0, keepdims=True)


def greet(seq=0, heads=0, line=0):
    barrier = pltpu.get_barrier_semaphore()
    me, h = lax.axis_index("seq"), lax.axis_index("heads")
    peers = 0
    for d in range(1, seq):
        pl.semaphore_signal(barrier, inc=1, device_id={"seq": lax.rem(me + d, seq)}, device_id_type=MESH)
        peers = peers + 1
    for d in range(1, heads):
        pl.semaphore_signal(
            barrier, inc=1, device_id={"heads": lax.rem(h + d, heads)}, device_id_type=MESH
        )
        peers = peers + 1
    if line:
        for step in (-1, 1):

            @pl.when((h + step >= 0) & (h + step < line))
            def _(step=step):
                pl.semaphore_signal(barrier, inc=1, device_id={"heads": h + step}, device_id_type=MESH)

        peers = peers + jnp.where((h == 0) | (h == line - 1), 1, 2)
    pl.semaphore_wait(barrier, peers)


def remote(src, dst, send_sem, recv_sem, **where):
    return pltpu.make_async_remote_copy(
        src_ref=src, dst_ref=dst, send_sem=send_sem, recv_sem=recv_sem, device_id=where, device_id_type=MESH
    )


class Exchange:
    def __init__(self, kind, seq_n, pairs, src, dst, send_sem, recv_sem):
        fan = seq_n // pairs
        me = lax.axis_index("seq")
        self.me, self.src, self.dst, self.send_sem, self.recv_sem = me, src, dst, send_sem, recv_sem
        self.count = self.slots(kind, seq_n, pairs)
        self.target, self.block, self.slot = {
            "queries": (lambda p: p * fan + lax.rem(me, fan), lambda p: p, me // fan),
            "keys": (lambda e: e, lambda e: e // fan, me),
            "queries_back": (lambda i: lax.rem(me, fan) + fan * i, lambda i: i, me // fan),
            "keys_back": (lambda e: e, lambda e: e, me),
        }[kind]

    @staticmethod
    def slots(kind, seq_n, pairs):
        return pairs if kind.startswith("queries") else seq_n

    def copy(self, j):
        return remote(
            self.src(self.block(j)),
            self.dst(self.slot),
            self.send_sem.at[j],
            self.recv_sem.at[self.slot],
            seq=self.target(j),
        )

    def start(self):
        def one(d, carry):
            j = lax.rem(self.me + d, self.count)

            @pl.when(self.target(j) != self.me)
            def _():
                self.copy(j).start()

            @pl.when(self.target(j) == self.me)
            def _():
                pltpu.make_async_copy(
                    self.src(self.block(j)), self.dst(self.slot), self.recv_sem.at[self.slot]
                ).start()

            return carry

        lax.fori_loop(0, self.count, one, 0)

    def wait_recv(self):
        def one(j, carry):
            pltpu.make_async_copy(self.dst(j), self.dst(j), self.recv_sem.at[j]).wait()
            return carry

        lax.fori_loop(0, self.count, one, 0)

    def wait_send(self):
        def one(j, carry):
            @pl.when(self.target(j) != self.me)
            def _():
                self.copy(j).wait_send()

            return carry

        lax.fori_loop(0, self.count, one, 0)


class Line:
    def __init__(self, depth, x, out, got, held, up_send, up_recv, down_send, down_recv, lag=2):
        self.depth, self.x, self.out, self.got, self.held, self.lag = depth, x, out, got, held, lag
        self.sems = up_send, up_recv, down_send, down_recv
        self.chunks, self.rows = got.shape[1], got.shape[2]
        self.steps = self.chunks + lag * (2 * depth - 3)
        self.h = lax.axis_index("heads")

    @staticmethod
    def scratch(count, width, rows):
        chunks = count // (2 * rows)
        return [pltpu.VMEM((2, chunks, rows, width), BF16)] * 2 + [dma(2, chunks)] * 4

    def ends(self, stream):
        if stream == 0:
            return self.h, self.h + 1, self.h - 1
        return self.depth - 1 - self.h, self.h - 1, self.h + 1

    def place(self, stream, c):
        rows = self.rows
        return pl.ds(pl.multiple_of((1 - stream) * self.chunks * rows + c * rows, rows), rows)

    def up(self, stream, c, src, to):
        return remote(
            src, self.got.at[stream, c], self.sems[0].at[stream, c], self.sems[1].at[stream, c], heads=to
        )

    def down(self, stream, c, to):
        part = self.out.at[self.place(stream, c)]
        return remote(part, part, self.sems[2].at[stream, c], self.sems[3].at[stream, c], heads=to)

    def first(self):
        def one(c, carry):
            for stream in range(2):
                pos, ahead, behind = self.ends(stream)

                @pl.when(pos == 0)
                def _():
                    self.up(stream, c, self.x.at[self.place(stream, c)], ahead).start()

            return carry

        lax.fori_loop(0, self.chunks, one, 0)

    def step(self, t):
        depth, lag = self.depth, self.lag
        for stream in range(2):
            pos, ahead, behind = self.ends(stream)
            c = t - (pos - 1) * lag

            @pl.when((c >= 0) & (c < self.chunks) & (pos > 0))
            def _():
                self.up(stream, c, self.held.at[stream, c], self.h).wait_recv()
                value = self.got[stream, c].astype(F32) + self.x[self.place(stream, c), :].astype(F32)

                @pl.when(pos < depth - 1)
                def _():
                    self.held[stream, c] = value.astype(BF16)
                    self.up(stream, c, self.held.at[stream, c], ahead).start()

                @pl.when(pos == depth - 1)
                def _():
                    self.out[self.place(stream, c), :] = value.astype(BF16)
                    self.down(stream, c, behind).start()

            b = t - lag * (2 * depth - 3 - pos)

            @pl.when((b >= 0) & (b < self.chunks) & (pos < depth - 1))
            def _():
                self.down(stream, b, self.h).wait_recv()

                @pl.when(pos > 0)
                def _():
                    self.down(stream, b, behind).start()

    def run(self, start, stop):
        def one(t, carry):
            self.step(t)
            return carry

        lax.fori_loop(start, stop, one, 0)

    def drain(self):
        def one(c, carry):
            for stream in range(2):
                pos, ahead, behind = self.ends(stream)

                @pl.when(pos < self.depth - 1)
                def _():
                    self.up(stream, c, self.held.at[stream, c], self.h).wait_send()

                @pl.when(pos > 0)
                def _():
                    self.down(stream, c, self.h).wait_send()

            return carry

        lax.fori_loop(0, self.chunks, one, 0)


class Across:
    def __init__(self, depth, part, others, send_sem, recv_sem):
        self.depth, self.part, self.others, self.sems = depth, part, others, (send_sem, recv_sem)
        self.h = lax.axis_index("heads")

    def copy(self, d):
        to = lax.rem(self.h + d, self.depth)
        return remote(
            self.part, self.others.at[self.h], self.sems[0].at[d], self.sems[1].at[self.h], heads=to
        )

    def start(self):
        for d in range(1, self.depth):
            self.copy(d).start()

    def finish(self):
        value = self.part[...].astype(F32)
        for d in range(1, self.depth):
            came = self.others.at[lax.rem(self.h + d, self.depth)]
            pltpu.make_async_copy(came, came, self.sems[1].at[lax.rem(self.h + d, self.depth)]).wait()
            value = value + came[...].astype(F32)
        for d in range(1, self.depth):
            self.copy(d).wait_send()
        return value


def column_stats(w, at, b, aw):
    ab = dot(dot(at, at, NT), b)
    bf = b.astype(F32)

    def square(rows, acc):
        v = w[rows, :].astype(F32)
        return acc + fold(v * v)

    acc = row_loop(w.shape[0], 128, square, jnp.zeros((8, w.shape[1]), F32))
    squares = total(acc) + 2.0 * ADAPT_SCALE * total(bf * aw) + ADAPT_SCALE**2 * total(bf * ab)
    return squares, aw + ADAPT_SCALE * ab


def front_kernel(
    seq_n, depth, rows_n, group, heads,
    x, gain, cos, sin, at_qkv, b_qkv, m_qkv, at_out, b_out, at_down, b_down, at_gu, b_gu,
    w_qkv, w_out, w_down, w_gu,
    q, k, v, h1, pre, low, norm_qkv, v_qkv, norms, v_out, v_down, norm_gu, v_gu,
    wq, wo, wd, wg, turned, part, others, q_send, q_recv, k_send, k_recv, v_send, v_recv, z_send, z_recv, load,
):
    count, pairs = rows_n * group, rows_n * heads
    loads = [pltpu.make_async_copy(w_qkv.at[i], wq.at[i], load.at[i]) for i in range(3)]
    loads += [
        pltpu.make_async_copy(w_out, wo, load.at[3]),
        pltpu.make_async_copy(w_down, wd, load.at[4]),
        pltpu.make_async_copy(w_gu, wg, load.at[5]),
    ]
    for one in loads:
        one.start()
    greet(seq=seq_n, heads=depth)

    def norm(rows, carry):
        v = x[rows, :].astype(F32)
        inverse = lax.rsqrt(jnp.mean(v * v, axis=-1, keepdims=True) + NORM_EPS)
        h1[rows, :] = (v * inverse * gain[...]).astype(BF16)
        return carry

    row_loop(count, 32, norm)
    for i in range(3):
        h1[count + i * RANK : count + (i + 1) * RANK, :] = at_qkv[i]
    for i in range(3):
        low[i] = dot(h1[:count, :], at_qkv[i], NT).astype(BF16)
    exchanges = [
        Exchange(kind, seq_n, pairs, lambda j, i=i: turned.at[i, j], lambda j, to=to: to.at[j], *sems)
        for i, (kind, to, sems) in enumerate(
            (("queries", q, (q_send, q_recv)), ("keys", k, (k_send, k_recv)), ("keys", v, (v_send, v_recv)))
        )
    ]
    for i in range(3):
        loads[i].wait()

        def project(over, t, i=i):
            width = over.size
            r = dot(h1[...], wq[i, :, over])
            b = b_qkv[i, :, over]
            value = r[:count] + ADAPT_SCALE * dot(low[i], b)
            aw = r[count + i * RANK : count + (i + 1) * RANK]
            squares, av = column_stats(wq.at[i, :, over], at_qkv[i], b, aw)
            n = jnp.sqrt(squares + COLUMN_EPS)
            norm_qkv[i : i + 1, over] = n
            v_qkv[i, :, over] = av
            pre[i, :, over] = value.astype(BF16)
            scaled = value * (m_qkv[i : i + 1, over] / n)
            for row in range(rows_n):
                rows = slice(row * group, (row + 1) * group)
                for hh in range(width // HD):
                    part_ = scaled[rows, hh * HD : (hh + 1) * HD]
                    if i < 2:
                        part_ = part_ * cos[rows, :] + pltpu.roll(part_, HD // 2, 1) * sin[rows, :]
                    turned[i, row * heads + t * (width // HD) + hh] = part_.astype(BF16)

        tiles(heads * HD, 256, project)
        exchanges[i].start()

    part[...] = jnp.zeros_like(part)
    for row, (w, at, b, av, loaded) in enumerate(
        ((wo, at_out, b_out, v_out, loads[3]), (wd, at_down, b_down, v_down, loads[4]))
    ):
        loaded.wait()

        def stats(over, t, row=row, w=w, at=at, b=b, av=av):
            squares, value = column_stats(w.at[:, over], at[...], b[:, over], dot(at[...], w[:, over]))
            part[row : row + 1, over] = squares
            av[:, over] = value

        tiles(w.shape[1], 256, stats)
    across = Across(depth, part, others, z_send, z_recv)
    across.start()
    loads[5].wait()
    for i in range(2):

        def stats_gu(over, t, i=i):
            b = b_gu[i, :, over]
            squares, value = column_stats(wg.at[i, :, over], at_gu[i], b, dot(at_gu[i], wg[i, :, over]))
            norm_gu[i : i + 1, over] = jnp.sqrt(squares + COLUMN_EPS)
            v_gu[i, :, over] = value

        tiles(wg.shape[2], 256, stats_gu)
    norms[...] = jnp.sqrt(across.finish() + COLUMN_EPS)
    for one in exchanges:
        one.wait_recv()
    for one in exchanges:
        one.wait_send()


def front(sizes, x, gain, cos, sin, qkv, out, down, gu):
    seq_n, depth, rows_n, group, heads = sizes
    count, pairs, width = rows_n * group, rows_n * heads, x.shape[1]
    local, hidden = qkv[0].shape[2], gu[0].shape[2]
    return pl.pallas_call(
        functools.partial(front_kernel, *sizes),
        out_shape=[
            shape(pairs, group, HD), shape(seq_n, group, HD), shape(seq_n, group, HD),
            shape(count + 3 * RANK, width), shape(3, count, local), shape(3, count, RANK),
            shape(3, local, dtype=F32), shape(3, RANK, local, dtype=F32), shape(8, width, dtype=F32),
            shape(RANK, width, dtype=F32), shape(RANK, width, dtype=F32),
            shape(2, hidden, dtype=F32), shape(2, RANK, hidden, dtype=F32),
        ],
        in_specs=[IN_VMEM] * 13 + [ANYWHERE] * 4,
        out_specs=[IN_VMEM] * 13,
        scratch_shapes=[
            pltpu.VMEM(qkv[0].shape, BF16), pltpu.VMEM(out[0].shape, BF16), pltpu.VMEM(down[0].shape, BF16),
            pltpu.VMEM(gu[0].shape, BF16), pltpu.VMEM((3, pairs, group, HD), BF16),
            pltpu.VMEM((8, width), F32), pltpu.VMEM((depth, 8, width), F32),
            dma(pairs), dma(pairs), dma(seq_n), dma(seq_n), dma(seq_n), dma(seq_n), dma(depth), dma(depth), dma(6),
        ],
        compiler_params=params(56, 1),
    )(
        x, gain, cos, sin, qkv[1], qkv[2], qkv[3], out[1], out[2], down[1], down[2], gu[1], gu[2],
        qkv[0], out[0], down[0], gu[0],
    )


def attend_kernel(block, low_ref, high_ref, q_ref, k_ref, v_ref, start_ref, place_ref, o_ref, lse_ref, vt):
    scale = HD**-0.5
    vt[...] = v_ref[...].T

    def per_query(i, carry):
        at = pl.ds(pl.multiple_of(i * block, block), block)
        q = q_ref[at, :]
        start, place = start_ref[:, at], place_ref[:, at]

        def per_key(j, state):
            top, count, acc = state
            over = pl.ds(pl.multiple_of(j * block, block), block)
            s = dot(k_ref[over, :], q, NT) * scale
            key = j * block + lax.broadcasted_iota(jnp.int32, (block, block), 0)
            s = jnp.where((key >= start) & (key <= place), s, NEG_LARGE)
            new_top = jnp.maximum(top, jnp.max(s, axis=0, keepdims=True))
            p = jnp.exp(s - new_top)
            fade = jnp.exp(top - new_top)
            count = count * fade + total(p)
            acc = acc * fade + dot(vt[:, over], p)
            return new_top, count, acc

        begin = (
            jnp.full((1, block), -1e29, F32),
            jnp.zeros((1, block), F32),
            jnp.zeros((HD, block), F32),
        )
        top, count, acc = lax.fori_loop(low_ref[i], high_ref[i] + 1, per_key, begin)
        o_ref[at, :] = (acc / count).T.astype(BF16)
        lse_ref[:, at] = top + jnp.log(count)
        return carry

    lax.fori_loop(0, q_ref.shape[0] // block, per_query, 0)


def attend(q, k, v, low, high, start, place, block):
    return pl.pallas_call(
        functools.partial(attend_kernel, block),
        out_shape=[shape(*q.shape), shape(1, q.shape[0], dtype=F32)],
        in_specs=[IN_SMEM] * 2 + [IN_VMEM] * 5,
        out_specs=[IN_VMEM] * 2,
        scratch_shapes=[pltpu.VMEM((HD, k.shape[0]), BF16)],
        compiler_params=params(24),
    )(low, high, q, k, v, start, place)


def attend_back_kernel(
    block, low_ref, high_ref, q_ref, k_ref, v_ref, o_ref, do_ref, lse_ref, start_ref, place_ref,
    dq_ref, dk_ref, dv_ref, kt, dk_acc, dv_acc,
):
    scale = HD**-0.5
    kt[...] = k_ref[...].T
    dk_acc[...] = jnp.zeros_like(dk_acc)
    dv_acc[...] = jnp.zeros_like(dv_acc)

    def per_query(i, carry):
        at = pl.ds(pl.multiple_of(i * block, block), block)
        q, do = q_ref[at, :], do_ref[at, :]
        start, place, lse = start_ref[:, at], place_ref[:, at], lse_ref[:, at]
        delta = total((do.astype(F32) * o_ref[at, :].astype(F32)).T)

        def per_key(j, acc):
            over = pl.ds(pl.multiple_of(j * block, block), block)
            k = k_ref[over, :]
            s = dot(k, q, NT) * scale
            key = j * block + lax.broadcasted_iota(jnp.int32, (block, block), 0)
            p = jnp.exp(jnp.where((key >= start) & (key <= place), s - lse, NEG_LARGE))
            dp = dot(v_ref[over, :], do, NT)
            ds = (p * (dp - delta)).astype(BF16)
            dv_acc[over, :] += dot(p, do)
            dk_acc[over, :] += dot(ds, q)
            return acc + dot(kt[:, over], ds)

        acc = lax.fori_loop(low_ref[i], high_ref[i] + 1, per_key, jnp.zeros((HD, block), F32))
        dq_ref[at, :] = (acc * scale).T.astype(BF16)
        return carry

    lax.fori_loop(0, q_ref.shape[0] // block, per_query, 0)
    dk_ref[...] = (dk_acc[...] * scale).astype(BF16)
    dv_ref[...] = dv_acc[...].astype(BF16)


def attend_back(q, k, v, o, do, lse, low, high, start, place, block):
    return pl.pallas_call(
        functools.partial(attend_back_kernel, block),
        out_shape=[shape(*a.shape) for a in (q, k, v)],
        in_specs=[IN_SMEM] * 2 + [IN_VMEM] * 8,
        out_specs=[IN_VMEM] * 3,
        scratch_shapes=[
            pltpu.VMEM((HD, k.shape[0]), BF16), pltpu.VMEM(k.shape, F32), pltpu.VMEM(v.shape, F32)
        ],
        compiler_params=params(24),
    )(low, high, q, k, v, o, do, lse, start, place)


def out_kernel(
    seq_n, depth, rows_n, group, heads, o, w, at, b, out, attn, low, part, send, recv, *line_refs
):
    greet(seq=seq_n, line=depth)

    def landing(pair):
        row, head = pair // heads, lax.rem(pair, heads)
        return attn.at[
            pl.ds(pl.multiple_of(row * group, group), group), pl.ds(pl.multiple_of(head * HD, HD), HD)
        ]

    exchange = Exchange("queries_back", seq_n, rows_n * heads, lambda i: o.at[i], landing, send, recv)
    exchange.start()
    exchange.wait_recv()
    low[...] = dot(attn[...], at[...], NT).astype(BF16)

    def project(over, t):
        part[:, over] = (dot(attn[...], w[:, over]) + ADAPT_SCALE * dot(low[...], b[:, over])).astype(BF16)

    tiles(w.shape[1], 256, project)
    line = Line(depth, part, out, *line_refs)
    line.first()
    line.run(0, line.steps)
    line.drain()
    exchange.wait_send()


def out_project(sizes, o, w, at, b):
    seq_n, depth, rows_n, group, heads = sizes
    count, pairs, width = rows_n * group, rows_n * heads, w.shape[1]
    return pl.pallas_call(
        functools.partial(out_kernel, *sizes),
        out_shape=[shape(count, width), shape(count, heads * HD), shape(count, RANK)],
        in_specs=[IN_VMEM] * 4,
        out_specs=[IN_VMEM] * 3,
        scratch_shapes=[pltpu.VMEM((count, width), BF16), dma(pairs), dma(pairs)]
        + Line.scratch(count, width, 32),
        compiler_params=params(24, 2),
    )(o, w, at, b)


def ffn_kernel(
    out_pre, x, m_out, norms, gain, at_gu, b_gu, m_gu, norm_gu, v_gu, at_down, b_down, m_down, cotangent,
    w_gu, w_down,
    dh2, down_part, s_down, ga_gu, gb_gu, gm_gu, g_gain, ga_down, gb_down,
    wg, wd, h2, pre, z, dp, dpd, tmp, low, load,
):
    count = x.shape[0]
    hidden, width = wg.shape[2], wd.shape[1]
    loads = [pltpu.make_async_copy(w_gu.at[i], wg.at[i], load.at[i]) for i in range(2)]
    loads.append(pltpu.make_async_copy(w_down, wd, load.at[2]))
    for one in loads:
        one.start()
    c_out = m_out[...] / norms[0:1, :]
    c_down = m_down[...] / norms[1:2, :]

    def norm(rows, carry):
        x2 = x[rows, :].astype(F32) + out_pre[rows, :].astype(F32) * c_out
        inverse = lax.rsqrt(jnp.mean(x2 * x2, axis=-1, keepdims=True) + NORM_EPS)
        h2[rows, :] = (x2 * inverse * gain[...]).astype(BF16)
        dpd[rows, :] = (cotangent[rows, :].astype(F32) * c_down).astype(BF16)
        return carry

    row_loop(count, 32, norm)
    for i in range(2):
        low[i] = dot(h2[...], at_gu[i], NT).astype(BF16)
    loads[0].wait()
    loads[1].wait()

    def forward(over, t):
        n = over.size
        for i in range(2):
            tmp[i, :, :n] = dot(h2[...], wg[i, :, over]) + ADAPT_SCALE * dot(low[i], b_gu[i, :, over])
        scale = [m_gu[i : i + 1, over] / norm_gu[i : i + 1, over] for i in range(2)]

        def gated(rows, carry):
            g, u = tmp[0, rows, :n], tmp[1, rows, :n]
            pre[0, rows, over] = g.astype(BF16)
            pre[1, rows, over] = u.astype(BF16)
            g = g * scale[0]
            z[rows, over] = (g * jax.nn.sigmoid(g) * (u * scale[1])).astype(BF16)
            return carry

        row_loop(count, 64, gated)

    tiles(hidden, 256, forward)
    loads[2].wait()
    low_down = dot(z[...], at_down[...], NT).astype(BF16)
    s_down[...] = jnp.zeros_like(s_down)

    def down(over, t):
        value = dot(z[...], wd[:, over]) + ADAPT_SCALE * dot(low_down, b_down[:, over])
        down_part[:, over] = value.astype(BF16)
        s_down[0:1, over] = total(value * cotangent[:, over].astype(F32))
        gb_down[:, over] = ADAPT_SCALE * dot(low_down, dpd[:, over], TN)

    tiles(width, 256, down)
    dlow_down = (ADAPT_SCALE * dot(dpd[...], b_down[...], NT)).astype(BF16)

    def backward(over, t):
        n = over.size
        tmp[0, :, :n] = dot(dpd[...], wd[over, :], NT) + dot(dlow_down, at_down[:, over])
        ga_down[:, over] = dot(dlow_down, z[:, over], TN)
        scale = [m_gu[i : i + 1, over] / norm_gu[i : i + 1, over] for i in range(2)]

        def gated(rows, sums):
            dz = tmp[0, rows, :n]
            pg, pu = pre[0, rows, over].astype(F32), pre[1, rows, over].astype(F32)
            g, u = pg * scale[0], pu * scale[1]
            sigma = jax.nn.sigmoid(g)
            e_g = dz * u * sigma * (1.0 + g * (1.0 - sigma))
            e_u = dz * g * sigma
            dp[0, rows, over] = (e_g * scale[0]).astype(BF16)
            dp[1, rows, over] = (e_u * scale[1]).astype(BF16)
            return sums[0] + fold(e_g * pg), sums[1] + fold(e_u * pu)

        zero = jnp.zeros((8, n), F32)
        sums = row_loop(count, 64, gated, (zero, zero))
        for i in range(2):
            s, inverse = total(sums[i]), 1.0 / norm_gu[i : i + 1, over]
            gm_gu[i : i + 1, over] = s * inverse
            turn = m_gu[i : i + 1, over] * s * inverse * inverse * inverse
            dp[i, count : count + RANK, over] = (b_gu[i, :, over].astype(F32) * turn).astype(BF16)
            gb_gu[i, :, over] = ADAPT_SCALE * (
                dot(low[i], dp[i, :count, over], TN) - v_gu[i, :, over] * turn
            )

    tiles(hidden, 256, backward)
    both = [dot(dp[i], b_gu[i], NT) for i in range(2)]
    dlow = [(ADAPT_SCALE * both[i][:count]).astype(BF16) for i in range(2)]
    turned = [both[i][count:] for i in range(2)]

    def inputs(over, t):
        r = [dot(dp[i], wg[i, over, :], NT) for i in range(2)]
        value = r[0][:count] + r[1][:count]
        for i in range(2):
            value = value + dot(dlow[i], at_gu[i, :, over])
            v_tb = r[i][count:] + ADAPT_SCALE * dot(turned[i], at_gu[i, :, over])
            ga_gu[i, :, over] = dot(dlow[i], h2[:, over], TN) - ADAPT_SCALE * v_tb
        dh2[:, over] = value.astype(BF16)
        g_gain[:, over] = total(value * h2[:, over].astype(F32)) / gain[:, over]

    tiles(width, 256, inputs)


def ffn(out_pre, x, m_out, norms, gain, gu, m_gu, norm_gu, v_gu, down, m_down, cotangent):
    count, width = x.shape
    hidden = gu[0].shape[2]
    return pl.pallas_call(
        ffn_kernel,
        out_shape=[
            shape(count, width), shape(count, width), shape(8, width, dtype=F32),
            shape(2, RANK, width, dtype=F32), shape(2, RANK, hidden, dtype=F32), shape(2, hidden, dtype=F32),
            shape(1, width, dtype=F32), shape(RANK, hidden, dtype=F32), shape(RANK, width, dtype=F32),
        ],
        in_specs=[IN_VMEM] * 14 + [ANYWHERE] * 2,
        out_specs=[IN_VMEM] * 9,
        scratch_shapes=[
            pltpu.VMEM(gu[0].shape, BF16), pltpu.VMEM(down[0].shape, BF16), pltpu.VMEM((count, width), BF16),
            pltpu.VMEM((2, count, hidden), BF16), pltpu.VMEM((count, hidden), BF16),
            pltpu.VMEM((2, count + RANK, hidden), BF16), pltpu.VMEM((count, width), BF16),
            pltpu.VMEM((2, count, 256), F32), pltpu.VMEM((2, count, RANK), BF16), dma(3),
        ],
        compiler_params=params(60),
    )(
        out_pre, x, m_out, norms, gain, gu[1], gu[2], m_gu, norm_gu, v_gu, down[1], down[2], m_down,
        cotangent, gu[0], down[0],
    )


def middle_kernel(depth, x, s_part, out, s_out, others, z_send, z_recv, *line_refs):
    greet(heads=depth)
    across = Across(depth, s_part, others, z_send, z_recv)
    line = Line(depth, x, out, *line_refs)
    across.start()
    line.first()
    line.run(0, line.steps)
    line.drain()
    s_out[...] = across.finish()


def middle(sizes, x, s_part):
    depth = sizes[1]
    count, width = x.shape
    return pl.pallas_call(
        functools.partial(middle_kernel, depth),
        out_shape=[shape(count, width), shape(8, width, dtype=F32)],
        in_specs=[IN_VMEM] * 2,
        out_specs=[IN_VMEM] * 2,
        scratch_shapes=[pltpu.VMEM((depth, 8, width), F32), dma(depth), dma(depth)]
        + Line.scratch(count, width, 32),
        compiler_params=params(20, 3),
    )(x, s_part)


def out_back_kernel(
    seq_n, depth, rows_n, group, heads,
    dh2, x, out_pre, cotangent, gain, m_out, norms, w, at, b, v_out, attn, low,
    do, dx2, ga, gb, gm, dp, blocks, send, recv,
):
    count = rows_n * group
    greet(seq=seq_n)
    inverse_n = 1.0 / norms[0:1, :]
    c = m_out[...] * inverse_n

    def back(rows, sums):
        pre = out_pre[rows, :].astype(F32)
        x2 = x[rows, :].astype(F32) + pre * c
        inverse = lax.rsqrt(jnp.mean(x2 * x2, axis=-1, keepdims=True) + NORM_EPS)
        scaled = dh2[rows, :].astype(F32) * gain[...]
        mean = jnp.mean(scaled * x2, axis=-1, keepdims=True)
        e = cotangent[rows, :].astype(F32) + inverse * scaled - x2 * (inverse**3 * mean)
        dx2[rows, :] = e.astype(BF16)
        dp[rows, :] = (e * c).astype(BF16)
        return sums + fold(e * pre)

    s = total(row_loop(count, 16, back, jnp.zeros((8, x.shape[1]), F32)))
    turn = m_out[...] * s * inverse_n * inverse_n * inverse_n
    gm[...] = s * inverse_n
    dp[count : count + RANK, :] = (b[...].astype(F32) * turn).astype(BF16)
    both = dot(dp[...], b[...], NT)
    dlow, turned = (ADAPT_SCALE * both[:count]).astype(BF16), both[count:]
    exchange = Exchange(
        "queries", seq_n, rows_n * heads, lambda p: blocks.at[p], lambda s_: do.at[s_], send, recv
    )

    def inputs(over, t):
        r = dot(dp[...], w[over, :], NT)
        value = (r[:count] + dot(dlow, at[:, over])).astype(BF16)
        for row in range(rows_n):
            for hh in range(over.size // HD):
                blocks[row * heads + t * (over.size // HD) + hh] = value[
                    row * group : (row + 1) * group, hh * HD : (hh + 1) * HD
                ]
        ga[:, over] = dot(dlow, attn[:, over], TN) - ADAPT_SCALE * (
            r[count:] + ADAPT_SCALE * dot(turned, at[:, over])
        )

    tiles(heads * HD, 256, inputs)
    exchange.start()

    gb[...] = ADAPT_SCALE * (dot(low[...], dp[:count, :], TN) - v_out[...] * turn)
    exchange.wait_recv()
    exchange.wait_send()


def out_back(sizes, dh2, x, out_pre, cotangent, gain, m_out, norms, w, at, b, v_out, attn, low):
    seq_n, depth, rows_n, group, heads = sizes
    count, pairs, width = rows_n * group, rows_n * heads, x.shape[1]
    return pl.pallas_call(
        functools.partial(out_back_kernel, *sizes),
        out_shape=[
            shape(pairs, group, HD), shape(count, width), shape(RANK, heads * HD, dtype=F32),
            shape(RANK, width, dtype=F32), shape(1, width, dtype=F32),
        ],
        in_specs=[IN_VMEM] * 13,
        out_specs=[IN_VMEM] * 5,
        scratch_shapes=[
            pltpu.VMEM((count + RANK, width), BF16), pltpu.VMEM((pairs, group, HD), BF16), dma(pairs), dma(pairs)
        ],
        compiler_params=params(40, 4),
    )(dh2, x, out_pre, cotangent, gain, m_out, norms, w, at, b, v_out, attn, low)


def last_kernel(
    seq_n, depth, rows_n, group, heads,
    dq, dk, dv, cos, sin, h1, pre, low, gain, at, b, m, norm, v_qkv,
    ga_gu, gb_out, gb_down, g_gain2, gm_out, s_down, ga_out, gb_gu, gm_gu, ga_down,
    m_down, norms, at_down, b_down, v_down, w_qkv, w_down,
    dh1, wide, local, hid,
    wq, wd, gq, gk, gv, dp, part, wide_in, local_in, hid_in, wide_got, local_got, hid_got,
    piece, pieces, done, q_send, q_recv, k_send, k_recv, v_send, v_recv, load,
    r_send, r_recv, g_send, g_recv, z_send, z_recv, *line_refs,
):
    count, pairs, width = rows_n * group, rows_n * heads, h1.shape[1]
    fan, me = seq_n // pairs, lax.axis_index("seq")
    loads = [pltpu.make_async_copy(w_qkv, wq, load.at[0]), pltpu.make_async_copy(w_down, wd, load.at[1])]
    for one in loads:
        one.start()
    greet(seq=seq_n, heads=depth)
    exchanges = [
        Exchange(kind, seq_n, pairs, lambda j, a=a: a.at[j], lambda j, to=to: to.at[j], *sems)
        for kind, a, to, sems in (
            ("queries_back", dq, gq, (q_send, q_recv)),
            ("keys_back", dk, gk, (k_send, k_recv)),
            ("keys_back", dv, gv, (v_send, v_recv)),
        )
    ]
    for one in exchanges:
        one.start()

    wide_in[...] = jnp.zeros_like(wide_in)
    local_in[...] = jnp.zeros_like(local_in)
    hid_in[...] = jnp.zeros_like(hid_in)
    inverse_n = 1.0 / norms[1:2, :]
    s = s_down[0:1, :]
    turn = m_down[...] * s * inverse_n * inverse_n * inverse_n
    tb = (b_down[...].astype(F32) * turn).astype(BF16)
    loads[1].wait()
    v_tb = ADAPT_SCALE * dot(dot(tb, b_down[...], NT), at_down[...])
    share = 1.0 / depth
    for i in range(2):
        wide_in[(3 + i) * RANK : (4 + i) * RANK, :] = ga_gu[i].astype(BF16)
        hid_in[i * RANK : (i + 1) * RANK, :] = gb_gu[i].astype(BF16)
    wide_in[5 * RANK : 6 * RANK, :] = gb_out[...].astype(BF16)
    wide_in[6 * RANK : 7 * RANK, :] = (gb_down[...] - ADAPT_SCALE * v_down[...] * turn).astype(BF16)
    hid_in[3 * RANK : 4 * RANK, :] = (ga_down[...] - ADAPT_SCALE * (v_tb + dot(tb, wd[...], NT))).astype(BF16)
    local_in[4 * RANK : 5 * RANK, :] = ga_out[...].astype(BF16)
    hid_in[2 * RANK : 3 * RANK, :] = jnp.concatenate(
        [gm_gu[...], jnp.zeros((RANK - 2, hid_in.shape[1]), F32)], axis=0
    ).astype(BF16)

    sums = [None] * 3
    loads[0].wait()
    for i in range(3):
        exchanges[i].wait_recv()
        came = (gq, gk, gv)[i]
        for head in range(heads):
            cols = slice(head * HD, (head + 1) * HD)
            n = norm[i : i + 1, cols]
            c = m[i : i + 1, cols] / n
            s = jnp.zeros((1, HD), F32)
            for row in range(rows_n):
                rows = slice(row * group, (row + 1) * group)
                if i == 0:
                    e = came[row * heads + head].astype(F32)
                else:
                    e = came[(row * heads + head) * fan].astype(F32)
                    for g in range(1, fan):
                        e = e + came[(row * heads + head) * fan + g].astype(F32)
                if i < 2:
                    e = e * cos[rows, :] - pltpu.roll(e, HD // 2, 1) * sin[rows, :]
                s = s + total(e * pre[i, rows, cols].astype(F32))
                dp[i, rows, cols] = (e * c).astype(BF16)
            turn = m[i : i + 1, cols] * s / (n * n * n)
            dp[i, count : count + RANK, cols] = (b[i, :, cols].astype(F32) * turn).astype(BF16)
            local_in[i * RANK : (i + 1) * RANK, cols] = (
                ADAPT_SCALE * (dot(low[i], dp[i, :count, cols], TN) - v_qkv[i, :, cols] * turn)
            ).astype(BF16)
            sums[i] = [s / n] if head == 0 else sums[i] + [s / n]
    local_in[3 * RANK : 4 * RANK, :] = jnp.concatenate(
        [jnp.concatenate(one, axis=1) for one in sums]
        + [jnp.zeros((RANK - 3, heads * HD), F32)], axis=0
    ).astype(BF16)
    both = [dot(dp[i], b[i], NT) for i in range(3)]
    dlow = [(ADAPT_SCALE * both[i][:count]).astype(BF16) for i in range(3)]
    turned = [both[i][count:] for i in range(3)]

    def inputs(over, t):
        value = jnp.zeros((count, over.size), F32)
        for i in range(3):
            r = dot(dp[i], wq[i, over, :], NT)
            value = value + r[:count] + dot(dlow[i], at[i, :, over])
            wide_in[i * RANK : (i + 1) * RANK, over] = (
                dot(dlow[i], h1[:count, over], TN)
                - ADAPT_SCALE * (r[count:] + ADAPT_SCALE * dot(turned[i], at[i, :, over]))
            ).astype(BF16)
        part[:, over] = value.astype(BF16)
        g_gain1 = total(value * h1[:count, over].astype(F32)) / gain[:, over]
        wide_in[7 * RANK : 8 * RANK, over] = jnp.concatenate(
            [
                g_gain1, g_gain2[:, over], gm_out[:, over] * share,
                s_down[0:1, over] / norms[1:2, over] * share,
                jnp.zeros((RANK - 4, over.size), F32),
            ], axis=0,
        ).astype(BF16)

    tiles(width, 256, inputs)
    line = Line(depth, part, dh1, *line_refs)
    line.first()

    spread = seq_n // OWNERS
    slabs = (
        (wide_in, wide_got, wide, lambda j: j), (local_in, local_got, local, lambda j: j),
        (hid_in, hid_got, hid, lambda j: OWNERS - 1 - j),
    )
    own = me // spread
    chosen = lax.rem(me, spread) == 0

    def rows_of(j):
        return pl.ds(pl.multiple_of(j * RANK, RANK), RANK)

    def to_owner(i, j):
        src, got, _, owner = slabs[i]
        return remote(
            src.at[rows_of(j)], got.at[me], r_send.at[i, j], r_recv.at[i, me], seq=owner(j) * spread
        )

    def from_owner(i, j, target):
        result = slabs[i][2]
        return remote(
            done.at[i, :, : result.shape[1]], result.at[rows_of(j)], g_send.at[i, target], g_recv.at[i, j], seq=target
        )

    for i, (src, got, result, owner) in enumerate(slabs):
        for j in range(src.shape[0] // RANK):

            @pl.when(me != owner(j) * spread)
            def _(i=i, j=j):
                to_owner(i, j).start()

            @pl.when(me == owner(j) * spread)
            def _(src=src, got=got, i=i, j=j):
                pltpu.make_async_copy(src.at[rows_of(j)], got.at[me], r_recv.at[i, me]).start()

    line.run(0, 4)
    across = Across(depth, piece, pieces, z_send, z_recv)
    blocks_n = [slab[0].shape[0] // RANK for slab in slabs]
    owns = [chosen & (slab[3](own) < n) for slab, n in zip(slabs, blocks_n)]
    for i, (src, got, result, owner) in enumerate(slabs):

        @pl.when(owns[i])
        def _(i=i, got=got, result=result):
            def add(s_, acc):
                pltpu.make_async_copy(got.at[s_], got.at[s_], r_recv.at[i, s_]).wait()
                return acc + got[s_].astype(F32)

            value = lax.fori_loop(0, seq_n, add, jnp.zeros((RANK, result.shape[1]), F32))
            if i == 0:
                piece[...] = value.astype(BF16)
                across.start()
            else:
                done[i, :, : result.shape[1]] = value.astype(BF16)

    line.run(4, 8)

    @pl.when(owns[0])
    def _():
        done[0, :, :] = across.finish().astype(BF16)

    for i, (src, got, result, owner) in enumerate(slabs):

        @pl.when(owns[i])
        def _(i=i, result=result, owner=owner):
            mine = owner(own)

            def give(d, carry):
                from_owner(i, mine, lax.rem(me + d, seq_n)).start()
                return carry

            lax.fori_loop(1, seq_n, give, 0)
            pltpu.make_async_copy(
                done.at[i, :, : result.shape[1]], result.at[rows_of(mine)], g_recv.at[i, mine]
            ).start()

    line.run(8, line.steps)
    line.drain()
    for one in exchanges:
        one.wait_send()
    for i, (src, got, result, owner) in enumerate(slabs):
        for j in range(blocks_n[i]):

            @pl.when(me != owner(j) * spread)
            def _(i=i, j=j):
                to_owner(i, j).wait_send()

            pltpu.make_async_copy(result.at[rows_of(j)], result.at[rows_of(j)], g_recv.at[i, j]).wait()

        @pl.when(owns[i])
        def _(i=i, owner=owner):
            def given(d, carry):
                from_owner(i, owner(own), lax.rem(me + d, seq_n)).wait_send()
                return carry

            lax.fori_loop(1, seq_n, given, 0)


def last(sizes, ins, qkv_w, w_down):
    seq_n, depth, rows_n, group, heads = sizes
    count, pairs, width = rows_n * group, rows_n * heads, w_down.shape[1]
    local, hidden = qkv_w.shape[2], w_down.shape[0]
    blocks = {width: 8, local: 5, hidden: 4}
    slabs = [(n * RANK, w) for w, n in blocks.items()]
    return pl.pallas_call(
        functools.partial(last_kernel, *sizes),
        out_shape=[shape(count, width)] + [shape(*s) for s in slabs],
        in_specs=[IN_VMEM] * len(ins) + [ANYWHERE] * 2,
        out_specs=[IN_VMEM] * 4,
        scratch_shapes=[
            pltpu.VMEM(qkv_w.shape, BF16), pltpu.VMEM(w_down.shape, BF16),
            pltpu.VMEM((pairs, group, HD), BF16), pltpu.VMEM((seq_n, group, HD), BF16),
            pltpu.VMEM((seq_n, group, HD), BF16), pltpu.VMEM((3, count + RANK, local), BF16),
            pltpu.VMEM((count, width), BF16),
        ]
        + [pltpu.VMEM(s, BF16) for s in slabs]
        + [pltpu.VMEM((seq_n, RANK, s[1]), BF16) for s in slabs]
        + [
            pltpu.VMEM((RANK, width), BF16), pltpu.VMEM((depth, RANK, width), BF16), pltpu.VMEM((3, RANK, width), BF16),
            dma(pairs), dma(pairs), dma(seq_n), dma(seq_n), dma(seq_n), dma(seq_n), dma(2),
            dma(3, 8), dma(3, seq_n), dma(3, seq_n), dma(3, 8), dma(depth), dma(depth),
        ]
        + Line.scratch(count, width, 32),
        compiler_params=params(60, 5),
    )(*ins, qkv_w, w_down)


def per_device(
    tokens, attn_gain, base_qkv, adapt_a_qkv, adapt_b_qkv, magnitude_qkv, base_out, adapt_a_out,
    adapt_b_out, magnitude_out, ffn_gain, base_gu, adapt_a_gu, adapt_b_gu, magnitude_gu, base_down,
    adapt_a_down, adapt_b_down, magnitude_down, doc_lengths, cotangent,
):
    rows_n, group, width = tokens.shape
    count = rows_n * group
    local = base_qkv.shape[2]
    heads = local // HD
    pairs = rows_n * heads
    seq_n, depth = lax.axis_size("seq"), lax.axis_size("heads")
    sizes = (seq_n, depth, rows_n, group, heads)
    fan = seq_n // pairs
    length = group * seq_n
    me = lax.axis_index("seq")

    order = jnp.arange(doc_lengths.shape[1])
    doc_ends = jnp.sum(
        jnp.where(order[None, :, None] <= order[None, None, :], doc_lengths[:, :, None], 0), axis=1
    )
    doc_starts = doc_ends - doc_lengths

    def starts_of(places, ends, starts):
        inside = (places[..., None] >= starts) & (places[..., None] < ends)
        return jnp.sum(jnp.where(inside, starts, 0), axis=-1)

    mine = me * group + jnp.arange(group, dtype=jnp.int32)
    position = mine[None, :] - starts_of(
        jnp.broadcast_to(mine[None, :], (rows_n, group)), doc_ends[:, None], doc_starts[:, None]
    )
    half = HD // 2
    frequency = ROPE_BASE ** (jnp.arange(half, dtype=F32) * (-2.0 / HD))
    angles = position.reshape(count, 1).astype(F32) * frequency
    cos, sin = jnp.cos(angles), jnp.sin(angles)
    cos, sin = jnp.concatenate([cos, cos], axis=1), jnp.concatenate([-sin, sin], axis=1)
    row = me // fan // heads
    block_at = lax.rem(me, fan) + fan * jnp.arange(pairs, dtype=jnp.int32)
    place = (block_at[:, None] * group + jnp.arange(group, dtype=jnp.int32)[None, :]).reshape(-1)
    pick = (jnp.arange(rows_n) == row)[:, None]
    row_ends = jnp.sum(jnp.where(pick, doc_ends, 0), axis=0)
    row_starts = jnp.sum(jnp.where(pick, doc_starts, 0), axis=0)
    start = starts_of(place, row_ends, row_starts)
    low_block = start.reshape(-1, group)[:, 0] // group
    place, start = place[None, :], start[None, :]

    x = tokens.reshape(count, width)
    dy = cotangent.reshape(count, width)
    gain1, gain2 = attn_gain[None, :], ffn_gain[None, :]
    m_out, m_down = magnitude_out[None, :], magnitude_down[None, :]
    at_qkv, at_gu = adapt_a_qkv.transpose(0, 2, 1), adapt_a_gu.transpose(0, 2, 1)
    at_out, at_down = adapt_a_out.T, adapt_a_down.T

    q, k, v, h1, pre, low, norm_qkv, v_qkv, norms, v_out, v_down, norm_gu, v_gu = front(
        sizes, x, gain1, cos, sin, (base_qkv, at_qkv, adapt_b_qkv, magnitude_qkv), (base_out, at_out, adapt_b_out),
        (base_down, at_down, adapt_b_down), (base_gu, at_gu, adapt_b_gu),
    )
    q, k, v = q.reshape(-1, HD), k.reshape(length, HD), v.reshape(length, HD)
    o, lse = attend(q, k, v, low_block, block_at, start, place, group)
    out_pre, attn, low_out = out_project(sizes, o.reshape(-1, group, HD), base_out, at_out, adapt_b_out)
    dh2, down_part, s_down, ga_gu, gb_gu, gm_gu, g_gain2, ga_down, gb_down = ffn(
        out_pre, x, m_out, norms, gain2, (base_gu, at_gu, adapt_b_gu), magnitude_gu, norm_gu, v_gu,
        (base_down, at_down, adapt_b_down), m_down, dy,
    )
    dh2, s_down = middle(sizes, dh2, s_down)
    down_part, dh2 = lax.optimization_barrier((down_part, dh2))
    down_pre = lax.psum(down_part, "heads")
    do, dx2, ga_out, gb_out, gm_out = out_back(
        sizes, dh2, x, out_pre, dy, gain2, m_out, norms, base_out, at_out, adapt_b_out, v_out, attn, low_out
    )
    dq, dk, dv = attend_back(
        q, k, v, o, do.reshape(-1, HD), lse, low_block, block_at, start, place, group
    )
    dh1, wide, narrow, hid = last(
        sizes,
        (
            dq.reshape(-1, group, HD), dk.reshape(-1, group, HD), dv.reshape(-1, group, HD), cos, sin, h1, pre,
            low, gain1, at_qkv, adapt_b_qkv, magnitude_qkv, norm_qkv, v_qkv, ga_gu, gb_out, gb_down, g_gain2,
            gm_out, s_down, ga_out, gb_gu, gm_gu, ga_down, m_down, norms, at_down, adapt_b_down, v_down,
        ),
        base_qkv,
        base_down,
    )
    xf = x.astype(F32)
    inverse_one = lax.rsqrt(jnp.mean(xf * xf, axis=-1, keepdims=True) + NORM_EPS)
    scaled = dh1.astype(F32) * gain1
    dx = dx2.astype(F32) + inverse_one * scaled
    dx = dx - xf * inverse_one**3 * jnp.mean(scaled * xf, axis=-1, keepdims=True)
    x2 = xf + out_pre.astype(F32) * (m_out / norms[0:1])
    mixed = (x2 + down_pre.astype(F32) * (m_down / norms[1:2])).astype(BF16)
    wide, narrow, hid = wide.astype(F32), narrow.astype(F32), hid.astype(F32)
    return (
        mixed.reshape(rows_n, group, width),
        dx.reshape(rows_n, group, width),
        wide[112],
        wide[:48].reshape(3, RANK, width).transpose(0, 2, 1),
        narrow[:48].reshape(3, RANK, local),
        narrow[48:51],
        narrow[64:80].T,
        wide[80:96],
        wide[114],
        wide[113],
        wide[48:80].reshape(2, RANK, width).transpose(0, 2, 1),
        hid[:32].reshape(2, RANK, -1),
        hid[32:34],
        hid[48:64].T,
        wide[96:112],
        wide[115],
    )


def solution(mesh):
    in_specs = (
        P(None, "seq", None), P(), P(None, None, "heads"), P(), P(None, None, "heads"), P(None, "heads"),
        P("heads", None), P("heads", None), P(), P(), P(), P(None, None, "heads"), P(),
        P(None, None, "heads"), P(None, "heads"), P("heads", None), P("heads", None), P(), P(), P(),
        P(None, "seq", None),
    )
    out_specs = (
        P(None, "seq", None), P(None, "seq", None), P(), P(), P(None, None, "heads"), P(None, "heads"),
        P("heads", None), P(), P(), P(), P(), P(None, None, "heads"), P(None, "heads"),
        P("heads", None), P(), P(),
    )
    return jax.shard_map(
        per_device, mesh=mesh, in_specs=in_specs, out_specs=out_specs, check_vma=False
    )
```

```python
import functools

import jax
import jax.numpy as jnp
from jax import lax
from jax.experimental import pallas as pl
from jax.experimental.pallas import tpu as pltpu
from jax.sharding import PartitionSpec as P

HD = 128
RANK = 16
ADAPT_SCALE = 2.0
NORM_EPS = 1e-05
COLUMN_EPS = 1e-06
ROPE_BASE = 10000.0
NEG_LARGE = -1e30
F32 = jnp.float32
BF16 = jnp.bfloat16
MESH = pl.DeviceIdType.MESH
NN = (((1,), (0,)), ((), ()))
NT = (((1,), (1,)), ((), ()))
TN = (((0,), (0,)), ((), ()))
OWNERS = 8
CHUNK = 16
LAG = 2
LEAD = 4
NEAR_LATE = 1
EARLY = 8
WIDE = 512
IN_VMEM = pl.BlockSpec(memory_space=pltpu.VMEM)
IN_SMEM = pl.BlockSpec(memory_space=pltpu.SMEM)
ANYWHERE = pl.BlockSpec(memory_space=pl.ANY)


def dot(a, b, dims=NN):
    return lax.dot_general(a.astype(BF16), b.astype(BF16), dims, preferred_element_type=F32)


def shape(*dims, dtype=BF16):
    return jax.ShapeDtypeStruct(dims, dtype)


def dma(*dims):
    return pltpu.SemaphoreType.DMA(dims)


def params(mib, collective_id=None):
    more = {} if collective_id is None else {"collective_id": collective_id, "has_side_effects": True}
    return pltpu.CompilerParams(vmem_limit_bytes=mib * 2**20, **more)


def tiles(count, size, body, tick=lambda t: None):
    whole = count // size
    if whole:

        def step(t, carry):
            body(pl.ds(pl.multiple_of(t * size, 128), size), t)
            tick(t)
            return carry

        lax.fori_loop(0, whole, step, 0)
    if count - whole * size:
        body(pl.ds(whole * size, count - whole * size), whole)
        tick(whole)


def row_loop(count, size, body, init=0):
    def step(t, carry):
        return body(pl.ds(pl.multiple_of(t * size, size), size), carry)

    return lax.fori_loop(0, count // size, step, init)


def fold(v):
    return jnp.sum(v.reshape(v.shape[0] // 8, 8, v.shape[1]), axis=0)


def total(v):
    return jnp.sum(v, axis=0, keepdims=True)


def greet(seq=0, heads=0, line=0):
    barrier = pltpu.get_barrier_semaphore()
    me, h = lax.axis_index("seq"), lax.axis_index("heads")
    peers = 0
    for d in range(1, seq):
        pl.semaphore_signal(barrier, inc=1, device_id={"seq": lax.rem(me + d, seq)}, device_id_type=MESH)
        peers = peers + 1
    for d in range(1, heads):
        pl.semaphore_signal(
            barrier, inc=1, device_id={"heads": lax.rem(h + d, heads)}, device_id_type=MESH
        )
        peers = peers + 1
    if line:
        for step in (-1, 1):

            @pl.when((h + step >= 0) & (h + step < line))
            def _(step=step):
                pl.semaphore_signal(barrier, inc=1, device_id={"heads": h + step}, device_id_type=MESH)

        peers = peers + jnp.where((h == 0) | (h == line - 1), 1, 2)
    pl.semaphore_wait(barrier, peers)


def remote(src, dst, send_sem, recv_sem, **where):
    return pltpu.make_async_remote_copy(
        src_ref=src, dst_ref=dst, send_sem=send_sem, recv_sem=recv_sem, device_id=where, device_id_type=MESH
    )


class Exchange:
    def __init__(self, kind, seq_n, pairs, src, dst, send_sem, recv_sem):
        fan = seq_n // pairs
        me = lax.axis_index("seq")
        self.me, self.src, self.dst, self.send_sem, self.recv_sem = me, src, dst, send_sem, recv_sem
        self.count = self.slots(kind, seq_n, pairs)
        self.target, self.block, self.slot = {
            "queries": (lambda p: p * fan + lax.rem(me, fan), lambda p: p, me // fan),
            "keys": (lambda e: e, lambda e: e // fan, me),
            "queries_back": (lambda i: lax.rem(me, fan) + fan * i, lambda i: i, me // fan),
            "keys_back": (lambda e: e, lambda e: e, me),
        }[kind]

    @staticmethod
    def slots(kind, seq_n, pairs):
        return pairs if kind.startswith("queries") else seq_n

    def copy(self, j):
        return remote(
            self.src(self.block(j)),
            self.dst(self.slot),
            self.send_sem.at[j],
            self.recv_sem.at[self.slot],
            seq=self.target(j),
        )

    def start(self, low=0, high=None):
        number = (self.count if high is None else high) - low

        def one(d, carry):
            j = low + lax.rem(self.me + d, number)

            @pl.when(self.target(j) != self.me)
            def _():
                self.copy(j).start()

            @pl.when(self.target(j) == self.me)
            def _():
                pltpu.make_async_copy(
                    self.src(self.block(j)), self.dst(self.slot), self.recv_sem.at[self.slot]
                ).start()

            return carry

        lax.fori_loop(0, number, one, 0)

    def wait_recv(self):
        def one(j, carry):
            pltpu.make_async_copy(self.dst(j), self.dst(j), self.recv_sem.at[j]).wait()
            return carry

        lax.fori_loop(0, self.count, one, 0)

    def wait_send(self):
        def one(j, carry):
            @pl.when(self.target(j) != self.me)
            def _():
                self.copy(j).wait_send()

            return carry

        lax.fori_loop(0, self.count, one, 0)


class Line:
    def __init__(self, x, out, got, near, held, *sems, per=None, base=0, lead=None):
        self.x, self.out, self.got, self.near, self.held = x, out, got, near, held
        self.far_send, self.far_recv, self.near_send, self.near_recv, self.down_send, self.down_recv = sems
        self.chunks, self.rows = got.shape[1], got.shape[2]
        self.per, self.base = per or self.chunks, base
        self.lead = self.chunks if lead is None else lead
        self.steps = self.done(self.chunks)
        self.h = lax.axis_index("heads")

    @staticmethod
    def done(chunks):
        return chunks + 3 * LAG

    @staticmethod
    def scratch(count, width, rows):
        chunks = count // (2 * rows)
        one = pltpu.VMEM((chunks, rows, width), BF16)
        return [
            pltpu.VMEM((2, chunks, rows, width), BF16), one, one,
            dma(2, chunks), dma(2, chunks), dma(chunks), dma(chunks), dma(2, 2, chunks), dma(2, chunks),
        ]

    def ends(self, stream):
        if stream == 0:
            return self.h, self.h + 1, self.h - 1
        return 3 - self.h, self.h - 1, self.h + 1

    def place(self, stream, c):
        rows, per = self.rows, self.per
        first = self.base + ((c // per) * 2 + (1 - stream)) * (per * rows) + lax.rem(c, per) * rows
        return pl.ds(pl.multiple_of(first, rows), rows)

    def far(self, stream, c, src, to):
        return remote(
            src, self.got.at[stream, c], self.far_send.at[stream, c], self.far_recv.at[stream, c], heads=to
        )

    def close(self, stream, c, to):
        return remote(
            self.x.at[self.place(stream, c)], self.near.at[c], self.near_send.at[c], self.near_recv.at[c], heads=to
        )

    def down(self, stream, way, c, to):
        part = self.out.at[self.place(stream, c)]
        return remote(part, part, self.down_send.at[stream, way, c], self.down_recv.at[stream, c], heads=to)

    def give(self, c):
        for stream in range(2):
            pos, ahead, behind = self.ends(stream)

            @pl.when((pos == 0) & (c < self.chunks))
            def _():
                self.far(stream, c, self.x.at[self.place(stream, c)], ahead).start()

        c = c - NEAR_LATE
        for stream in range(2):
            pos, ahead, behind = self.ends(stream)

            @pl.when((pos == 3) & (c >= 0) & (c < self.chunks))
            def _():
                self.close(stream, c, behind).start()

    def first(self):
        def one(c, carry):
            self.give(c)
            return carry

        lax.fori_loop(0, self.lead, one, 0)

    def step(self, t):
        self.give(t + self.lead)
        for stream in range(2):
            pos, ahead, behind = self.ends(stream)

            @pl.when((pos == 1) & (t < self.chunks))
            def _():
                self.far(stream, t, self.held.at[t], self.h).wait_recv()
                at = self.place(stream, t)
                self.held[t] = (self.got[stream, t].astype(F32) + self.x[at, :].astype(F32)).astype(BF16)
                self.far(stream, t, self.held.at[t], ahead).start()

        for stream in range(2):
            pos, ahead, behind = self.ends(stream)
            c = t - LAG

            @pl.when((pos == 2) & (c >= 0) & (c < self.chunks))
            def _():
                self.far(stream, c, self.held.at[c], self.h).wait_recv()
                self.close(stream, c, self.h).wait_recv()
                at = self.place(stream, c)
                value = self.got[stream, c].astype(F32) + self.near[c].astype(F32) + self.x[at, :].astype(F32)
                self.out[at, :] = value.astype(BF16)
                self.down(stream, 0, c, behind).start()
                self.down(stream, 1, c, ahead).start()

        for stream in range(2):
            pos, ahead, behind = self.ends(stream)
            b = t - jnp.where(pos == 0, 3 * LAG, 2 * LAG)

            @pl.when((pos != 2) & (b >= 0) & (b < self.chunks))
            def _():
                self.down(stream, 0, b, self.h).wait_recv()

                @pl.when(pos == 1)
                def _():
                    self.down(stream, 0, b, behind).start()

    def run(self, start, stop):
        def one(t, carry):
            self.step(t)
            return carry

        lax.fori_loop(start, stop, one, 0)

    def spread(self, start, stop, ticks):
        def tick(k):
            now, then = (k * (stop - start)) // ticks, ((k + 1) * (stop - start)) // ticks
            self.run(start + now, start + then)

        return tick

    def drain(self):
        def one(c, carry):
            for stream in range(2):
                pos, ahead, behind = self.ends(stream)

                @pl.when(pos <= 1)
                def _():
                    self.far(stream, c, self.held.at[c], self.h).wait_send()

                @pl.when(pos == 3)
                def _():
                    self.close(stream, c, self.h).wait_send()

                @pl.when((pos == 1) | (pos == 2))
                def _():
                    self.down(stream, 0, c, self.h).wait_send()

                @pl.when(pos == 2)
                def _():
                    self.down(stream, 1, c, self.h).wait_send()

            return carry

        lax.fori_loop(0, self.chunks, one, 0)


class Across:
    def __init__(self, depth, part, others, send_sem, recv_sem):
        self.depth, self.part, self.others, self.sems = depth, part, others, (send_sem, recv_sem)
        self.h = lax.axis_index("heads")

    def copy(self, d):
        to = lax.rem(self.h + d, self.depth)
        return remote(
            self.part, self.others.at[self.h], self.sems[0].at[d], self.sems[1].at[self.h], heads=to
        )

    def start(self):
        for d in range(1, self.depth):
            self.copy(d).start()

    def finish(self):
        value = self.part[...].astype(F32)
        for d in range(1, self.depth):
            came = self.others.at[lax.rem(self.h + d, self.depth)]
            pltpu.make_async_copy(came, came, self.sems[1].at[lax.rem(self.h + d, self.depth)]).wait()
            value = value + came[...].astype(F32)
        for d in range(1, self.depth):
            self.copy(d).wait_send()
        return value


def column_stats(w, at, b, aw):
    ab = dot(dot(at, at, NT), b)
    bf = b.astype(F32)

    def square(rows, acc):
        v = w[rows, :].astype(F32)
        return acc + fold(v * v)

    acc = row_loop(w.shape[0], 128, square, jnp.zeros((8, w.shape[1]), F32))
    squares = total(acc) + 2.0 * ADAPT_SCALE * total(bf * aw) + ADAPT_SCALE**2 * total(bf * ab)
    return squares, aw + ADAPT_SCALE * ab


def front_kernel(
    seq_n, depth, rows_n, group, heads,
    x, gain, cos, sin, at_qkv, b_qkv, m_qkv, at_out, b_out, at_down, b_down, at_gu, b_gu,
    w_qkv, w_out, w_down, w_gu,
    q, k, v, h1, pre, low, norm_qkv, v_qkv, norms, v_out, v_down, norm_gu, v_gu,
    wq, wo, wd, wg, turned, part, others, q_send, q_recv, k_send, k_recv, v_send, v_recv, z_send, z_recv, load,
):
    count, pairs = rows_n * group, rows_n * heads
    loads = [pltpu.make_async_copy(w_qkv.at[i], wq.at[i], load.at[i]) for i in range(3)]
    loads += [
        pltpu.make_async_copy(w_out, wo, load.at[3]),
        pltpu.make_async_copy(w_down, wd, load.at[4]),
        pltpu.make_async_copy(w_gu, wg, load.at[5]),
    ]
    for one in loads:
        one.start()
    greet(seq=seq_n, heads=depth)

    def norm(rows, carry):
        v = x[rows, :].astype(F32)
        inverse = lax.rsqrt(jnp.mean(v * v, axis=-1, keepdims=True) + NORM_EPS)
        h1[rows, :] = (v * inverse * gain[...]).astype(BF16)
        return carry

    row_loop(count, 32, norm)
    for i in range(3):
        h1[count + i * RANK : count + (i + 1) * RANK, :] = at_qkv[i]
    for i in range(3):
        low[i] = dot(h1[:count, :], at_qkv[i], NT).astype(BF16)
    exchanges = [
        Exchange(kind, seq_n, pairs, lambda j, i=i: turned.at[i, j], lambda j, to=to: to.at[j], *sems)
        for i, (kind, to, sems) in enumerate(
            (("queries", q, (q_send, q_recv)), ("keys", k, (k_send, k_recv)), ("keys", v, (v_send, v_recv)))
        )
    ]
    for i in range(3):
        loads[i].wait()

        def project(over, t, i=i):
            width = over.size
            r = dot(h1[...], wq[i, :, over])
            b = b_qkv[i, :, over]
            value = r[:count] + ADAPT_SCALE * dot(low[i], b)
            aw = r[count + i * RANK : count + (i + 1) * RANK]
            squares, av = column_stats(wq.at[i, :, over], at_qkv[i], b, aw)
            n = jnp.sqrt(squares + COLUMN_EPS)
            norm_qkv[i : i + 1, over] = n
            v_qkv[i, :, over] = av
            pre[i, :, over] = value.astype(BF16)
            scaled = value * (m_qkv[i : i + 1, over] / n)
            for row in range(rows_n):
                rows = slice(row * group, (row + 1) * group)
                for hh in range(width // HD):
                    part_ = scaled[rows, hh * HD : (hh + 1) * HD]
                    if i < 2:
                        part_ = part_ * cos[rows, :] + pltpu.roll(part_, HD // 2, 1) * sin[rows, :]
                    turned[i, row * heads + t * (width // HD) + hh] = part_.astype(BF16)

        tiles(heads * HD, 256, project)
        exchanges[i].start()

    part[...] = jnp.zeros_like(part)
    for row, (w, at, b, av, loaded) in enumerate(
        ((wo, at_out, b_out, v_out, loads[3]), (wd, at_down, b_down, v_down, loads[4]))
    ):
        loaded.wait()

        def stats(over, t, row=row, w=w, at=at, b=b, av=av):
            squares, value = column_stats(w.at[:, over], at[...], b[:, over], dot(at[...], w[:, over]))
            part[row : row + 1, over] = squares
            av[:, over] = value

        tiles(w.shape[1], 256, stats)
    across = Across(depth, part, others, z_send, z_recv)
    across.start()
    loads[5].wait()
    for i in range(2):

        def stats_gu(over, t, i=i):
            b = b_gu[i, :, over]
            squares, value = column_stats(wg.at[i, :, over], at_gu[i], b, dot(at_gu[i], wg[i, :, over]))
            norm_gu[i : i + 1, over] = jnp.sqrt(squares + COLUMN_EPS)
            v_gu[i, :, over] = value

        tiles(wg.shape[2], 256, stats_gu)
    norms[...] = jnp.sqrt(across.finish() + COLUMN_EPS)
    for one in exchanges:
        one.wait_recv()
    for one in exchanges:
        one.wait_send()


def front(sizes, x, gain, cos, sin, qkv, out, down, gu):
    seq_n, depth, rows_n, group, heads = sizes
    count, pairs, width = rows_n * group, rows_n * heads, x.shape[1]
    local, hidden = qkv[0].shape[2], gu[0].shape[2]
    return pl.pallas_call(
        functools.partial(front_kernel, *sizes),
        out_shape=[
            shape(pairs, group, HD), shape(seq_n, group, HD), shape(seq_n, group, HD),
            shape(count + 3 * RANK, width), shape(3, count, local), shape(3, count, RANK),
            shape(3, local, dtype=F32), shape(3, RANK, local, dtype=F32), shape(8, width, dtype=F32),
            shape(RANK, width, dtype=F32), shape(RANK, width, dtype=F32),
            shape(2, hidden, dtype=F32), shape(2, RANK, hidden, dtype=F32),
        ],
        in_specs=[IN_VMEM] * 13 + [ANYWHERE] * 4,
        out_specs=[IN_VMEM] * 13,
        scratch_shapes=[
            pltpu.VMEM(qkv[0].shape, BF16), pltpu.VMEM(out[0].shape, BF16), pltpu.VMEM(down[0].shape, BF16),
            pltpu.VMEM(gu[0].shape, BF16), pltpu.VMEM((3, pairs, group, HD), BF16),
            pltpu.VMEM((8, width), F32), pltpu.VMEM((depth, 8, width), F32),
            dma(pairs), dma(pairs), dma(seq_n), dma(seq_n), dma(seq_n), dma(seq_n), dma(depth), dma(depth), dma(6),
        ],
        compiler_params=params(56, 1),
    )(
        x, gain, cos, sin, qkv[1], qkv[2], qkv[3], out[1], out[2], down[1], down[2], gu[1], gu[2],
        qkv[0], out[0], down[0], gu[0],
    )


def attend_kernel(block, low_ref, high_ref, q_ref, k_ref, v_ref, start_ref, place_ref, o_ref, lse_ref, vt):
    scale = HD**-0.5
    vt[...] = v_ref[...].T

    def per_query(i, carry):
        at = pl.ds(pl.multiple_of(i * block, block), block)
        q = q_ref[at, :]
        start, place = start_ref[:, at], place_ref[:, at]

        def per_key(j, state):
            top, count, acc = state
            over = pl.ds(pl.multiple_of(j * block, block), block)
            s = dot(k_ref[over, :], q, NT) * scale
            key = j * block + lax.broadcasted_iota(jnp.int32, (block, block), 0)
            s = jnp.where((key >= start) & (key <= place), s, NEG_LARGE)
            new_top = jnp.maximum(top, jnp.max(s, axis=0, keepdims=True))
            p = jnp.exp(s - new_top)
            fade = jnp.exp(top - new_top)
            count = count * fade + total(p)
            acc = acc * fade + dot(vt[:, over], p)
            return new_top, count, acc

        begin = (
            jnp.full((1, block), -1e29, F32),
            jnp.zeros((1, block), F32),
            jnp.zeros((HD, block), F32),
        )
        top, count, acc = lax.fori_loop(low_ref[i], high_ref[i] + 1, per_key, begin)
        o_ref[at, :] = (acc / count).T.astype(BF16)
        lse_ref[:, at] = top + jnp.log(count)
        return carry

    lax.fori_loop(0, q_ref.shape[0] // block, per_query, 0)


def attend(q, k, v, low, high, start, place, block):
    return pl.pallas_call(
        functools.partial(attend_kernel, block),
        out_shape=[shape(*q.shape), shape(1, q.shape[0], dtype=F32)],
        in_specs=[IN_SMEM] * 2 + [IN_VMEM] * 5,
        out_specs=[IN_VMEM] * 2,
        scratch_shapes=[pltpu.VMEM((HD, k.shape[0]), BF16)],
        compiler_params=params(24),
    )(low, high, q, k, v, start, place)


def attend_back(block, fan, q_ref, k_ref, v_ref, o_ref, do_ref, lse_ref, start_ref, place_ref, dq, dk, dv, kt, dk_acc, dv_acc, tick):
    scale = HD**-0.5
    mine = lax.rem(lax.axis_index("seq"), fan)
    kt[...] = k_ref[...].T
    dk_acc[...] = jnp.zeros_like(dk_acc)
    dv_acc[...] = jnp.zeros_like(dv_acc)

    def per_query(i, carry):
        at = pl.ds(pl.multiple_of(i * block, block), block)
        q, do = q_ref[at, :], do_ref[at, :]
        start, place, lse = start_ref[:, at], place_ref[:, at], lse_ref[:, at]
        delta = total((do.astype(F32) * o_ref[at, :].astype(F32)).T)

        def per_key(j, acc):
            over = pl.ds(pl.multiple_of(j * block, block), block)
            k = k_ref[over, :]
            s = dot(k, q, NT) * scale
            key = j * block + lax.broadcasted_iota(jnp.int32, (block, block), 0)
            p = jnp.exp(jnp.where((key >= start) & (key <= place), s - lse, NEG_LARGE))
            dp = dot(v_ref[over, :], do, NT)
            ds = (p * (dp - delta)).astype(BF16)
            dv_acc[over, :] += dot(p, do)
            dk_acc[over, :] += dot(ds, q)
            return acc + dot(kt[:, over], ds)

        acc = lax.fori_loop(0, mine + fan * i + 1, per_key, jnp.zeros((HD, block), F32))
        dq[i] = (acc * scale).T.astype(BF16)
        tick(i)
        return carry

    lax.fori_loop(0, q_ref.shape[0] // block, per_query, 0)

    def store(j, carry):
        over = pl.ds(pl.multiple_of(j * block, block), block)
        dk[j] = (dk_acc[over, :] * scale).astype(BF16)
        dv[j] = dv_acc[over, :].astype(BF16)
        return carry

    lax.fori_loop(0, k_ref.shape[0] // block, store, 0)


def core_kernel(
    seq_n, depth, rows_n, group, heads,
    o, gain, m_out, norms, at_out, b_out, v_out, at_gu, b_gu, m_gu, norm_gu, v_gu, at_down, b_down, m_down, v_down,
    x_far, cotangent_far, w_out, w_gu, w_down,
    do, dx2, out_pre, down_part, gm_down, ga_gu, gb_gu, gm_gu, g_gain, ga_down, gb_down, ga_out, gb_out, gm_out,
    x, cotangent, wo, wg, wd, attn, low_out, part, part2, dh2, h2, pre, z, dp, dpd, tmp, low, mix, dpo, blocks,
    s_part, others, load, send, recv, back_send, back_recv, z_send, z_recv, *line_refs,
):
    count, pairs = rows_n * group, rows_n * heads
    half = count // 2
    hidden, width = wd.shape
    loads = [
        pltpu.make_async_copy(far, near, load.at[i])
        for i, (far, near) in enumerate(
            ((w_out, wo), (x_far, x), (w_gu.at[0], wg.at[0]), (w_gu.at[1], wg.at[1]), (cotangent_far, cotangent), (w_down, wd))
        )
    ]
    for one in loads:
        one.start()
    greet(seq=seq_n, heads=depth)

    def landing(pair):
        row, head = pair // heads, lax.rem(pair, heads)
        return attn.at[
            pl.ds(pl.multiple_of(row * group, group), group), pl.ds(pl.multiple_of(head * HD, HD), HD)
        ]

    come = Exchange("queries_back", seq_n, pairs, lambda i: o.at[i], landing, send, recv)
    leave = Exchange("queries", seq_n, pairs, lambda p: blocks.at[p], lambda s_: do.at[s_], back_send, back_recv)
    come.start()
    for ref in (s_part, ga_gu, gb_gu, gm_gu, g_gain, ga_down, gb_down, ga_out, gb_out, gm_out):
        ref[...] = jnp.zeros_like(ref)
    one_out = Line(part, out_pre, *line_refs[:9], per=half // (2 * CHUNK), lead=LEAD)
    two = [
        Line(part2, dh2, *line_refs[9 + 9 * r : 18 + 9 * r], base=r * half, lead=LEAD) for r in range(2)
    ]
    loads[0].wait()
    come.wait_recv()
    low_out[...] = dot(attn[...], at_out[...], NT).astype(BF16)

    def project(over, t):
        part[:, over] = (dot(attn[...], wo[:, over]) + ADAPT_SCALE * dot(low_out[...], b_out[:, over])).astype(BF16)

    tiles(width, WIDE, project)
    one_out.first()
    for one in loads[1:]:
        one.wait()
    n_out, n_down = 1.0 / norms[0:1, :], 1.0 / norms[1:2, :]
    c_out, c_down = m_out[...] * n_out, m_down[...] * n_down

    def feed_forward(r, tick):
        mine = slice(r * half, (r + 1) * half)
        base = r * half
        n_hidden, n_width = -(-hidden // WIDE), -(-width // WIDE)

        def there(rows):
            return pl.ds(pl.multiple_of(base + rows.start, rows.size), rows.size)

        def norm(rows, carry):
            x2 = x[there(rows), :].astype(F32) + out_pre[there(rows), :].astype(F32) * c_out
            inverse = lax.rsqrt(jnp.mean(x2 * x2, axis=-1, keepdims=True) + NORM_EPS)
            h2[rows, :] = (x2 * inverse * gain[...]).astype(BF16)
            dpd[rows, :] = (cotangent[there(rows), :].astype(F32) * c_down).astype(BF16)
            return carry

        row_loop(half, 32, norm)
        low[...] = dot(h2[...], at_gu[...].reshape(2 * RANK, width), NT).astype(BF16)

        def forward(over, t):
            n = over.size
            for i in range(2):
                tmp[i, :, :n] = dot(h2[...], wg[i, :, over]) + ADAPT_SCALE * dot(
                    low[:, i * RANK : (i + 1) * RANK], b_gu[i, :, over]
                )
            scale = [m_gu[i : i + 1, over] / norm_gu[i : i + 1, over] for i in range(2)]

            def gated(rows, carry):
                g, u = tmp[0, rows, :n], tmp[1, rows, :n]
                pre[0, rows, over] = g.astype(BF16)
                pre[1, rows, over] = u.astype(BF16)
                g = g * scale[0]
                z[rows, over] = (g * jax.nn.sigmoid(g) * (u * scale[1])).astype(BF16)
                return carry

            row_loop(half, 32, gated)

        tiles(hidden, WIDE, forward, tick)
        low_down = dot(z[...], at_down[...], NT).astype(BF16)

        def down(over, t):
            value = dot(z[...], wd[:, over]) + ADAPT_SCALE * dot(low_down, b_down[:, over])
            down_part[mine, over] = value.astype(BF16)
            s_part[0:1, over] += total(value * cotangent[mine, over].astype(F32))
            gb_down[:, over] += ADAPT_SCALE * dot(low_down, dpd[:, over], TN)

        tiles(width, WIDE, down, lambda t: tick(n_hidden + t))
        dlow_down = (ADAPT_SCALE * dot(dpd[...], b_down[...], NT)).astype(BF16)

        def backward(over, t):
            n = over.size
            tmp[0, :, :n] = dot(dpd[...], wd[over, :], NT) + dot(dlow_down, at_down[:, over])
            ga_down[:, over] += dot(dlow_down, z[:, over], TN)
            scale = [m_gu[i : i + 1, over] / norm_gu[i : i + 1, over] for i in range(2)]

            def gated(rows, sums):
                dz = tmp[0, rows, :n]
                pg, pu = pre[0, rows, over].astype(F32), pre[1, rows, over].astype(F32)
                g, u = pg * scale[0], pu * scale[1]
                sigma = jax.nn.sigmoid(g)
                dzs = dz * sigma
                e_g = dzs * u * (1.0 + g * (1.0 - sigma))
                e_u = dzs * g
                dp[0, rows, over] = (e_g * scale[0]).astype(BF16)
                dp[1, rows, over] = (e_u * scale[1]).astype(BF16)
                return sums[0] + fold(e_g * pg), sums[1] + fold(e_u * pu)

            zero = jnp.zeros((8, n), F32)
            sums = row_loop(half, 32, gated, (zero, zero))
            for i in range(2):
                s, inverse = total(sums[i]), 1.0 / norm_gu[i : i + 1, over]
                gm_gu[i : i + 1, over] += s * inverse
                turn = m_gu[i : i + 1, over] * s * inverse * inverse * inverse
                dp[i, half : half + RANK, over] = (b_gu[i, :, over].astype(F32) * turn).astype(BF16)
                gb_gu[i, :, over] += ADAPT_SCALE * (
                    dot(low[:, i * RANK : (i + 1) * RANK], dp[i, :half, over], TN) - v_gu[i, :, over] * turn
                )

        tiles(hidden, WIDE, backward, lambda t: tick(n_hidden + n_width + t))
        for i in range(2):
            both = ADAPT_SCALE * dot(dp[i], b_gu[i], NT)
            mix[:half, i * RANK : (i + 1) * RANK] = both[:half].astype(BF16)
            for k in range(2):
                mix[half + k * RANK : half + (k + 1) * RANK, i * RANK : (i + 1) * RANK] = (
                    both[half:] if i == k else jnp.zeros((RANK, RANK), F32)
                ).astype(BF16)

        def inputs(over, t):
            products = [dot(dp[i], wg[i, over, :], NT) for i in range(2)]
            through = dot(mix[...], at_gu[:, :, over].reshape(2 * RANK, over.size))
            value = products[0][:half] + products[1][:half] + through[:half]
            straight = dot(mix[:half, :], h2[:, over], TN)
            for i in range(2):
                v_tb = products[i][half:] + through[half + i * RANK : half + (i + 1) * RANK]
                ga_gu[i, :, over] += straight[i * RANK : (i + 1) * RANK] - ADAPT_SCALE * v_tb
            part2[mine, over] = value.astype(BF16)
            g_gain[:, over] += total(value * h2[:, over].astype(F32)) / gain[:, over]

        tiles(width, WIDE, inputs, lambda t: tick(2 * n_hidden + n_width + t))

    def out_back(r, tick):
        base, mine = r * half, slice(r * half, (r + 1) * half)
        rows_here = rows_n // 2

        def back(rows, sums):
            there = pl.ds(pl.multiple_of(base + rows.start, rows.size), rows.size)
            value = out_pre[there, :].astype(F32)
            x2 = x[there, :].astype(F32) + value * c_out
            inverse = lax.rsqrt(jnp.mean(x2 * x2, axis=-1, keepdims=True) + NORM_EPS)
            scaled = dh2[there, :].astype(F32) * gain[...]
            mean = jnp.mean(scaled * x2, axis=-1, keepdims=True)
            e = cotangent[there, :].astype(F32) + inverse * scaled - x2 * (inverse**3 * mean)
            dx2[there, :] = e.astype(BF16)
            dpo[rows, :] = (e * c_out).astype(BF16)
            tick(rows.start // rows.size)
            return sums + fold(e * value)

        s = total(row_loop(half, 16, back, jnp.zeros((8, width), F32)))
        turn = m_out[...] * s * n_out * n_out * n_out
        gm_out[...] += s * n_out
        dpo[half : half + RANK, :] = (b_out[...].astype(F32) * turn).astype(BF16)
        both = dot(dpo[...], b_out[...], NT)
        dlow, turned = (ADAPT_SCALE * both[:half]).astype(BF16), both[half:]

        def inputs(over, t):
            product = dot(dpo[...], wo[over, :], NT)
            value = (product[:half] + dot(dlow, at_out[:, over])).astype(BF16)
            for row in range(rows_here):
                for hh in range(over.size // HD):
                    blocks[(r * rows_here + row) * heads + t * (over.size // HD) + hh] = value[
                        row * group : (row + 1) * group, hh * HD : (hh + 1) * HD
                    ]
            ga_out[:, over] += dot(dlow, attn[mine, over], TN) - ADAPT_SCALE * (
                product[half:] + ADAPT_SCALE * dot(turned, at_out[:, over])
            )

        tiles(heads * HD, WIDE, inputs)
        leave.start(r * rows_here * heads, (r + 1) * rows_here * heads)
        gb_out[...] += ADAPT_SCALE * (dot(low_out[mine, :], dpo[:half, :], TN) - v_out[...] * turn)

    half_done = one_out.done(one_out.per)
    one_out.run(0, half_done)
    ticks = 2 * (-(-hidden // WIDE) - (-width // WIDE))
    feed_forward(0, one_out.spread(half_done, one_out.steps, ticks))
    two[0].first()
    feed_forward(1, two[0].spread(0, EARLY, ticks))
    across = Across(depth, s_part, others, z_send, z_recv)
    across.start()
    two[1].first()

    def together(k, carry):
        two[0].step(EARLY + k)
        two[1].step(k)
        return carry

    begun = two[0].steps - EARLY
    lax.fori_loop(0, begun, together, 0)
    out_back(0, two[1].spread(begun, two[1].steps, half // 16))
    out_back(1, lambda t: None)
    for line in [one_out] + two:
        line.drain()
    s = across.finish()[0:1, :]
    turn = m_down[...] * s * n_down * n_down * n_down
    tb = (b_down[...].astype(F32) * turn).astype(BF16)
    v_tb = dot(tb, wd[...], NT) + ADAPT_SCALE * dot(dot(tb, b_down[...], NT), at_down[...])
    ga_down[...] -= ADAPT_SCALE * v_tb
    gb_down[...] -= ADAPT_SCALE * v_down[...] * turn
    gm_down[...] = s * n_down
    come.wait_send()
    leave.wait_recv()
    leave.wait_send()


def core(sizes, o, x, cotangent, gain, norms, out, down, gu):
    seq_n, depth, rows_n, group, heads = sizes
    count, pairs, width = rows_n * group, rows_n * heads, x.shape[1]
    hidden, half = down[0].shape[0], rows_n * group // 2
    return pl.pallas_call(
        functools.partial(core_kernel, *sizes),
        out_shape=[
            shape(pairs, group, HD), shape(count, width), shape(count, width), shape(count, width),
            shape(1, width, dtype=F32), shape(2, RANK, width, dtype=F32), shape(2, RANK, hidden, dtype=F32),
            shape(2, hidden, dtype=F32), shape(1, width, dtype=F32), shape(RANK, hidden, dtype=F32),
            shape(RANK, width, dtype=F32), shape(RANK, heads * HD, dtype=F32), shape(RANK, width, dtype=F32),
            shape(1, width, dtype=F32),
        ],
        in_specs=[IN_VMEM] * 16 + [ANYWHERE] * 5,
        out_specs=[IN_VMEM] * 14,
        scratch_shapes=[
            pltpu.VMEM((count, width), BF16), pltpu.VMEM((count, width), BF16), pltpu.VMEM(out[0].shape, BF16),
            pltpu.VMEM(gu[0].shape, BF16), pltpu.VMEM(down[0].shape, BF16), pltpu.VMEM((count, heads * HD), BF16),
            pltpu.VMEM((count, RANK), BF16), pltpu.VMEM((count, width), BF16), pltpu.VMEM((count, width), BF16),
            pltpu.VMEM((count, width), BF16), pltpu.VMEM((half, width), BF16), pltpu.VMEM((2, half, hidden), BF16),
            pltpu.VMEM((half, hidden), BF16), pltpu.VMEM((2, half + RANK, hidden), BF16),
            pltpu.VMEM((half, width), BF16), pltpu.VMEM((2, half, WIDE), F32), pltpu.VMEM((half, 2 * RANK), BF16),
            pltpu.VMEM((half + 2 * RANK, 2 * RANK), BF16),
            pltpu.VMEM((half + RANK, width), BF16), pltpu.VMEM((pairs, group, HD), BF16),
            pltpu.VMEM((8, width), F32), pltpu.VMEM((depth, 8, width), F32),
            dma(6), dma(pairs), dma(pairs), dma(pairs), dma(pairs), dma(depth), dma(depth),
        ]
        + Line.scratch(count, width, CHUNK)
        + Line.scratch(half, width, CHUNK) * 2,
        compiler_params=params(62, 2),
    )(o, gain, out[3], norms, *out[1:3], out[4], *gu[1:], *down[1:], x, cotangent, out[0], gu[0], down[0])


def last_kernel(
    seq_n, depth, rows_n, group, heads,
    q, k, v, o, do, lse, start, place, down_part, cos, sin, h1, pre, low, gain, at, b, m, norm, v_qkv,
    ga_gu, gb_out, gb_down, g_gain2, gm_out, gm_down, ga_out, gb_gu, gm_gu, ga_down, w_qkv,
    dh1, down_sum, wide, local, hid,
    kt, dk_acc, dv_acc, dq, dk, dv,
    wq, gq, gk, gv, dp, mix, part, wide_in, local_in, hid_in, wide_got, local_got, hid_got,
    piece, pieces, done, q_send, q_recv, k_send, k_recv, v_send, v_recv, load,
    r_send, r_recv, g_send, g_recv, z_send, z_recv, *line_refs,
):
    count, pairs, width = rows_n * group, rows_n * heads, h1.shape[1]
    fan, me = seq_n // pairs, lax.axis_index("seq")
    loaded = pltpu.make_async_copy(w_qkv, wq, load.at[0])
    loaded.start()
    greet(seq=seq_n, heads=depth)
    line_down = Line(down_part, down_sum, *line_refs[:9], lead=LEAD)
    line_down.first()
    exchanges = [
        Exchange(kind, seq_n, pairs, lambda j, a=a: a.at[j], lambda j, to=to: to.at[j], *sems)
        for kind, a, to, sems in (
            ("queries_back", dq, gq, (q_send, q_recv)),
            ("keys_back", dk, gk, (k_send, k_recv)),
            ("keys_back", dv, gv, (v_send, v_recv)),
        )
    ]
    first, second = line_down.steps // 3, line_down.steps * 2 // 3
    attend_back(
        group, fan, q, k, v, o, do, lse, start, place, dq, dk, dv, kt, dk_acc, dv_acc,
        line_down.spread(0, first, pairs),
    )
    for one in exchanges:
        one.start()

    wide_in[...] = jnp.zeros_like(wide_in)
    local_in[...] = jnp.zeros_like(local_in)
    hid_in[...] = jnp.zeros_like(hid_in)
    share = 1.0 / depth
    for i in range(2):
        wide_in[(3 + i) * RANK : (4 + i) * RANK, :] = ga_gu[i].astype(BF16)
        hid_in[i * RANK : (i + 1) * RANK, :] = gb_gu[i].astype(BF16)
    wide_in[5 * RANK : 6 * RANK, :] = gb_out[...].astype(BF16)
    wide_in[6 * RANK : 7 * RANK, :] = gb_down[...].astype(BF16)
    hid_in[3 * RANK : 4 * RANK, :] = ga_down[...].astype(BF16)
    local_in[4 * RANK : 5 * RANK, :] = ga_out[...].astype(BF16)
    hid_in[2 * RANK : 3 * RANK, :] = jnp.concatenate(
        [gm_gu[...], jnp.zeros((RANK - 2, hid_in.shape[1]), F32)], axis=0
    ).astype(BF16)

    sums = [None] * 3
    line_down.run(first, second)
    loaded.wait()
    for i in range(3):
        exchanges[i].wait_recv()
        came = (gq, gk, gv)[i]
        for head in range(heads):
            cols = slice(head * HD, (head + 1) * HD)
            n = norm[i : i + 1, cols]
            c = m[i : i + 1, cols] / n
            s = jnp.zeros((1, HD), F32)
            for row in range(rows_n):
                rows = slice(row * group, (row + 1) * group)
                if i == 0:
                    e = came[row * heads + head].astype(F32)
                else:
                    e = came[(row * heads + head) * fan].astype(F32)
                    for g in range(1, fan):
                        e = e + came[(row * heads + head) * fan + g].astype(F32)
                if i < 2:
                    e = e * cos[rows, :] - pltpu.roll(e, HD // 2, 1) * sin[rows, :]
                s = s + total(e * pre[i, rows, cols].astype(F32))
                dp[i, rows, cols] = (e * c).astype(BF16)
            turn = m[i : i + 1, cols] * s / (n * n * n)
            dp[i, count : count + RANK, cols] = (b[i, :, cols].astype(F32) * turn).astype(BF16)
            local_in[i * RANK : (i + 1) * RANK, cols] = (
                ADAPT_SCALE * (dot(low[i], dp[i, :count, cols], TN) - v_qkv[i, :, cols] * turn)
            ).astype(BF16)
            sums[i] = [s / n] if head == 0 else sums[i] + [s / n]
    local_in[3 * RANK : 4 * RANK, :] = jnp.concatenate(
        [jnp.concatenate(one, axis=1) for one in sums]
        + [jnp.zeros((RANK - 3, heads * HD), F32)], axis=0
    ).astype(BF16)
    mix[...] = jnp.zeros_like(mix)
    for i in range(3):
        both = (ADAPT_SCALE * dot(dp[i], b[i], NT)).astype(BF16)
        cols = slice(i * RANK, (i + 1) * RANK)
        mix[:count, cols] = both[:count]
        mix[count + i * RANK : count + (i + 1) * RANK, cols] = both[count:]

    def inputs(over, t):
        through = dot(mix[...], at[:, :, over].reshape(3 * RANK, over.size))
        straight = dot(mix[:count, :], h1[:count, over], TN)
        value = through[:count]
        for i in range(3):
            product = dot(dp[i], wq[i, over, :], NT)
            value = value + product[:count]
            rows = slice(i * RANK, (i + 1) * RANK)
            v_tb = product[count:] + through[count + i * RANK : count + (i + 1) * RANK]
            wide_in[rows, over] = (straight[rows] - ADAPT_SCALE * v_tb).astype(BF16)
        part[:, over] = value.astype(BF16)
        g_gain1 = total(value * h1[:count, over].astype(F32)) / gain[:, over]
        wide_in[7 * RANK : 8 * RANK, over] = jnp.concatenate(
            [
                g_gain1, g_gain2[:, over], gm_out[:, over] * share,
                gm_down[:, over] * share,
                jnp.zeros((RANK - 4, over.size), F32),
            ], axis=0,
        ).astype(BF16)

    tiles(width, WIDE, inputs, line_down.spread(second, line_down.steps, -(-width // WIDE)))
    line = Line(part, dh1, *line_refs[9:], lead=LEAD)
    line.first()

    spread = seq_n // OWNERS
    slabs = (
        (wide_in, wide_got, wide, lambda j: j), (local_in, local_got, local, lambda j: j),
        (hid_in, hid_got, hid, lambda j: OWNERS - 1 - j),
    )
    own = me // spread
    chosen = lax.rem(me, spread) == 0

    def rows_of(j):
        return pl.ds(pl.multiple_of(j * RANK, RANK), RANK)

    def to_owner(i, j):
        src, got, _, owner = slabs[i]
        return remote(
            src.at[rows_of(j)], got.at[me], r_send.at[i, j], r_recv.at[i, me], seq=owner(j) * spread
        )

    def from_owner(i, j, target):
        result = slabs[i][2]
        return remote(
            done.at[i, :, : result.shape[1]], result.at[rows_of(j)], g_send.at[i, target], g_recv.at[i, j], seq=target
        )

    for i, (src, got, result, owner) in enumerate(slabs):
        for j in range(src.shape[0] // RANK):

            @pl.when(me != owner(j) * spread)
            def _(i=i, j=j):
                to_owner(i, j).start()

            @pl.when(me == owner(j) * spread)
            def _(src=src, got=got, i=i, j=j):
                pltpu.make_async_copy(src.at[rows_of(j)], got.at[me], r_recv.at[i, me]).start()

    line.run(0, 10)
    across = Across(depth, piece, pieces, z_send, z_recv)
    blocks_n = [slab[0].shape[0] // RANK for slab in slabs]
    owns = [chosen & (slab[3](own) < n) for slab, n in zip(slabs, blocks_n)]
    for i, (src, got, result, owner) in enumerate(slabs):

        @pl.when(owns[i])
        def _(i=i, got=got, result=result):
            def add(s_, acc):
                pltpu.make_async_copy(got.at[s_], got.at[s_], r_recv.at[i, s_]).wait()
                return acc + got[s_].astype(F32)

            value = lax.fori_loop(0, seq_n, add, jnp.zeros((RANK, result.shape[1]), F32))
            if i == 0:
                piece[...] = value.astype(BF16)
                across.start()
            else:
                done[i, :, : result.shape[1]] = value.astype(BF16)

    line.run(10, 14)

    @pl.when(owns[0])
    def _():
        done[0, :, :] = across.finish().astype(BF16)

    for i, (src, got, result, owner) in enumerate(slabs):

        @pl.when(owns[i])
        def _(i=i, result=result, owner=owner):
            mine = owner(own)

            def give(d, carry):
                from_owner(i, mine, lax.rem(me + d, seq_n)).start()
                return carry

            lax.fori_loop(1, seq_n, give, 0)
            pltpu.make_async_copy(
                done.at[i, :, : result.shape[1]], result.at[rows_of(mine)], g_recv.at[i, mine]
            ).start()

    line.run(14, line.steps)
    line.drain()
    line_down.drain()
    for one in exchanges:
        one.wait_send()
    for i, (src, got, result, owner) in enumerate(slabs):
        for j in range(blocks_n[i]):

            @pl.when(me != owner(j) * spread)
            def _(i=i, j=j):
                to_owner(i, j).wait_send()

            pltpu.make_async_copy(result.at[rows_of(j)], result.at[rows_of(j)], g_recv.at[i, j]).wait()

        @pl.when(owns[i])
        def _(i=i, owner=owner):
            def given(d, carry):
                from_owner(i, owner(own), lax.rem(me + d, seq_n)).wait_send()
                return carry

            lax.fori_loop(1, seq_n, given, 0)


def last(sizes, ins, qkv_w, hidden):
    seq_n, depth, rows_n, group, heads = sizes
    count, pairs, width = rows_n * group, rows_n * heads, qkv_w.shape[1]
    local, length = qkv_w.shape[2], seq_n * group
    blocks = {width: 8, local: 5, hidden: 4}
    slabs = [(n * RANK, w) for w, n in blocks.items()]
    some, every = pltpu.VMEM((pairs, group, HD), BF16), pltpu.VMEM((seq_n, group, HD), BF16)
    return pl.pallas_call(
        functools.partial(last_kernel, *sizes),
        out_shape=[shape(count, width)] * 2 + [shape(*s) for s in slabs],
        in_specs=[IN_VMEM] * len(ins) + [ANYWHERE],
        out_specs=[IN_VMEM] * 5,
        scratch_shapes=[
            pltpu.VMEM((HD, length), BF16), pltpu.VMEM((length, HD), F32), pltpu.VMEM((length, HD), F32),
            some, every, every,
            pltpu.VMEM(qkv_w.shape, BF16), some, every, every,
            pltpu.VMEM((3, count + RANK, local), BF16), pltpu.VMEM((count + 3 * RANK, 3 * RANK), BF16),
            pltpu.VMEM((count, width), BF16),
        ]
        + [pltpu.VMEM(s, BF16) for s in slabs]
        + [pltpu.VMEM((seq_n, RANK, s[1]), BF16) for s in slabs]
        + [
            pltpu.VMEM((RANK, width), BF16), pltpu.VMEM((depth, RANK, width), BF16), pltpu.VMEM((3, RANK, width), BF16),
            dma(pairs), dma(pairs), dma(seq_n), dma(seq_n), dma(seq_n), dma(seq_n), dma(1),
            dma(3, 8), dma(3, seq_n), dma(3, seq_n), dma(3, 8), dma(depth), dma(depth),
        ]
        + Line.scratch(count, width, CHUNK) * 2,
        compiler_params=params(62, 5),
    )(*ins, qkv_w)


def per_device(
    tokens, attn_gain, base_qkv, adapt_a_qkv, adapt_b_qkv, magnitude_qkv, base_out, adapt_a_out,
    adapt_b_out, magnitude_out, ffn_gain, base_gu, adapt_a_gu, adapt_b_gu, magnitude_gu, base_down,
    adapt_a_down, adapt_b_down, magnitude_down, doc_lengths, cotangent,
):
    rows_n, group, width = tokens.shape
    count = rows_n * group
    local = base_qkv.shape[2]
    heads = local // HD
    pairs = rows_n * heads
    seq_n, depth = lax.axis_size("seq"), lax.axis_size("heads")
    sizes = (seq_n, depth, rows_n, group, heads)
    fan = seq_n // pairs
    length = group * seq_n
    me = lax.axis_index("seq")

    order = jnp.arange(doc_lengths.shape[1])
    doc_ends = jnp.sum(
        jnp.where(order[None, :, None] <= order[None, None, :], doc_lengths[:, :, None], 0), axis=1
    )
    doc_starts = doc_ends - doc_lengths

    def starts_of(places, ends, starts):
        inside = (places[..., None] >= starts) & (places[..., None] < ends)
        return jnp.sum(jnp.where(inside, starts, 0), axis=-1)

    mine = me * group + jnp.arange(group, dtype=jnp.int32)
    position = mine[None, :] - starts_of(
        jnp.broadcast_to(mine[None, :], (rows_n, group)), doc_ends[:, None], doc_starts[:, None]
    )
    half = HD // 2
    frequency = ROPE_BASE ** (jnp.arange(half, dtype=F32) * (-2.0 / HD))
    angles = position.reshape(count, 1).astype(F32) * frequency
    cos, sin = jnp.cos(angles), jnp.sin(angles)
    cos, sin = jnp.concatenate([cos, cos], axis=1), jnp.concatenate([-sin, sin], axis=1)
    row = me // fan // heads
    block_at = lax.rem(me, fan) + fan * jnp.arange(pairs, dtype=jnp.int32)
    place = (block_at[:, None] * group + jnp.arange(group, dtype=jnp.int32)[None, :]).reshape(-1)
    pick = (jnp.arange(rows_n) == row)[:, None]
    row_ends = jnp.sum(jnp.where(pick, doc_ends, 0), axis=0)
    row_starts = jnp.sum(jnp.where(pick, doc_starts, 0), axis=0)
    start = starts_of(place, row_ends, row_starts)
    low_block = start.reshape(-1, group)[:, 0] // group
    place, start = place[None, :], start[None, :]

    x = tokens.reshape(count, width)
    dy = cotangent.reshape(count, width)
    gain1, gain2 = attn_gain[None, :], ffn_gain[None, :]
    m_out, m_down = magnitude_out[None, :], magnitude_down[None, :]
    at_qkv, at_gu = adapt_a_qkv.transpose(0, 2, 1), adapt_a_gu.transpose(0, 2, 1)
    at_out, at_down = adapt_a_out.T, adapt_a_down.T

    q, k, v, h1, pre, low, norm_qkv, v_qkv, norms, v_out, v_down, norm_gu, v_gu = front(
        sizes, x, gain1, cos, sin, (base_qkv, at_qkv, adapt_b_qkv, magnitude_qkv), (base_out, at_out, adapt_b_out),
        (base_down, at_down, adapt_b_down), (base_gu, at_gu, adapt_b_gu),
    )
    q, k, v = q.reshape(-1, HD), k.reshape(length, HD), v.reshape(length, HD)
    o, lse = attend(q, k, v, low_block, block_at, start, place, group)
    do, dx2, out_pre, down_part, gm_down, ga_gu, gb_gu, gm_gu, g_gain2, ga_down, gb_down, ga_out, gb_out, gm_out = core(
        sizes, o.reshape(-1, group, HD), x, dy, gain2, norms, (base_out, at_out, adapt_b_out, m_out, v_out),
        (base_down, at_down, adapt_b_down, m_down, v_down), (base_gu, at_gu, adapt_b_gu, magnitude_gu, norm_gu, v_gu),
    )
    dh1, down_pre, wide, narrow, hid = last(
        sizes,
        (
            q, k, v, o, do.reshape(-1, HD), lse, start, place, down_part, cos, sin, h1, pre,
            low, gain1, at_qkv, adapt_b_qkv, magnitude_qkv, norm_qkv, v_qkv, ga_gu, gb_out, gb_down, g_gain2,
            gm_out, gm_down, ga_out, gb_gu, gm_gu, ga_down,
        ),
        base_qkv,
        base_down.shape[0],
    )
    xf = x.astype(F32)
    inverse_one = lax.rsqrt(jnp.mean(xf * xf, axis=-1, keepdims=True) + NORM_EPS)
    scaled = dh1.astype(F32) * gain1
    dx = dx2.astype(F32) + inverse_one * scaled
    dx = dx - xf * inverse_one**3 * jnp.mean(scaled * xf, axis=-1, keepdims=True)
    x2 = xf + out_pre.astype(F32) * (m_out / norms[0:1])
    mixed = (x2 + down_pre.astype(F32) * (m_down / norms[1:2])).astype(BF16)
    wide, narrow, hid = wide.astype(F32), narrow.astype(F32), hid.astype(F32)
    return (
        mixed.reshape(rows_n, group, width),
        dx.reshape(rows_n, group, width),
        wide[112],
        wide[:48].reshape(3, RANK, width).transpose(0, 2, 1),
        narrow[:48].reshape(3, RANK, local),
        narrow[48:51],
        narrow[64:80].T,
        wide[80:96],
        wide[114],
        wide[113],
        wide[48:80].reshape(2, RANK, width).transpose(0, 2, 1),
        hid[:32].reshape(2, RANK, -1),
        hid[32:34],
        hid[48:64].T,
        wide[96:112],
        wide[115],
    )


def solution(mesh):
    in_specs = (
        P(None, "seq", None), P(), P(None, None, "heads"), P(), P(None, None, "heads"), P(None, "heads"),
        P("heads", None), P("heads", None), P(), P(), P(), P(None, None, "heads"), P(),
        P(None, None, "heads"), P(None, "heads"), P("heads", None), P("heads", None), P(), P(), P(),
        P(None, "seq", None),
    )
    out_specs = (
        P(None, "seq", None), P(None, "seq", None), P(), P(), P(None, None, "heads"), P(None, "heads"),
        P("heads", None), P(), P(), P(), P(), P(None, None, "heads"), P(None, "heads"),
        P("heads", None), P(), P(),
    )
    return jax.shard_map(
        per_device, mesh=mesh, in_specs=in_specs, out_specs=out_specs, check_vma=False
    )
```

```python
import functools

import jax
import jax.numpy as jnp
from jax import lax
from jax.experimental import pallas as pl
from jax.experimental.pallas import tpu as pltpu
from jax.sharding import PartitionSpec as P

HD = 128
RANK = 16
ADAPT_SCALE = 2.0
NORM_EPS = 1e-05
COLUMN_EPS = 1e-06
ROPE_BASE = 10000.0
NEG_LARGE = -1e30
LOG2E = 1.4426950408889634
F32 = jnp.float32
BF16 = jnp.bfloat16
MESH = pl.DeviceIdType.MESH
NN = (((1,), (0,)), ((), ()))
NT = (((1,), (1,)), ((), ()))
TN = (((0,), (0,)), ((), ()))
OWNERS = 8
CHUNK = 16
PIECES = 1
LAG = 2
LEAD = 4
NEAR_LATE = 1
EARLY = 8
LAST_LEAD = 4
FIRST, SECOND = 7, 14
GATHER, GIVE = 10, 14
WIDE = 512
IN_VMEM = pl.BlockSpec(memory_space=pltpu.VMEM)
IN_SMEM = pl.BlockSpec(memory_space=pltpu.SMEM)
ANYWHERE = pl.BlockSpec(memory_space=pl.ANY)


def dot(a, b, dims=NN):
    return lax.dot_general(a.astype(BF16), b.astype(BF16), dims, preferred_element_type=F32)


def shape(*dims, dtype=BF16):
    return jax.ShapeDtypeStruct(dims, dtype)


def dma(*dims):
    return pltpu.SemaphoreType.DMA(dims)


def params(mib, collective_id=None):
    more = {} if collective_id is None else {"collective_id": collective_id, "has_side_effects": True}
    return pltpu.CompilerParams(vmem_limit_bytes=mib * 2**20, **more)


def tiles(count, size, body, tick=lambda t: None):
    whole = count // size
    if whole:

        def step(t, carry):
            body(pl.ds(pl.multiple_of(t * size, 128), size), t)
            tick(t)
            return carry

        lax.fori_loop(0, whole, step, 0)
    if count - whole * size:
        body(pl.ds(whole * size, count - whole * size), whole)
        tick(whole)


def row_loop(count, size, body, init=0):
    def step(t, carry):
        return body(pl.ds(pl.multiple_of(t * size, size), size), carry)

    return lax.fori_loop(0, count // size, step, init)


def fold(v):
    return jnp.sum(v.reshape(v.shape[0] // 8, 8, v.shape[1]), axis=0)


def total(v):
    return jnp.sum(v, axis=0, keepdims=True)


def greet(seq=0, heads=0, line=0):
    barrier = pltpu.get_barrier_semaphore()
    me, h = lax.axis_index("seq"), lax.axis_index("heads")
    peers = 0
    for d in range(1, seq):
        pl.semaphore_signal(barrier, inc=1, device_id={"seq": lax.rem(me + d, seq)}, device_id_type=MESH)
        peers = peers + 1
    for d in range(1, heads):
        pl.semaphore_signal(
            barrier, inc=1, device_id={"heads": lax.rem(h + d, heads)}, device_id_type=MESH
        )
        peers = peers + 1
    if line:
        for step in (-1, 1):

            @pl.when((h + step >= 0) & (h + step < line))
            def _(step=step):
                pl.semaphore_signal(barrier, inc=1, device_id={"heads": h + step}, device_id_type=MESH)

        peers = peers + jnp.where((h == 0) | (h == line - 1), 1, 2)
    pl.semaphore_wait(barrier, peers)


def remote(src, dst, send_sem, recv_sem, **where):
    return pltpu.make_async_remote_copy(
        src_ref=src, dst_ref=dst, send_sem=send_sem, recv_sem=recv_sem, device_id=where, device_id_type=MESH
    )


class Exchange:
    def __init__(self, kind, seq_n, pairs, src, dst, send_sem, recv_sem):
        fan = seq_n // pairs
        me = lax.axis_index("seq")
        self.me, self.src, self.dst, self.send_sem, self.recv_sem = me, src, dst, send_sem, recv_sem
        self.count = self.slots(kind, seq_n, pairs)
        self.target, self.block, self.slot = {
            "queries": (lambda p: p * fan + lax.rem(me, fan), lambda p: p, me // fan),
            "keys": (lambda e: e, lambda e: e // fan, me),
            "queries_back": (lambda i: lax.rem(me, fan) + fan * i, lambda i: i, me // fan),
            "keys_back": (lambda e: e, lambda e: e, me),
        }[kind]

    @staticmethod
    def slots(kind, seq_n, pairs):
        return pairs if kind.startswith("queries") else seq_n

    def copy(self, j):
        return remote(
            self.src(self.block(j)),
            self.dst(self.slot),
            self.send_sem.at[j],
            self.recv_sem.at[self.slot],
            seq=self.target(j),
        )

    def start(self, low=0, high=None):
        number = (self.count if high is None else high) - low

        def one(d, carry):
            j = low + lax.rem(self.me + d, number)

            @pl.when(self.target(j) != self.me)
            def _():
                self.copy(j).start()

            @pl.when(self.target(j) == self.me)
            def _():
                pltpu.make_async_copy(
                    self.src(self.block(j)), self.dst(self.slot), self.recv_sem.at[self.slot]
                ).start()

            return carry

        lax.fori_loop(0, number, one, 0)

    def wait_recv(self):
        def one(j, carry):
            pltpu.make_async_copy(self.dst(j), self.dst(j), self.recv_sem.at[j]).wait()
            return carry

        lax.fori_loop(0, self.count, one, 0)

    def wait_send(self):
        def one(j, carry):
            @pl.when(self.target(j) != self.me)
            def _():
                self.copy(j).wait_send()

            return carry

        lax.fori_loop(0, self.count, one, 0)


class Line:
    def __init__(self, x, out, got, near, held, *sems, per=None, base=0, lead=None):
        self.x, self.out, self.got, self.near, self.held = x, out, got, near, held
        self.far_send, self.far_recv, self.near_send, self.near_recv, self.down_send, self.down_recv = sems
        self.chunks, self.rows = got.shape[1], got.shape[2]
        self.per, self.base = per or self.chunks, base
        self.lead = self.chunks if lead is None else lead
        self.steps = self.done(self.chunks)
        self.h = lax.axis_index("heads")

    @staticmethod
    def done(chunks):
        return chunks + 3 * LAG

    @staticmethod
    def scratch(count, width, rows):
        chunks = count // (2 * rows) * PIECES
        one = pltpu.VMEM((chunks, rows, width // PIECES), BF16)
        return [
            pltpu.VMEM((2, chunks, rows, width // PIECES), BF16), one, one,
            dma(2, chunks), dma(2, chunks), dma(chunks), dma(chunks), dma(2, 2, chunks), dma(2, chunks),
        ]

    def ends(self, stream):
        if stream == 0:
            return self.h, self.h + 1, self.h - 1
        return 3 - self.h, self.h - 1, self.h + 1

    def place(self, stream, c):
        rows, per, width = self.rows, self.per // PIECES, self.got.shape[3]
        r, piece = c // PIECES, lax.rem(c, PIECES)
        first = self.base + ((r // per) * 2 + (1 - stream)) * (per * rows) + lax.rem(r, per) * rows
        return pl.ds(pl.multiple_of(first, rows), rows), pl.ds(pl.multiple_of(piece * width, width), width)

    def far(self, stream, c, src, to):
        return remote(
            src, self.got.at[stream, c], self.far_send.at[stream, c], self.far_recv.at[stream, c], heads=to
        )

    def close(self, stream, c, to):
        return remote(
            self.x.at[*self.place(stream, c)], self.near.at[c], self.near_send.at[c], self.near_recv.at[c], heads=to
        )

    def down(self, stream, way, c, to):
        part = self.out.at[*self.place(stream, c)]
        return remote(part, part, self.down_send.at[stream, way, c], self.down_recv.at[stream, c], heads=to)

    def give(self, c):
        for stream in range(2):
            pos, ahead, behind = self.ends(stream)

            @pl.when((pos == 0) & (c < self.chunks))
            def _():
                self.far(stream, c, self.x.at[*self.place(stream, c)], ahead).start()

        c = c - NEAR_LATE
        for stream in range(2):
            pos, ahead, behind = self.ends(stream)

            @pl.when((pos == 3) & (c >= 0) & (c < self.chunks))
            def _():
                self.close(stream, c, behind).start()

    def first(self):
        def one(c, carry):
            self.give(c)
            return carry

        lax.fori_loop(0, self.lead, one, 0)

    def step(self, t):
        self.give(t + self.lead)
        for stream in range(2):
            pos, ahead, behind = self.ends(stream)

            @pl.when((pos == 1) & (t < self.chunks))
            def _():
                self.far(stream, t, self.held.at[t], self.h).wait_recv()
                at = self.place(stream, t)
                self.held[t] = (self.got[stream, t].astype(F32) + self.x[*at].astype(F32)).astype(BF16)
                self.far(stream, t, self.held.at[t], ahead).start()

        for stream in range(2):
            pos, ahead, behind = self.ends(stream)
            c = t - LAG

            @pl.when((pos == 2) & (c >= 0) & (c < self.chunks))
            def _():
                self.far(stream, c, self.held.at[c], self.h).wait_recv()
                self.close(stream, c, self.h).wait_recv()
                at = self.place(stream, c)
                value = self.got[stream, c].astype(F32) + self.near[c].astype(F32) + self.x[*at].astype(F32)
                self.out[*at] = value.astype(BF16)
                self.down(stream, 0, c, behind).start()
                self.down(stream, 1, c, ahead).start()

        for stream in range(2):
            pos, ahead, behind = self.ends(stream)
            b = t - jnp.where(pos == 0, 3 * LAG, 2 * LAG)

            @pl.when((pos != 2) & (b >= 0) & (b < self.chunks))
            def _():
                self.down(stream, 0, b, self.h).wait_recv()

                @pl.when(pos == 1)
                def _():
                    self.down(stream, 0, b, behind).start()

    def run(self, start, stop):
        def one(t, carry):
            self.step(t)
            return carry

        lax.fori_loop(start, stop, one, 0)

    def spread(self, start, stop, ticks):
        def tick(k):
            now, then = (k * (stop - start)) // ticks, ((k + 1) * (stop - start)) // ticks
            self.run(start + now, start + then)

        return tick

    def drain(self):
        def one(c, carry):
            for stream in range(2):
                pos, ahead, behind = self.ends(stream)

                @pl.when(pos <= 1)
                def _():
                    self.far(stream, c, self.held.at[c], self.h).wait_send()

                @pl.when(pos == 3)
                def _():
                    self.close(stream, c, self.h).wait_send()

                @pl.when((pos == 1) | (pos == 2))
                def _():
                    self.down(stream, 0, c, self.h).wait_send()

                @pl.when(pos == 2)
                def _():
                    self.down(stream, 1, c, self.h).wait_send()

            return carry

        lax.fori_loop(0, self.chunks, one, 0)


class Across:
    def __init__(self, depth, part, others, send_sem, recv_sem):
        self.depth, self.part, self.others, self.sems = depth, part, others, (send_sem, recv_sem)
        self.h = lax.axis_index("heads")

    def copy(self, d):
        to = lax.rem(self.h + d, self.depth)
        return remote(
            self.part, self.others.at[self.h], self.sems[0].at[d], self.sems[1].at[self.h], heads=to
        )

    def start(self):
        for d in range(1, self.depth):
            self.copy(d).start()

    def finish(self):
        value = self.part[...].astype(F32)
        for d in range(1, self.depth):
            came = self.others.at[lax.rem(self.h + d, self.depth)]
            pltpu.make_async_copy(came, came, self.sems[1].at[lax.rem(self.h + d, self.depth)]).wait()
            value = value + came[...].astype(F32)
        for d in range(1, self.depth):
            self.copy(d).wait_send()
        return value


def column_stats(w, at, b, aw):
    ab = dot(dot(at, at, NT), b)
    bf = b.astype(F32)

    acc = jnp.zeros((8, w.shape[1]), F32)
    for first in range(0, w.shape[0], 64):
        v = w[first : first + 64, :].astype(F32)
        acc = acc + fold(v * v)
    squares = total(acc) + 2.0 * ADAPT_SCALE * total(bf * aw) + ADAPT_SCALE**2 * total(bf * ab)
    return squares, aw + ADAPT_SCALE * ab


def front_kernel(
    seq_n, depth, rows_n, group, heads,
    x, gain, cos, sin, at_qkv, b_qkv, m_qkv, at_out, b_out, at_down, b_down, at_gu, b_gu,
    w_qkv, w_out, w_down, w_gu,
    h1_far, pre_far, q, k, v, inverse_one, low, norm_qkv, v_qkv, norms, v_out, v_down, norm_gu, v_gu,
    h1, pre, wq, wo, wd, wg, turned, part, others, q_send, q_recv, k_send, k_recv, v_send, v_recv, z_send, z_recv, load, leave,
):
    count, pairs = rows_n * group, rows_n * heads
    leaving = [pltpu.make_async_copy(pre.at[i], pre_far.at[i], leave.at[i]) for i in range(3)]
    leaving.append(pltpu.make_async_copy(h1, h1_far, leave.at[3]))
    loads = [pltpu.make_async_copy(w_qkv.at[i], wq.at[i], load.at[i]) for i in range(3)]
    loads += [
        pltpu.make_async_copy(w_out, wo, load.at[3]),
        pltpu.make_async_copy(w_down, wd, load.at[4]),
        pltpu.make_async_copy(w_gu, wg, load.at[5]),
    ]
    for one in loads[:3]:
        one.start()
    greet(seq=seq_n, heads=depth)

    def norm(rows, carry):
        v = x[rows, :].astype(F32)
        inverse = lax.rsqrt(jnp.mean(v * v, axis=-1, keepdims=True) + NORM_EPS)
        h1[rows, :] = (v * inverse * gain[...]).astype(BF16)
        inverse_one[rows, :] = jnp.broadcast_to(inverse, (rows.size, HD))
        return carry

    row_loop(count, 32, norm)
    for i in range(3):
        h1[count + i * RANK : count + (i + 1) * RANK, :] = at_qkv[i]
    leaving[3].start()
    low[...] = dot(h1[:count, :], h1[count:, :], NT).astype(BF16)
    exchanges = [
        Exchange(kind, seq_n, pairs, lambda j, i=i: turned.at[i, j], lambda j, to=to: to.at[j], *sems)
        for i, (kind, to, sems) in enumerate(
            (("queries", q, (q_send, q_recv)), ("keys", k, (k_send, k_recv)), ("keys", v, (v_send, v_recv)))
        )
    ]
    for i in range(3):
        loads[i].wait()
        loads[3 + i].start()

        def project(over, t, i=i):
            width = over.size
            r = dot(h1[...], wq[i, :, over])
            b = b_qkv[i, :, over]
            value = r[:count] + ADAPT_SCALE * dot(low[:, i * RANK : (i + 1) * RANK], b)
            aw = r[count + i * RANK : count + (i + 1) * RANK]
            squares, av = column_stats(wq.at[i, :, over], at_qkv[i], b, aw)
            n = jnp.sqrt(squares + COLUMN_EPS)
            norm_qkv[i : i + 1, over] = n
            v_qkv[i, :, over] = av
            pre[i, :, over] = value.astype(BF16)
            scaled = value * (m_qkv[i : i + 1, over] / n)
            for row in range(rows_n):
                rows = slice(row * group, (row + 1) * group)
                for hh in range(width // HD):
                    part_ = scaled[rows, hh * HD : (hh + 1) * HD]
                    if i < 2:
                        part_ = part_ * cos[rows, :] + pltpu.roll(part_, HD // 2, 1) * sin[rows, :]
                    turned[i, row * heads + t * (width // HD) + hh] = part_.astype(BF16)

        tiles(heads * HD, WIDE, project)
        exchanges[i].start()
        leaving[i].start()

    part[...] = jnp.zeros_like(part)
    for row, (w, at, b, av, loaded) in enumerate(
        ((wo, at_out, b_out, v_out, loads[3]), (wd, at_down, b_down, v_down, loads[4]))
    ):
        loaded.wait()

        def stats(over, t, row=row, w=w, at=at, b=b, av=av):
            squares, value = column_stats(w.at[:, over], at[...], b[:, over], dot(at[...], w[:, over]))
            part[row : row + 1, over] = squares
            av[:, over] = value

        tiles(w.shape[1], WIDE, stats)
    across = Across(depth, part, others, z_send, z_recv)
    across.start()
    loads[5].wait()
    for i in range(2):

        def stats_gu(over, t, i=i):
            b = b_gu[i, :, over]
            squares, value = column_stats(wg.at[i, :, over], at_gu[i], b, dot(at_gu[i], wg[i, :, over]))
            norm_gu[i : i + 1, over] = jnp.sqrt(squares + COLUMN_EPS)
            v_gu[i, :, over] = value

        tiles(wg.shape[2], WIDE, stats_gu)
    norms[...] = jnp.sqrt(across.finish() + COLUMN_EPS)
    for one in exchanges:
        one.wait_recv()
    for one in exchanges:
        one.wait_send()
    for one in leaving:
        one.wait()


def front(sizes, x, gain, cos, sin, qkv, out, down, gu):
    seq_n, depth, rows_n, group, heads = sizes
    count, pairs, width = rows_n * group, rows_n * heads, x.shape[1]
    local, hidden = qkv[0].shape[2], gu[0].shape[2]
    return pl.pallas_call(
        functools.partial(front_kernel, *sizes),
        out_shape=[
            shape(count + 3 * RANK, width), shape(3, count, local),
            shape(pairs, group, HD), shape(seq_n, group, HD), shape(seq_n, group, HD),
            shape(count, HD, dtype=F32), shape(count, 3 * RANK),
            shape(3, local, dtype=F32), shape(3, RANK, local, dtype=F32), shape(8, width, dtype=F32),
            shape(RANK, width, dtype=F32), shape(RANK, width, dtype=F32),
            shape(2, hidden, dtype=F32), shape(2, RANK, hidden, dtype=F32),
        ],
        in_specs=[IN_VMEM] * 13 + [ANYWHERE] * 4,
        out_specs=[ANYWHERE] * 2 + [IN_VMEM] * 12,
        scratch_shapes=[
            pltpu.VMEM((count + 3 * RANK, width), BF16), pltpu.VMEM((3, count, local), BF16),
            pltpu.VMEM(qkv[0].shape, BF16), pltpu.VMEM(out[0].shape, BF16), pltpu.VMEM(down[0].shape, BF16),
            pltpu.VMEM(gu[0].shape, BF16), pltpu.VMEM((3, pairs, group, HD), BF16),
            pltpu.VMEM((8, width), F32), pltpu.VMEM((depth, 8, width), F32),
            dma(pairs), dma(pairs), dma(seq_n), dma(seq_n), dma(seq_n), dma(seq_n), dma(depth), dma(depth), dma(6), dma(4),
        ],
        compiler_params=params(60, 1),
    )(
        x, gain, cos, sin, qkv[1], qkv[2], qkv[3], out[1], out[2], down[1], down[2], gu[1], gu[2],
        qkv[0], out[0], down[0], gu[0],
    )


def attend_kernel(block, low_ref, high_ref, q_ref, k_ref, v_ref, start_ref, place_ref, o_ref, lse_ref, vt):
    scale = HD**-0.5 * LOG2E
    vt[...] = v_ref[...].T

    def per_query(i, carry):
        at = pl.ds(pl.multiple_of(i * block, block), block)
        q = q_ref[at, :]
        start, place = start_ref[:, at], place_ref[:, at]

        def per_key(j, state):
            top, count, acc = state
            over = pl.ds(pl.multiple_of(j * block, block), block)
            s = dot(k_ref[over, :], q, NT) * scale
            key = j * block + lax.broadcasted_iota(jnp.int32, (block, block), 0)
            s = jnp.where((key >= start) & (key <= place), s, NEG_LARGE)
            new_top = jnp.maximum(top, jnp.max(s, axis=0, keepdims=True))
            p = jnp.exp2(s - new_top)
            fade = jnp.exp2(top - new_top)
            count = count * fade + total(p)
            acc = acc * fade + dot(vt[:, over], p)
            return new_top, count, acc

        begin = (
            jnp.full((1, block), -1e29, F32),
            jnp.zeros((1, block), F32),
            jnp.zeros((HD, block), F32),
        )
        top, count, acc = lax.fori_loop(low_ref[i], high_ref[i] + 1, per_key, begin)
        o_ref[at, :] = (acc / count).T.astype(BF16)
        lse_ref[:, at] = top + jnp.log2(count)
        return carry

    lax.fori_loop(0, q_ref.shape[0] // block, per_query, 0)


def attend(q, k, v, low, high, start, place, block):
    return pl.pallas_call(
        functools.partial(attend_kernel, block),
        out_shape=[shape(*q.shape), shape(1, q.shape[0], dtype=F32)],
        in_specs=[IN_SMEM] * 2 + [IN_VMEM] * 5,
        out_specs=[IN_VMEM] * 2,
        scratch_shapes=[pltpu.VMEM((HD, k.shape[0]), BF16)],
        compiler_params=params(62),
    )(low, high, q, k, v, start, place)


def attend_back(block, fan, q_ref, k_ref, v_ref, o_ref, do_ref, lse_ref, start_ref, place_ref, dq, dk, dv, kt, dk_acc, dv_acc, spread):
    scale = HD**-0.5
    mine = lax.rem(lax.axis_index("seq"), fan)
    group = dq.shape[1]
    split = block // group
    blocks = q_ref.shape[0] // block

    def reach(i):
        return ((mine + fan * ((i + 1) * split - 1) + 1) * group - 1) // block + 1

    tick = spread(sum(reach(i) for i in range(blocks)))
    kt[...] = k_ref[...].T
    dk_acc[...] = jnp.zeros_like(dk_acc)
    dv_acc[...] = jnp.zeros_like(dv_acc)

    def per_query(i, before):
        at = pl.ds(pl.multiple_of(i * block, block), block)
        q, do = q_ref[at, :], do_ref[at, :]
        start, place, lse = start_ref[:, at], place_ref[:, at], lse_ref[:, at]
        delta = total((do.astype(F32) * o_ref[at, :].astype(F32)).T)

        def per_key(j, acc):
            over = pl.ds(pl.multiple_of(j * block, block), block)
            k = k_ref[over, :]
            s = dot(k, q, NT) * (scale * LOG2E)
            key = j * block + lax.broadcasted_iota(jnp.int32, (block, block), 0)
            p = jnp.exp2(jnp.where((key >= start) & (key <= place), s - lse, NEG_LARGE))
            dp = dot(v_ref[over, :], do, NT)
            ds = (p * (dp - delta)).astype(BF16)
            dv_acc[over, :] += dot(p, do)
            dk_acc[over, :] += dot(ds, q)
            tick(before + j)
            return acc + dot(kt[:, over], ds)

        acc = lax.fori_loop(0, reach(i), per_key, jnp.zeros((HD, block), F32))
        acc = (acc * scale).T.astype(BF16)
        for n in range(split):
            dq[i * split + n] = acc[n * group : (n + 1) * group]
        return before + reach(i)

    lax.fori_loop(0, blocks, per_query, 0)

    def store(j, carry):
        over = pl.ds(pl.multiple_of(j * group, group), group)
        dk[j] = (dk_acc[over, :] * scale).astype(BF16)
        dv[j] = dv_acc[over, :].astype(BF16)
        return carry

    lax.fori_loop(0, k_ref.shape[0] // group, store, 0)


def core_kernel(
    seq_n, depth, rows_n, group, heads,
    o, gain, m_out, norms, at_out, b_out, v_out, at_gu, b_gu, m_gu, norm_gu, v_gu, at_down, b_down, m_down, v_down,
    x_far, cotangent_far, w_out, w_gu, w_down,
    dx2_far, x2_far, down_far, do, gm_down, ga_gu, gb_gu, gm_gu, g_gain, ga_down, gb_down, ga_out, gb_out, gm_out,
    dx2, x2_out, down_part, out_pre, x, cotangent, wo, wg, wd, attn, low_out, part, part2, dh2, h2, pre, z, dp, dpd, tmp, low, mix, dpo, blocks,
    s_part, others, load, send, recv, back_send, back_recv, z_send, z_recv, away, *line_refs,
):
    count, pairs = rows_n * group, rows_n * heads
    half = count // 2
    hidden, width = wd.shape
    loads = [
        pltpu.make_async_copy(far, near, load.at[i])
        for i, (far, near) in enumerate(
            ((w_out, wo), (x_far, x), (w_gu.at[0], wg.at[0]), (w_gu.at[1], wg.at[1]), (cotangent_far, cotangent), (w_down, wd))
        )
    ]
    for one in loads:
        one.start()
    greet(seq=seq_n, heads=depth)

    def landing(pair):
        row, head = pair // heads, lax.rem(pair, heads)
        return attn.at[
            pl.ds(pl.multiple_of(row * group, group), group), pl.ds(pl.multiple_of(head * HD, HD), HD)
        ]

    def leaving(i, r):
        near, far = ((dx2, dx2_far), (x2_out, x2_far), (down_part, down_far))[i]
        return pltpu.make_async_copy(
            near.at[r * half : (r + 1) * half], far.at[r * half : (r + 1) * half], away.at[i, r]
        )

    come = Exchange("queries_back", seq_n, pairs, lambda i: o.at[i], landing, send, recv)
    leave = Exchange("queries", seq_n, pairs, lambda p: blocks.at[p], lambda s_: do.at[s_], back_send, back_recv)
    come.start()
    for ref in (s_part, ga_gu, gb_gu, gm_gu, g_gain, ga_down, gb_down, ga_out, gb_out, gm_out):
        ref[...] = jnp.zeros_like(ref)
    one_out = Line(part, out_pre, *line_refs[:9], per=half // (2 * CHUNK) * PIECES, lead=LEAD)
    two = [
        Line(part2, dh2, *line_refs[9 + 9 * r : 18 + 9 * r], base=r * half, lead=LEAD) for r in range(2)
    ]
    loads[0].wait()
    come.wait_recv()
    low_out[...] = dot(attn[...], at_out[...], NT).astype(BF16)

    def project(over, t):
        part[:, over] = (dot(attn[...], wo[:, over]) + ADAPT_SCALE * dot(low_out[...], b_out[:, over])).astype(BF16)

    tiles(width, WIDE, project)
    one_out.first()
    for one in loads[1:]:
        one.wait()
    n_out, n_down = 1.0 / norms[0:1, :], 1.0 / norms[1:2, :]
    c_out, c_down = m_out[...] * n_out, m_down[...] * n_down

    def feed_forward(r, tick):
        mine = slice(r * half, (r + 1) * half)
        base = r * half
        n_hidden, n_width = -(-hidden // WIDE), -(-width // WIDE)

        def there(rows):
            return pl.ds(pl.multiple_of(base + rows.start, rows.size), rows.size)

        def norm(rows, carry):
            x2 = x[there(rows), :].astype(F32) + out_pre[there(rows), :].astype(F32) * c_out
            inverse = lax.rsqrt(jnp.mean(x2 * x2, axis=-1, keepdims=True) + NORM_EPS)
            h2[rows, :] = (x2 * inverse * gain[...]).astype(BF16)
            dpd[rows, :] = (cotangent[there(rows), :].astype(F32) * c_down).astype(BF16)
            return carry

        row_loop(half, 32, norm)
        low[...] = dot(h2[...], at_gu[...].reshape(2 * RANK, width), NT).astype(BF16)

        def forward(over, t):
            n = over.size
            for i in range(2):
                tmp[i, :, :n] = dot(h2[...], wg[i, :, over]) + ADAPT_SCALE * dot(
                    low[:, i * RANK : (i + 1) * RANK], b_gu[i, :, over]
                )
            scale = [m_gu[i : i + 1, over] / norm_gu[i : i + 1, over] for i in range(2)]

            def gated(rows, carry):
                g, u = tmp[0, rows, :n], tmp[1, rows, :n]
                pre[0, rows, over] = g.astype(BF16)
                pre[1, rows, over] = u.astype(BF16)
                g = g * scale[0]
                z[rows, over] = (g * jax.nn.sigmoid(g) * (u * scale[1])).astype(BF16)
                return carry

            row_loop(half, 32, gated)

        tiles(hidden, WIDE, forward, tick)
        low_down = dot(z[...], at_down[...], NT).astype(BF16)

        def down(over, t):
            value = dot(z[...], wd[:, over]) + ADAPT_SCALE * dot(low_down, b_down[:, over])
            down_part[mine, over] = value.astype(BF16)
            s_part[0:1, over] += total(value * cotangent[mine, over].astype(F32))
            gb_down[:, over] += ADAPT_SCALE * dot(low_down, dpd[:, over], TN)

        tiles(width, WIDE, down, lambda t: tick(n_hidden + t))
        leaving(2, r).start()
        dlow_down = (ADAPT_SCALE * dot(dpd[...], b_down[...], NT)).astype(BF16)

        def backward(over, t):
            n = over.size
            tmp[0, :, :n] = dot(dpd[...], wd[over, :], NT) + dot(dlow_down, at_down[:, over])
            ga_down[:, over] += dot(dlow_down, z[:, over], TN)
            scale = [m_gu[i : i + 1, over] / norm_gu[i : i + 1, over] for i in range(2)]

            def gated(rows, sums):
                dz = tmp[0, rows, :n]
                pg, pu = pre[0, rows, over].astype(F32), pre[1, rows, over].astype(F32)
                g, u = pg * scale[0], pu * scale[1]
                sigma = jax.nn.sigmoid(g)
                dzs = dz * sigma
                e_g = dzs * u * (1.0 + g * (1.0 - sigma))
                e_u = dzs * g
                dp[0, rows, over] = (e_g * scale[0]).astype(BF16)
                dp[1, rows, over] = (e_u * scale[1]).astype(BF16)
                return sums[0] + fold(e_g * pg), sums[1] + fold(e_u * pu)

            zero = jnp.zeros((8, n), F32)
            sums = row_loop(half, 32, gated, (zero, zero))
            for i in range(2):
                s, inverse = total(sums[i]), 1.0 / norm_gu[i : i + 1, over]
                gm_gu[i : i + 1, over] += s * inverse
                turn = m_gu[i : i + 1, over] * s * inverse * inverse * inverse
                dp[i, half : half + RANK, over] = (b_gu[i, :, over].astype(F32) * turn).astype(BF16)
                gb_gu[i, :, over] += ADAPT_SCALE * (
                    dot(low[:, i * RANK : (i + 1) * RANK], dp[i, :half, over], TN) - v_gu[i, :, over] * turn
                )

        tiles(hidden, WIDE, backward, lambda t: tick(n_hidden + n_width + t))
        for i in range(2):
            both = ADAPT_SCALE * dot(dp[i], b_gu[i], NT)
            mix[:half, i * RANK : (i + 1) * RANK] = both[:half].astype(BF16)
            for k in range(2):
                mix[half + k * RANK : half + (k + 1) * RANK, i * RANK : (i + 1) * RANK] = (
                    both[half:] if i == k else jnp.zeros((RANK, RANK), F32)
                ).astype(BF16)

        def inputs(over, t):
            products = [dot(dp[i], wg[i, over, :], NT) for i in range(2)]
            through = dot(mix[...], at_gu[:, :, over].reshape(2 * RANK, over.size))
            value = products[0][:half] + products[1][:half] + through[:half]
            straight = dot(mix[:half, :], h2[:, over], TN)
            for i in range(2):
                v_tb = products[i][half:] + through[half + i * RANK : half + (i + 1) * RANK]
                ga_gu[i, :, over] += straight[i * RANK : (i + 1) * RANK] - ADAPT_SCALE * v_tb
            part2[mine, over] = value.astype(BF16)
            g_gain[:, over] += total(value * h2[:, over].astype(F32)) / gain[:, over]

        tiles(width, WIDE, inputs, lambda t: tick(2 * n_hidden + n_width + t))

    def out_back(r, tick):
        base, mine = r * half, slice(r * half, (r + 1) * half)
        rows_here = rows_n // 2

        def back(rows, sums):
            there = pl.ds(pl.multiple_of(base + rows.start, rows.size), rows.size)
            value = out_pre[there, :].astype(F32)
            x2 = x[there, :].astype(F32) + value * c_out
            inverse = lax.rsqrt(jnp.mean(x2 * x2, axis=-1, keepdims=True) + NORM_EPS)
            scaled = dh2[there, :].astype(F32) * gain[...]
            mean = jnp.mean(scaled * x2, axis=-1, keepdims=True)
            e = cotangent[there, :].astype(F32) + inverse * scaled - x2 * (inverse**3 * mean)
            dx2[there, :] = e.astype(BF16)
            x2_out[there, :] = x2.astype(BF16)
            dpo[rows, :] = (e * c_out).astype(BF16)
            tick(rows.start // rows.size)
            return sums + fold(e * value)

        s = total(row_loop(half, 16, back, jnp.zeros((8, width), F32)))
        turn = m_out[...] * s * n_out * n_out * n_out
        gm_out[...] += s * n_out
        dpo[half : half + RANK, :] = (b_out[...].astype(F32) * turn).astype(BF16)
        both = dot(dpo[...], b_out[...], NT)
        dlow, turned = (ADAPT_SCALE * both[:half]).astype(BF16), both[half:]

        def inputs(over, t):
            product = dot(dpo[...], wo[over, :], NT)
            value = (product[:half] + dot(dlow, at_out[:, over])).astype(BF16)
            for row in range(rows_here):
                for hh in range(over.size // HD):
                    blocks[(r * rows_here + row) * heads + t * (over.size // HD) + hh] = value[
                        row * group : (row + 1) * group, hh * HD : (hh + 1) * HD
                    ]
            ga_out[:, over] += dot(dlow, attn[mine, over], TN) - ADAPT_SCALE * (
                product[half:] + ADAPT_SCALE * dot(turned, at_out[:, over])
            )

        tiles(heads * HD, WIDE, inputs)
        leave.start(r * rows_here * heads, (r + 1) * rows_here * heads)
        leaving(0, r).start()
        leaving(1, r).start()
        gb_out[...] += ADAPT_SCALE * (dot(low_out[mine, :], dpo[:half, :], TN) - v_out[...] * turn)

    half_done = one_out.done(one_out.per)
    one_out.run(0, half_done)
    ticks = 2 * (-(-hidden // WIDE) - (-width // WIDE))
    feed_forward(0, one_out.spread(half_done, one_out.steps, ticks))
    two[0].first()
    feed_forward(1, two[0].spread(0, EARLY, ticks))
    across = Across(depth, s_part, others, z_send, z_recv)
    across.start()
    two[1].first()

    def together(k, carry):
        two[0].step(EARLY + k)
        two[1].step(k)
        return carry

    begun = two[0].steps - EARLY
    lax.fori_loop(0, begun, together, 0)
    out_back(0, two[1].spread(begun, two[1].steps, half // 16))
    out_back(1, lambda t: None)
    for line in [one_out] + two:
        line.drain()
    s = across.finish()[0:1, :]
    turn = m_down[...] * s * n_down * n_down * n_down
    tb = (b_down[...].astype(F32) * turn).astype(BF16)
    v_tb = dot(tb, wd[...], NT) + ADAPT_SCALE * dot(dot(tb, b_down[...], NT), at_down[...])
    ga_down[...] -= ADAPT_SCALE * v_tb
    gb_down[...] -= ADAPT_SCALE * v_down[...] * turn
    gm_down[...] = s * n_down
    come.wait_send()
    for i in range(3):
        for r in range(2):
            leaving(i, r).wait()
    leave.wait_recv()
    leave.wait_send()


def core(sizes, o, x, cotangent, gain, norms, out, down, gu):
    seq_n, depth, rows_n, group, heads = sizes
    count, pairs, width = rows_n * group, rows_n * heads, x.shape[1]
    hidden, half = down[0].shape[0], rows_n * group // 2
    return pl.pallas_call(
        functools.partial(core_kernel, *sizes),
        out_shape=[
            shape(count, width), shape(count, width), shape(count, width), shape(pairs, group, HD),
            shape(1, width, dtype=F32), shape(2, RANK, width, dtype=F32), shape(2, RANK, hidden, dtype=F32),
            shape(2, hidden, dtype=F32), shape(1, width, dtype=F32), shape(RANK, hidden, dtype=F32),
            shape(RANK, width, dtype=F32), shape(RANK, heads * HD, dtype=F32), shape(RANK, width, dtype=F32),
            shape(1, width, dtype=F32),
        ],
        in_specs=[IN_VMEM] * 16 + [ANYWHERE] * 5,
        out_specs=[ANYWHERE] * 3 + [IN_VMEM] * 11,
        scratch_shapes=[pltpu.VMEM((count, width), BF16)] * 3
        + [
            pltpu.VMEM((count, width), BF16), pltpu.VMEM((count, width), BF16), pltpu.VMEM((count, width), BF16),
            pltpu.VMEM(out[0].shape, BF16),
            pltpu.VMEM(gu[0].shape, BF16), pltpu.VMEM(down[0].shape, BF16), pltpu.VMEM((count, heads * HD), BF16),
            pltpu.VMEM((count, RANK), BF16), pltpu.VMEM((count, width), BF16), pltpu.VMEM((count, width), BF16),
            pltpu.VMEM((count, width), BF16), pltpu.VMEM((half, width), BF16), pltpu.VMEM((2, half, hidden), BF16),
            pltpu.VMEM((half, hidden), BF16), pltpu.VMEM((2, half + RANK, hidden), BF16),
            pltpu.VMEM((half, width), BF16), pltpu.VMEM((2, half, WIDE), F32), pltpu.VMEM((half, 2 * RANK), BF16),
            pltpu.VMEM((half + 2 * RANK, 2 * RANK), BF16),
            pltpu.VMEM((half + RANK, width), BF16), pltpu.VMEM((pairs, group, HD), BF16),
            pltpu.VMEM((8, width), F32), pltpu.VMEM((depth, 8, width), F32),
            dma(6), dma(pairs), dma(pairs), dma(pairs), dma(pairs), dma(depth), dma(depth), dma(3, 2),
        ]
        + Line.scratch(count, width, CHUNK)
        + Line.scratch(half, width, CHUNK) * 2,
        compiler_params=params(62, 2),
    )(o, gain, out[3], norms, *out[1:3], out[4], *gu[1:], *down[1:], x, cotangent, out[0], gu[0], down[0])


def last_kernel(
    seq_n, depth, rows_n, group, heads,
    lse, start, place, cos, sin, low, gain, at, b, m, norm, v_qkv,
    ga_gu, gb_out, gb_down, g_gain2, gm_out, gm_down, ga_out, gb_gu, gm_gu, ga_down, inverse_one, norms, m_down,
    down_far, q_far, k_far, v_far, o_far, do_far, h1_far, pre_far, w_qkv, x2_far, dx2_far,
    dx_far, mixed, wide, local, hid,
    dh1, dx, x2, down_part, q, k, v, o, do, h1, pre, kt, dk_acc, dv_acc, dq, dk, dv,
    wq, gq, gk, gv, dp, mix, part, wide_in, local_in, hid_in, wide_got, local_got, hid_got,
    piece, pieces, done, q_send, q_recv, k_send, k_recv, v_send, v_recv, load,
    r_send, r_recv, g_send, g_recv, z_send, z_recv, leave, *line_refs,
):
    count, pairs, width = rows_n * group, rows_n * heads, h1.shape[1]
    fan, me = seq_n // pairs, lax.axis_index("seq")
    loads = [
        pltpu.make_async_copy(far, near, load.at[i])
        for i, (far, near) in enumerate(
            (
                (down_far, down_part), (q_far, q), (k_far, k), (v_far, v), (o_far, o), (do_far, do), (h1_far, h1),
                (pre_far, pre), (w_qkv, wq), (x2_far, x2), (dx2_far, dx),
            )
        )
    ]
    for one in loads[:6]:
        one.start()
    greet(seq=seq_n, heads=depth)
    line_down = Line(down_part, mixed, *line_refs[:9], lead=LAST_LEAD)
    loads[0].wait()
    line_down.first()
    for one in loads[1:6]:
        one.wait()
    for one in loads[6:]:
        one.start()
    exchanges = [
        Exchange(kind, seq_n, pairs, lambda j, a=a: a.at[j], lambda j, to=to: to.at[j], *sems)
        for kind, a, to, sems in (
            ("queries_back", dq, gq, (q_send, q_recv)),
            ("keys_back", dk, gk, (k_send, k_recv)),
            ("keys_back", dv, gv, (v_send, v_recv)),
        )
    ]
    first, second = FIRST, SECOND
    attend_back(
        2 * group if fan == 1 else group, fan, q, k, v, o, do, lse, start, place, dq, dk, dv, kt, dk_acc, dv_acc,
        lambda ticks: line_down.spread(0, first, ticks),
    )
    for one in exchanges:
        one.start()

    wide_in[...] = jnp.zeros_like(wide_in)
    local_in[...] = jnp.zeros_like(local_in)
    hid_in[...] = jnp.zeros_like(hid_in)
    share = 1.0 / depth
    for i in range(2):
        wide_in[(3 + i) * RANK : (4 + i) * RANK, :] = ga_gu[i].astype(BF16)
        hid_in[i * RANK : (i + 1) * RANK, :] = gb_gu[i].astype(BF16)
    wide_in[5 * RANK : 6 * RANK, :] = gb_out[...].astype(BF16)
    wide_in[6 * RANK : 7 * RANK, :] = gb_down[...].astype(BF16)
    hid_in[3 * RANK : 4 * RANK, :] = ga_down[...].astype(BF16)
    local_in[4 * RANK : 5 * RANK, :] = ga_out[...].astype(BF16)
    hid_in[2 * RANK : 3 * RANK, :] = jnp.concatenate(
        [gm_gu[...], jnp.zeros((RANK - 2, hid_in.shape[1]), F32)], axis=0
    ).astype(BF16)

    sums = [None] * 3
    line_down.run(first, second)
    for one in loads[6:9]:
        one.wait()
    for i in range(3):
        exchanges[i].wait_recv()
        came = (gq, gk, gv)[i]
        for head in range(heads):
            cols = slice(head * HD, (head + 1) * HD)
            n = norm[i : i + 1, cols]
            c = m[i : i + 1, cols] / n
            s = jnp.zeros((1, HD), F32)
            for row in range(rows_n):
                rows = slice(row * group, (row + 1) * group)
                if i == 0:
                    e = came[row * heads + head].astype(F32)
                else:
                    e = came[(row * heads + head) * fan].astype(F32)
                    for g in range(1, fan):
                        e = e + came[(row * heads + head) * fan + g].astype(F32)
                if i < 2:
                    e = e * cos[rows, :] - pltpu.roll(e, HD // 2, 1) * sin[rows, :]
                s = s + total(e * pre[i, rows, cols].astype(F32))
                dp[i, rows, cols] = (e * c).astype(BF16)
            turn = m[i : i + 1, cols] * s / (n * n * n)
            dp[i, count : count + RANK, cols] = (b[i, :, cols].astype(F32) * turn).astype(BF16)
            local_in[i * RANK : (i + 1) * RANK, cols] = (
                ADAPT_SCALE * (dot(low[:, i * RANK : (i + 1) * RANK], dp[i, :count, cols], TN) - v_qkv[i, :, cols] * turn)
            ).astype(BF16)
            sums[i] = [s / n] if head == 0 else sums[i] + [s / n]
    local_in[3 * RANK : 4 * RANK, :] = jnp.concatenate(
        [jnp.concatenate(one, axis=1) for one in sums]
        + [jnp.zeros((RANK - 3, heads * HD), F32)], axis=0
    ).astype(BF16)
    mix[...] = jnp.zeros_like(mix)
    for i in range(3):
        both = (ADAPT_SCALE * dot(dp[i], b[i], NT)).astype(BF16)
        cols = slice(i * RANK, (i + 1) * RANK)
        mix[:count, cols] = both[:count]
        mix[count + i * RANK : count + (i + 1) * RANK, cols] = both[count:]

    def inputs(over, t):
        through = dot(mix[...], at[:, :, over].reshape(3 * RANK, over.size))
        straight = dot(mix[:count, :], h1[:count, over], TN)
        value = through[:count]
        for i in range(3):
            product = dot(dp[i], wq[i, over, :], NT)
            value = value + product[:count]
            rows = slice(i * RANK, (i + 1) * RANK)
            v_tb = product[count:] + through[count + i * RANK : count + (i + 1) * RANK]
            wide_in[rows, over] = (straight[rows] - ADAPT_SCALE * v_tb).astype(BF16)
        part[:, over] = value.astype(BF16)
        g_gain1 = total(value * h1[:count, over].astype(F32)) / gain[:, over]
        wide_in[7 * RANK : 8 * RANK, over] = jnp.concatenate(
            [
                g_gain1, g_gain2[:, over], gm_out[:, over] * share,
                gm_down[:, over] * share,
                jnp.zeros((RANK - 4, over.size), F32),
            ], axis=0,
        ).astype(BF16)

    tiles(width, WIDE, inputs, line_down.spread(second, line_down.steps, -(-width // WIDE)))
    line_down.drain()
    line = Line(part, dh1, *line_refs[:3], *line_refs[9:], lead=LAST_LEAD)
    line.first()
    for one in loads[9:]:
        one.wait()
    c_down = m_down[...] / norms[1:2, :]

    over_gain = 1.0 / gain[...]

    def sent(stream, r):
        at_ = line.place(stream, r * PIECES)[0]
        return pltpu.make_async_copy(dx.at[at_], dx_far.at[at_], leave.at[stream, r])

    def advance(t, carry):
        line.step(t)

        @pl.when(t < count // (2 * CHUNK))
        def _():
            rows = pl.ds(pl.multiple_of(t * (2 * CHUNK), 2 * CHUNK), 2 * CHUNK)
            mixed[rows, :] = (x2[rows, :].astype(F32) + mixed[rows, :].astype(F32) * c_down).astype(BF16)

        c = t - 3 * LAG
        r = c // PIECES

        @pl.when((c >= 0) & (lax.rem(c, PIECES) == PIECES - 1))
        def _():
            for stream in range(2):
                at_ = line.place(stream, c)[0]
                unit = h1[at_, :].astype(F32) * over_gain
                scaled = dh1[at_, :].astype(F32) * gain[...]
                mean = jnp.mean(scaled * unit, axis=-1, keepdims=True)
                change = inverse_one[at_, :1] * (scaled - unit * mean)
                dx[at_, :] = (dx[at_, :].astype(F32) + change).astype(BF16)
                sent(stream, r).start()

        return carry


    spread = seq_n // OWNERS
    slabs = (
        (wide_in, wide_got, wide, lambda j: j), (local_in, local_got, local, lambda j: j),
        (hid_in, hid_got, hid, lambda j: OWNERS - 1 - j),
    )
    own = me // spread
    chosen = lax.rem(me, spread) == 0

    def rows_of(j):
        return pl.ds(pl.multiple_of(j * RANK, RANK), RANK)

    def to_owner(i, j):
        src, got, _, owner = slabs[i]
        return remote(
            src.at[rows_of(j)], got.at[me], r_send.at[i, j], r_recv.at[i, me], seq=owner(j) * spread
        )

    def from_owner(i, j, target):
        result = slabs[i][2]
        return remote(
            done.at[i, :, : result.shape[1]], result.at[rows_of(j)], g_send.at[i, target], g_recv.at[i, j], seq=target
        )

    for i, (src, got, result, owner) in enumerate(slabs):
        for j in range(src.shape[0] // RANK):

            @pl.when(me != owner(j) * spread)
            def _(i=i, j=j):
                to_owner(i, j).start()

            @pl.when(me == owner(j) * spread)
            def _(src=src, got=got, i=i, j=j):
                pltpu.make_async_copy(src.at[rows_of(j)], got.at[me], r_recv.at[i, me]).start()

    lax.fori_loop(0, GATHER, advance, 0)
    across = Across(depth, piece, pieces, z_send, z_recv)
    blocks_n = [slab[0].shape[0] // RANK for slab in slabs]
    owns = [chosen & (slab[3](own) < n) for slab, n in zip(slabs, blocks_n)]
    for i, (src, got, result, owner) in enumerate(slabs):

        @pl.when(owns[i])
        def _(i=i, got=got, result=result):
            def add(s_, acc):
                pltpu.make_async_copy(got.at[s_], got.at[s_], r_recv.at[i, s_]).wait()
                return acc + got[s_].astype(F32)

            value = lax.fori_loop(0, seq_n, add, jnp.zeros((RANK, result.shape[1]), F32))
            if i == 0:
                piece[...] = value.astype(BF16)
                across.start()
            else:
                done[i, :, : result.shape[1]] = value.astype(BF16)

    lax.fori_loop(GATHER, GIVE, advance, 0)

    @pl.when(owns[0])
    def _():
        done[0, :, :] = across.finish().astype(BF16)

    for i, (src, got, result, owner) in enumerate(slabs):

        @pl.when(owns[i])
        def _(i=i, result=result, owner=owner):
            mine = owner(own)

            def give(d, carry):
                from_owner(i, mine, lax.rem(me + d, seq_n)).start()
                return carry

            lax.fori_loop(1, seq_n, give, 0)
            pltpu.make_async_copy(
                done.at[i, :, : result.shape[1]], result.at[rows_of(mine)], g_recv.at[i, mine]
            ).start()

    lax.fori_loop(GIVE, line.steps, advance, 0)
    line.drain()

    def gone(c, carry):
        for stream in range(2):
            sent(stream, c).wait()
        return carry

    lax.fori_loop(0, line.chunks // PIECES, gone, 0)
    for one in exchanges:
        one.wait_send()
    for i, (src, got, result, owner) in enumerate(slabs):
        for j in range(blocks_n[i]):

            @pl.when(me != owner(j) * spread)
            def _(i=i, j=j):
                to_owner(i, j).wait_send()

            pltpu.make_async_copy(result.at[rows_of(j)], result.at[rows_of(j)], g_recv.at[i, j]).wait()

        @pl.when(owns[i])
        def _(i=i, owner=owner):
            def given(d, carry):
                from_owner(i, owner(own), lax.rem(me + d, seq_n)).wait_send()
                return carry

            lax.fori_loop(1, seq_n, given, 0)


def last(sizes, ins, far, hidden):
    seq_n, depth, rows_n, group, heads = sizes
    qkv_w = far[8]
    count, pairs, width = rows_n * group, rows_n * heads, qkv_w.shape[1]
    local, length = qkv_w.shape[2], seq_n * group
    blocks = {width: 8, local: 5, hidden: 4}
    slabs = [(n * RANK, w) for w, n in blocks.items()]
    some, every = pltpu.VMEM((pairs, group, HD), BF16), pltpu.VMEM((seq_n, group, HD), BF16)
    return pl.pallas_call(
        functools.partial(last_kernel, *sizes),
        out_shape=[shape(count, width)] * 2 + [shape(*s) for s in slabs],
        in_specs=[IN_VMEM] * len(ins) + [ANYWHERE] * len(far),
        out_specs=[ANYWHERE] + [IN_VMEM] * 4,
        scratch_shapes=[pltpu.VMEM((count, width), BF16)] * 3
        + [pltpu.VMEM(a.shape, BF16) for a in far[:8]]
        + [
            pltpu.VMEM((HD, length), BF16), pltpu.VMEM((length, HD), F32), pltpu.VMEM((length, HD), F32),
            some, every, every,
            pltpu.VMEM(qkv_w.shape, BF16), some, every, every,
            pltpu.VMEM((3, count + RANK, local), BF16), pltpu.VMEM((count + 3 * RANK, 3 * RANK), BF16),
            pltpu.VMEM((count, width), BF16),
        ]
        + [pltpu.VMEM(s, BF16) for s in slabs]
        + [pltpu.VMEM((seq_n, RANK, s[1]), BF16) for s in slabs]
        + [
            pltpu.VMEM((RANK, width), BF16), pltpu.VMEM((depth, RANK, width), BF16), pltpu.VMEM((3, RANK, width), BF16),
            dma(pairs), dma(pairs), dma(seq_n), dma(seq_n), dma(seq_n), dma(seq_n), dma(11),
            dma(3, 8), dma(3, seq_n), dma(3, seq_n), dma(3, 8), dma(depth), dma(depth), dma(2, count // (2 * CHUNK)),
        ]
        + Line.scratch(count, width, CHUNK)
        + Line.scratch(count, width, CHUNK)[3:],
        compiler_params=params(62, 5),
    )(*ins, *far)


def leave_kernel(wide, local, hid, *outs):
    places = (
        (wide, 112, 1), (wide, 0, 48), (local, 0, 48), (local, 48, 3), (local, 64, 16), (wide, 80, 16), (wide, 114, 1),
        (wide, 113, 1), (wide, 48, 32), (hid, 0, 32), (hid, 32, 2), (hid, 48, 16), (wide, 96, 16), (wide, 115, 1),
    )
    for out, (slab, first, rows) in zip(outs, places):
        begin = first // RANK * RANK
        value = slab[begin : begin + -(-rows // RANK) * RANK, :].astype(F32)
        out[...] = value[first - begin : first - begin + rows].reshape(out.shape)


def large_kernel(dx, mixed, dx_out, mixed_out):
    dx_out[...] = dx[...].astype(F32)
    mixed_out[...] = mixed[...]


def large(dx, mixed):
    spec = pl.BlockSpec((64, dx.shape[1]), lambda i: (i, 0))
    return pl.pallas_call(
        large_kernel, out_shape=[shape(*dx.shape, dtype=F32), shape(*mixed.shape)], grid=(dx.shape[0] // 64,),
        in_specs=[spec] * 2, out_specs=[spec] * 2, compiler_params=params(62),
    )(dx, mixed)


def adapter_grads(wide, local, hid):
    w, n, f = wide.shape[1], local.shape[1], hid.shape[1]
    dims = (
        (1, w), (3, RANK, w), (3, RANK, n), (3, n), (RANK, n), (RANK, w), (1, w), (1, w), (2, RANK, w), (2, RANK, f),
        (2, f), (RANK, f), (RANK, w), (1, w),
    )
    return pl.pallas_call(
        leave_kernel,
        out_shape=[shape(*d, dtype=F32) for d in dims],
        in_specs=[IN_VMEM] * 3,
        out_specs=[IN_VMEM] * len(dims),
        compiler_params=params(62),
    )(wide, local, hid)


def per_device(
    tokens, attn_gain, base_qkv, adapt_a_qkv, adapt_b_qkv, magnitude_qkv, base_out, adapt_a_out,
    adapt_b_out, magnitude_out, ffn_gain, base_gu, adapt_a_gu, adapt_b_gu, magnitude_gu, base_down,
    adapt_a_down, adapt_b_down, magnitude_down, doc_lengths, cotangent,
):
    rows_n, group, width = tokens.shape
    count = rows_n * group
    local = base_qkv.shape[2]
    heads = local // HD
    pairs = rows_n * heads
    seq_n, depth = lax.axis_size("seq"), lax.axis_size("heads")
    sizes = (seq_n, depth, rows_n, group, heads)
    fan = seq_n // pairs
    length = group * seq_n
    me = lax.axis_index("seq")

    order = jnp.arange(doc_lengths.shape[1])
    doc_ends = jnp.sum(
        jnp.where(order[None, :, None] <= order[None, None, :], doc_lengths[:, :, None], 0), axis=1
    )
    doc_starts = doc_ends - doc_lengths

    def starts_of(places, ends, starts):
        inside = (places[..., None] >= starts) & (places[..., None] < ends)
        return jnp.sum(jnp.where(inside, starts, 0), axis=-1)

    mine = me * group + jnp.arange(group, dtype=jnp.int32)
    position = mine[None, :] - starts_of(
        jnp.broadcast_to(mine[None, :], (rows_n, group)), doc_ends[:, None], doc_starts[:, None]
    )
    half = HD // 2
    frequency = ROPE_BASE ** (jnp.arange(half, dtype=F32) * (-2.0 / HD))
    angles = position.reshape(count, 1).astype(F32) * frequency
    cos, sin = jnp.cos(angles), jnp.sin(angles)
    cos, sin = jnp.concatenate([cos, cos], axis=1), jnp.concatenate([-sin, sin], axis=1)
    row = me // fan // heads
    block_at = lax.rem(me, fan) + fan * jnp.arange(pairs, dtype=jnp.int32)
    place = (block_at[:, None] * group + jnp.arange(group, dtype=jnp.int32)[None, :]).reshape(-1)
    pick = (jnp.arange(rows_n) == row)[:, None]
    row_ends = jnp.sum(jnp.where(pick, doc_ends, 0), axis=0)
    row_starts = jnp.sum(jnp.where(pick, doc_starts, 0), axis=0)
    start = starts_of(place, row_ends, row_starts)
    low_block = start.reshape(-1, 2 * group)[:, 0] // (2 * group)
    high_block = place.reshape(-1, 2 * group)[:, -1] // (2 * group)
    place, start = place[None, :], start[None, :]

    x = tokens.reshape(count, width)
    dy = cotangent.reshape(count, width)
    gain1, gain2 = attn_gain[None, :], ffn_gain[None, :]
    m_out, m_down = magnitude_out[None, :], magnitude_down[None, :]
    at_qkv, at_gu = adapt_a_qkv.transpose(0, 2, 1), adapt_a_gu.transpose(0, 2, 1)
    at_out, at_down = adapt_a_out.T, adapt_a_down.T

    h1, pre, q, k, v, inverse_one, low, norm_qkv, v_qkv, norms, v_out, v_down, norm_gu, v_gu = front(
        sizes, x, gain1, cos, sin, (base_qkv, at_qkv, adapt_b_qkv, magnitude_qkv), (base_out, at_out, adapt_b_out),
        (base_down, at_down, adapt_b_down), (base_gu, at_gu, adapt_b_gu),
    )
    q, k, v = q.reshape(-1, HD), k.reshape(length, HD), v.reshape(length, HD)
    o, lse = attend(q, k, v, low_block, high_block, start, place, 2 * group)
    dx2, x2, down_part, do, gm_down, ga_gu, gb_gu, gm_gu, g_gain2, ga_down, gb_down, ga_out, gb_out, gm_out = core(
        sizes, o.reshape(-1, group, HD), x, dy, gain2, norms, (base_out, at_out, adapt_b_out, m_out, v_out),
        (base_down, at_down, adapt_b_down, m_down, v_down), (base_gu, at_gu, adapt_b_gu, magnitude_gu, norm_gu, v_gu),
    )
    dx, mixed, wide, narrow, hid = last(
        sizes,
        (
            lse, start, place, cos, sin, low, gain1, at_qkv, adapt_b_qkv, magnitude_qkv, norm_qkv, v_qkv, ga_gu, gb_out,
            gb_down, g_gain2, gm_out, gm_down, ga_out, gb_gu, gm_gu, ga_down, inverse_one, norms, m_down,
        ),
        (down_part, q, k, v, o, do.reshape(-1, HD), h1, pre, base_qkv, x2, dx2),
        base_down.shape[0],
    )
    g = adapter_grads(wide, narrow, hid)
    dx, mixed = large(dx, mixed)
    return (
        mixed.reshape(rows_n, group, width),
        dx.reshape(rows_n, group, width),
        g[0][0], g[1].transpose(0, 2, 1), g[2], g[3], g[4].T, g[5], g[6][0], g[7][0], g[8].transpose(0, 2, 1), g[9],
        g[10], g[11].T, g[12], g[13][0],
    )


def solution(mesh):
    in_specs = (
        P(None, "seq", None), P(), P(None, None, "heads"), P(), P(None, None, "heads"), P(None, "heads"),
        P("heads", None), P("heads", None), P(), P(), P(), P(None, None, "heads"), P(),
        P(None, None, "heads"), P(None, "heads"), P("heads", None), P("heads", None), P(), P(), P(),
        P(None, "seq", None),
    )
    out_specs = (
        P(None, "seq", None), P(None, "seq", None), P(), P(), P(None, None, "heads"), P(None, "heads"),
        P("heads", None), P(), P(), P(), P(), P(None, None, "heads"), P(None, "heads"),
        P("heads", None), P(), P(),
    )
    return jax.shard_map(
        per_device, mesh=mesh, in_specs=in_specs, out_specs=out_specs, check_vma=False
    )
```

```python
import functools

import jax
import jax.numpy as jnp
from jax import lax
from jax.experimental import pallas as pl
from jax.experimental.pallas import tpu as pltpu
from jax.sharding import PartitionSpec as P

HD = 128
RANK = 16
ADAPT_SCALE = 2.0
NORM_EPS = 1e-05
COLUMN_EPS = 1e-06
ROPE_BASE = 10000.0
NEG_LARGE = -1e30
LOG2E = 1.4426950408889634
F32 = jnp.float32
BF16 = jnp.bfloat16
MESH = pl.DeviceIdType.MESH
NN = (((1,), (0,)), ((), ()))
NT = (((1,), (1,)), ((), ()))
TN = (((0,), (0,)), ((), ()))
OWNERS = 8
CHUNK = 16
PIECES = 1
LAG = 2
LEAD = 4
NEAR_LATE = 1
EARLY = 8
LAST_LEAD = 4
FIRST, SECOND = 7, 13
GATHER, GIVE = 10, 14
WIDE = 512
IN_VMEM = pl.BlockSpec(memory_space=pltpu.VMEM)
IN_SMEM = pl.BlockSpec(memory_space=pltpu.SMEM)
ANYWHERE = pl.BlockSpec(memory_space=pl.ANY)


def dot(a, b, dims=NN):
    return lax.dot_general(a.astype(BF16), b.astype(BF16), dims, preferred_element_type=F32)


def shape(*dims, dtype=BF16):
    return jax.ShapeDtypeStruct(dims, dtype)


def dma(*dims):
    return pltpu.SemaphoreType.DMA(dims)


def params(mib, collective_id=None):
    more = {} if collective_id is None else {"collective_id": collective_id, "has_side_effects": True}
    return pltpu.CompilerParams(vmem_limit_bytes=mib * 2**20, **more)


def tiles(count, size, body, tick=lambda t: None):
    whole = count // size
    if whole:

        def step(t, carry):
            body(pl.ds(pl.multiple_of(t * size, 128), size), t)
            tick(t)
            return carry

        lax.fori_loop(0, whole, step, 0)
    if count - whole * size:
        body(pl.ds(whole * size, count - whole * size), whole)
        tick(whole)


def row_loop(count, size, body, init=0):
    def step(t, carry):
        return body(pl.ds(pl.multiple_of(t * size, size), size), carry)

    return lax.fori_loop(0, count // size, step, init)


def fold(v):
    return jnp.sum(v.reshape(v.shape[0] // 8, 8, v.shape[1]), axis=0)


def total(v):
    return jnp.sum(v, axis=0, keepdims=True)


def greet(seq=0, heads=0, line=0):
    barrier = pltpu.get_barrier_semaphore()
    me, h = lax.axis_index("seq"), lax.axis_index("heads")
    peers = 0
    for d in range(1, seq):
        pl.semaphore_signal(barrier, inc=1, device_id={"seq": lax.rem(me + d, seq)}, device_id_type=MESH)
        peers = peers + 1
    for d in range(1, heads):
        pl.semaphore_signal(
            barrier, inc=1, device_id={"heads": lax.rem(h + d, heads)}, device_id_type=MESH
        )
        peers = peers + 1
    if line:
        for step in (-1, 1):

            @pl.when((h + step >= 0) & (h + step < line))
            def _(step=step):
                pl.semaphore_signal(barrier, inc=1, device_id={"heads": h + step}, device_id_type=MESH)

        peers = peers + jnp.where((h == 0) | (h == line - 1), 1, 2)
    pl.semaphore_wait(barrier, peers)


def remote(src, dst, send_sem, recv_sem, **where):
    return pltpu.make_async_remote_copy(
        src_ref=src, dst_ref=dst, send_sem=send_sem, recv_sem=recv_sem, device_id=where, device_id_type=MESH
    )


class Exchange:
    def __init__(self, kind, seq_n, pairs, src, dst, send_sem, recv_sem):
        fan = seq_n // pairs
        me = lax.axis_index("seq")
        self.me, self.src, self.dst, self.send_sem, self.recv_sem = me, src, dst, send_sem, recv_sem
        self.count = self.slots(kind, seq_n, pairs)
        self.target, self.block, self.slot = {
            "queries": (lambda p: p * fan + lax.rem(me, fan), lambda p: p, me // fan),
            "keys": (lambda e: e, lambda e: e // fan, me),
            "queries_back": (lambda i: lax.rem(me, fan) + fan * i, lambda i: i, me // fan),
            "keys_back": (lambda e: e, lambda e: e, me),
        }[kind]

    @staticmethod
    def slots(kind, seq_n, pairs):
        return pairs if kind.startswith("queries") else seq_n

    def copy(self, j):
        return remote(
            self.src(self.block(j)),
            self.dst(self.slot),
            self.send_sem.at[j],
            self.recv_sem.at[self.slot],
            seq=self.target(j),
        )

    def start(self, low=0, high=None):
        number = (self.count if high is None else high) - low

        def one(d, carry):
            j = low + lax.rem(self.me + d, number)

            @pl.when(self.target(j) != self.me)
            def _():
                self.copy(j).start()

            @pl.when(self.target(j) == self.me)
            def _():
                pltpu.make_async_copy(
                    self.src(self.block(j)), self.dst(self.slot), self.recv_sem.at[self.slot]
                ).start()

            return carry

        lax.fori_loop(0, number, one, 0)

    def wait_recv(self):
        def one(j, carry):
            pltpu.make_async_copy(self.dst(j), self.dst(j), self.recv_sem.at[j]).wait()
            return carry

        lax.fori_loop(0, self.count, one, 0)

    def wait_send(self):
        def one(j, carry):
            @pl.when(self.target(j) != self.me)
            def _():
                self.copy(j).wait_send()

            return carry

        lax.fori_loop(0, self.count, one, 0)


class Line:
    def __init__(self, x, out, got, near, held, *sems, per=None, base=0, lead=None):
        self.x, self.out, self.got, self.near, self.held = x, out, got, near, held
        self.far_send, self.far_recv, self.near_send, self.near_recv, self.down_send, self.down_recv = sems
        self.chunks, self.rows = got.shape[1], got.shape[2]
        self.per, self.base = per or self.chunks, base
        self.lead = self.chunks if lead is None else lead
        self.steps = self.done(self.chunks)
        self.h = lax.axis_index("heads")

    @staticmethod
    def done(chunks):
        return chunks + 3 * LAG

    @staticmethod
    def scratch(count, width, rows):
        chunks = count // (2 * rows) * PIECES
        one = pltpu.VMEM((chunks, rows, width // PIECES), BF16)
        return [
            pltpu.VMEM((2, chunks, rows, width // PIECES), BF16), one, one,
            dma(2, chunks), dma(2, chunks), dma(chunks), dma(chunks), dma(2, 2, chunks), dma(2, chunks),
        ]

    def ends(self, stream):
        if stream == 0:
            return self.h, self.h + 1, self.h - 1
        return 3 - self.h, self.h - 1, self.h + 1

    def place(self, stream, c):
        rows, per, width = self.rows, self.per // PIECES, self.got.shape[3]
        r, piece = c // PIECES, lax.rem(c, PIECES)
        first = self.base + ((r // per) * 2 + (1 - stream)) * (per * rows) + lax.rem(r, per) * rows
        return pl.ds(pl.multiple_of(first, rows), rows), pl.ds(pl.multiple_of(piece * width, width), width)

    def far(self, stream, c, src, to):
        return remote(
            src, self.got.at[stream, c], self.far_send.at[stream, c], self.far_recv.at[stream, c], heads=to
        )

    def close(self, stream, c, to):
        return remote(
            self.x.at[*self.place(stream, c)], self.near.at[c], self.near_send.at[c], self.near_recv.at[c], heads=to
        )

    def down(self, stream, way, c, to):
        part = self.out.at[*self.place(stream, c)]
        return remote(part, part, self.down_send.at[stream, way, c], self.down_recv.at[stream, c], heads=to)

    def give(self, c):
        for stream in range(2):
            pos, ahead, behind = self.ends(stream)

            @pl.when((pos == 0) & (c < self.chunks))
            def _():
                self.far(stream, c, self.x.at[*self.place(stream, c)], ahead).start()

        c = c - NEAR_LATE
        for stream in range(2):
            pos, ahead, behind = self.ends(stream)

            @pl.when((pos == 3) & (c >= 0) & (c < self.chunks))
            def _():
                self.close(stream, c, behind).start()

    def first(self):
        def one(c, carry):
            self.give(c)
            return carry

        lax.fori_loop(0, self.lead, one, 0)

    def step(self, t):
        self.give(t + self.lead)
        for stream in range(2):
            pos, ahead, behind = self.ends(stream)

            @pl.when((pos == 1) & (t < self.chunks))
            def _():
                self.far(stream, t, self.held.at[t], self.h).wait_recv()
                at = self.place(stream, t)
                self.held[t] = (self.got[stream, t].astype(F32) + self.x[*at].astype(F32)).astype(BF16)
                self.far(stream, t, self.held.at[t], ahead).start()

        for stream in range(2):
            pos, ahead, behind = self.ends(stream)
            c = t - LAG

            @pl.when((pos == 2) & (c >= 0) & (c < self.chunks))
            def _():
                self.far(stream, c, self.held.at[c], self.h).wait_recv()
                self.close(stream, c, self.h).wait_recv()
                at = self.place(stream, c)
                value = self.got[stream, c].astype(F32) + self.near[c].astype(F32) + self.x[*at].astype(F32)
                self.out[*at] = value.astype(BF16)
                self.down(stream, 0, c, behind).start()
                self.down(stream, 1, c, ahead).start()

        for stream in range(2):
            pos, ahead, behind = self.ends(stream)
            b = t - jnp.where(pos == 0, 3 * LAG, 2 * LAG)

            @pl.when((pos != 2) & (b >= 0) & (b < self.chunks))
            def _():
                self.down(stream, 0, b, self.h).wait_recv()

                @pl.when(pos == 1)
                def _():
                    self.down(stream, 0, b, behind).start()

    def run(self, start, stop):
        def one(t, carry):
            self.step(t)
            return carry

        lax.fori_loop(start, stop, one, 0)

    def spread(self, start, stop, ticks):
        def tick(k):
            now, then = (k * (stop - start)) // ticks, ((k + 1) * (stop - start)) // ticks
            self.run(start + now, start + then)

        return tick

    def drain(self):
        def one(c, carry):
            for stream in range(2):
                pos, ahead, behind = self.ends(stream)

                @pl.when(pos <= 1)
                def _():
                    self.far(stream, c, self.held.at[c], self.h).wait_send()

                @pl.when(pos == 3)
                def _():
                    self.close(stream, c, self.h).wait_send()

                @pl.when((pos == 1) | (pos == 2))
                def _():
                    self.down(stream, 0, c, self.h).wait_send()

                @pl.when(pos == 2)
                def _():
                    self.down(stream, 1, c, self.h).wait_send()

            return carry

        lax.fori_loop(0, self.chunks, one, 0)


class Across:
    def __init__(self, depth, part, others, send_sem, recv_sem):
        self.depth, self.part, self.others, self.sems = depth, part, others, (send_sem, recv_sem)
        self.h = lax.axis_index("heads")

    def copy(self, d):
        to = lax.rem(self.h + d, self.depth)
        return remote(
            self.part, self.others.at[self.h], self.sems[0].at[d], self.sems[1].at[self.h], heads=to
        )

    def start(self):
        for d in range(1, self.depth):
            self.copy(d).start()

    def finish(self):
        value = self.part[...].astype(F32)
        for d in range(1, self.depth):
            came = self.others.at[lax.rem(self.h + d, self.depth)]
            pltpu.make_async_copy(came, came, self.sems[1].at[lax.rem(self.h + d, self.depth)]).wait()
            value = value + came[...].astype(F32)
        for d in range(1, self.depth):
            self.copy(d).wait_send()
        return value


def column_stats(w, at, b, aw):
    ab = dot(dot(at, at, NT), b)
    bf = b.astype(F32)

    acc = jnp.zeros((8, w.shape[1]), F32)
    for first in range(0, w.shape[0], 64):
        v = w[first : first + 64, :].astype(F32)
        acc = acc + fold(v * v)
    squares = total(acc) + 2.0 * ADAPT_SCALE * total(bf * aw) + ADAPT_SCALE**2 * total(bf * ab)
    return squares, aw + ADAPT_SCALE * ab


def front_kernel(
    seq_n, depth, rows_n, group, heads,
    x, gain, cos, sin, at_qkv, b_qkv, m_qkv, at_out, b_out, at_down, b_down, at_gu, b_gu,
    w_qkv, w_out, w_down, w_gu,
    h1_far, pre_far, q, k, v, inverse_one, low, norm_qkv, v_qkv, norms, v_out, v_down, norm_gu, v_gu,
    h1, pre, wq, wo, wd, wg, turned, part, others, q_send, q_recv, k_send, k_recv, v_send, v_recv, z_send, z_recv, load, leave,
):
    count, pairs = rows_n * group, rows_n * heads
    leaving = [pltpu.make_async_copy(pre.at[i], pre_far.at[i], leave.at[i]) for i in range(3)]
    leaving.append(pltpu.make_async_copy(h1, h1_far, leave.at[3]))
    loads = [pltpu.make_async_copy(w_qkv.at[i], wq.at[i], load.at[i]) for i in range(3)]
    loads += [
        pltpu.make_async_copy(w_out, wo, load.at[3]),
        pltpu.make_async_copy(w_down, wd, load.at[4]),
        pltpu.make_async_copy(w_gu, wg, load.at[5]),
    ]
    for one in loads[:3]:
        one.start()
    greet(seq=seq_n, heads=depth)

    def norm(rows, carry):
        v = x[rows, :].astype(F32)
        inverse = lax.rsqrt(jnp.mean(v * v, axis=-1, keepdims=True) + NORM_EPS)
        h1[rows, :] = (v * inverse * gain[...]).astype(BF16)
        inverse_one[rows, :] = jnp.broadcast_to(inverse, (rows.size, HD))
        return carry

    row_loop(count, 32, norm)
    for i in range(3):
        h1[count + i * RANK : count + (i + 1) * RANK, :] = at_qkv[i]
    leaving[3].start()
    low[...] = dot(h1[:count, :], h1[count:, :], NT).astype(BF16)
    exchanges = [
        Exchange(kind, seq_n, pairs, lambda j, i=i: turned.at[i, j], lambda j, to=to: to.at[j], *sems)
        for i, (kind, to, sems) in enumerate(
            (("queries", q, (q_send, q_recv)), ("keys", k, (k_send, k_recv)), ("keys", v, (v_send, v_recv)))
        )
    ]
    for i in range(3):
        loads[i].wait()
        loads[3 + i].start()

        def project(over, t, i=i):
            width = over.size
            r = dot(h1[...], wq[i, :, over])
            b = b_qkv[i, :, over]
            value = r[:count] + ADAPT_SCALE * dot(low[:, i * RANK : (i + 1) * RANK], b)
            aw = r[count + i * RANK : count + (i + 1) * RANK]
            squares, av = column_stats(wq.at[i, :, over], at_qkv[i], b, aw)
            n = jnp.sqrt(squares + COLUMN_EPS)
            norm_qkv[i : i + 1, over] = n
            v_qkv[i, :, over] = av
            pre[i, :, over] = value.astype(BF16)
            scaled = value * (m_qkv[i : i + 1, over] / n)
            for row in range(rows_n):
                rows = slice(row * group, (row + 1) * group)
                for hh in range(width // HD):
                    part_ = scaled[rows, hh * HD : (hh + 1) * HD]
                    if i < 2:
                        part_ = part_ * cos[rows, :] + pltpu.roll(part_, HD // 2, 1) * sin[rows, :]
                    turned[i, row * heads + t * (width // HD) + hh] = part_.astype(BF16)

        tiles(heads * HD, WIDE, project)
        exchanges[i].start()
        leaving[i].start()

    part[...] = jnp.zeros_like(part)
    for row, (w, at, b, av, loaded) in enumerate(
        ((wo, at_out, b_out, v_out, loads[3]), (wd, at_down, b_down, v_down, loads[4]))
    ):
        loaded.wait()

        def stats(over, t, row=row, w=w, at=at, b=b, av=av):
            squares, value = column_stats(w.at[:, over], at[...], b[:, over], dot(at[...], w[:, over]))
            part[row : row + 1, over] = squares
            av[:, over] = value

        tiles(w.shape[1], WIDE, stats)
    across = Across(depth, part, others, z_send, z_recv)
    across.start()
    loads[5].wait()
    for i in range(2):

        def stats_gu(over, t, i=i):
            b = b_gu[i, :, over]
            squares, value = column_stats(wg.at[i, :, over], at_gu[i], b, dot(at_gu[i], wg[i, :, over]))
            norm_gu[i : i + 1, over] = jnp.sqrt(squares + COLUMN_EPS)
            v_gu[i, :, over] = value

        tiles(wg.shape[2], WIDE, stats_gu)
    norms[...] = jnp.sqrt(across.finish() + COLUMN_EPS)
    for one in exchanges:
        one.wait_recv()
    for one in exchanges:
        one.wait_send()
    for one in leaving:
        one.wait()


def front(sizes, x, gain, cos, sin, qkv, out, down, gu):
    seq_n, depth, rows_n, group, heads = sizes
    count, pairs, width = rows_n * group, rows_n * heads, x.shape[1]
    local, hidden = qkv[0].shape[2], gu[0].shape[2]
    return pl.pallas_call(
        functools.partial(front_kernel, *sizes),
        out_shape=[
            shape(count + 3 * RANK, width), shape(3, count, local),
            shape(pairs, group, HD), shape(seq_n, group, HD), shape(seq_n, group, HD),
            shape(count, HD, dtype=F32), shape(count, 3 * RANK),
            shape(3, local, dtype=F32), shape(3, RANK, local, dtype=F32), shape(8, width, dtype=F32),
            shape(RANK, width, dtype=F32), shape(RANK, width, dtype=F32),
            shape(2, hidden, dtype=F32), shape(2, RANK, hidden, dtype=F32),
        ],
        in_specs=[IN_VMEM] * 13 + [ANYWHERE] * 4,
        out_specs=[ANYWHERE] * 2 + [IN_VMEM] * 12,
        scratch_shapes=[
            pltpu.VMEM((count + 3 * RANK, width), BF16), pltpu.VMEM((3, count, local), BF16),
            pltpu.VMEM(qkv[0].shape, BF16), pltpu.VMEM(out[0].shape, BF16), pltpu.VMEM(down[0].shape, BF16),
            pltpu.VMEM(gu[0].shape, BF16), pltpu.VMEM((3, pairs, group, HD), BF16),
            pltpu.VMEM((8, width), F32), pltpu.VMEM((depth, 8, width), F32),
            dma(pairs), dma(pairs), dma(seq_n), dma(seq_n), dma(seq_n), dma(seq_n), dma(depth), dma(depth), dma(6), dma(4),
        ],
        compiler_params=params(60, 1),
    )(
        x, gain, cos, sin, qkv[1], qkv[2], qkv[3], out[1], out[2], down[1], down[2], gu[1], gu[2],
        qkv[0], out[0], down[0], gu[0],
    )


def attend_kernel(block, low_ref, high_ref, q_ref, k_ref, v_ref, start_ref, place_ref, o_ref, lse_ref, vt):
    scale = HD**-0.5 * LOG2E
    vt[...] = v_ref[...].T

    def per_query(i, carry):
        at = pl.ds(pl.multiple_of(i * block, block), block)
        q = q_ref[at, :]
        start, place = start_ref[:, at], place_ref[:, at]

        def per_key(j, state):
            top, count, acc = state
            over = pl.ds(pl.multiple_of(j * block, block), block)
            s = dot(k_ref[over, :], q, NT) * scale
            key = j * block + lax.broadcasted_iota(jnp.int32, (block, block), 0)
            s = jnp.where((key >= start) & (key <= place), s, NEG_LARGE)
            new_top = jnp.maximum(top, jnp.max(s, axis=0, keepdims=True))
            p = jnp.exp2(s - new_top)
            fade = jnp.exp2(top - new_top)
            count = count * fade + total(p)
            acc = acc * fade + dot(vt[:, over], p)
            return new_top, count, acc

        begin = (
            jnp.full((1, block), -1e29, F32),
            jnp.zeros((1, block), F32),
            jnp.zeros((HD, block), F32),
        )
        top, count, acc = lax.fori_loop(low_ref[i], high_ref[i] + 1, per_key, begin)
        o_ref[at, :] = (acc / count).T.astype(BF16)
        lse_ref[:, at] = top + jnp.log2(count)
        return carry

    lax.fori_loop(0, q_ref.shape[0] // block, per_query, 0)


def attend(q, k, v, low, high, start, place, block):
    return pl.pallas_call(
        functools.partial(attend_kernel, block),
        out_shape=[shape(*q.shape), shape(1, q.shape[0], dtype=F32)],
        in_specs=[IN_SMEM] * 2 + [IN_VMEM] * 5,
        out_specs=[IN_VMEM] * 2,
        scratch_shapes=[pltpu.VMEM((HD, k.shape[0]), BF16)],
        compiler_params=params(62),
    )(low, high, q, k, v, start, place)


def attend_back(block, fan, q_ref, k_ref, v_ref, o_ref, do_ref, lse_ref, start_ref, place_ref, dq, dk, dv, kt, dk_acc, dv_acc, spread):
    scale = HD**-0.5
    mine = lax.rem(lax.axis_index("seq"), fan)
    group = dq.shape[1]
    split = block // group
    blocks = q_ref.shape[0] // block

    def reach(i):
        return ((mine + fan * ((i + 1) * split - 1) + 1) * group - 1) // block + 1

    tick = spread(sum(reach(i) for i in range(blocks)))
    kt[...] = k_ref[...].T
    dk_acc[...] = jnp.zeros_like(dk_acc)
    dv_acc[...] = jnp.zeros_like(dv_acc)

    def per_query(i, before):
        at = pl.ds(pl.multiple_of(i * block, block), block)
        q, do = q_ref[at, :], do_ref[at, :]
        start, place, lse = start_ref[:, at], place_ref[:, at], lse_ref[:, at]
        delta = total((do.astype(F32) * o_ref[at, :].astype(F32)).T)

        def per_key(j, acc):
            over = pl.ds(pl.multiple_of(j * block, block), block)
            k = k_ref[over, :]
            s = dot(k, q, NT) * (scale * LOG2E)
            key = j * block + lax.broadcasted_iota(jnp.int32, (block, block), 0)
            p = jnp.exp2(jnp.where((key >= start) & (key <= place), s - lse, NEG_LARGE))
            dp = dot(v_ref[over, :], do, NT)
            ds = (p * (dp - delta)).astype(BF16)
            dv_acc[over, :] += dot(p, do)
            dk_acc[over, :] += dot(ds, q)
            tick(before + j)
            return acc + dot(kt[:, over], ds)

        acc = lax.fori_loop(0, reach(i), per_key, jnp.zeros((HD, block), F32))
        acc = (acc * scale).T.astype(BF16)
        for n in range(split):
            dq[i * split + n] = acc[n * group : (n + 1) * group]
        return before + reach(i)

    lax.fori_loop(0, blocks, per_query, 0)

    def store(j, carry):
        over = pl.ds(pl.multiple_of(j * group, group), group)
        dk[j] = (dk_acc[over, :] * scale).astype(BF16)
        dv[j] = dv_acc[over, :].astype(BF16)
        return carry

    lax.fori_loop(0, k_ref.shape[0] // group, store, 0)


def core_kernel(
    seq_n, depth, rows_n, group, heads,
    o, gain, m_out, norms, at_out, b_out, v_out, at_gu, b_gu, m_gu, norm_gu, v_gu, at_down, b_down, m_down, v_down,
    x_far, cotangent_far, w_out, w_gu, w_down,
    dx2_far, x2_far, down_far, do, gm_down, ga_gu, gb_gu, gm_gu, g_gain, ga_down, gb_down, ga_out, gb_out, gm_out,
    dx2, x2_out, down_part, out_pre, x, cotangent, wo, wg, wd, attn, low_out, part, part2, dh2, h2, pre, z, dp, dpd, tmp, low, mix, dpo, blocks,
    s_part, others, row_sums, load, send, recv, back_send, back_recv, z_send, z_recv, away, *line_refs,
):
    count, pairs = rows_n * group, rows_n * heads
    half = count // 2
    hidden, width = wd.shape
    loads = [
        pltpu.make_async_copy(far, near, load.at[i])
        for i, (far, near) in enumerate(
            ((w_out, wo), (x_far, x), (w_gu.at[0], wg.at[0]), (w_gu.at[1], wg.at[1]), (cotangent_far, cotangent), (w_down, wd))
        )
    ]
    for one in loads:
        one.start()
    greet(seq=seq_n, heads=depth)

    def landing(pair):
        row, head = pair // heads, lax.rem(pair, heads)
        return attn.at[
            pl.ds(pl.multiple_of(row * group, group), group), pl.ds(pl.multiple_of(head * HD, HD), HD)
        ]

    def leaving(i, r):
        near, far = ((dx2, dx2_far), (x2_out, x2_far), (down_part, down_far))[i]
        return pltpu.make_async_copy(
            near.at[r * half : (r + 1) * half], far.at[r * half : (r + 1) * half], away.at[i, r]
        )

    come = Exchange("queries_back", seq_n, pairs, lambda i: o.at[i], landing, send, recv)
    leave = Exchange("queries", seq_n, pairs, lambda p: blocks.at[p], lambda s_: do.at[s_], back_send, back_recv)
    come.start()
    for ref in (s_part, ga_gu, gb_gu, gm_gu, g_gain, ga_down, gb_down, ga_out, gb_out, gm_out):
        ref[...] = jnp.zeros_like(ref)
    one_out = Line(part, out_pre, *line_refs[:9], per=half // (2 * CHUNK) * PIECES, lead=LEAD)
    two = [
        Line(part2, dh2, *line_refs[9 + 9 * r : 18 + 9 * r], base=r * half, lead=LEAD) for r in range(2)
    ]
    loads[0].wait()
    come.wait_recv()
    low_out[...] = dot(attn[...], at_out[...], NT).astype(BF16)

    def project(over, t):
        part[:, over] = (dot(attn[...], wo[:, over]) + ADAPT_SCALE * dot(low_out[...], b_out[:, over])).astype(BF16)

    tiles(width, WIDE, project)
    one_out.first()
    for one in loads[1:]:
        one.wait()
    n_out, n_down = 1.0 / norms[0:1, :], 1.0 / norms[1:2, :]
    c_out, c_down = m_out[...] * n_out, m_down[...] * n_down

    def feed_forward(r, tick):
        mine = slice(r * half, (r + 1) * half)
        base = r * half
        n_hidden, n_width = -(-hidden // WIDE), -(-width // WIDE)

        def there(rows):
            return pl.ds(pl.multiple_of(base + rows.start, rows.size), rows.size)

        def norm(rows, carry):
            x2 = x[there(rows), :].astype(F32) + out_pre[there(rows), :].astype(F32) * c_out
            inverse = lax.rsqrt(jnp.mean(x2 * x2, axis=-1, keepdims=True) + NORM_EPS)
            h2[rows, :] = (x2 * inverse * gain[...]).astype(BF16)
            dpd[rows, :] = (cotangent[there(rows), :].astype(F32) * c_down).astype(BF16)
            return carry

        row_loop(half, 32, norm)
        low[...] = dot(h2[...], at_gu[...].reshape(2 * RANK, width), NT).astype(BF16)

        def forward(over, t):
            n = over.size
            for i in range(2):
                tmp[i, :, :n] = dot(h2[...], wg[i, :, over]) + ADAPT_SCALE * dot(
                    low[:, i * RANK : (i + 1) * RANK], b_gu[i, :, over]
                )
            scale = [m_gu[i : i + 1, over] / norm_gu[i : i + 1, over] for i in range(2)]

            def gated(rows, carry):
                g, u = tmp[0, rows, :n], tmp[1, rows, :n]
                pre[0, rows, over] = g.astype(BF16)
                pre[1, rows, over] = u.astype(BF16)
                g = g * scale[0]
                z[rows, over] = (g * jax.nn.sigmoid(g) * (u * scale[1])).astype(BF16)
                return carry

            row_loop(half, 32, gated)

        tiles(hidden, WIDE, forward, tick)
        low_down = dot(z[...], at_down[...], NT).astype(BF16)

        def down(over, t):
            value = dot(z[...], wd[:, over]) + ADAPT_SCALE * dot(low_down, b_down[:, over])
            down_part[mine, over] = value.astype(BF16)
            s_part[0:1, over] += total(value * cotangent[mine, over].astype(F32))
            gb_down[:, over] += ADAPT_SCALE * dot(low_down, dpd[:, over], TN)

        tiles(width, WIDE, down, lambda t: tick(n_hidden + t))
        leaving(2, r).start()
        dlow_down = (ADAPT_SCALE * dot(dpd[...], b_down[...], NT)).astype(BF16)

        def backward(over, t):
            n = over.size
            tmp[0, :, :n] = dot(dpd[...], wd[over, :], NT) + dot(dlow_down, at_down[:, over])
            ga_down[:, over] += dot(dlow_down, z[:, over], TN)
            scale = [m_gu[i : i + 1, over] / norm_gu[i : i + 1, over] for i in range(2)]

            def gated(rows, sums):
                dz = tmp[0, rows, :n]
                pg, pu = pre[0, rows, over].astype(F32), pre[1, rows, over].astype(F32)
                g, u = pg * scale[0], pu * scale[1]
                sigma = jax.nn.sigmoid(g)
                dzs = dz * sigma
                e_g = dzs * u * (1.0 + g * (1.0 - sigma))
                e_u = dzs * g
                dp[0, rows, over] = (e_g * scale[0]).astype(BF16)
                dp[1, rows, over] = (e_u * scale[1]).astype(BF16)
                return sums[0] + fold(e_g * pg), sums[1] + fold(e_u * pu)

            zero = jnp.zeros((8, n), F32)
            sums = row_loop(half, 32, gated, (zero, zero))
            for i in range(2):
                s, inverse = total(sums[i]), 1.0 / norm_gu[i : i + 1, over]
                gm_gu[i : i + 1, over] += s * inverse
                turn = m_gu[i : i + 1, over] * s * inverse * inverse * inverse
                dp[i, half : half + RANK, over] = (b_gu[i, :, over].astype(F32) * turn).astype(BF16)
                gb_gu[i, :, over] += ADAPT_SCALE * (
                    dot(low[:, i * RANK : (i + 1) * RANK], dp[i, :half, over], TN) - v_gu[i, :, over] * turn
                )

        tiles(hidden, WIDE, backward, lambda t: tick(n_hidden + n_width + t))
        for i in range(2):
            both = ADAPT_SCALE * dot(dp[i], b_gu[i], NT)
            mix[:half, i * RANK : (i + 1) * RANK] = both[:half].astype(BF16)
            for k in range(2):
                mix[half + k * RANK : half + (k + 1) * RANK, i * RANK : (i + 1) * RANK] = (
                    both[half:] if i == k else jnp.zeros((RANK, RANK), F32)
                ).astype(BF16)

        def inputs(over, t):
            products = [dot(dp[i], wg[i, over, :], NT) for i in range(2)]
            through = dot(mix[...], at_gu[:, :, over].reshape(2 * RANK, over.size))
            value = products[0][:half] + products[1][:half] + through[:half]
            straight = dot(mix[:half, :], h2[:, over], TN)
            for i in range(2):
                v_tb = products[i][half:] + through[half + i * RANK : half + (i + 1) * RANK]
                ga_gu[i, :, over] += straight[i * RANK : (i + 1) * RANK] - ADAPT_SCALE * v_tb
            part2[mine, over] = value.astype(BF16)
            g_gain[:, over] += total(value * h2[:, over].astype(F32)) / gain[:, over]

        tiles(width, WIDE, inputs, lambda t: tick(2 * n_hidden + n_width + t))

    def norm_back(r, first):
        rows = pl.ds(pl.multiple_of(first, 16), 16)
        there = pl.ds(pl.multiple_of(r * half + first, 16), 16)
        value = out_pre[there, :].astype(F32)
        x2 = x[there, :].astype(F32) + value * c_out
        inverse = lax.rsqrt(jnp.mean(x2 * x2, axis=-1, keepdims=True) + NORM_EPS)
        scaled = dh2[there, :].astype(F32) * gain[...]
        mean = jnp.mean(scaled * x2, axis=-1, keepdims=True)
        e = cotangent[there, :].astype(F32) + inverse * scaled - x2 * (inverse**3 * mean)
        dx2[there, :] = e.astype(BF16)
        x2_out[there, :] = x2.astype(BF16)
        dpo[rows, :] = (e * c_out).astype(BF16)
        row_sums[...] += fold(e * value)

    def out_back(r):
        mine = slice(r * half, (r + 1) * half)
        rows_here = rows_n // 2

        s = total(row_sums[...])
        turn = m_out[...] * s * n_out * n_out * n_out
        gm_out[...] += s * n_out
        dpo[half : half + RANK, :] = (b_out[...].astype(F32) * turn).astype(BF16)
        both = dot(dpo[...], b_out[...], NT)
        dlow, turned = (ADAPT_SCALE * both[:half]).astype(BF16), both[half:]

        def inputs(over, t):
            product = dot(dpo[...], wo[over, :], NT)
            value = (product[:half] + dot(dlow, at_out[:, over])).astype(BF16)
            for row in range(rows_here):
                for hh in range(over.size // HD):
                    blocks[(r * rows_here + row) * heads + t * (over.size // HD) + hh] = value[
                        row * group : (row + 1) * group, hh * HD : (hh + 1) * HD
                    ]
            ga_out[:, over] += dot(dlow, attn[mine, over], TN) - ADAPT_SCALE * (
                product[half:] + ADAPT_SCALE * dot(turned, at_out[:, over])
            )

        tiles(heads * HD, WIDE, inputs)
        leave.start(r * rows_here * heads, (r + 1) * rows_here * heads)
        leaving(0, r).start()
        leaving(1, r).start()
        gb_out[...] += ADAPT_SCALE * (dot(low_out[mine, :], dpo[:half, :], TN) - v_out[...] * turn)

    half_done = one_out.done(one_out.per)
    one_out.run(0, half_done)
    ticks = 2 * (-(-hidden // WIDE) - (-width // WIDE))
    feed_forward(0, one_out.spread(half_done, one_out.steps, ticks))
    two[0].first()
    feed_forward(1, two[0].spread(0, EARLY, ticks))
    across = Across(depth, s_part, others, z_send, z_recv)
    across.start()
    two[1].first()

    def together(k, carry):
        two[0].step(EARLY + k)
        two[1].step(k)
        return carry

    begun = two[0].steps - EARLY
    lax.fori_loop(0, begun, together, 0)
    row_sums[...] = jnp.zeros_like(row_sums)
    tick_two = two[1].spread(begun, begun + 2, half // 16)

    def first_half(k, carry):
        norm_back(0, k * 16)
        tick_two(k)
        return carry

    lax.fori_loop(0, half // 16, first_half, 0)
    out_back(0)
    row_sums[...] = jnp.zeros_like(row_sums)

    def second_half(t, carry):
        @pl.when(t >= begun + 2)
        def _():
            two[1].step(t)

        for stream in range(2):
            norm_back(1, ((1 - stream) * two[1].chunks + t - 3 * LAG) * CHUNK)
        return carry

    lax.fori_loop(3 * LAG, two[1].steps, second_half, 0)
    out_back(1)
    for line in [one_out] + two:
        line.drain()
    s = across.finish()[0:1, :]
    turn = m_down[...] * s * n_down * n_down * n_down
    tb = (b_down[...].astype(F32) * turn).astype(BF16)
    v_tb = dot(tb, wd[...], NT) + ADAPT_SCALE * dot(dot(tb, b_down[...], NT), at_down[...])
    ga_down[...] -= ADAPT_SCALE * v_tb
    gb_down[...] -= ADAPT_SCALE * v_down[...] * turn
    gm_down[...] = s * n_down
    come.wait_send()
    for i in range(3):
        for r in range(2):
            leaving(i, r).wait()
    leave.wait_recv()
    leave.wait_send()


def core(sizes, o, x, cotangent, gain, norms, out, down, gu):
    seq_n, depth, rows_n, group, heads = sizes
    count, pairs, width = rows_n * group, rows_n * heads, x.shape[1]
    hidden, half = down[0].shape[0], rows_n * group // 2
    return pl.pallas_call(
        functools.partial(core_kernel, *sizes),
        out_shape=[
            shape(count, width), shape(count, width), shape(count, width), shape(pairs, group, HD),
            shape(1, width, dtype=F32), shape(2, RANK, width, dtype=F32), shape(2, RANK, hidden, dtype=F32),
            shape(2, hidden, dtype=F32), shape(1, width, dtype=F32), shape(RANK, hidden, dtype=F32),
            shape(RANK, width, dtype=F32), shape(RANK, heads * HD, dtype=F32), shape(RANK, width, dtype=F32),
            shape(1, width, dtype=F32),
        ],
        in_specs=[IN_VMEM] * 16 + [ANYWHERE] * 5,
        out_specs=[ANYWHERE] * 3 + [IN_VMEM] * 11,
        scratch_shapes=[pltpu.VMEM((count, width), BF16)] * 3
        + [
            pltpu.VMEM((count, width), BF16), pltpu.VMEM((count, width), BF16), pltpu.VMEM((count, width), BF16),
            pltpu.VMEM(out[0].shape, BF16),
            pltpu.VMEM(gu[0].shape, BF16), pltpu.VMEM(down[0].shape, BF16), pltpu.VMEM((count, heads * HD), BF16),
            pltpu.VMEM((count, RANK), BF16), pltpu.VMEM((count, width), BF16), pltpu.VMEM((count, width), BF16),
            pltpu.VMEM((count, width), BF16), pltpu.VMEM((half, width), BF16), pltpu.VMEM((2, half, hidden), BF16),
            pltpu.VMEM((half, hidden), BF16), pltpu.VMEM((2, half + RANK, hidden), BF16),
            pltpu.VMEM((half, width), BF16), pltpu.VMEM((2, half, WIDE), F32), pltpu.VMEM((half, 2 * RANK), BF16),
            pltpu.VMEM((half + 2 * RANK, 2 * RANK), BF16),
            pltpu.VMEM((half + RANK, width), BF16), pltpu.VMEM((pairs, group, HD), BF16),
            pltpu.VMEM((8, width), F32), pltpu.VMEM((depth, 8, width), F32), pltpu.VMEM((8, width), F32),
            dma(6), dma(pairs), dma(pairs), dma(pairs), dma(pairs), dma(depth), dma(depth), dma(3, 2),
        ]
        + Line.scratch(count, width, CHUNK)
        + Line.scratch(half, width, CHUNK) * 2,
        compiler_params=params(62, 2),
    )(o, gain, out[3], norms, *out[1:3], out[4], *gu[1:], *down[1:], x, cotangent, out[0], gu[0], down[0])


def last_kernel(
    seq_n, depth, rows_n, group, heads,
    lse, start, place, cos, sin, low, gain, at, b, m, norm, v_qkv,
    ga_gu, gb_out, gb_down, g_gain2, gm_out, gm_down, ga_out, gb_gu, gm_gu, ga_down, inverse_one, norms, m_down,
    down_far, q_far, k_far, v_far, o_far, do_far, h1_far, pre_far, w_qkv, x2_far, dx2_far,
    dx_far, mixed, wide, local, hid,
    dh1, dx, x2, down_part, q, k, v, o, do, h1, pre, kt, dk_acc, dv_acc, dq, dk, dv,
    wq, gq, gk, gv, dp, mix, part, wide_in, local_in, hid_in, wide_got, local_got, hid_got,
    piece, pieces, done, q_send, q_recv, k_send, k_recv, v_send, v_recv, load,
    r_send, r_recv, g_send, g_recv, z_send, z_recv, leave, *line_refs,
):
    count, pairs, width = rows_n * group, rows_n * heads, h1.shape[1]
    fan, me = seq_n // pairs, lax.axis_index("seq")
    loads = [
        pltpu.make_async_copy(far, near, load.at[i])
        for i, (far, near) in enumerate(
            (
                (down_far, down_part), (q_far, q), (k_far, k), (v_far, v), (o_far, o), (do_far, do), (h1_far, h1),
                (pre_far, pre), (w_qkv, wq), (x2_far, x2), (dx2_far, dx),
            )
        )
    ]
    for one in loads[:6]:
        one.start()
    greet(seq=seq_n, heads=depth)
    line_down = Line(down_part, mixed, *line_refs[:9], lead=LAST_LEAD)
    loads[0].wait()
    line_down.first()
    for one in loads[1:6]:
        one.wait()
    for one in loads[6:]:
        one.start()
    exchanges = [
        Exchange(kind, seq_n, pairs, lambda j, a=a: a.at[j], lambda j, to=to: to.at[j], *sems)
        for kind, a, to, sems in (
            ("queries_back", dq, gq, (q_send, q_recv)),
            ("keys_back", dk, gk, (k_send, k_recv)),
            ("keys_back", dv, gv, (v_send, v_recv)),
        )
    ]
    first, second = FIRST, SECOND
    attend_back(
        2 * group if fan == 1 else group, fan, q, k, v, o, do, lse, start, place, dq, dk, dv, kt, dk_acc, dv_acc,
        lambda ticks: line_down.spread(0, first, ticks),
    )
    for one in exchanges:
        one.start()

    wide_in[...] = jnp.zeros_like(wide_in)
    local_in[...] = jnp.zeros_like(local_in)
    hid_in[...] = jnp.zeros_like(hid_in)
    share = 1.0 / depth
    for i in range(2):
        wide_in[(3 + i) * RANK : (4 + i) * RANK, :] = ga_gu[i].astype(BF16)
        hid_in[i * RANK : (i + 1) * RANK, :] = gb_gu[i].astype(BF16)
    wide_in[5 * RANK : 6 * RANK, :] = gb_out[...].astype(BF16)
    wide_in[6 * RANK : 7 * RANK, :] = gb_down[...].astype(BF16)
    hid_in[3 * RANK : 4 * RANK, :] = ga_down[...].astype(BF16)
    local_in[4 * RANK : 5 * RANK, :] = ga_out[...].astype(BF16)
    hid_in[2 * RANK : 3 * RANK, :] = jnp.concatenate(
        [gm_gu[...], jnp.zeros((RANK - 2, hid_in.shape[1]), F32)], axis=0
    ).astype(BF16)

    sums = [None] * 3
    line_down.run(first, second)
    for one in loads[6:9]:
        one.wait()
    for i in range(3):
        exchanges[i].wait_recv()
        came = (gq, gk, gv)[i]
        for head in range(heads):
            cols = slice(head * HD, (head + 1) * HD)
            n = norm[i : i + 1, cols]
            c = m[i : i + 1, cols] / n
            s = jnp.zeros((1, HD), F32)
            for row in range(rows_n):
                rows = slice(row * group, (row + 1) * group)
                if i == 0:
                    e = came[row * heads + head].astype(F32)
                else:
                    e = came[(row * heads + head) * fan].astype(F32)
                    for g in range(1, fan):
                        e = e + came[(row * heads + head) * fan + g].astype(F32)
                if i < 2:
                    e = e * cos[rows, :] - pltpu.roll(e, HD // 2, 1) * sin[rows, :]
                s = s + total(e * pre[i, rows, cols].astype(F32))
                dp[i, rows, cols] = (e * c).astype(BF16)
            turn = m[i : i + 1, cols] * s / (n * n * n)
            dp[i, count : count + RANK, cols] = (b[i, :, cols].astype(F32) * turn).astype(BF16)
            local_in[i * RANK : (i + 1) * RANK, cols] = (
                ADAPT_SCALE * (dot(low[:, i * RANK : (i + 1) * RANK], dp[i, :count, cols], TN) - v_qkv[i, :, cols] * turn)
            ).astype(BF16)
            sums[i] = [s / n] if head == 0 else sums[i] + [s / n]
        line_down.run(second + i, second + i + 1)
    local_in[3 * RANK : 4 * RANK, :] = jnp.concatenate(
        [jnp.concatenate(one, axis=1) for one in sums]
        + [jnp.zeros((RANK - 3, heads * HD), F32)], axis=0
    ).astype(BF16)
    mix[...] = jnp.zeros_like(mix)
    for i in range(3):
        both = (ADAPT_SCALE * dot(dp[i], b[i], NT)).astype(BF16)
        cols = slice(i * RANK, (i + 1) * RANK)
        mix[:count, cols] = both[:count]
        mix[count + i * RANK : count + (i + 1) * RANK, cols] = both[count:]

    def inputs(over, t):
        through = dot(mix[...], at[:, :, over].reshape(3 * RANK, over.size))
        straight = dot(mix[:count, :], h1[:count, over], TN)
        value = through[:count]
        for i in range(3):
            product = dot(dp[i], wq[i, over, :], NT)
            value = value + product[:count]
            rows = slice(i * RANK, (i + 1) * RANK)
            v_tb = product[count:] + through[count + i * RANK : count + (i + 1) * RANK]
            wide_in[rows, over] = (straight[rows] - ADAPT_SCALE * v_tb).astype(BF16)
        part[:, over] = value.astype(BF16)
        g_gain1 = total(value * h1[:count, over].astype(F32)) / gain[:, over]
        wide_in[7 * RANK : 8 * RANK, over] = jnp.concatenate(
            [
                g_gain1, g_gain2[:, over], gm_out[:, over] * share,
                gm_down[:, over] * share,
                jnp.zeros((RANK - 4, over.size), F32),
            ], axis=0,
        ).astype(BF16)

    tiles(width, WIDE, inputs, line_down.spread(second + 3, line_down.steps, -(-width // WIDE)))
    line_down.drain()
    line = Line(part, dh1, *line_refs[:3], *line_refs[9:], lead=LAST_LEAD)
    line.first()
    for one in loads[9:]:
        one.wait()
    c_down = m_down[...] / norms[1:2, :]

    over_gain = 1.0 / gain[...]

    def sent(stream, r):
        at_ = line.place(stream, r * PIECES)[0]
        return pltpu.make_async_copy(dx.at[at_], dx_far.at[at_], leave.at[stream, r])

    def advance(t, carry):
        line.step(t)

        @pl.when(t < count // (2 * CHUNK))
        def _():
            rows = pl.ds(pl.multiple_of(t * (2 * CHUNK), 2 * CHUNK), 2 * CHUNK)
            mixed[rows, :] = (x2[rows, :].astype(F32) + mixed[rows, :].astype(F32) * c_down).astype(BF16)

        c = t - 3 * LAG
        r = c // PIECES

        @pl.when((c >= 0) & (lax.rem(c, PIECES) == PIECES - 1))
        def _():
            for stream in range(2):
                at_ = line.place(stream, c)[0]
                unit = h1[at_, :].astype(F32) * over_gain
                scaled = dh1[at_, :].astype(F32) * gain[...]
                mean = jnp.mean(scaled * unit, axis=-1, keepdims=True)
                change = inverse_one[at_, :1] * (scaled - unit * mean)
                dx[at_, :] = (dx[at_, :].astype(F32) + change).astype(BF16)
                sent(stream, r).start()

        return carry


    spread = seq_n // OWNERS
    slabs = (
        (wide_in, wide_got, wide, lambda j: j), (local_in, local_got, local, lambda j: j),
        (hid_in, hid_got, hid, lambda j: OWNERS - 1 - j),
    )
    own = me // spread
    chosen = lax.rem(me, spread) == 0

    def rows_of(j):
        return pl.ds(pl.multiple_of(j * RANK, RANK), RANK)

    def to_owner(i, j):
        src, got, _, owner = slabs[i]
        return remote(
            src.at[rows_of(j)], got.at[me], r_send.at[i, j], r_recv.at[i, me], seq=owner(j) * spread
        )

    def from_owner(i, j, target):
        result = slabs[i][2]
        return remote(
            done.at[i, :, : result.shape[1]], result.at[rows_of(j)], g_send.at[i, target], g_recv.at[i, j], seq=target
        )

    for i, (src, got, result, owner) in enumerate(slabs):
        for j in range(src.shape[0] // RANK):

            @pl.when(me != owner(j) * spread)
            def _(i=i, j=j):
                to_owner(i, j).start()

            @pl.when(me == owner(j) * spread)
            def _(src=src, got=got, i=i, j=j):
                pltpu.make_async_copy(src.at[rows_of(j)], got.at[me], r_recv.at[i, me]).start()

    lax.fori_loop(0, GATHER, advance, 0)
    across = Across(depth, piece, pieces, z_send, z_recv)
    blocks_n = [slab[0].shape[0] // RANK for slab in slabs]
    owns = [chosen & (slab[3](own) < n) for slab, n in zip(slabs, blocks_n)]
    for i, (src, got, result, owner) in enumerate(slabs):

        @pl.when(owns[i])
        def _(i=i, got=got, result=result):
            def add(s_, acc):
                pltpu.make_async_copy(got.at[s_], got.at[s_], r_recv.at[i, s_]).wait()
                return acc + got[s_].astype(F32)

            value = lax.fori_loop(0, seq_n, add, jnp.zeros((RANK, result.shape[1]), F32))
            if i == 0:
                piece[...] = value.astype(BF16)
                across.start()
            else:
                done[i, :, : result.shape[1]] = value.astype(BF16)

    lax.fori_loop(GATHER, GIVE, advance, 0)

    @pl.when(owns[0])
    def _():
        done[0, :, :] = across.finish().astype(BF16)

    for i, (src, got, result, owner) in enumerate(slabs):

        @pl.when(owns[i])
        def _(i=i, result=result, owner=owner):
            mine = owner(own)

            def give(d, carry):
                from_owner(i, mine, lax.rem(me + d, seq_n)).start()
                return carry

            lax.fori_loop(1, seq_n, give, 0)
            pltpu.make_async_copy(
                done.at[i, :, : result.shape[1]], result.at[rows_of(mine)], g_recv.at[i, mine]
            ).start()

    lax.fori_loop(GIVE, line.steps, advance, 0)
    line.drain()

    def gone(c, carry):
        for stream in range(2):
            sent(stream, c).wait()
        return carry

    lax.fori_loop(0, line.chunks // PIECES, gone, 0)
    for one in exchanges:
        one.wait_send()
    for i, (src, got, result, owner) in enumerate(slabs):
        for j in range(blocks_n[i]):

            @pl.when(me != owner(j) * spread)
            def _(i=i, j=j):
                to_owner(i, j).wait_send()

            pltpu.make_async_copy(result.at[rows_of(j)], result.at[rows_of(j)], g_recv.at[i, j]).wait()

        @pl.when(owns[i])
        def _(i=i, owner=owner):
            def given(d, carry):
                from_owner(i, owner(own), lax.rem(me + d, seq_n)).wait_send()
                return carry

            lax.fori_loop(1, seq_n, given, 0)


def last(sizes, ins, far, hidden):
    seq_n, depth, rows_n, group, heads = sizes
    qkv_w = far[8]
    count, pairs, width = rows_n * group, rows_n * heads, qkv_w.shape[1]
    local, length = qkv_w.shape[2], seq_n * group
    blocks = {width: 8, local: 5, hidden: 4}
    slabs = [(n * RANK, w) for w, n in blocks.items()]
    some, every = pltpu.VMEM((pairs, group, HD), BF16), pltpu.VMEM((seq_n, group, HD), BF16)
    return pl.pallas_call(
        functools.partial(last_kernel, *sizes),
        out_shape=[shape(count, width)] * 2 + [shape(*s) for s in slabs],
        in_specs=[IN_VMEM] * len(ins) + [ANYWHERE] * len(far),
        out_specs=[ANYWHERE] + [IN_VMEM] * 4,
        scratch_shapes=[pltpu.VMEM((count, width), BF16)] * 3
        + [pltpu.VMEM(a.shape, BF16) for a in far[:8]]
        + [
            pltpu.VMEM((HD, length), BF16), pltpu.VMEM((length, HD), F32), pltpu.VMEM((length, HD), F32),
            some, every, every,
            pltpu.VMEM(qkv_w.shape, BF16), some, every, every,
            pltpu.VMEM((3, count + RANK, local), BF16), pltpu.VMEM((count + 3 * RANK, 3 * RANK), BF16),
            pltpu.VMEM((count, width), BF16),
        ]
        + [pltpu.VMEM(s, BF16) for s in slabs]
        + [pltpu.VMEM((seq_n, RANK, s[1]), BF16) for s in slabs]
        + [
            pltpu.VMEM((RANK, width), BF16), pltpu.VMEM((depth, RANK, width), BF16), pltpu.VMEM((3, RANK, width), BF16),
            dma(pairs), dma(pairs), dma(seq_n), dma(seq_n), dma(seq_n), dma(seq_n), dma(11),
            dma(3, 8), dma(3, seq_n), dma(3, seq_n), dma(3, 8), dma(depth), dma(depth), dma(2, count // (2 * CHUNK)),
        ]
        + Line.scratch(count, width, CHUNK)
        + Line.scratch(count, width, CHUNK)[3:],
        compiler_params=params(62, 5),
    )(*ins, *far)


PARTS = 4


def leave_kernel(wide, local, hid, dx_far, mixed_far, *refs):
    outs, (dx_out, mixed_out, dx, dx_wide, mixed, sems) = refs[:14], refs[14:]
    rows = dx.shape[0] // PARTS
    parts = [slice(i * rows, (i + 1) * rows) for i in range(PARTS)]
    moves = [
        [pltpu.make_async_copy(src.at[p], dst.at[p], sems.at[k, i]) for i, p in enumerate(parts)]
        for k, (src, dst) in enumerate(
            ((dx_far, dx), (dx_wide, dx_out), (mixed_far, mixed), (mixed, mixed_out))
        )
    ]
    for k in (0, 2):
        for one in moves[k]:
            one.start()
    for i, p in enumerate(parts):
        moves[0][i].wait()
        dx_wide[p, :] = dx[p, :].astype(F32)
        moves[1][i].start()
    for i in range(PARTS):
        moves[2][i].wait()
        moves[3][i].start()
    places = (
        (wide, 112, 1), (wide, 0, 48), (local, 0, 48), (local, 48, 3), (local, 64, 16), (wide, 80, 16), (wide, 114, 1),
        (wide, 113, 1), (wide, 48, 32), (hid, 0, 32), (hid, 32, 2), (hid, 48, 16), (wide, 96, 16), (wide, 115, 1),
    )
    for out, (slab, first, n) in zip(outs, places):
        begin = first // RANK * RANK
        value = slab[begin : begin + -(-n // RANK) * RANK, :].astype(F32)
        out[...] = value[first - begin : first - begin + n].reshape(out.shape)
    for k in (1, 3):
        for one in moves[k]:
            one.wait()


def outputs(wide, local, hid, dx, mixed):
    w, n, f = wide.shape[1], local.shape[1], hid.shape[1]
    dims = (
        (1, w), (3, RANK, w), (3, RANK, n), (3, n), (RANK, n), (RANK, w), (1, w), (1, w), (2, RANK, w), (2, RANK, f),
        (2, f), (RANK, f), (RANK, w), (1, w),
    )
    return pl.pallas_call(
        leave_kernel,
        out_shape=[shape(*d, dtype=F32) for d in dims] + [shape(*dx.shape, dtype=F32), shape(*mixed.shape)],
        in_specs=[IN_VMEM] * 3 + [ANYWHERE] * 2,
        out_specs=[IN_VMEM] * len(dims) + [ANYWHERE] * 2,
        scratch_shapes=[
            pltpu.VMEM(dx.shape, BF16), pltpu.VMEM(dx.shape, F32), pltpu.VMEM(mixed.shape, BF16), dma(4, PARTS)
        ],
        compiler_params=params(62),
    )(wide, local, hid, dx, mixed)


def per_device(
    tokens, attn_gain, base_qkv, adapt_a_qkv, adapt_b_qkv, magnitude_qkv, base_out, adapt_a_out,
    adapt_b_out, magnitude_out, ffn_gain, base_gu, adapt_a_gu, adapt_b_gu, magnitude_gu, base_down,
    adapt_a_down, adapt_b_down, magnitude_down, doc_lengths, cotangent,
):
    rows_n, group, width = tokens.shape
    count = rows_n * group
    local = base_qkv.shape[2]
    heads = local // HD
    pairs = rows_n * heads
    seq_n, depth = lax.axis_size("seq"), lax.axis_size("heads")
    sizes = (seq_n, depth, rows_n, group, heads)
    fan = seq_n // pairs
    length = group * seq_n
    me = lax.axis_index("seq")

    order = jnp.arange(doc_lengths.shape[1])
    doc_ends = jnp.sum(
        jnp.where(order[None, :, None] <= order[None, None, :], doc_lengths[:, :, None], 0), axis=1
    )
    doc_starts = doc_ends - doc_lengths

    def starts_of(places, ends, starts):
        inside = (places[..., None] >= starts) & (places[..., None] < ends)
        return jnp.sum(jnp.where(inside, starts, 0), axis=-1)

    mine = me * group + jnp.arange(group, dtype=jnp.int32)
    position = mine[None, :] - starts_of(
        jnp.broadcast_to(mine[None, :], (rows_n, group)), doc_ends[:, None], doc_starts[:, None]
    )
    half = HD // 2
    frequency = ROPE_BASE ** (jnp.arange(half, dtype=F32) * (-2.0 / HD))
    angles = position.reshape(count, 1).astype(F32) * frequency
    cos, sin = jnp.cos(angles), jnp.sin(angles)
    cos, sin = jnp.concatenate([cos, cos], axis=1), jnp.concatenate([-sin, sin], axis=1)
    row = me // fan // heads
    block_at = lax.rem(me, fan) + fan * jnp.arange(pairs, dtype=jnp.int32)
    place = (block_at[:, None] * group + jnp.arange(group, dtype=jnp.int32)[None, :]).reshape(-1)
    pick = (jnp.arange(rows_n) == row)[:, None]
    row_ends = jnp.sum(jnp.where(pick, doc_ends, 0), axis=0)
    row_starts = jnp.sum(jnp.where(pick, doc_starts, 0), axis=0)
    start = starts_of(place, row_ends, row_starts)
    low_block = start.reshape(-1, 2 * group)[:, 0] // (2 * group)
    high_block = place.reshape(-1, 2 * group)[:, -1] // (2 * group)
    place, start = place[None, :], start[None, :]

    x = tokens.reshape(count, width)
    dy = cotangent.reshape(count, width)
    gain1, gain2 = attn_gain[None, :], ffn_gain[None, :]
    m_out, m_down = magnitude_out[None, :], magnitude_down[None, :]
    at_qkv, at_gu = adapt_a_qkv.transpose(0, 2, 1), adapt_a_gu.transpose(0, 2, 1)
    at_out, at_down = adapt_a_out.T, adapt_a_down.T

    h1, pre, q, k, v, inverse_one, low, norm_qkv, v_qkv, norms, v_out, v_down, norm_gu, v_gu = front(
        sizes, x, gain1, cos, sin, (base_qkv, at_qkv, adapt_b_qkv, magnitude_qkv), (base_out, at_out, adapt_b_out),
        (base_down, at_down, adapt_b_down), (base_gu, at_gu, adapt_b_gu),
    )
    q, k, v = q.reshape(-1, HD), k.reshape(length, HD), v.reshape(length, HD)
    o, lse = attend(q, k, v, low_block, high_block, start, place, 2 * group)
    dx2, x2, down_part, do, gm_down, ga_gu, gb_gu, gm_gu, g_gain2, ga_down, gb_down, ga_out, gb_out, gm_out = core(
        sizes, o.reshape(-1, group, HD), x, dy, gain2, norms, (base_out, at_out, adapt_b_out, m_out, v_out),
        (base_down, at_down, adapt_b_down, m_down, v_down), (base_gu, at_gu, adapt_b_gu, magnitude_gu, norm_gu, v_gu),
    )
    dx, mixed, wide, narrow, hid = last(
        sizes,
        (
            lse, start, place, cos, sin, low, gain1, at_qkv, adapt_b_qkv, magnitude_qkv, norm_qkv, v_qkv, ga_gu, gb_out,
            gb_down, g_gain2, gm_out, gm_down, ga_out, gb_gu, gm_gu, ga_down, inverse_one, norms, m_down,
        ),
        (down_part, q, k, v, o, do.reshape(-1, HD), h1, pre, base_qkv, x2, dx2),
        base_down.shape[0],
    )
    *g, dx, mixed = outputs(wide, narrow, hid, dx, mixed)
    return (
        mixed.reshape(rows_n, group, width),
        dx.reshape(rows_n, group, width),
        g[0][0], g[1].transpose(0, 2, 1), g[2], g[3], g[4].T, g[5], g[6][0], g[7][0], g[8].transpose(0, 2, 1), g[9],
        g[10], g[11].T, g[12], g[13][0],
    )


def solution(mesh):
    in_specs = (
        P(None, "seq", None), P(), P(None, None, "heads"), P(), P(None, None, "heads"), P(None, "heads"),
        P("heads", None), P("heads", None), P(), P(), P(), P(None, None, "heads"), P(),
        P(None, None, "heads"), P(None, "heads"), P("heads", None), P("heads", None), P(), P(), P(),
        P(None, "seq", None),
    )
    out_specs = (
        P(None, "seq", None), P(None, "seq", None), P(), P(), P(None, None, "heads"), P(None, "heads"),
        P("heads", None), P(), P(), P(), P(), P(None, None, "heads"), P(None, "heads"),
        P("heads", None), P(), P(),
    )
    return jax.shard_map(
        per_device, mesh=mesh, in_specs=in_specs, out_specs=out_specs, check_vma=False
    )
```

```python
import functools

import jax
import jax.numpy as jnp
from jax import lax
from jax.experimental import pallas as pl
from jax.experimental.pallas import tpu as pltpu
from jax.sharding import PartitionSpec as P

HD = 128
RANK = 16
ADAPT_SCALE = 2.0
NORM_EPS = 1e-05
COLUMN_EPS = 1e-06
ROPE_BASE = 10000.0
NEG_LARGE = -1e30
LOG2E = 1.4426950408889634
F32 = jnp.float32
BF16 = jnp.bfloat16
MESH = pl.DeviceIdType.MESH
NN = (((1,), (0,)), ((), ()))
NT = (((1,), (1,)), ((), ()))
TN = (((0,), (0,)), ((), ()))
OWNERS = 8
CHUNK = 16
PIECES = 1
LAG = 2
LEAD = 4
NEAR_LATE = 1
IN_A, IN_B = 4, 5
LAST_LEAD = 4
FIRST, SECOND = 7, 13
GATHER, GIVE = 10, 14
WIDE = 512
IN_VMEM = pl.BlockSpec(memory_space=pltpu.VMEM)
IN_SMEM = pl.BlockSpec(memory_space=pltpu.SMEM)
ANYWHERE = pl.BlockSpec(memory_space=pl.ANY)


def dot(a, b, dims=NN):
    return lax.dot_general(a.astype(BF16), b.astype(BF16), dims, preferred_element_type=F32)


def shape(*dims, dtype=BF16):
    return jax.ShapeDtypeStruct(dims, dtype)


def dma(*dims):
    return pltpu.SemaphoreType.DMA(dims)


def params(mib, collective_id=None):
    more = {} if collective_id is None else {"collective_id": collective_id, "has_side_effects": True}
    return pltpu.CompilerParams(vmem_limit_bytes=mib * 2**20, **more)


def tiles(count, size, body, tick=lambda t: None):
    whole = count // size
    if whole:

        def step(t, carry):
            body(pl.ds(pl.multiple_of(t * size, 128), size), t)
            tick(t)
            return carry

        lax.fori_loop(0, whole, step, 0)
    if count - whole * size:
        body(pl.ds(whole * size, count - whole * size), whole)
        tick(whole)


def row_loop(count, size, body, init=0):
    def step(t, carry):
        return body(pl.ds(pl.multiple_of(t * size, size), size), carry)

    return lax.fori_loop(0, count // size, step, init)


def fold(v):
    return jnp.sum(v.reshape(v.shape[0] // 8, 8, v.shape[1]), axis=0)


def total(v):
    return jnp.sum(v, axis=0, keepdims=True)


def greet(seq=0, heads=0, line=0):
    barrier = pltpu.get_barrier_semaphore()
    me, h = lax.axis_index("seq"), lax.axis_index("heads")
    peers = 0
    for d in range(1, seq):
        pl.semaphore_signal(barrier, inc=1, device_id={"seq": lax.rem(me + d, seq)}, device_id_type=MESH)
        peers = peers + 1
    for d in range(1, heads):
        pl.semaphore_signal(
            barrier, inc=1, device_id={"heads": lax.rem(h + d, heads)}, device_id_type=MESH
        )
        peers = peers + 1
    if line:
        for step in (-1, 1):

            @pl.when((h + step >= 0) & (h + step < line))
            def _(step=step):
                pl.semaphore_signal(barrier, inc=1, device_id={"heads": h + step}, device_id_type=MESH)

        peers = peers + jnp.where((h == 0) | (h == line - 1), 1, 2)
    pl.semaphore_wait(barrier, peers)


def remote(src, dst, send_sem, recv_sem, **where):
    return pltpu.make_async_remote_copy(
        src_ref=src, dst_ref=dst, send_sem=send_sem, recv_sem=recv_sem, device_id=where, device_id_type=MESH
    )


class Exchange:
    def __init__(self, kind, seq_n, pairs, src, dst, send_sem, recv_sem):
        fan = seq_n // pairs
        me = lax.axis_index("seq")
        self.me, self.src, self.dst, self.send_sem, self.recv_sem = me, src, dst, send_sem, recv_sem
        self.count = self.slots(kind, seq_n, pairs)
        self.target, self.block, self.slot = {
            "queries": (lambda p: p * fan + lax.rem(me, fan), lambda p: p, me // fan),
            "keys": (lambda e: e, lambda e: e // fan, me),
            "queries_back": (lambda i: lax.rem(me, fan) + fan * i, lambda i: i, me // fan),
            "keys_back": (lambda e: e, lambda e: e, me),
        }[kind]

    @staticmethod
    def slots(kind, seq_n, pairs):
        return pairs if kind.startswith("queries") else seq_n

    def copy(self, j):
        return remote(
            self.src(self.block(j)),
            self.dst(self.slot),
            self.send_sem.at[j],
            self.recv_sem.at[self.slot],
            seq=self.target(j),
        )

    def start(self, low=0, high=None):
        number = (self.count if high is None else high) - low

        def one(d, carry):
            j = low + lax.rem(self.me + d, number)

            @pl.when(self.target(j) != self.me)
            def _():
                self.copy(j).start()

            @pl.when(self.target(j) == self.me)
            def _():
                pltpu.make_async_copy(
                    self.src(self.block(j)), self.dst(self.slot), self.recv_sem.at[self.slot]
                ).start()

            return carry

        lax.fori_loop(0, number, one, 0)

    def wait_recv(self):
        def one(j, carry):
            pltpu.make_async_copy(self.dst(j), self.dst(j), self.recv_sem.at[j]).wait()
            return carry

        lax.fori_loop(0, self.count, one, 0)

    def wait_send(self):
        def one(j, carry):
            @pl.when(self.target(j) != self.me)
            def _():
                self.copy(j).wait_send()

            return carry

        lax.fori_loop(0, self.count, one, 0)


class Line:
    def __init__(self, x, out, got, near, held, *sems, per=None, base=0, lead=None):
        self.x, self.out, self.got, self.near, self.held = x, out, got, near, held
        self.far_send, self.far_recv, self.near_send, self.near_recv, self.down_send, self.down_recv = sems
        self.chunks, self.rows = got.shape[1], got.shape[2]
        self.per, self.base = per or self.chunks, base
        self.lead = self.chunks if lead is None else lead
        self.steps = self.done(self.chunks)
        self.h = lax.axis_index("heads")

    @staticmethod
    def done(chunks):
        return chunks + 3 * LAG

    @staticmethod
    def scratch(count, width, rows):
        chunks = count // (2 * rows) * PIECES
        one = pltpu.VMEM((chunks, rows, width // PIECES), BF16)
        return [
            pltpu.VMEM((2, chunks, rows, width // PIECES), BF16), one, one,
            dma(2, chunks), dma(2, chunks), dma(chunks), dma(chunks), dma(2, 2, chunks), dma(2, chunks),
        ]

    def ends(self, stream):
        if stream == 0:
            return self.h, self.h + 1, self.h - 1
        return 3 - self.h, self.h - 1, self.h + 1

    def place(self, stream, c):
        rows, per, width = self.rows, self.per // PIECES, self.got.shape[3]
        r, piece = c // PIECES, lax.rem(c, PIECES)
        first = self.base + ((r // per) * 2 + (1 - stream)) * (per * rows) + lax.rem(r, per) * rows
        return pl.ds(pl.multiple_of(first, rows), rows), pl.ds(pl.multiple_of(piece * width, width), width)

    def far(self, stream, c, src, to):
        return remote(
            src, self.got.at[stream, c], self.far_send.at[stream, c], self.far_recv.at[stream, c], heads=to
        )

    def close(self, stream, c, to):
        return remote(
            self.x.at[*self.place(stream, c)], self.near.at[c], self.near_send.at[c], self.near_recv.at[c], heads=to
        )

    def down(self, stream, way, c, to):
        part = self.out.at[*self.place(stream, c)]
        return remote(part, part, self.down_send.at[stream, way, c], self.down_recv.at[stream, c], heads=to)

    def give(self, c):
        for stream in range(2):
            pos, ahead, behind = self.ends(stream)

            @pl.when((pos == 0) & (c < self.chunks))
            def _():
                self.far(stream, c, self.x.at[*self.place(stream, c)], ahead).start()

        c = c - NEAR_LATE
        for stream in range(2):
            pos, ahead, behind = self.ends(stream)

            @pl.when((pos == 3) & (c >= 0) & (c < self.chunks))
            def _():
                self.close(stream, c, behind).start()

    def first(self):
        def one(c, carry):
            self.give(c)
            return carry

        lax.fori_loop(0, self.lead, one, 0)

    def step(self, t):
        self.give(t + self.lead)
        for stream in range(2):
            pos, ahead, behind = self.ends(stream)

            @pl.when((pos == 1) & (t < self.chunks))
            def _():
                self.far(stream, t, self.held.at[t], self.h).wait_recv()
                at = self.place(stream, t)
                self.held[t] = (self.got[stream, t].astype(F32) + self.x[*at].astype(F32)).astype(BF16)
                self.far(stream, t, self.held.at[t], ahead).start()

        for stream in range(2):
            pos, ahead, behind = self.ends(stream)
            c = t - LAG

            @pl.when((pos == 2) & (c >= 0) & (c < self.chunks))
            def _():
                self.far(stream, c, self.held.at[c], self.h).wait_recv()
                self.close(stream, c, self.h).wait_recv()
                at = self.place(stream, c)
                value = self.got[stream, c].astype(F32) + self.near[c].astype(F32) + self.x[*at].astype(F32)
                self.out[*at] = value.astype(BF16)
                self.down(stream, 0, c, behind).start()
                self.down(stream, 1, c, ahead).start()

        for stream in range(2):
            pos, ahead, behind = self.ends(stream)
            b = t - jnp.where(pos == 0, 3 * LAG, 2 * LAG)

            @pl.when((pos != 2) & (b >= 0) & (b < self.chunks))
            def _():
                self.down(stream, 0, b, self.h).wait_recv()

                @pl.when(pos == 1)
                def _():
                    self.down(stream, 0, b, behind).start()

    def run(self, start, stop):
        def one(t, carry):
            self.step(t)
            return carry

        lax.fori_loop(start, stop, one, 0)

    def spread(self, start, stop, ticks):
        def tick(k):
            now, then = (k * (stop - start)) // ticks, ((k + 1) * (stop - start)) // ticks
            self.run(start + now, start + then)

        return tick

    def drain(self):
        def one(c, carry):
            for stream in range(2):
                pos, ahead, behind = self.ends(stream)

                @pl.when(pos <= 1)
                def _():
                    self.far(stream, c, self.held.at[c], self.h).wait_send()

                @pl.when(pos == 3)
                def _():
                    self.close(stream, c, self.h).wait_send()

                @pl.when((pos == 1) | (pos == 2))
                def _():
                    self.down(stream, 0, c, self.h).wait_send()

                @pl.when(pos == 2)
                def _():
                    self.down(stream, 1, c, self.h).wait_send()

            return carry

        lax.fori_loop(0, self.chunks, one, 0)


class Across:
    def __init__(self, depth, part, others, send_sem, recv_sem):
        self.depth, self.part, self.others, self.sems = depth, part, others, (send_sem, recv_sem)
        self.h = lax.axis_index("heads")

    def copy(self, d):
        to = lax.rem(self.h + d, self.depth)
        return remote(
            self.part, self.others.at[self.h], self.sems[0].at[d], self.sems[1].at[self.h], heads=to
        )

    def start(self):
        for d in range(1, self.depth):
            self.copy(d).start()

    def finish(self):
        value = self.part[...].astype(F32)
        for d in range(1, self.depth):
            came = self.others.at[lax.rem(self.h + d, self.depth)]
            pltpu.make_async_copy(came, came, self.sems[1].at[lax.rem(self.h + d, self.depth)]).wait()
            value = value + came[...].astype(F32)
        for d in range(1, self.depth):
            self.copy(d).wait_send()
        return value


def column_stats(w, at, b, aw):
    ab = dot(dot(at, at, NT), b)
    bf = b.astype(F32)

    acc = jnp.zeros((8, w.shape[1]), F32)
    for first in range(0, w.shape[0], 64):
        v = w[first : first + 64, :].astype(F32)
        acc = acc + fold(v * v)
    squares = total(acc) + 2.0 * ADAPT_SCALE * total(bf * aw) + ADAPT_SCALE**2 * total(bf * ab)
    return squares, aw + ADAPT_SCALE * ab


def front_kernel(
    seq_n, depth, rows_n, group, heads,
    x, gain, cos, sin, at_qkv, b_qkv, m_qkv, at_out, b_out, at_down, b_down, at_gu, b_gu,
    w_qkv, w_out, w_down, w_gu,
    h1_far, pre_far, q, k, v, inverse_one, low, norm_qkv, v_qkv, norms, v_out, v_down, norm_gu, v_gu,
    h1, pre, wq, wo, wd, wg, turned, part, others, q_send, q_recv, k_send, k_recv, v_send, v_recv, z_send, z_recv, load, leave,
):
    count, pairs = rows_n * group, rows_n * heads
    leaving = [pltpu.make_async_copy(pre.at[i], pre_far.at[i], leave.at[i]) for i in range(3)]
    leaving.append(pltpu.make_async_copy(h1, h1_far, leave.at[3]))
    loads = [pltpu.make_async_copy(w_qkv.at[i], wq.at[i], load.at[i]) for i in range(3)]
    loads += [
        pltpu.make_async_copy(w_out, wo, load.at[3]),
        pltpu.make_async_copy(w_down, wd, load.at[4]),
        pltpu.make_async_copy(w_gu, wg, load.at[5]),
    ]
    for one in loads[:3]:
        one.start()
    greet(seq=seq_n, heads=depth)

    def norm(rows, carry):
        v = x[rows, :].astype(F32)
        inverse = lax.rsqrt(jnp.mean(v * v, axis=-1, keepdims=True) + NORM_EPS)
        h1[rows, :] = (v * inverse * gain[...]).astype(BF16)
        inverse_one[rows, :] = jnp.broadcast_to(inverse, (rows.size, HD))
        return carry

    row_loop(count, 32, norm)
    for i in range(3):
        h1[count + i * RANK : count + (i + 1) * RANK, :] = at_qkv[i]
    leaving[3].start()
    low[...] = dot(h1[:count, :], h1[count:, :], NT).astype(BF16)
    exchanges = [
        Exchange(kind, seq_n, pairs, lambda j, i=i: turned.at[i, j], lambda j, to=to: to.at[j], *sems)
        for i, (kind, to, sems) in enumerate(
            (("queries", q, (q_send, q_recv)), ("keys", k, (k_send, k_recv)), ("keys", v, (v_send, v_recv)))
        )
    ]
    for i in range(3):
        loads[i].wait()
        loads[3 + i].start()

        def project(over, t, i=i):
            width = over.size
            r = dot(h1[...], wq[i, :, over])
            b = b_qkv[i, :, over]
            value = r[:count] + ADAPT_SCALE * dot(low[:, i * RANK : (i + 1) * RANK], b)
            aw = r[count + i * RANK : count + (i + 1) * RANK]
            squares, av = column_stats(wq.at[i, :, over], at_qkv[i], b, aw)
            n = jnp.sqrt(squares + COLUMN_EPS)
            norm_qkv[i : i + 1, over] = n
            v_qkv[i, :, over] = av
            pre[i, :, over] = value.astype(BF16)
            scaled = value * (m_qkv[i : i + 1, over] / n)
            for row in range(rows_n):
                rows = slice(row * group, (row + 1) * group)
                for hh in range(width // HD):
                    part_ = scaled[rows, hh * HD : (hh + 1) * HD]
                    if i < 2:
                        part_ = part_ * cos[rows, :] + pltpu.roll(part_, HD // 2, 1) * sin[rows, :]
                    turned[i, row * heads + t * (width // HD) + hh] = part_.astype(BF16)

        tiles(heads * HD, WIDE, project)
        exchanges[i].start()
        leaving[i].start()

    part[...] = jnp.zeros_like(part)
    for row, (w, at, b, av, loaded) in enumerate(
        ((wo, at_out, b_out, v_out, loads[3]), (wd, at_down, b_down, v_down, loads[4]))
    ):
        loaded.wait()

        def stats(over, t, row=row, w=w, at=at, b=b, av=av):
            squares, value = column_stats(w.at[:, over], at[...], b[:, over], dot(at[...], w[:, over]))
            part[row : row + 1, over] = squares
            av[:, over] = value

        tiles(w.shape[1], WIDE, stats)
    across = Across(depth, part, others, z_send, z_recv)
    across.start()
    loads[5].wait()
    for i in range(2):

        def stats_gu(over, t, i=i):
            b = b_gu[i, :, over]
            squares, value = column_stats(wg.at[i, :, over], at_gu[i], b, dot(at_gu[i], wg[i, :, over]))
            norm_gu[i : i + 1, over] = jnp.sqrt(squares + COLUMN_EPS)
            v_gu[i, :, over] = value

        tiles(wg.shape[2], WIDE, stats_gu)
    norms[...] = jnp.sqrt(across.finish() + COLUMN_EPS)
    for one in exchanges:
        one.wait_recv()
    for one in exchanges:
        one.wait_send()
    for one in leaving:
        one.wait()


def front(sizes, x, gain, cos, sin, qkv, out, down, gu):
    seq_n, depth, rows_n, group, heads = sizes
    count, pairs, width = rows_n * group, rows_n * heads, x.shape[1]
    local, hidden = qkv[0].shape[2], gu[0].shape[2]
    return pl.pallas_call(
        functools.partial(front_kernel, *sizes),
        out_shape=[
            shape(count + 3 * RANK, width), shape(3, count, local),
            shape(pairs, group, HD), shape(seq_n, group, HD), shape(seq_n, group, HD),
            shape(count, HD, dtype=F32), shape(count, 3 * RANK),
            shape(3, local, dtype=F32), shape(3, RANK, local, dtype=F32), shape(8, width, dtype=F32),
            shape(RANK, width, dtype=F32), shape(RANK, width, dtype=F32),
            shape(2, hidden, dtype=F32), shape(2, RANK, hidden, dtype=F32),
        ],
        in_specs=[IN_VMEM] * 13 + [ANYWHERE] * 4,
        out_specs=[ANYWHERE] * 2 + [IN_VMEM] * 12,
        scratch_shapes=[
            pltpu.VMEM((count + 3 * RANK, width), BF16), pltpu.VMEM((3, count, local), BF16),
            pltpu.VMEM(qkv[0].shape, BF16), pltpu.VMEM(out[0].shape, BF16), pltpu.VMEM(down[0].shape, BF16),
            pltpu.VMEM(gu[0].shape, BF16), pltpu.VMEM((3, pairs, group, HD), BF16),
            pltpu.VMEM((8, width), F32), pltpu.VMEM((depth, 8, width), F32),
            dma(pairs), dma(pairs), dma(seq_n), dma(seq_n), dma(seq_n), dma(seq_n), dma(depth), dma(depth), dma(6), dma(4),
        ],
        compiler_params=params(60, 1),
    )(
        x, gain, cos, sin, qkv[1], qkv[2], qkv[3], out[1], out[2], down[1], down[2], gu[1], gu[2],
        qkv[0], out[0], down[0], gu[0],
    )


def attend_kernel(block, low_ref, high_ref, q_ref, k_ref, v_ref, start_ref, place_ref, o_ref, lse_ref, vt):
    scale = HD**-0.5 * LOG2E
    vt[...] = v_ref[...].T

    def per_query(i, carry):
        at = pl.ds(pl.multiple_of(i * block, block), block)
        q = q_ref[at, :]
        start, place = start_ref[:, at], place_ref[:, at]

        def per_key(j, state):
            top, count, acc = state
            over = pl.ds(pl.multiple_of(j * block, block), block)
            s = dot(k_ref[over, :], q, NT) * scale
            key = j * block + lax.broadcasted_iota(jnp.int32, (block, block), 0)
            s = jnp.where((key >= start) & (key <= place), s, NEG_LARGE)
            new_top = jnp.maximum(top, jnp.max(s, axis=0, keepdims=True))
            p = jnp.exp2(s - new_top)
            fade = jnp.exp2(top - new_top)
            count = count * fade + total(p)
            acc = acc * fade + dot(vt[:, over], p)
            return new_top, count, acc

        begin = (
            jnp.full((1, block), -1e29, F32),
            jnp.zeros((1, block), F32),
            jnp.zeros((HD, block), F32),
        )
        top, count, acc = lax.fori_loop(low_ref[i], high_ref[i] + 1, per_key, begin)
        o_ref[at, :] = (acc / count).T.astype(BF16)
        lse_ref[:, at] = top + jnp.log2(count)
        return carry

    lax.fori_loop(0, q_ref.shape[0] // block, per_query, 0)


def attend(q, k, v, low, high, start, place, block):
    return pl.pallas_call(
        functools.partial(attend_kernel, block),
        out_shape=[shape(*q.shape), shape(1, q.shape[0], dtype=F32)],
        in_specs=[IN_SMEM] * 2 + [IN_VMEM] * 5,
        out_specs=[IN_VMEM] * 2,
        scratch_shapes=[pltpu.VMEM((HD, k.shape[0]), BF16)],
        compiler_params=params(62),
    )(low, high, q, k, v, start, place)


def attend_back(block, fan, q_ref, k_ref, v_ref, o_ref, do_ref, lse_ref, start_ref, place_ref, dq, dk, dv, kt, dk_acc, dv_acc, spread):
    scale = HD**-0.5
    mine = lax.rem(lax.axis_index("seq"), fan)
    group = dq.shape[1]
    split = block // group
    blocks = q_ref.shape[0] // block

    def reach(i):
        return ((mine + fan * ((i + 1) * split - 1) + 1) * group - 1) // block + 1

    tick = spread(sum(reach(i) for i in range(blocks)))
    kt[...] = k_ref[...].T
    dk_acc[...] = jnp.zeros_like(dk_acc)
    dv_acc[...] = jnp.zeros_like(dv_acc)

    def per_query(i, before):
        at = pl.ds(pl.multiple_of(i * block, block), block)
        q, do = q_ref[at, :], do_ref[at, :]
        start, place, lse = start_ref[:, at], place_ref[:, at], lse_ref[:, at]
        delta = total((do.astype(F32) * o_ref[at, :].astype(F32)).T)

        def per_key(j, acc):
            over = pl.ds(pl.multiple_of(j * block, block), block)
            k = k_ref[over, :]
            s = dot(k, q, NT) * (scale * LOG2E)
            key = j * block + lax.broadcasted_iota(jnp.int32, (block, block), 0)
            p = jnp.exp2(jnp.where((key >= start) & (key <= place), s - lse, NEG_LARGE))
            dp = dot(v_ref[over, :], do, NT)
            ds = (p * (dp - delta)).astype(BF16)
            dv_acc[over, :] += dot(p, do)
            dk_acc[over, :] += dot(ds, q)
            tick(before + j)
            return acc + dot(kt[:, over], ds)

        acc = lax.fori_loop(0, reach(i), per_key, jnp.zeros((HD, block), F32))
        acc = (acc * scale).T.astype(BF16)
        for n in range(split):
            dq[i * split + n] = acc[n * group : (n + 1) * group]
        return before + reach(i)

    lax.fori_loop(0, blocks, per_query, 0)

    def store(j, carry):
        over = pl.ds(pl.multiple_of(j * group, group), group)
        dk[j] = (dk_acc[over, :] * scale).astype(BF16)
        dv[j] = dv_acc[over, :].astype(BF16)
        return carry

    lax.fori_loop(0, k_ref.shape[0] // group, store, 0)


def core_kernel(
    seq_n, depth, rows_n, group, heads,
    o, gain, m_out, norms, at_out, b_out, v_out, at_gu, b_gu, m_gu, norm_gu, v_gu, at_down, b_down, m_down, v_down,
    x_far, cotangent_far, w_out, w_gu, w_down,
    dx2_far, x2_far, down_far, do, gm_down, ga_gu, gb_gu, gm_gu, g_gain, ga_down, gb_down, ga_out, gb_out, gm_out,
    dx2, x2_out, down_part, out_pre, x, cotangent, wo, wg, wd, attn, low_out, part, part2, dh2, h2, z, dz, dp, dpd, tmp, low, mix, dpo, blocks,
    s_part, others, row_sums, load, send, recv, back_send, back_recv, z_send, z_recv, away, *line_refs,
):
    count, pairs = rows_n * group, rows_n * heads
    half = count // 2
    hidden, width = wd.shape
    loads = [
        pltpu.make_async_copy(far, near, load.at[i])
        for i, (far, near) in enumerate(
            ((w_out, wo), (x_far, x), (w_gu.at[0], wg.at[0]), (w_gu.at[1], wg.at[1]), (cotangent_far, cotangent), (w_down, wd))
        )
    ]
    for one in loads:
        one.start()
    greet(seq=seq_n, heads=depth)

    def landing(pair):
        row, head = pair // heads, lax.rem(pair, heads)
        return attn.at[
            pl.ds(pl.multiple_of(row * group, group), group), pl.ds(pl.multiple_of(head * HD, HD), HD)
        ]

    def leaving(i, r):
        near, far = ((dx2, dx2_far), (x2_out, x2_far), (down_part, down_far))[i]
        return pltpu.make_async_copy(
            near.at[r * half : (r + 1) * half], far.at[r * half : (r + 1) * half], away.at[i, r]
        )

    come = Exchange("queries_back", seq_n, pairs, lambda i: o.at[i], landing, send, recv)
    leave = Exchange("queries", seq_n, pairs, lambda p: blocks.at[p], lambda s_: do.at[s_], back_send, back_recv)
    come.start()
    for ref in (s_part, ga_gu, gb_gu, gm_gu, g_gain, ga_down, gb_down, ga_out, gb_out, gm_out):
        ref[...] = jnp.zeros_like(ref)
    one_out = Line(part, out_pre, *line_refs[:9], per=half // (2 * CHUNK) * PIECES, lead=LEAD)
    two = [
        Line(part2, dh2, *line_refs[9 + 9 * r : 18 + 9 * r], base=r * half, lead=LEAD) for r in range(2)
    ]
    loads[0].wait()
    come.wait_recv()
    low_out[...] = dot(attn[...], at_out[...], NT).astype(BF16)

    def project(over, t):
        part[:, over] = (dot(attn[...], wo[:, over]) + ADAPT_SCALE * dot(low_out[...], b_out[:, over])).astype(BF16)

    tiles(width, WIDE, project)
    one_out.first()
    for one in loads[1:]:
        one.wait()
    n_out, n_down = 1.0 / norms[0:1, :], 1.0 / norms[1:2, :]
    c_out, c_down = m_out[...] * n_out, m_down[...] * n_down

    n_hidden, n_width = -(-hidden // WIDE), -(-width // WIDE)
    half_done = one_out.done(one_out.per)
    tick_first = one_out.spread(0, half_done, count // 64 + n_hidden)

    def scaled_gradient(rows, carry):
        dpd[rows, :] = (cotangent[rows, :].astype(F32) * c_down).astype(BF16)
        tick_first(rows.start // rows.size)
        return carry

    row_loop(count, 64, scaled_gradient)
    dlow_down = (ADAPT_SCALE * dot(dpd[...], b_down[...], NT)).astype(BF16)

    def hidden_gradient(over, t):
        dz[:, over] = (dot(dpd[...], wd[over, :], NT) + dot(dlow_down, at_down[:, over])).astype(BF16)

    tiles(hidden, WIDE, hidden_gradient, lambda t: tick_first(count // 64 + t))

    def feed_forward(r, tick):
        mine = slice(r * half, (r + 1) * half)
        base = r * half

        def there(rows):
            return pl.ds(pl.multiple_of(base + rows.start, rows.size), rows.size)

        def norm(rows, carry):
            x2 = x[there(rows), :].astype(F32) + out_pre[there(rows), :].astype(F32) * c_out
            inverse = lax.rsqrt(jnp.mean(x2 * x2, axis=-1, keepdims=True) + NORM_EPS)
            h2[rows, :] = (x2 * inverse * gain[...]).astype(BF16)
            tick(rows.start // rows.size)
            return carry

        row_loop(half, 32, norm)
        low[...] = dot(h2[...], at_gu[...].reshape(2 * RANK, width), NT).astype(BF16)

        def there_and_back(over, t):
            n = over.size
            for i in range(2):
                tmp[i, :, :n] = dot(h2[...], wg[i, :, over]) + ADAPT_SCALE * dot(
                    low[:, i * RANK : (i + 1) * RANK], b_gu[i, :, over]
                )
            scale = [m_gu[i : i + 1, over] / norm_gu[i : i + 1, over] for i in range(2)]

            def gated(rows, sums):
                pg, pu = tmp[0, rows, :n], tmp[1, rows, :n]
                g, u = pg * scale[0], pu * scale[1]
                sigma = jax.nn.sigmoid(g)
                silu = g * sigma
                z[there(rows), over] = (silu * u).astype(BF16)
                d = dz[there(rows), over].astype(F32)
                e_g = d * u * (sigma + silu * (1.0 - sigma))
                e_u = d * silu
                dp[0, rows, over] = (e_g * scale[0]).astype(BF16)
                dp[1, rows, over] = (e_u * scale[1]).astype(BF16)
                return sums[0] + fold(e_g * pg), sums[1] + fold(e_u * pu)

            zero = jnp.zeros((8, n), F32)
            sums = row_loop(half, 32, gated, (zero, zero))
            for i in range(2):
                s, inverse = total(sums[i]), 1.0 / norm_gu[i : i + 1, over]
                gm_gu[i : i + 1, over] += s * inverse
                turn = m_gu[i : i + 1, over] * s * inverse * inverse * inverse
                dp[i, half : half + RANK, over] = (b_gu[i, :, over].astype(F32) * turn).astype(BF16)
                gb_gu[i, :, over] += ADAPT_SCALE * (
                    dot(low[:, i * RANK : (i + 1) * RANK], dp[i, :half, over], TN) - v_gu[i, :, over] * turn
                )

        tiles(hidden, WIDE, there_and_back, lambda t: tick(half // 32 + t))
        for i in range(2):
            both = ADAPT_SCALE * dot(dp[i], b_gu[i], NT)
            mix[:half, i * RANK : (i + 1) * RANK] = both[:half].astype(BF16)
            for k in range(2):
                mix[half + k * RANK : half + (k + 1) * RANK, i * RANK : (i + 1) * RANK] = (
                    both[half:] if i == k else jnp.zeros((RANK, RANK), F32)
                ).astype(BF16)

        def inputs(over, t):
            products = [dot(dp[i], wg[i, over, :], NT) for i in range(2)]
            through = dot(mix[...], at_gu[:, :, over].reshape(2 * RANK, over.size))
            value = products[0][:half] + products[1][:half] + through[:half]
            straight = dot(mix[:half, :], h2[:, over], TN)
            for i in range(2):
                v_tb = products[i][half:] + through[half + i * RANK : half + (i + 1) * RANK]
                ga_gu[i, :, over] += straight[i * RANK : (i + 1) * RANK] - ADAPT_SCALE * v_tb
            part2[mine, over] = value.astype(BF16)
            g_gain[:, over] += total(value * h2[:, over].astype(F32)) / gain[:, over]

        tiles(width, WIDE, inputs, lambda t: tick(half // 32 + n_hidden + t))

    def norm_back(r, first):
        rows = pl.ds(pl.multiple_of(first, 16), 16)
        there = pl.ds(pl.multiple_of(r * half + first, 16), 16)
        value = out_pre[there, :].astype(F32)
        x2 = x[there, :].astype(F32) + value * c_out
        inverse = lax.rsqrt(jnp.mean(x2 * x2, axis=-1, keepdims=True) + NORM_EPS)
        scaled = dh2[there, :].astype(F32) * gain[...]
        mean = jnp.mean(scaled * x2, axis=-1, keepdims=True)
        e = cotangent[there, :].astype(F32) + inverse * scaled - x2 * (inverse**3 * mean)
        dx2[there, :] = e.astype(BF16)
        x2_out[there, :] = x2.astype(BF16)
        dpo[rows, :] = (e * c_out).astype(BF16)
        row_sums[...] += fold(e * value)

    def out_back(r):
        mine = slice(r * half, (r + 1) * half)
        rows_here = rows_n // 2

        s = total(row_sums[...])
        turn = m_out[...] * s * n_out * n_out * n_out
        gm_out[...] += s * n_out
        dpo[half : half + RANK, :] = (b_out[...].astype(F32) * turn).astype(BF16)
        both = dot(dpo[...], b_out[...], NT)
        dlow, turned = (ADAPT_SCALE * both[:half]).astype(BF16), both[half:]

        def inputs(over, t):
            product = dot(dpo[...], wo[over, :], NT)
            value = (product[:half] + dot(dlow, at_out[:, over])).astype(BF16)
            for row in range(rows_here):
                for hh in range(over.size // HD):
                    blocks[(r * rows_here + row) * heads + t * (over.size // HD) + hh] = value[
                        row * group : (row + 1) * group, hh * HD : (hh + 1) * HD
                    ]
            ga_out[:, over] += dot(dlow, attn[mine, over], TN) - ADAPT_SCALE * (
                product[half:] + ADAPT_SCALE * dot(turned, at_out[:, over])
            )

        tiles(heads * HD, WIDE, inputs)
        leave.start(r * rows_here * heads, (r + 1) * rows_here * heads)
        leaving(0, r).start()
        leaving(1, r).start()
        gb_out[...] += ADAPT_SCALE * (dot(low_out[mine, :], dpo[:half, :], TN) - v_out[...] * turn)

    ticks = half // 32 + n_hidden + n_width
    feed_forward(0, one_out.spread(half_done, half_done + IN_A, ticks))
    two[0].first()
    left = one_out.steps - half_done - IN_A

    def between(k, carry):
        one_out.step(half_done + IN_A + k)
        two[0].step(k)
        return carry

    lax.fori_loop(0, left, between, 0)
    feed_forward(1, two[0].spread(left, left + IN_B, ticks))
    two[1].first()
    rest = two[0].steps - left - IN_B

    def together(k, carry):
        two[0].step(left + IN_B + k)
        two[1].step(k)
        return carry

    lax.fori_loop(0, rest, together, 0)

    low_down = dot(z[...], at_down[...], NT).astype(BF16)

    def down(over, t):
        value = dot(z[...], wd[:, over]) + ADAPT_SCALE * dot(low_down, b_down[:, over])
        down_part[:, over] = value.astype(BF16)
        s_part[0:1, over] = total(value * cotangent[:, over].astype(F32))
        gb_down[:, over] = ADAPT_SCALE * dot(low_down, dpd[:, over], TN)

    tiles(width, WIDE, down, two[1].spread(rest, rest + 2, n_width))
    leaving(2, 0).start()
    leaving(2, 1).start()
    across = Across(depth, s_part, others, z_send, z_recv)
    across.start()

    def down_factor(over, t):
        ga_down[:, over] = dot(dlow_down, z[:, over], TN)

    tiles(hidden, WIDE, down_factor)
    row_sums[...] = jnp.zeros_like(row_sums)
    taken = rest + 4
    tick_two = two[1].spread(rest + 2, taken, half // 16)

    def first_half(k, carry):
        norm_back(0, k * 16)
        tick_two(k)
        return carry

    lax.fori_loop(0, half // 16, first_half, 0)
    out_back(0)
    row_sums[...] = jnp.zeros_like(row_sums)

    def second_half(t, carry):
        @pl.when(t >= taken)
        def _():
            two[1].step(t)

        for stream in range(2):
            norm_back(1, ((1 - stream) * two[1].chunks + t - 3 * LAG) * CHUNK)
        return carry

    lax.fori_loop(3 * LAG, two[1].steps, second_half, 0)
    out_back(1)
    for line in [one_out] + two:
        line.drain()
    s = across.finish()[0:1, :]
    turn = m_down[...] * s * n_down * n_down * n_down
    tb = (b_down[...].astype(F32) * turn).astype(BF16)
    v_tb = dot(tb, wd[...], NT) + ADAPT_SCALE * dot(dot(tb, b_down[...], NT), at_down[...])
    ga_down[...] -= ADAPT_SCALE * v_tb
    gb_down[...] -= ADAPT_SCALE * v_down[...] * turn
    gm_down[...] = s * n_down
    come.wait_send()
    for i in range(3):
        for r in range(2):
            leaving(i, r).wait()
    leave.wait_recv()
    leave.wait_send()


def core(sizes, o, x, cotangent, gain, norms, out, down, gu):
    seq_n, depth, rows_n, group, heads = sizes
    count, pairs, width = rows_n * group, rows_n * heads, x.shape[1]
    hidden, half = down[0].shape[0], rows_n * group // 2
    return pl.pallas_call(
        functools.partial(core_kernel, *sizes),
        out_shape=[
            shape(count, width), shape(count, width), shape(count, width), shape(pairs, group, HD),
            shape(1, width, dtype=F32), shape(2, RANK, width, dtype=F32), shape(2, RANK, hidden, dtype=F32),
            shape(2, hidden, dtype=F32), shape(1, width, dtype=F32), shape(RANK, hidden, dtype=F32),
            shape(RANK, width, dtype=F32), shape(RANK, heads * HD, dtype=F32), shape(RANK, width, dtype=F32),
            shape(1, width, dtype=F32),
        ],
        in_specs=[IN_VMEM] * 16 + [ANYWHERE] * 5,
        out_specs=[ANYWHERE] * 3 + [IN_VMEM] * 11,
        scratch_shapes=[pltpu.VMEM((count, width), BF16)] * 3
        + [
            pltpu.VMEM((count, width), BF16), pltpu.VMEM((count, width), BF16), pltpu.VMEM((count, width), BF16),
            pltpu.VMEM(out[0].shape, BF16),
            pltpu.VMEM(gu[0].shape, BF16), pltpu.VMEM(down[0].shape, BF16), pltpu.VMEM((count, heads * HD), BF16),
            pltpu.VMEM((count, RANK), BF16), pltpu.VMEM((count, width), BF16), pltpu.VMEM((count, width), BF16),
            pltpu.VMEM((count, width), BF16), pltpu.VMEM((half, width), BF16), pltpu.VMEM((count, hidden), BF16),
            pltpu.VMEM((count, hidden), BF16), pltpu.VMEM((2, half + RANK, hidden), BF16),
            pltpu.VMEM((count, width), BF16), pltpu.VMEM((2, half, WIDE), F32), pltpu.VMEM((half, 2 * RANK), BF16),
            pltpu.VMEM((half + 2 * RANK, 2 * RANK), BF16),
            pltpu.VMEM((half + RANK, width), BF16), pltpu.VMEM((pairs, group, HD), BF16),
            pltpu.VMEM((8, width), F32), pltpu.VMEM((depth, 8, width), F32), pltpu.VMEM((8, width), F32),
            dma(6), dma(pairs), dma(pairs), dma(pairs), dma(pairs), dma(depth), dma(depth), dma(3, 2),
        ]
        + Line.scratch(count, width, CHUNK)
        + Line.scratch(half, width, CHUNK) * 2,
        compiler_params=params(62, 2),
    )(o, gain, out[3], norms, *out[1:3], out[4], *gu[1:], *down[1:], x, cotangent, out[0], gu[0], down[0])


def last_kernel(
    seq_n, depth, rows_n, group, heads,
    lse, start, place, cos, sin, low, gain, at, b, m, norm, v_qkv,
    ga_gu, gb_out, gb_down, g_gain2, gm_out, gm_down, ga_out, gb_gu, gm_gu, ga_down, inverse_one, norms, m_down,
    down_far, q_far, k_far, v_far, o_far, do_far, h1_far, pre_far, w_qkv, x2_far, dx2_far,
    dx_far, mixed, wide, local, hid,
    dh1, dx, x2, down_part, q, k, v, o, do, h1, pre, kt, dk_acc, dv_acc, dq, dk, dv,
    wq, gq, gk, gv, dp, mix, part, wide_in, local_in, hid_in, wide_got, local_got, hid_got,
    piece, pieces, done, q_send, q_recv, k_send, k_recv, v_send, v_recv, load,
    r_send, r_recv, g_send, g_recv, z_send, z_recv, leave, *line_refs,
):
    count, pairs, width = rows_n * group, rows_n * heads, h1.shape[1]
    fan, me = seq_n // pairs, lax.axis_index("seq")
    loads = [
        pltpu.make_async_copy(far, near, load.at[i])
        for i, (far, near) in enumerate(
            (
                (down_far, down_part), (q_far, q), (k_far, k), (v_far, v), (o_far, o), (do_far, do), (h1_far, h1),
                (pre_far, pre), (w_qkv, wq), (x2_far, x2), (dx2_far, dx),
            )
        )
    ]
    for one in loads[:6]:
        one.start()
    greet(seq=seq_n, heads=depth)
    line_down = Line(down_part, mixed, *line_refs[:9], lead=LAST_LEAD)
    loads[0].wait()
    line_down.first()
    for one in loads[1:6]:
        one.wait()
    for one in loads[6:]:
        one.start()
    exchanges = [
        Exchange(kind, seq_n, pairs, lambda j, a=a: a.at[j], lambda j, to=to: to.at[j], *sems)
        for kind, a, to, sems in (
            ("queries_back", dq, gq, (q_send, q_recv)),
            ("keys_back", dk, gk, (k_send, k_recv)),
            ("keys_back", dv, gv, (v_send, v_recv)),
        )
    ]
    first, second = FIRST, SECOND
    attend_back(
        2 * group if fan == 1 else group, fan, q, k, v, o, do, lse, start, place, dq, dk, dv, kt, dk_acc, dv_acc,
        lambda ticks: line_down.spread(0, first, ticks),
    )
    for one in exchanges:
        one.start()

    wide_in[...] = jnp.zeros_like(wide_in)
    local_in[...] = jnp.zeros_like(local_in)
    hid_in[...] = jnp.zeros_like(hid_in)
    share = 1.0 / depth
    for i in range(2):
        wide_in[(3 + i) * RANK : (4 + i) * RANK, :] = ga_gu[i].astype(BF16)
        hid_in[i * RANK : (i + 1) * RANK, :] = gb_gu[i].astype(BF16)
    wide_in[5 * RANK : 6 * RANK, :] = gb_out[...].astype(BF16)
    wide_in[6 * RANK : 7 * RANK, :] = gb_down[...].astype(BF16)
    hid_in[3 * RANK : 4 * RANK, :] = ga_down[...].astype(BF16)
    local_in[4 * RANK : 5 * RANK, :] = ga_out[...].astype(BF16)
    hid_in[2 * RANK : 3 * RANK, :] = jnp.concatenate(
        [gm_gu[...], jnp.zeros((RANK - 2, hid_in.shape[1]), F32)], axis=0
    ).astype(BF16)

    sums = [None] * 3
    line_down.run(first, second)
    for one in loads[6:9]:
        one.wait()
    for i in range(3):
        exchanges[i].wait_recv()
        came = (gq, gk, gv)[i]
        for head in range(heads):
            cols = slice(head * HD, (head + 1) * HD)
            n = norm[i : i + 1, cols]
            c = m[i : i + 1, cols] / n
            s = jnp.zeros((1, HD), F32)
            for row in range(rows_n):
                rows = slice(row * group, (row + 1) * group)
                if i == 0:
                    e = came[row * heads + head].astype(F32)
                else:
                    e = came[(row * heads + head) * fan].astype(F32)
                    for g in range(1, fan):
                        e = e + came[(row * heads + head) * fan + g].astype(F32)
                if i < 2:
                    e = e * cos[rows, :] - pltpu.roll(e, HD // 2, 1) * sin[rows, :]
                s = s + total(e * pre[i, rows, cols].astype(F32))
                dp[i, rows, cols] = (e * c).astype(BF16)
            turn = m[i : i + 1, cols] * s / (n * n * n)
            dp[i, count : count + RANK, cols] = (b[i, :, cols].astype(F32) * turn).astype(BF16)
            local_in[i * RANK : (i + 1) * RANK, cols] = (
                ADAPT_SCALE * (dot(low[:, i * RANK : (i + 1) * RANK], dp[i, :count, cols], TN) - v_qkv[i, :, cols] * turn)
            ).astype(BF16)
            sums[i] = [s / n] if head == 0 else sums[i] + [s / n]
        line_down.run(second + i, second + i + 1)
    local_in[3 * RANK : 4 * RANK, :] = jnp.concatenate(
        [jnp.concatenate(one, axis=1) for one in sums]
        + [jnp.zeros((RANK - 3, heads * HD), F32)], axis=0
    ).astype(BF16)
    mix[...] = jnp.zeros_like(mix)
    for i in range(3):
        both = (ADAPT_SCALE * dot(dp[i], b[i], NT)).astype(BF16)
        cols = slice(i * RANK, (i + 1) * RANK)
        mix[:count, cols] = both[:count]
        mix[count + i * RANK : count + (i + 1) * RANK, cols] = both[count:]

    def inputs(over, t):
        through = dot(mix[...], at[:, :, over].reshape(3 * RANK, over.size))
        straight = dot(mix[:count, :], h1[:count, over], TN)
        value = through[:count]
        for i in range(3):
            product = dot(dp[i], wq[i, over, :], NT)
            value = value + product[:count]
            rows = slice(i * RANK, (i + 1) * RANK)
            v_tb = product[count:] + through[count + i * RANK : count + (i + 1) * RANK]
            wide_in[rows, over] = (straight[rows] - ADAPT_SCALE * v_tb).astype(BF16)
        part[:, over] = value.astype(BF16)
        g_gain1 = total(value * h1[:count, over].astype(F32)) / gain[:, over]
        wide_in[7 * RANK : 8 * RANK, over] = jnp.concatenate(
            [
                g_gain1, g_gain2[:, over], gm_out[:, over] * share,
                gm_down[:, over] * share,
                jnp.zeros((RANK - 4, over.size), F32),
            ], axis=0,
        ).astype(BF16)

    tiles(width, WIDE, inputs, line_down.spread(second + 3, line_down.steps, -(-width // WIDE)))
    line_down.drain()
    line = Line(part, dh1, *line_refs[:3], *line_refs[9:], lead=LAST_LEAD)
    line.first()
    for one in loads[9:]:
        one.wait()
    c_down = m_down[...] / norms[1:2, :]

    over_gain = 1.0 / gain[...]

    def sent(stream, r):
        at_ = line.place(stream, r * PIECES)[0]
        return pltpu.make_async_copy(dx.at[at_], dx_far.at[at_], leave.at[stream, r])

    def advance(t, carry):
        line.step(t)

        @pl.when(t < count // (2 * CHUNK))
        def _():
            rows = pl.ds(pl.multiple_of(t * (2 * CHUNK), 2 * CHUNK), 2 * CHUNK)
            mixed[rows, :] = (x2[rows, :].astype(F32) + mixed[rows, :].astype(F32) * c_down).astype(BF16)

        c = t - 3 * LAG
        r = c // PIECES

        @pl.when((c >= 0) & (lax.rem(c, PIECES) == PIECES - 1))
        def _():
            for stream in range(2):
                at_ = line.place(stream, c)[0]
                unit = h1[at_, :].astype(F32) * over_gain
                scaled = dh1[at_, :].astype(F32) * gain[...]
                mean = jnp.mean(scaled * unit, axis=-1, keepdims=True)
                change = inverse_one[at_, :1] * (scaled - unit * mean)
                dx[at_, :] = (dx[at_, :].astype(F32) + change).astype(BF16)
                sent(stream, r).start()

        return carry


    spread = seq_n // OWNERS
    slabs = (
        (wide_in, wide_got, wide, lambda j: j), (local_in, local_got, local, lambda j: j),
        (hid_in, hid_got, hid, lambda j: OWNERS - 1 - j),
    )
    own = me // spread
    chosen = lax.rem(me, spread) == 0

    def rows_of(j):
        return pl.ds(pl.multiple_of(j * RANK, RANK), RANK)

    def to_owner(i, j):
        src, got, _, owner = slabs[i]
        return remote(
            src.at[rows_of(j)], got.at[me], r_send.at[i, j], r_recv.at[i, me], seq=owner(j) * spread
        )

    def from_owner(i, j, target):
        result = slabs[i][2]
        return remote(
            done.at[i, :, : result.shape[1]], result.at[rows_of(j)], g_send.at[i, target], g_recv.at[i, j], seq=target
        )

    for i, (src, got, result, owner) in enumerate(slabs):
        for j in range(src.shape[0] // RANK):

            @pl.when(me != owner(j) * spread)
            def _(i=i, j=j):
                to_owner(i, j).start()

            @pl.when(me == owner(j) * spread)
            def _(src=src, got=got, i=i, j=j):
                pltpu.make_async_copy(src.at[rows_of(j)], got.at[me], r_recv.at[i, me]).start()

    lax.fori_loop(0, GATHER, advance, 0)
    across = Across(depth, piece, pieces, z_send, z_recv)
    blocks_n = [slab[0].shape[0] // RANK for slab in slabs]
    owns = [chosen & (slab[3](own) < n) for slab, n in zip(slabs, blocks_n)]
    for i, (src, got, result, owner) in enumerate(slabs):

        @pl.when(owns[i])
        def _(i=i, got=got, result=result):
            def add(s_, acc):
                pltpu.make_async_copy(got.at[s_], got.at[s_], r_recv.at[i, s_]).wait()
                return acc + got[s_].astype(F32)

            value = lax.fori_loop(0, seq_n, add, jnp.zeros((RANK, result.shape[1]), F32))
            if i == 0:
                piece[...] = value.astype(BF16)
                across.start()
            else:
                done[i, :, : result.shape[1]] = value.astype(BF16)

    lax.fori_loop(GATHER, GIVE, advance, 0)

    @pl.when(owns[0])
    def _():
        done[0, :, :] = across.finish().astype(BF16)

    for i, (src, got, result, owner) in enumerate(slabs):

        @pl.when(owns[i])
        def _(i=i, result=result, owner=owner):
            mine = owner(own)

            def give(d, carry):
                from_owner(i, mine, lax.rem(me + d, seq_n)).start()
                return carry

            lax.fori_loop(1, seq_n, give, 0)
            pltpu.make_async_copy(
                done.at[i, :, : result.shape[1]], result.at[rows_of(mine)], g_recv.at[i, mine]
            ).start()

    lax.fori_loop(GIVE, line.steps, advance, 0)
    line.drain()

    def gone(c, carry):
        for stream in range(2):
            sent(stream, c).wait()
        return carry

    lax.fori_loop(0, line.chunks // PIECES, gone, 0)
    for one in exchanges:
        one.wait_send()
    for i, (src, got, result, owner) in enumerate(slabs):
        for j in range(blocks_n[i]):

            @pl.when(me != owner(j) * spread)
            def _(i=i, j=j):
                to_owner(i, j).wait_send()

            pltpu.make_async_copy(result.at[rows_of(j)], result.at[rows_of(j)], g_recv.at[i, j]).wait()

        @pl.when(owns[i])
        def _(i=i, owner=owner):
            def given(d, carry):
                from_owner(i, owner(own), lax.rem(me + d, seq_n)).wait_send()
                return carry

            lax.fori_loop(1, seq_n, given, 0)


def last(sizes, ins, far, hidden):
    seq_n, depth, rows_n, group, heads = sizes
    qkv_w = far[8]
    count, pairs, width = rows_n * group, rows_n * heads, qkv_w.shape[1]
    local, length = qkv_w.shape[2], seq_n * group
    blocks = {width: 8, local: 5, hidden: 4}
    slabs = [(n * RANK, w) for w, n in blocks.items()]
    some, every = pltpu.VMEM((pairs, group, HD), BF16), pltpu.VMEM((seq_n, group, HD), BF16)
    return pl.pallas_call(
        functools.partial(last_kernel, *sizes),
        out_shape=[shape(count, width)] * 2 + [shape(*s) for s in slabs],
        in_specs=[IN_VMEM] * len(ins) + [ANYWHERE] * len(far),
        out_specs=[ANYWHERE] + [IN_VMEM] * 4,
        scratch_shapes=[pltpu.VMEM((count, width), BF16)] * 3
        + [pltpu.VMEM(a.shape, BF16) for a in far[:8]]
        + [
            pltpu.VMEM((HD, length), BF16), pltpu.VMEM((length, HD), F32), pltpu.VMEM((length, HD), F32),
            some, every, every,
            pltpu.VMEM(qkv_w.shape, BF16), some, every, every,
            pltpu.VMEM((3, count + RANK, local), BF16), pltpu.VMEM((count + 3 * RANK, 3 * RANK), BF16),
            pltpu.VMEM((count, width), BF16),
        ]
        + [pltpu.VMEM(s, BF16) for s in slabs]
        + [pltpu.VMEM((seq_n, RANK, s[1]), BF16) for s in slabs]
        + [
            pltpu.VMEM((RANK, width), BF16), pltpu.VMEM((depth, RANK, width), BF16), pltpu.VMEM((3, RANK, width), BF16),
            dma(pairs), dma(pairs), dma(seq_n), dma(seq_n), dma(seq_n), dma(seq_n), dma(11),
            dma(3, 8), dma(3, seq_n), dma(3, seq_n), dma(3, 8), dma(depth), dma(depth), dma(2, count // (2 * CHUNK)),
        ]
        + Line.scratch(count, width, CHUNK)
        + Line.scratch(count, width, CHUNK)[3:],
        compiler_params=params(62, 5),
    )(*ins, *far)


PARTS = 4


def leave_kernel(wide, local, hid, dx_far, mixed_far, *refs):
    outs, (dx_out, mixed_out, dx, dx_wide, mixed, sems) = refs[:14], refs[14:]
    rows = dx.shape[0] // PARTS
    parts = [slice(i * rows, (i + 1) * rows) for i in range(PARTS)]
    moves = [
        [pltpu.make_async_copy(src.at[p], dst.at[p], sems.at[k, i]) for i, p in enumerate(parts)]
        for k, (src, dst) in enumerate(
            ((dx_far, dx), (dx_wide, dx_out), (mixed_far, mixed), (mixed, mixed_out))
        )
    ]
    for k in (0, 2):
        for one in moves[k]:
            one.start()
    for i, p in enumerate(parts):
        moves[0][i].wait()
        dx_wide[p, :] = dx[p, :].astype(F32)
        moves[1][i].start()
    for i in range(PARTS):
        moves[2][i].wait()
        moves[3][i].start()
    places = (
        (wide, 112, 1), (wide, 0, 48), (local, 0, 48), (local, 48, 3), (local, 64, 16), (wide, 80, 16), (wide, 114, 1),
        (wide, 113, 1), (wide, 48, 32), (hid, 0, 32), (hid, 32, 2), (hid, 48, 16), (wide, 96, 16), (wide, 115, 1),
    )
    for out, (slab, first, n) in zip(outs, places):
        begin = first // RANK * RANK
        value = slab[begin : begin + -(-n // RANK) * RANK, :].astype(F32)
        out[...] = value[first - begin : first - begin + n].reshape(out.shape)
    for k in (1, 3):
        for one in moves[k]:
            one.wait()


def outputs(wide, local, hid, dx, mixed):
    w, n, f = wide.shape[1], local.shape[1], hid.shape[1]
    dims = (
        (1, w), (3, RANK, w), (3, RANK, n), (3, n), (RANK, n), (RANK, w), (1, w), (1, w), (2, RANK, w), (2, RANK, f),
        (2, f), (RANK, f), (RANK, w), (1, w),
    )
    return pl.pallas_call(
        leave_kernel,
        out_shape=[shape(*d, dtype=F32) for d in dims] + [shape(*dx.shape, dtype=F32), shape(*mixed.shape)],
        in_specs=[IN_VMEM] * 3 + [ANYWHERE] * 2,
        out_specs=[IN_VMEM] * len(dims) + [ANYWHERE] * 2,
        scratch_shapes=[
            pltpu.VMEM(dx.shape, BF16), pltpu.VMEM(dx.shape, F32), pltpu.VMEM(mixed.shape, BF16), dma(4, PARTS)
        ],
        compiler_params=params(62),
    )(wide, local, hid, dx, mixed)


def per_device(
    tokens, attn_gain, base_qkv, adapt_a_qkv, adapt_b_qkv, magnitude_qkv, base_out, adapt_a_out,
    adapt_b_out, magnitude_out, ffn_gain, base_gu, adapt_a_gu, adapt_b_gu, magnitude_gu, base_down,
    adapt_a_down, adapt_b_down, magnitude_down, doc_lengths, cotangent,
):
    rows_n, group, width = tokens.shape
    count = rows_n * group
    local = base_qkv.shape[2]
    heads = local // HD
    pairs = rows_n * heads
    seq_n, depth = lax.axis_size("seq"), lax.axis_size("heads")
    sizes = (seq_n, depth, rows_n, group, heads)
    fan = seq_n // pairs
    length = group * seq_n
    me = lax.axis_index("seq")

    order = jnp.arange(doc_lengths.shape[1])
    doc_ends = jnp.sum(
        jnp.where(order[None, :, None] <= order[None, None, :], doc_lengths[:, :, None], 0), axis=1
    )
    doc_starts = doc_ends - doc_lengths

    def starts_of(places, ends, starts):
        inside = (places[..., None] >= starts) & (places[..., None] < ends)
        return jnp.sum(jnp.where(inside, starts, 0), axis=-1)

    mine = me * group + jnp.arange(group, dtype=jnp.int32)
    position = mine[None, :] - starts_of(
        jnp.broadcast_to(mine[None, :], (rows_n, group)), doc_ends[:, None], doc_starts[:, None]
    )
    half = HD // 2
    frequency = ROPE_BASE ** (jnp.arange(half, dtype=F32) * (-2.0 / HD))
    angles = position.reshape(count, 1).astype(F32) * frequency
    cos, sin = jnp.cos(angles), jnp.sin(angles)
    cos, sin = jnp.concatenate([cos, cos], axis=1), jnp.concatenate([-sin, sin], axis=1)
    row = me // fan // heads
    block_at = lax.rem(me, fan) + fan * jnp.arange(pairs, dtype=jnp.int32)
    place = (block_at[:, None] * group + jnp.arange(group, dtype=jnp.int32)[None, :]).reshape(-1)
    pick = (jnp.arange(rows_n) == row)[:, None]
    row_ends = jnp.sum(jnp.where(pick, doc_ends, 0), axis=0)
    row_starts = jnp.sum(jnp.where(pick, doc_starts, 0), axis=0)
    start = starts_of(place, row_ends, row_starts)
    low_block = start.reshape(-1, 2 * group)[:, 0] // (2 * group)
    high_block = place.reshape(-1, 2 * group)[:, -1] // (2 * group)
    place, start = place[None, :], start[None, :]

    x = tokens.reshape(count, width)
    dy = cotangent.reshape(count, width)
    gain1, gain2 = attn_gain[None, :], ffn_gain[None, :]
    m_out, m_down = magnitude_out[None, :], magnitude_down[None, :]
    at_qkv, at_gu = adapt_a_qkv.transpose(0, 2, 1), adapt_a_gu.transpose(0, 2, 1)
    at_out, at_down = adapt_a_out.T, adapt_a_down.T

    h1, pre, q, k, v, inverse_one, low, norm_qkv, v_qkv, norms, v_out, v_down, norm_gu, v_gu = front(
        sizes, x, gain1, cos, sin, (base_qkv, at_qkv, adapt_b_qkv, magnitude_qkv), (base_out, at_out, adapt_b_out),
        (base_down, at_down, adapt_b_down), (base_gu, at_gu, adapt_b_gu),
    )
    q, k, v = q.reshape(-1, HD), k.reshape(length, HD), v.reshape(length, HD)
    o, lse = attend(q, k, v, low_block, high_block, start, place, 2 * group)
    dx2, x2, down_part, do, gm_down, ga_gu, gb_gu, gm_gu, g_gain2, ga_down, gb_down, ga_out, gb_out, gm_out = core(
        sizes, o.reshape(-1, group, HD), x, dy, gain2, norms, (base_out, at_out, adapt_b_out, m_out, v_out),
        (base_down, at_down, adapt_b_down, m_down, v_down), (base_gu, at_gu, adapt_b_gu, magnitude_gu, norm_gu, v_gu),
    )
    dx, mixed, wide, narrow, hid = last(
        sizes,
        (
            lse, start, place, cos, sin, low, gain1, at_qkv, adapt_b_qkv, magnitude_qkv, norm_qkv, v_qkv, ga_gu, gb_out,
            gb_down, g_gain2, gm_out, gm_down, ga_out, gb_gu, gm_gu, ga_down, inverse_one, norms, m_down,
        ),
        (down_part, q, k, v, o, do.reshape(-1, HD), h1, pre, base_qkv, x2, dx2),
        base_down.shape[0],
    )
    *g, dx, mixed = outputs(wide, narrow, hid, dx, mixed)
    return (
        mixed.reshape(rows_n, group, width),
        dx.reshape(rows_n, group, width),
        g[0][0], g[1].transpose(0, 2, 1), g[2], g[3], g[4].T, g[5], g[6][0], g[7][0], g[8].transpose(0, 2, 1), g[9],
        g[10], g[11].T, g[12], g[13][0],
    )


def solution(mesh):
    in_specs = (
        P(None, "seq", None), P(), P(None, None, "heads"), P(), P(None, None, "heads"), P(None, "heads"),
        P("heads", None), P("heads", None), P(), P(), P(), P(None, None, "heads"), P(),
        P(None, None, "heads"), P(None, "heads"), P("heads", None), P("heads", None), P(), P(), P(),
        P(None, "seq", None),
    )
    out_specs = (
        P(None, "seq", None), P(None, "seq", None), P(), P(), P(None, None, "heads"), P(None, "heads"),
        P("heads", None), P(), P(), P(), P(), P(None, None, "heads"), P(None, "heads"),
        P("heads", None), P(), P(),
    )
    return jax.shard_map(
        per_device, mesh=mesh, in_specs=in_specs, out_specs=out_specs, check_vma=False
    )
```

```python
import functools

import jax
import jax.numpy as jnp
from jax import lax
from jax.experimental import pallas as pl
from jax.experimental.pallas import tpu as pltpu
from jax.sharding import PartitionSpec as P

HD = 128
RANK = 16
ADAPT_SCALE = 2.0
NORM_EPS = 1e-05
COLUMN_EPS = 1e-06
ROPE_BASE = 10000.0
NEG_LARGE = -1e30
LOG2E = 1.4426950408889634
F32 = jnp.float32
BF16 = jnp.bfloat16
MESH = pl.DeviceIdType.MESH
NN = (((1,), (0,)), ((), ()))
NT = (((1,), (1,)), ((), ()))
TN = (((0,), (0,)), ((), ()))
OWNERS = 8
CHUNK = 16
PIECES = 1
LAG = 2
LEAD = 4
NEAR_LATE = 1
IN_A, IN_B = 4, 5
LAST_LEAD = 4
FIRST, SECOND = 7, 13
GATHER, GIVE = 10, 14
WIDE = 512
IN_VMEM = pl.BlockSpec(memory_space=pltpu.VMEM)
IN_SMEM = pl.BlockSpec(memory_space=pltpu.SMEM)
ANYWHERE = pl.BlockSpec(memory_space=pl.ANY)


def dot(a, b, dims=NN):
    return lax.dot_general(a.astype(BF16), b.astype(BF16), dims, preferred_element_type=F32)


def shape(*dims, dtype=BF16):
    return jax.ShapeDtypeStruct(dims, dtype)


def dma(*dims):
    return pltpu.SemaphoreType.DMA(dims)


def params(mib, collective_id=None):
    more = {} if collective_id is None else {"collective_id": collective_id, "has_side_effects": True}
    return pltpu.CompilerParams(vmem_limit_bytes=mib * 2**20, **more)


def tiles(count, size, body, tick=lambda t: None):
    whole = count // size
    if whole:

        def step(t, carry):
            body(pl.ds(pl.multiple_of(t * size, 128), size), t)
            tick(t)
            return carry

        lax.fori_loop(0, whole, step, 0)
    if count - whole * size:
        body(pl.ds(whole * size, count - whole * size), whole)
        tick(whole)


def row_loop(count, size, body, init=0):
    def step(t, carry):
        return body(pl.ds(pl.multiple_of(t * size, size), size), carry)

    return lax.fori_loop(0, count // size, step, init)


def fold(v):
    return jnp.sum(v.reshape(v.shape[0] // 8, 8, v.shape[1]), axis=0)


def total(v):
    return jnp.sum(v, axis=0, keepdims=True)


def greet(seq, heads):
    barrier = pltpu.get_barrier_semaphore()
    me, h = lax.axis_index("seq"), lax.axis_index("heads")
    peers = 0
    for d in range(1, seq):
        pl.semaphore_signal(barrier, inc=1, device_id={"seq": lax.rem(me + d, seq)}, device_id_type=MESH)
        peers = peers + 1
    for d in range(1, heads):
        pl.semaphore_signal(
            barrier, inc=1, device_id={"heads": lax.rem(h + d, heads)}, device_id_type=MESH
        )
        peers = peers + 1
    return lambda: pl.semaphore_wait(barrier, peers)


def remote(src, dst, send_sem, recv_sem, **where):
    return pltpu.make_async_remote_copy(
        src_ref=src, dst_ref=dst, send_sem=send_sem, recv_sem=recv_sem, device_id=where, device_id_type=MESH
    )


class Exchange:
    def __init__(self, kind, seq_n, pairs, src, dst, send_sem, recv_sem):
        fan = seq_n // pairs
        me = lax.axis_index("seq")
        self.me, self.src, self.dst, self.send_sem, self.recv_sem = me, src, dst, send_sem, recv_sem
        self.count = self.slots(kind, seq_n, pairs)
        self.target, self.block, self.slot = {
            "queries": (lambda p: p * fan + lax.rem(me, fan), lambda p: p, me // fan),
            "keys": (lambda e: e, lambda e: e // fan, me),
            "queries_back": (lambda i: lax.rem(me, fan) + fan * i, lambda i: i, me // fan),
            "keys_back": (lambda e: e, lambda e: e, me),
        }[kind]

    @staticmethod
    def slots(kind, seq_n, pairs):
        return pairs if kind.startswith("queries") else seq_n

    def copy(self, j):
        return remote(
            self.src(self.block(j)),
            self.dst(self.slot),
            self.send_sem.at[j],
            self.recv_sem.at[self.slot],
            seq=self.target(j),
        )

    def start(self, low=0, high=None):
        number = (self.count if high is None else high) - low

        def one(d, carry):
            j = low + lax.rem(self.me + d, number)

            @pl.when(self.target(j) != self.me)
            def _():
                self.copy(j).start()

            @pl.when(self.target(j) == self.me)
            def _():
                pltpu.make_async_copy(
                    self.src(self.block(j)), self.dst(self.slot), self.recv_sem.at[self.slot]
                ).start()

            return carry

        lax.fori_loop(0, number, one, 0)

    def wait_recv(self):
        def one(j, carry):
            pltpu.make_async_copy(self.dst(j), self.dst(j), self.recv_sem.at[j]).wait()
            return carry

        lax.fori_loop(0, self.count, one, 0)

    def wait_send(self):
        def one(j, carry):
            @pl.when(self.target(j) != self.me)
            def _():
                self.copy(j).wait_send()

            return carry

        lax.fori_loop(0, self.count, one, 0)


class Line:
    def __init__(self, x, out, got, near, held, *sems, per=None, base=0, lead=None):
        self.x, self.out, self.got, self.near, self.held = x, out, got, near, held
        self.far_send, self.far_recv, self.near_send, self.near_recv, self.down_send, self.down_recv = sems
        self.chunks, self.rows = got.shape[1], got.shape[2]
        self.per, self.base = per or self.chunks, base
        self.lead = self.chunks if lead is None else lead
        self.steps = self.done(self.chunks)
        self.h = lax.axis_index("heads")

    @staticmethod
    def done(chunks):
        return chunks + 3 * LAG

    @staticmethod
    def scratch(count, width, rows):
        chunks = count // (2 * rows) * PIECES
        one = pltpu.VMEM((chunks, rows, width // PIECES), BF16)
        return [
            pltpu.VMEM((2, chunks, rows, width // PIECES), BF16), one, one,
            dma(2, chunks), dma(2, chunks), dma(chunks), dma(chunks), dma(2, 2, chunks), dma(2, chunks),
        ]

    def ends(self, stream):
        if stream == 0:
            return self.h, self.h + 1, self.h - 1
        return 3 - self.h, self.h - 1, self.h + 1

    def place(self, stream, c):
        rows, per, width = self.rows, self.per // PIECES, self.got.shape[3]
        r, piece = c // PIECES, lax.rem(c, PIECES)
        first = self.base + ((r // per) * 2 + (1 - stream)) * (per * rows) + lax.rem(r, per) * rows
        return pl.ds(pl.multiple_of(first, rows), rows), pl.ds(pl.multiple_of(piece * width, width), width)

    def far(self, stream, c, src, to):
        return remote(
            src, self.got.at[stream, c], self.far_send.at[stream, c], self.far_recv.at[stream, c], heads=to
        )

    def close(self, stream, c, to):
        return remote(
            self.x.at[*self.place(stream, c)], self.near.at[c], self.near_send.at[c], self.near_recv.at[c], heads=to
        )

    def down(self, stream, way, c, to):
        part = self.out.at[*self.place(stream, c)]
        return remote(part, part, self.down_send.at[stream, way, c], self.down_recv.at[stream, c], heads=to)

    def give(self, c):
        for stream in range(2):
            pos, ahead, behind = self.ends(stream)

            @pl.when((pos == 0) & (c < self.chunks))
            def _():
                self.far(stream, c, self.x.at[*self.place(stream, c)], ahead).start()

        c = c - NEAR_LATE
        for stream in range(2):
            pos, ahead, behind = self.ends(stream)

            @pl.when((pos == 3) & (c >= 0) & (c < self.chunks))
            def _():
                self.close(stream, c, behind).start()

    def first(self):
        def one(c, carry):
            self.give(c)
            return carry

        lax.fori_loop(0, self.lead, one, 0)

    def step(self, t):
        self.give(t + self.lead)
        for stream in range(2):
            pos, ahead, behind = self.ends(stream)

            @pl.when((pos == 1) & (t < self.chunks))
            def _():
                self.far(stream, t, self.held.at[t], self.h).wait_recv()
                at = self.place(stream, t)
                self.held[t] = (self.got[stream, t].astype(F32) + self.x[*at].astype(F32)).astype(BF16)
                self.far(stream, t, self.held.at[t], ahead).start()

        for stream in range(2):
            pos, ahead, behind = self.ends(stream)
            c = t - LAG

            @pl.when((pos == 2) & (c >= 0) & (c < self.chunks))
            def _():
                self.far(stream, c, self.held.at[c], self.h).wait_recv()
                self.close(stream, c, self.h).wait_recv()
                at = self.place(stream, c)
                value = self.got[stream, c].astype(F32) + self.near[c].astype(F32) + self.x[*at].astype(F32)
                self.out[*at] = value.astype(BF16)
                self.down(stream, 0, c, behind).start()
                self.down(stream, 1, c, ahead).start()

        for stream in range(2):
            pos, ahead, behind = self.ends(stream)
            b = t - jnp.where(pos == 0, 3 * LAG, 2 * LAG)

            @pl.when((pos != 2) & (b >= 0) & (b < self.chunks))
            def _():
                self.down(stream, 0, b, self.h).wait_recv()

                @pl.when(pos == 1)
                def _():
                    self.down(stream, 0, b, behind).start()

    def run(self, start, stop):
        def one(t, carry):
            self.step(t)
            return carry

        lax.fori_loop(start, stop, one, 0)

    def spread(self, start, stop, ticks):
        def tick(k):
            now, then = (k * (stop - start)) // ticks, ((k + 1) * (stop - start)) // ticks
            self.run(start + now, start + then)

        return tick

    def drain(self):
        def one(c, carry):
            for stream in range(2):
                pos, ahead, behind = self.ends(stream)

                @pl.when(pos <= 1)
                def _():
                    self.far(stream, c, self.held.at[c], self.h).wait_send()

                @pl.when(pos == 3)
                def _():
                    self.close(stream, c, self.h).wait_send()

                @pl.when((pos == 1) | (pos == 2))
                def _():
                    self.down(stream, 0, c, self.h).wait_send()

                @pl.when(pos == 2)
                def _():
                    self.down(stream, 1, c, self.h).wait_send()

            return carry

        lax.fori_loop(0, self.chunks, one, 0)


class Across:
    def __init__(self, depth, part, others, send_sem, recv_sem):
        self.depth, self.part, self.others, self.sems = depth, part, others, (send_sem, recv_sem)
        self.h = lax.axis_index("heads")

    def copy(self, d):
        to = lax.rem(self.h + d, self.depth)
        return remote(
            self.part, self.others.at[self.h], self.sems[0].at[d], self.sems[1].at[self.h], heads=to
        )

    def start(self):
        for d in range(1, self.depth):
            self.copy(d).start()

    def finish(self):
        value = self.part[...].astype(F32)
        for d in range(1, self.depth):
            came = self.others.at[lax.rem(self.h + d, self.depth)]
            pltpu.make_async_copy(came, came, self.sems[1].at[lax.rem(self.h + d, self.depth)]).wait()
            value = value + came[...].astype(F32)
        for d in range(1, self.depth):
            self.copy(d).wait_send()
        return value


def column_stats(w, at, b, aw):
    ab = dot(dot(at, at, NT), b)
    bf = b.astype(F32)

    acc = jnp.zeros((8, w.shape[1]), F32)
    for first in range(0, w.shape[0], 64):
        v = w[first : first + 64, :].astype(F32)
        acc = acc + fold(v * v)
    squares = total(acc) + 2.0 * ADAPT_SCALE * total(bf * aw) + ADAPT_SCALE**2 * total(bf * ab)
    return squares, aw + ADAPT_SCALE * ab


def widen_tables(cos_half, sin_half, cos, sin):
    cos[...] = jnp.concatenate([cos_half[...], cos_half[...]], axis=1)
    sin[...] = jnp.concatenate([-sin_half[...], sin_half[...]], axis=1)


def front_kernel(
    seq_n, depth, rows_n, group, heads,
    x, gain, cos_half, sin_half, at_qkv, b_qkv, m_qkv, at_out, b_out, at_down, b_down, at_gu, b_gu,
    w_qkv, w_out, w_down, w_gu,
    h1_far, pre_far, q, k, v, inverse_one, low, norm_qkv, v_qkv, norms, v_out, v_down, norm_gu, v_gu,
    cos, sin, h1, pre, wq, wo, wd, wg, turned, part, others, q_send, q_recv, k_send, k_recv, v_send, v_recv, z_send, z_recv, load, leave,
):
    count, pairs = rows_n * group, rows_n * heads
    leaving = [pltpu.make_async_copy(pre.at[i], pre_far.at[i], leave.at[i]) for i in range(3)]
    leaving.append(pltpu.make_async_copy(h1, h1_far, leave.at[3]))
    loads = [pltpu.make_async_copy(w_qkv.at[i], wq.at[i], load.at[i]) for i in range(3)]
    loads += [
        pltpu.make_async_copy(w_out, wo, load.at[3]),
        pltpu.make_async_copy(w_down, wd, load.at[4]),
        pltpu.make_async_copy(w_gu, wg, load.at[5]),
    ]
    for one in loads[:3]:
        one.start()
    all_here = greet(seq=seq_n, heads=depth)
    widen_tables(cos_half, sin_half, cos, sin)

    def norm(rows, carry):
        v = x[rows, :].astype(F32)
        inverse = lax.rsqrt(jnp.mean(v * v, axis=-1, keepdims=True) + NORM_EPS)
        h1[rows, :] = (v * inverse * gain[...]).astype(BF16)
        inverse_one[rows, :] = jnp.broadcast_to(inverse, (rows.size, HD))
        return carry

    row_loop(count, 32, norm)
    for i in range(3):
        h1[count + i * RANK : count + (i + 1) * RANK, :] = at_qkv[i]
    leaving[3].start()
    low[...] = dot(h1[:count, :], h1[count:, :], NT).astype(BF16)
    exchanges = [
        Exchange(kind, seq_n, pairs, lambda j, i=i: turned.at[i, j], lambda j, to=to: to.at[j], *sems)
        for i, (kind, to, sems) in enumerate(
            (("queries", q, (q_send, q_recv)), ("keys", k, (k_send, k_recv)), ("keys", v, (v_send, v_recv)))
        )
    ]
    for i in range(3):
        loads[i].wait()
        loads[3 + i].start()

        def project(over, t, i=i):
            width = over.size
            r = dot(h1[...], wq[i, :, over])
            b = b_qkv[i, :, over]
            value = r[:count] + ADAPT_SCALE * dot(low[:, i * RANK : (i + 1) * RANK], b)
            aw = r[count + i * RANK : count + (i + 1) * RANK]
            squares, av = column_stats(wq.at[i, :, over], at_qkv[i], b, aw)
            n = jnp.sqrt(squares + COLUMN_EPS)
            norm_qkv[i : i + 1, over] = n
            v_qkv[i, :, over] = av
            pre[i, :, over] = value.astype(BF16)
            scaled = value * (m_qkv[i : i + 1, over] / n)
            for row in range(rows_n):
                rows = slice(row * group, (row + 1) * group)
                for hh in range(width // HD):
                    part_ = scaled[rows, hh * HD : (hh + 1) * HD]
                    if i < 2:
                        part_ = part_ * cos[rows, :] + pltpu.roll(part_, HD // 2, 1) * sin[rows, :]
                    turned[i, row * heads + t * (width // HD) + hh] = part_.astype(BF16)

        tiles(heads * HD, WIDE, project)
        if i == 0:
            all_here()
        exchanges[i].start()
        leaving[i].start()

    part[...] = jnp.zeros_like(part)
    for row, (w, at, b, av, loaded) in enumerate(
        ((wo, at_out, b_out, v_out, loads[3]), (wd, at_down, b_down, v_down, loads[4]))
    ):
        loaded.wait()

        def stats(over, t, row=row, w=w, at=at, b=b, av=av):
            squares, value = column_stats(w.at[:, over], at[...], b[:, over], dot(at[...], w[:, over]))
            part[row : row + 1, over] = squares
            av[:, over] = value

        tiles(w.shape[1], WIDE, stats)
    across = Across(depth, part, others, z_send, z_recv)
    across.start()
    loads[5].wait()
    for i in range(2):

        def stats_gu(over, t, i=i):
            b = b_gu[i, :, over]
            squares, value = column_stats(wg.at[i, :, over], at_gu[i], b, dot(at_gu[i], wg[i, :, over]))
            norm_gu[i : i + 1, over] = jnp.sqrt(squares + COLUMN_EPS)
            v_gu[i, :, over] = value

        tiles(wg.shape[2], WIDE, stats_gu)
    norms[...] = jnp.sqrt(across.finish() + COLUMN_EPS)
    for one in exchanges:
        one.wait_recv()
    for one in exchanges:
        one.wait_send()
    for one in leaving:
        one.wait()


def front(sizes, x, gain, cos, sin, qkv, out, down, gu):
    seq_n, depth, rows_n, group, heads = sizes
    count, pairs, width = rows_n * group, rows_n * heads, x.shape[1]
    local, hidden = qkv[0].shape[2], gu[0].shape[2]
    return pl.pallas_call(
        functools.partial(front_kernel, *sizes),
        out_shape=[
            shape(count + 3 * RANK, width), shape(3, count, local),
            shape(pairs, group, HD), shape(seq_n, group, HD), shape(seq_n, group, HD),
            shape(count, HD, dtype=F32), shape(count, 3 * RANK),
            shape(3, local, dtype=F32), shape(3, RANK, local, dtype=F32), shape(8, width, dtype=F32),
            shape(RANK, width, dtype=F32), shape(RANK, width, dtype=F32),
            shape(2, hidden, dtype=F32), shape(2, RANK, hidden, dtype=F32),
        ],
        in_specs=[IN_VMEM] * 13 + [ANYWHERE] * 4,
        out_specs=[ANYWHERE] * 2 + [IN_VMEM] * 12,
        scratch_shapes=[
            pltpu.VMEM((count, HD), F32), pltpu.VMEM((count, HD), F32),
            pltpu.VMEM((count + 3 * RANK, width), BF16), pltpu.VMEM((3, count, local), BF16),
            pltpu.VMEM(qkv[0].shape, BF16), pltpu.VMEM(out[0].shape, BF16), pltpu.VMEM(down[0].shape, BF16),
            pltpu.VMEM(gu[0].shape, BF16), pltpu.VMEM((3, pairs, group, HD), BF16),
            pltpu.VMEM((8, width), F32), pltpu.VMEM((depth, 8, width), F32),
            dma(pairs), dma(pairs), dma(seq_n), dma(seq_n), dma(seq_n), dma(seq_n), dma(depth), dma(depth), dma(6), dma(4),
        ],
        compiler_params=params(60, 1),
    )(
        x, gain, cos, sin, qkv[1], qkv[2], qkv[3], out[1], out[2], down[1], down[2], gu[1], gu[2],
        qkv[0], out[0], down[0], gu[0],
    )


def attend_kernel(block, fan, heads, group, docs, q_ref, k_ref, v_ref, o_ref, lse_ref, start_ref, place_ref, vt):
    scale = HD**-0.5 * LOG2E
    vt[...] = v_ref[...].T
    me = lax.axis_index("seq")
    mine, row, split = lax.rem(me, fan), me // fan // heads, block // group
    lengths = [docs[row, d] for d in range(docs.shape[1])]

    def starts_of(places):
        end, begin = 0, 0
        for n in lengths:
            end = end + n
            begin = begin + jnp.where(places >= end, n, 0)
        return begin

    for b in range(q_ref.shape[0] // group):
        over = slice(b * group, (b + 1) * group)
        places = (mine + fan * b) * group + lax.broadcasted_iota(jnp.int32, (1, group), 1)
        place_ref[:, over] = places
        start_ref[:, over] = starts_of(places)

    def per_query(i, carry):
        at = pl.ds(pl.multiple_of(i * block, block), block)
        q = q_ref[at, :]
        start, place = start_ref[:, at], place_ref[:, at]

        def per_key(j, state):
            top, count, acc = state
            over = pl.ds(pl.multiple_of(j * block, block), block)
            s = dot(k_ref[over, :], q, NT) * scale
            key = j * block + lax.broadcasted_iota(jnp.int32, (block, block), 0)
            s = jnp.where((key >= start) & (key <= place), s, NEG_LARGE)
            new_top = jnp.maximum(top, jnp.max(s, axis=0, keepdims=True))
            p = jnp.exp2(s - new_top)
            fade = jnp.exp2(top - new_top)
            count = count * fade + total(p)
            acc = acc * fade + dot(vt[:, over], p)
            return new_top, count, acc

        low = starts_of((mine + fan * (i * split)) * group) // block
        high = ((mine + fan * ((i + 1) * split - 1) + 1) * group - 1) // block + 1
        begin = (
            jnp.full((1, block), -1e29, F32),
            jnp.zeros((1, block), F32),
            jnp.zeros((HD, block), F32),
        )
        top, count, acc = lax.fori_loop(low, high, per_key, begin)
        o_ref[at, :] = (acc / count).T.astype(BF16)
        lse_ref[:, at] = top + jnp.log2(count)
        return carry

    lax.fori_loop(0, q_ref.shape[0] // block, per_query, 0)


def attend(sizes, docs, q, k, v):
    seq_n, depth, rows_n, group, heads = sizes
    count, fan = q.shape[0], seq_n // (rows_n * heads)
    return pl.pallas_call(
        functools.partial(attend_kernel, 2 * group, fan, heads, group),
        out_shape=[
            shape(*q.shape), shape(1, count, dtype=F32), shape(1, count, dtype=jnp.int32),
            shape(1, count, dtype=jnp.int32),
        ],
        in_specs=[IN_SMEM] + [IN_VMEM] * 3,
        out_specs=[IN_VMEM] * 4,
        scratch_shapes=[pltpu.VMEM((HD, k.shape[0]), BF16)],
        compiler_params=params(62),
    )(docs, q, k, v)


def attend_back(block, fan, q_ref, k_ref, v_ref, o_ref, do_ref, lse_ref, start_ref, place_ref, dq, dk, dv, kt, dk_acc, dv_acc, spread):
    scale = HD**-0.5
    mine = lax.rem(lax.axis_index("seq"), fan)
    group = dq.shape[1]
    split = block // group
    blocks = q_ref.shape[0] // block

    def reach(i):
        return ((mine + fan * ((i + 1) * split - 1) + 1) * group - 1) // block + 1

    tick = spread(sum(reach(i) for i in range(blocks)))
    kt[...] = k_ref[...].T
    dk_acc[...] = jnp.zeros_like(dk_acc)
    dv_acc[...] = jnp.zeros_like(dv_acc)

    def per_query(i, before):
        at = pl.ds(pl.multiple_of(i * block, block), block)
        q, do = q_ref[at, :], do_ref[at, :]
        start, place, lse = start_ref[:, at], place_ref[:, at], lse_ref[:, at]
        delta = total((do.astype(F32) * o_ref[at, :].astype(F32)).T)

        def per_key(j, acc):
            over = pl.ds(pl.multiple_of(j * block, block), block)
            k = k_ref[over, :]
            s = dot(k, q, NT) * (scale * LOG2E)
            key = j * block + lax.broadcasted_iota(jnp.int32, (block, block), 0)
            p = jnp.exp2(jnp.where((key >= start) & (key <= place), s - lse, NEG_LARGE))
            dp = dot(v_ref[over, :], do, NT)
            ds = (p * (dp - delta)).astype(BF16)
            dv_acc[over, :] += dot(p, do)
            dk_acc[over, :] += dot(ds, q)
            tick(before + j)
            return acc + dot(kt[:, over], ds)

        acc = lax.fori_loop(0, reach(i), per_key, jnp.zeros((HD, block), F32))
        acc = (acc * scale).T.astype(BF16)
        for n in range(split):
            dq[i * split + n] = acc[n * group : (n + 1) * group]
        return before + reach(i)

    lax.fori_loop(0, blocks, per_query, 0)

    def store(j, carry):
        over = pl.ds(pl.multiple_of(j * group, group), group)
        dk[j] = (dk_acc[over, :] * scale).astype(BF16)
        dv[j] = dv_acc[over, :].astype(BF16)
        return carry

    lax.fori_loop(0, k_ref.shape[0] // group, store, 0)


def core_kernel(
    seq_n, depth, rows_n, group, heads,
    o, gain, m_out, norms, at_out, b_out, v_out, at_gu, b_gu, m_gu, norm_gu, v_gu, at_down, b_down, m_down, v_down,
    x_far, cotangent_far, w_out, w_gu, w_down,
    dx2_far, x2_far, down_far, do, gm_down, ga_gu, gb_gu, gm_gu, g_gain, ga_down, gb_down, ga_out, gb_out, gm_out,
    dx2, x2_out, down_part, out_pre, x, cotangent, wo, wg, wd, attn, low_out, part, part2, dh2, h2, z, dz, dp, dpd, tmp, low, mix, dpo, blocks,
    s_part, others, row_sums, load, send, recv, back_send, back_recv, z_send, z_recv, away, *line_refs,
):
    count, pairs = rows_n * group, rows_n * heads
    half = count // 2
    hidden, width = wd.shape
    loads = [
        pltpu.make_async_copy(far, near, load.at[i])
        for i, (far, near) in enumerate(
            ((w_out, wo), (x_far, x), (w_gu.at[0], wg.at[0]), (w_gu.at[1], wg.at[1]), (cotangent_far, cotangent), (w_down, wd))
        )
    ]
    for one in loads:
        one.start()
    greet(seq=seq_n, heads=depth)()

    def landing(pair):
        row, head = pair // heads, lax.rem(pair, heads)
        return attn.at[
            pl.ds(pl.multiple_of(row * group, group), group), pl.ds(pl.multiple_of(head * HD, HD), HD)
        ]

    def leaving(i, r):
        near, far = ((dx2, dx2_far), (x2_out, x2_far), (down_part, down_far))[i]
        return pltpu.make_async_copy(
            near.at[r * half : (r + 1) * half], far.at[r * half : (r + 1) * half], away.at[i, r]
        )

    come = Exchange("queries_back", seq_n, pairs, lambda i: o.at[i], landing, send, recv)
    leave = Exchange("queries", seq_n, pairs, lambda p: blocks.at[p], lambda s_: do.at[s_], back_send, back_recv)
    come.start()
    for ref in (s_part, ga_gu, gb_gu, gm_gu, g_gain, ga_down, gb_down, ga_out, gb_out, gm_out):
        ref[...] = jnp.zeros_like(ref)
    one_out = Line(part, out_pre, *line_refs[:9], per=half // (2 * CHUNK) * PIECES, lead=LEAD)
    two = [
        Line(part2, dh2, *line_refs[9 + 9 * r : 18 + 9 * r], base=r * half, lead=LEAD) for r in range(2)
    ]
    loads[0].wait()
    come.wait_recv()
    low_out[...] = dot(attn[...], at_out[...], NT).astype(BF16)

    def project(over, t):
        part[:, over] = (dot(attn[...], wo[:, over]) + ADAPT_SCALE * dot(low_out[...], b_out[:, over])).astype(BF16)

    tiles(width, WIDE, project)
    one_out.first()
    for one in loads[1:]:
        one.wait()
    n_out, n_down = 1.0 / norms[0:1, :], 1.0 / norms[1:2, :]
    c_out, c_down = m_out[...] * n_out, m_down[...] * n_down

    n_hidden, n_width = -(-hidden // WIDE), -(-width // WIDE)
    half_done = one_out.done(one_out.per)
    tick_first = one_out.spread(0, half_done, count // 64 + n_hidden)

    def scaled_gradient(rows, carry):
        dpd[rows, :] = (cotangent[rows, :].astype(F32) * c_down).astype(BF16)
        tick_first(rows.start // rows.size)
        return carry

    row_loop(count, 64, scaled_gradient)
    dlow_down = (ADAPT_SCALE * dot(dpd[...], b_down[...], NT)).astype(BF16)

    def hidden_gradient(over, t):
        dz[:, over] = (dot(dpd[...], wd[over, :], NT) + dot(dlow_down, at_down[:, over])).astype(BF16)

    tiles(hidden, WIDE, hidden_gradient, lambda t: tick_first(count // 64 + t))

    def feed_forward(r, tick):
        mine = slice(r * half, (r + 1) * half)
        base = r * half

        def there(rows):
            return pl.ds(pl.multiple_of(base + rows.start, rows.size), rows.size)

        def norm(rows, carry):
            x2 = x[there(rows), :].astype(F32) + out_pre[there(rows), :].astype(F32) * c_out
            inverse = lax.rsqrt(jnp.mean(x2 * x2, axis=-1, keepdims=True) + NORM_EPS)
            h2[rows, :] = (x2 * inverse * gain[...]).astype(BF16)
            tick(rows.start // rows.size)
            return carry

        row_loop(half, 32, norm)
        low[...] = dot(h2[...], at_gu[...].reshape(2 * RANK, width), NT).astype(BF16)

        def there_and_back(over, t):
            n = over.size
            for i in range(2):
                tmp[i, :, :n] = dot(h2[...], wg[i, :, over]) + ADAPT_SCALE * dot(
                    low[:, i * RANK : (i + 1) * RANK], b_gu[i, :, over]
                )
            scale = [m_gu[i : i + 1, over] / norm_gu[i : i + 1, over] for i in range(2)]

            def gated(rows, sums):
                pg, pu = tmp[0, rows, :n], tmp[1, rows, :n]
                g, u = pg * scale[0], pu * scale[1]
                sigma = jax.nn.sigmoid(g)
                silu = g * sigma
                z[there(rows), over] = (silu * u).astype(BF16)
                d = dz[there(rows), over].astype(F32)
                e_g = d * u * (sigma + silu * (1.0 - sigma))
                e_u = d * silu
                dp[0, rows, over] = (e_g * scale[0]).astype(BF16)
                dp[1, rows, over] = (e_u * scale[1]).astype(BF16)
                return sums[0] + fold(e_g * pg), sums[1] + fold(e_u * pu)

            zero = jnp.zeros((8, n), F32)
            sums = row_loop(half, 32, gated, (zero, zero))
            for i in range(2):
                s, inverse = total(sums[i]), 1.0 / norm_gu[i : i + 1, over]
                gm_gu[i : i + 1, over] += s * inverse
                turn = m_gu[i : i + 1, over] * s * inverse * inverse * inverse
                dp[i, half : half + RANK, over] = (b_gu[i, :, over].astype(F32) * turn).astype(BF16)
                gb_gu[i, :, over] += ADAPT_SCALE * (
                    dot(low[:, i * RANK : (i + 1) * RANK], dp[i, :half, over], TN) - v_gu[i, :, over] * turn
                )

        tiles(hidden, WIDE, there_and_back, lambda t: tick(half // 32 + t))
        for i in range(2):
            both = ADAPT_SCALE * dot(dp[i], b_gu[i], NT)
            mix[:half, i * RANK : (i + 1) * RANK] = both[:half].astype(BF16)
            for k in range(2):
                mix[half + k * RANK : half + (k + 1) * RANK, i * RANK : (i + 1) * RANK] = (
                    both[half:] if i == k else jnp.zeros((RANK, RANK), F32)
                ).astype(BF16)

        def inputs(over, t):
            products = [dot(dp[i], wg[i, over, :], NT) for i in range(2)]
            through = dot(mix[...], at_gu[:, :, over].reshape(2 * RANK, over.size))
            value = products[0][:half] + products[1][:half] + through[:half]
            straight = dot(mix[:half, :], h2[:, over], TN)
            for i in range(2):
                v_tb = products[i][half:] + through[half + i * RANK : half + (i + 1) * RANK]
                ga_gu[i, :, over] += straight[i * RANK : (i + 1) * RANK] - ADAPT_SCALE * v_tb
            part2[mine, over] = value.astype(BF16)
            g_gain[:, over] += total(value * h2[:, over].astype(F32)) / gain[:, over]

        tiles(width, WIDE, inputs, lambda t: tick(half // 32 + n_hidden + t))

    def norm_back(r, first):
        rows = pl.ds(pl.multiple_of(first, 16), 16)
        there = pl.ds(pl.multiple_of(r * half + first, 16), 16)
        value = out_pre[there, :].astype(F32)
        x2 = x[there, :].astype(F32) + value * c_out
        inverse = lax.rsqrt(jnp.mean(x2 * x2, axis=-1, keepdims=True) + NORM_EPS)
        scaled = dh2[there, :].astype(F32) * gain[...]
        mean = jnp.mean(scaled * x2, axis=-1, keepdims=True)
        e = cotangent[there, :].astype(F32) + inverse * scaled - x2 * (inverse**3 * mean)
        dx2[there, :] = e.astype(BF16)
        x2_out[there, :] = x2.astype(BF16)
        dpo[rows, :] = (e * c_out).astype(BF16)
        row_sums[...] += fold(e * value)

    def out_back(r):
        mine = slice(r * half, (r + 1) * half)
        rows_here = rows_n // 2

        s = total(row_sums[...])
        turn = m_out[...] * s * n_out * n_out * n_out
        gm_out[...] += s * n_out
        dpo[half : half + RANK, :] = (b_out[...].astype(F32) * turn).astype(BF16)
        both = dot(dpo[...], b_out[...], NT)
        dlow, turned = (ADAPT_SCALE * both[:half]).astype(BF16), both[half:]

        def inputs(over, t):
            product = dot(dpo[...], wo[over, :], NT)
            value = (product[:half] + dot(dlow, at_out[:, over])).astype(BF16)
            for row in range(rows_here):
                for hh in range(over.size // HD):
                    blocks[(r * rows_here + row) * heads + t * (over.size // HD) + hh] = value[
                        row * group : (row + 1) * group, hh * HD : (hh + 1) * HD
                    ]
            ga_out[:, over] += dot(dlow, attn[mine, over], TN) - ADAPT_SCALE * (
                product[half:] + ADAPT_SCALE * dot(turned, at_out[:, over])
            )

        tiles(heads * HD, WIDE, inputs)
        leave.start(r * rows_here * heads, (r + 1) * rows_here * heads)
        leaving(0, r).start()
        leaving(1, r).start()
        gb_out[...] += ADAPT_SCALE * (dot(low_out[mine, :], dpo[:half, :], TN) - v_out[...] * turn)

    ticks = half // 32 + n_hidden + n_width
    feed_forward(0, one_out.spread(half_done, half_done + IN_A, ticks))
    two[0].first()
    left = one_out.steps - half_done - IN_A

    def between(k, carry):
        one_out.step(half_done + IN_A + k)
        two[0].step(k)
        return carry

    lax.fori_loop(0, left, between, 0)
    feed_forward(1, two[0].spread(left, left + IN_B, ticks))
    two[1].first()
    rest = two[0].steps - left - IN_B

    def together(k, carry):
        two[0].step(left + IN_B + k)
        two[1].step(k)
        return carry

    lax.fori_loop(0, rest, together, 0)

    low_down = dot(z[...], at_down[...], NT).astype(BF16)

    def down(over, t):
        value = dot(z[...], wd[:, over]) + ADAPT_SCALE * dot(low_down, b_down[:, over])
        down_part[:, over] = value.astype(BF16)
        s_part[0:1, over] = total(value * cotangent[:, over].astype(F32))
        gb_down[:, over] = ADAPT_SCALE * dot(low_down, dpd[:, over], TN)

    tiles(width, WIDE, down, two[1].spread(rest, rest + 2, n_width))
    leaving(2, 0).start()
    leaving(2, 1).start()
    across = Across(depth, s_part, others, z_send, z_recv)
    across.start()

    def down_factor(over, t):
        ga_down[:, over] = dot(dlow_down, z[:, over], TN)

    tiles(hidden, WIDE, down_factor)
    row_sums[...] = jnp.zeros_like(row_sums)
    taken = rest + 4
    tick_two = two[1].spread(rest + 2, taken, half // 16)

    def first_half(k, carry):
        norm_back(0, k * 16)
        tick_two(k)
        return carry

    lax.fori_loop(0, half // 16, first_half, 0)
    out_back(0)
    row_sums[...] = jnp.zeros_like(row_sums)

    def second_half(t, carry):
        @pl.when(t >= taken)
        def _():
            two[1].step(t)

        for stream in range(2):
            norm_back(1, ((1 - stream) * two[1].chunks + t - 3 * LAG) * CHUNK)
        return carry

    lax.fori_loop(3 * LAG, two[1].steps, second_half, 0)
    out_back(1)
    for line in [one_out] + two:
        line.drain()
    s = across.finish()[0:1, :]
    turn = m_down[...] * s * n_down * n_down * n_down
    tb = (b_down[...].astype(F32) * turn).astype(BF16)
    v_tb = dot(tb, wd[...], NT) + ADAPT_SCALE * dot(dot(tb, b_down[...], NT), at_down[...])
    ga_down[...] -= ADAPT_SCALE * v_tb
    gb_down[...] -= ADAPT_SCALE * v_down[...] * turn
    gm_down[...] = s * n_down
    come.wait_send()
    for i in range(3):
        for r in range(2):
            leaving(i, r).wait()
    leave.wait_recv()
    leave.wait_send()


def core(sizes, o, x, cotangent, gain, norms, out, down, gu):
    seq_n, depth, rows_n, group, heads = sizes
    count, pairs, width = rows_n * group, rows_n * heads, x.shape[1]
    hidden, half = down[0].shape[0], rows_n * group // 2
    return pl.pallas_call(
        functools.partial(core_kernel, *sizes),
        out_shape=[
            shape(count, width), shape(count, width), shape(count, width), shape(pairs, group, HD),
            shape(1, width, dtype=F32), shape(2, RANK, width, dtype=F32), shape(2, RANK, hidden, dtype=F32),
            shape(2, hidden, dtype=F32), shape(1, width, dtype=F32), shape(RANK, hidden, dtype=F32),
            shape(RANK, width, dtype=F32), shape(RANK, heads * HD, dtype=F32), shape(RANK, width, dtype=F32),
            shape(1, width, dtype=F32),
        ],
        in_specs=[IN_VMEM] * 16 + [ANYWHERE] * 5,
        out_specs=[ANYWHERE] * 3 + [IN_VMEM] * 11,
        scratch_shapes=[pltpu.VMEM((count, width), BF16)] * 3
        + [
            pltpu.VMEM((count, width), BF16), pltpu.VMEM((count, width), BF16), pltpu.VMEM((count, width), BF16),
            pltpu.VMEM(out[0].shape, BF16),
            pltpu.VMEM(gu[0].shape, BF16), pltpu.VMEM(down[0].shape, BF16), pltpu.VMEM((count, heads * HD), BF16),
            pltpu.VMEM((count, RANK), BF16), pltpu.VMEM((count, width), BF16), pltpu.VMEM((count, width), BF16),
            pltpu.VMEM((count, width), BF16), pltpu.VMEM((half, width), BF16), pltpu.VMEM((count, hidden), BF16),
            pltpu.VMEM((count, hidden), BF16), pltpu.VMEM((2, half + RANK, hidden), BF16),
            pltpu.VMEM((count, width), BF16), pltpu.VMEM((2, half, WIDE), F32), pltpu.VMEM((half, 2 * RANK), BF16),
            pltpu.VMEM((half + 2 * RANK, 2 * RANK), BF16),
            pltpu.VMEM((half + RANK, width), BF16), pltpu.VMEM((pairs, group, HD), BF16),
            pltpu.VMEM((8, width), F32), pltpu.VMEM((depth, 8, width), F32), pltpu.VMEM((8, width), F32),
            dma(6), dma(pairs), dma(pairs), dma(pairs), dma(pairs), dma(depth), dma(depth), dma(3, 2),
        ]
        + Line.scratch(count, width, CHUNK)
        + Line.scratch(half, width, CHUNK) * 2,
        compiler_params=params(62, 2),
    )(o, gain, out[3], norms, *out[1:3], out[4], *gu[1:], *down[1:], x, cotangent, out[0], gu[0], down[0])


def last_kernel(
    seq_n, depth, rows_n, group, heads,
    lse, start, place, cos_half, sin_half, low, gain, at, b, m, norm, v_qkv,
    ga_gu, gb_out, gb_down, g_gain2, gm_out, gm_down, ga_out, gb_gu, gm_gu, ga_down, inverse_one, norms, m_down,
    down_far, q_far, k_far, v_far, o_far, do_far, h1_far, pre_far, w_qkv, x2_far, dx2_far,
    dx_far, mixed_far, wide, local, hid,
    mixed, cos, sin, dh1, dx, x2, down_part, q, k, v, o, do, h1, pre, kt, dk_acc, dv_acc, dq, dk, dv,
    wq, gq, gk, gv, dp, mix, part, wide_in, local_in, hid_in, wide_got, local_got, hid_got,
    piece, pieces, done, q_send, q_recv, k_send, k_recv, v_send, v_recv, load,
    r_send, r_recv, g_send, g_recv, z_send, z_recv, leave, *line_refs,
):
    count, pairs, width = rows_n * group, rows_n * heads, h1.shape[1]
    fan, me = seq_n // pairs, lax.axis_index("seq")
    loads = [
        pltpu.make_async_copy(far, near, load.at[i])
        for i, (far, near) in enumerate(
            (
                (down_far, down_part), (q_far, q), (k_far, k), (v_far, v), (o_far, o), (do_far, do), (h1_far, h1),
                (pre_far, pre), (w_qkv, wq), (x2_far, x2), (dx2_far, dx),
            )
        )
    ]
    for one in loads[:6]:
        one.start()
    greet(seq=seq_n, heads=depth)()
    line_down = Line(down_part, mixed, *line_refs[:9], lead=LAST_LEAD)
    loads[0].wait()
    line_down.first()
    for one in loads[1:6]:
        one.wait()
    for one in loads[6:]:
        one.start()
    exchanges = [
        Exchange(kind, seq_n, pairs, lambda j, a=a: a.at[j], lambda j, to=to: to.at[j], *sems)
        for kind, a, to, sems in (
            ("queries_back", dq, gq, (q_send, q_recv)),
            ("keys_back", dk, gk, (k_send, k_recv)),
            ("keys_back", dv, gv, (v_send, v_recv)),
        )
    ]
    first, second = FIRST, SECOND
    attend_back(
        2 * group if fan == 1 else group, fan, q, k, v, o, do, lse, start, place, dq, dk, dv, kt, dk_acc, dv_acc,
        lambda ticks: line_down.spread(0, first, ticks),
    )
    for one in exchanges:
        one.start()

    widen_tables(cos_half, sin_half, cos, sin)
    wide_in[...] = jnp.zeros_like(wide_in)
    local_in[...] = jnp.zeros_like(local_in)
    hid_in[...] = jnp.zeros_like(hid_in)
    share = 1.0 / depth
    for i in range(2):
        wide_in[(3 + i) * RANK : (4 + i) * RANK, :] = ga_gu[i].astype(BF16)
        hid_in[i * RANK : (i + 1) * RANK, :] = gb_gu[i].astype(BF16)
    wide_in[5 * RANK : 6 * RANK, :] = gb_out[...].astype(BF16)
    wide_in[6 * RANK : 7 * RANK, :] = gb_down[...].astype(BF16)
    hid_in[3 * RANK : 4 * RANK, :] = ga_down[...].astype(BF16)
    local_in[4 * RANK : 5 * RANK, :] = ga_out[...].astype(BF16)
    hid_in[2 * RANK : 3 * RANK, :] = jnp.concatenate(
        [gm_gu[...], jnp.zeros((RANK - 2, hid_in.shape[1]), F32)], axis=0
    ).astype(BF16)

    sums = [None] * 3
    line_down.run(first, second)
    for one in loads[6:9]:
        one.wait()
    for i in range(3):
        exchanges[i].wait_recv()
        came = (gq, gk, gv)[i]
        for head in range(heads):
            cols = slice(head * HD, (head + 1) * HD)
            n = norm[i : i + 1, cols]
            c = m[i : i + 1, cols] / n
            s = jnp.zeros((1, HD), F32)
            for row in range(rows_n):
                rows = slice(row * group, (row + 1) * group)
                if i == 0:
                    e = came[row * heads + head].astype(F32)
                else:
                    e = came[(row * heads + head) * fan].astype(F32)
                    for g in range(1, fan):
                        e = e + came[(row * heads + head) * fan + g].astype(F32)
                if i < 2:
                    e = e * cos[rows, :] - pltpu.roll(e, HD // 2, 1) * sin[rows, :]
                s = s + total(e * pre[i, rows, cols].astype(F32))
                dp[i, rows, cols] = (e * c).astype(BF16)
            turn = m[i : i + 1, cols] * s / (n * n * n)
            dp[i, count : count + RANK, cols] = (b[i, :, cols].astype(F32) * turn).astype(BF16)
            local_in[i * RANK : (i + 1) * RANK, cols] = (
                ADAPT_SCALE * (dot(low[:, i * RANK : (i + 1) * RANK], dp[i, :count, cols], TN) - v_qkv[i, :, cols] * turn)
            ).astype(BF16)
            sums[i] = [s / n] if head == 0 else sums[i] + [s / n]
        line_down.run(second + i, second + i + 1)
    local_in[3 * RANK : 4 * RANK, :] = jnp.concatenate(
        [jnp.concatenate(one, axis=1) for one in sums]
        + [jnp.zeros((RANK - 3, heads * HD), F32)], axis=0
    ).astype(BF16)
    mix[...] = jnp.zeros_like(mix)
    for i in range(3):
        both = (ADAPT_SCALE * dot(dp[i], b[i], NT)).astype(BF16)
        cols = slice(i * RANK, (i + 1) * RANK)
        mix[:count, cols] = both[:count]
        mix[count + i * RANK : count + (i + 1) * RANK, cols] = both[count:]

    def inputs(over, t):
        through = dot(mix[...], at[:, :, over].reshape(3 * RANK, over.size))
        straight = dot(mix[:count, :], h1[:count, over], TN)
        value = through[:count]
        for i in range(3):
            product = dot(dp[i], wq[i, over, :], NT)
            value = value + product[:count]
            rows = slice(i * RANK, (i + 1) * RANK)
            v_tb = product[count:] + through[count + i * RANK : count + (i + 1) * RANK]
            wide_in[rows, over] = (straight[rows] - ADAPT_SCALE * v_tb).astype(BF16)
        part[:, over] = value.astype(BF16)
        g_gain1 = total(value * h1[:count, over].astype(F32)) / gain[:, over]
        wide_in[7 * RANK : 8 * RANK, over] = jnp.concatenate(
            [
                g_gain1, g_gain2[:, over], gm_out[:, over] * share,
                gm_down[:, over] * share,
                jnp.zeros((RANK - 4, over.size), F32),
            ], axis=0,
        ).astype(BF16)

    tiles(width, WIDE, inputs, line_down.spread(second + 3, line_down.steps, -(-width // WIDE)))
    line_down.drain()
    line = Line(part, dh1, *line_refs[:3], *line_refs[9:], lead=LAST_LEAD)
    line.first()
    for one in loads[9:]:
        one.wait()
    c_down = m_down[...] / norms[1:2, :]

    over_gain = 1.0 / gain[...]

    def sent(stream, r):
        at_ = line.place(stream, r * PIECES)[0]
        return pltpu.make_async_copy(dx.at[at_], dx_far.at[at_], leave.at[stream, r])

    mixed_leaves = pltpu.make_async_copy(mixed, mixed_far, load.at[0])

    def advance(t, carry):
        line.step(t)

        @pl.when(t < count // (2 * CHUNK))
        def _():
            rows = pl.ds(pl.multiple_of(t * (2 * CHUNK), 2 * CHUNK), 2 * CHUNK)
            mixed[rows, :] = (x2[rows, :].astype(F32) + mixed[rows, :].astype(F32) * c_down).astype(BF16)

        @pl.when(t == count // (2 * CHUNK))
        def _():
            mixed_leaves.start()

        c = t - 3 * LAG
        r = c // PIECES

        @pl.when((c >= 0) & (lax.rem(c, PIECES) == PIECES - 1))
        def _():
            for stream in range(2):
                at_ = line.place(stream, c)[0]
                unit = h1[at_, :].astype(F32) * over_gain
                scaled = dh1[at_, :].astype(F32) * gain[...]
                mean = jnp.mean(scaled * unit, axis=-1, keepdims=True)
                change = inverse_one[at_, :1] * (scaled - unit * mean)
                dx[at_, :] = (dx[at_, :].astype(F32) + change).astype(BF16)
                sent(stream, r).start()

        return carry


    spread = seq_n // OWNERS
    slabs = (
        (wide_in, wide_got, wide, lambda j: j), (local_in, local_got, local, lambda j: j),
        (hid_in, hid_got, hid, lambda j: OWNERS - 1 - j),
    )
    own = me // spread
    chosen = lax.rem(me, spread) == 0

    def rows_of(j):
        return pl.ds(pl.multiple_of(j * RANK, RANK), RANK)

    def to_owner(i, j):
        src, got, _, owner = slabs[i]
        return remote(
            src.at[rows_of(j)], got.at[me], r_send.at[i, j], r_recv.at[i, me], seq=owner(j) * spread
        )

    def from_owner(i, j, target):
        result = slabs[i][2]
        return remote(
            done.at[i, :, : result.shape[1]], result.at[rows_of(j)], g_send.at[i, target], g_recv.at[i, j], seq=target
        )

    for i, (src, got, result, owner) in enumerate(slabs):
        for j in range(src.shape[0] // RANK):

            @pl.when(me != owner(j) * spread)
            def _(i=i, j=j):
                to_owner(i, j).start()

            @pl.when(me == owner(j) * spread)
            def _(src=src, got=got, i=i, j=j):
                pltpu.make_async_copy(src.at[rows_of(j)], got.at[me], r_recv.at[i, me]).start()

    lax.fori_loop(0, GATHER, advance, 0)
    across = Across(depth, piece, pieces, z_send, z_recv)
    blocks_n = [slab[0].shape[0] // RANK for slab in slabs]
    owns = [chosen & (slab[3](own) < n) for slab, n in zip(slabs, blocks_n)]
    for i, (src, got, result, owner) in enumerate(slabs):

        @pl.when(owns[i])
        def _(i=i, got=got, result=result):
            def add(s_, acc):
                pltpu.make_async_copy(got.at[s_], got.at[s_], r_recv.at[i, s_]).wait()
                return acc + got[s_].astype(F32)

            value = lax.fori_loop(0, seq_n, add, jnp.zeros((RANK, result.shape[1]), F32))
            if i == 0:
                piece[...] = value.astype(BF16)
                across.start()
            else:
                done[i, :, : result.shape[1]] = value.astype(BF16)

    lax.fori_loop(GATHER, GIVE, advance, 0)

    @pl.when(owns[0])
    def _():
        done[0, :, :] = across.finish().astype(BF16)

    for i, (src, got, result, owner) in enumerate(slabs):

        @pl.when(owns[i])
        def _(i=i, result=result, owner=owner):
            mine = owner(own)

            def give(d, carry):
                from_owner(i, mine, lax.rem(me + d, seq_n)).start()
                return carry

            lax.fori_loop(1, seq_n, give, 0)
            pltpu.make_async_copy(
                done.at[i, :, : result.shape[1]], result.at[rows_of(mine)], g_recv.at[i, mine]
            ).start()

    lax.fori_loop(GIVE, line.steps, advance, 0)
    line.drain()

    def gone(c, carry):
        for stream in range(2):
            sent(stream, c).wait()
        return carry

    lax.fori_loop(0, line.chunks // PIECES, gone, 0)
    mixed_leaves.wait()
    for one in exchanges:
        one.wait_send()
    for i, (src, got, result, owner) in enumerate(slabs):
        for j in range(blocks_n[i]):

            @pl.when(me != owner(j) * spread)
            def _(i=i, j=j):
                to_owner(i, j).wait_send()

            pltpu.make_async_copy(result.at[rows_of(j)], result.at[rows_of(j)], g_recv.at[i, j]).wait()

        @pl.when(owns[i])
        def _(i=i, owner=owner):
            def given(d, carry):
                from_owner(i, owner(own), lax.rem(me + d, seq_n)).wait_send()
                return carry

            lax.fori_loop(1, seq_n, given, 0)


def last(sizes, ins, far, hidden):
    seq_n, depth, rows_n, group, heads = sizes
    qkv_w = far[8]
    count, pairs, width = rows_n * group, rows_n * heads, qkv_w.shape[1]
    local, length = qkv_w.shape[2], seq_n * group
    blocks = {width: 8, local: 5, hidden: 4}
    slabs = [(n * RANK, w) for w, n in blocks.items()]
    some, every = pltpu.VMEM((pairs, group, HD), BF16), pltpu.VMEM((seq_n, group, HD), BF16)
    return pl.pallas_call(
        functools.partial(last_kernel, *sizes),
        out_shape=[shape(count, width)] * 2 + [shape(*s) for s in slabs],
        in_specs=[IN_VMEM] * len(ins) + [ANYWHERE] * len(far),
        out_specs=[ANYWHERE] * 2 + [IN_VMEM] * 3,
        scratch_shapes=[pltpu.VMEM((count, width), BF16), pltpu.VMEM((count, HD), F32), pltpu.VMEM((count, HD), F32)]
        + [pltpu.VMEM((count, width), BF16)] * 3
        + [pltpu.VMEM(a.shape, BF16) for a in far[:8]]
        + [
            pltpu.VMEM((HD, length), BF16), pltpu.VMEM((length, HD), F32), pltpu.VMEM((length, HD), F32),
            some, every, every,
            pltpu.VMEM(qkv_w.shape, BF16), some, every, every,
            pltpu.VMEM((3, count + RANK, local), BF16), pltpu.VMEM((count + 3 * RANK, 3 * RANK), BF16),
            pltpu.VMEM((count, width), BF16),
        ]
        + [pltpu.VMEM(s, BF16) for s in slabs]
        + [pltpu.VMEM((seq_n, RANK, s[1]), BF16) for s in slabs]
        + [
            pltpu.VMEM((RANK, width), BF16), pltpu.VMEM((depth, RANK, width), BF16), pltpu.VMEM((3, RANK, width), BF16),
            dma(pairs), dma(pairs), dma(seq_n), dma(seq_n), dma(seq_n), dma(seq_n), dma(11),
            dma(3, 8), dma(3, seq_n), dma(3, seq_n), dma(3, 8), dma(depth), dma(depth), dma(2, count // (2 * CHUNK)),
        ]
        + Line.scratch(count, width, CHUNK)
        + Line.scratch(count, width, CHUNK)[3:],
        compiler_params=params(62, 5),
    )(*ins, *far)


PARTS = 4


def leave_kernel(wide, local, hid, dx_far, mixed_far, *refs):
    outs, (dx_out, mixed_out, dx, dx_wide, mixed, sems) = refs[:14], refs[14:]
    rows = dx.shape[0] // PARTS
    parts = [slice(i * rows, (i + 1) * rows) for i in range(PARTS)]
    moves = [
        [pltpu.make_async_copy(src.at[p], dst.at[p], sems.at[k, i]) for i, p in enumerate(parts)]
        for k, (src, dst) in enumerate(
            ((dx_far, dx), (dx_wide, dx_out), (mixed_far, mixed), (mixed, mixed_out))
        )
    ]
    for k in (0, 2):
        for one in moves[k]:
            one.start()
    for i, p in enumerate(parts):
        moves[0][i].wait()
        dx_wide[p, :] = dx[p, :].astype(F32)
        moves[1][i].start()
    for i in range(PARTS):
        moves[2][i].wait()
        moves[3][i].start()
    places = (
        (wide, 112, 1), (wide, 0, 48), (local, 0, 48), (local, 48, 3), (local, 64, 16), (wide, 80, 16), (wide, 114, 1),
        (wide, 113, 1), (wide, 48, 32), (hid, 0, 32), (hid, 32, 2), (hid, 48, 16), (wide, 96, 16), (wide, 115, 1),
    )
    for out, (slab, first, n) in zip(outs, places):
        begin = first // RANK * RANK
        value = slab[begin : begin + -(-n // RANK) * RANK, :].astype(F32)
        out[...] = value[first - begin : first - begin + n].reshape(out.shape)
    for k in (1, 3):
        for one in moves[k]:
            one.wait()


def outputs(wide, local, hid, dx, mixed):
    w, n, f = wide.shape[1], local.shape[1], hid.shape[1]
    dims = (
        (1, w), (3, RANK, w), (3, RANK, n), (3, n), (RANK, n), (RANK, w), (1, w), (1, w), (2, RANK, w), (2, RANK, f),
        (2, f), (RANK, f), (RANK, w), (1, w),
    )
    return pl.pallas_call(
        leave_kernel,
        out_shape=[shape(*d, dtype=F32) for d in dims] + [shape(*dx.shape, dtype=F32), shape(*mixed.shape)],
        in_specs=[IN_VMEM] * 3 + [ANYWHERE] * 2,
        out_specs=[IN_VMEM] * len(dims) + [ANYWHERE] * 2,
        scratch_shapes=[
            pltpu.VMEM(dx.shape, BF16), pltpu.VMEM(dx.shape, F32), pltpu.VMEM(mixed.shape, BF16), dma(4, PARTS)
        ],
        compiler_params=params(62),
    )(wide, local, hid, dx, mixed)


def per_device(
    tokens, attn_gain, base_qkv, adapt_a_qkv, adapt_b_qkv, magnitude_qkv, base_out, adapt_a_out,
    adapt_b_out, magnitude_out, ffn_gain, base_gu, adapt_a_gu, adapt_b_gu, magnitude_gu, base_down,
    adapt_a_down, adapt_b_down, magnitude_down, doc_lengths, cotangent,
):
    rows_n, group, width = tokens.shape
    count = rows_n * group
    local = base_qkv.shape[2]
    heads = local // HD
    pairs = rows_n * heads
    seq_n, depth = lax.axis_size("seq"), lax.axis_size("heads")
    sizes = (seq_n, depth, rows_n, group, heads)
    length = group * seq_n
    me = lax.axis_index("seq")

    order = jnp.arange(doc_lengths.shape[1])
    doc_ends = jnp.sum(
        jnp.where(order[None, :, None] <= order[None, None, :], doc_lengths[:, :, None], 0), axis=1
    )
    doc_starts = doc_ends - doc_lengths

    def starts_of(places, ends, starts):
        inside = (places[..., None] >= starts) & (places[..., None] < ends)
        return jnp.sum(jnp.where(inside, starts, 0), axis=-1)

    mine = me * group + jnp.arange(group, dtype=jnp.int32)
    position = mine[None, :] - starts_of(
        jnp.broadcast_to(mine[None, :], (rows_n, group)), doc_ends[:, None], doc_starts[:, None]
    )
    frequency = ROPE_BASE ** (jnp.arange(HD // 2, dtype=F32) * (-2.0 / HD))
    angles = position.reshape(count, 1).astype(F32) * frequency
    cos, sin = jnp.cos(angles), jnp.sin(angles)

    x = tokens.reshape(count, width)
    dy = cotangent.reshape(count, width)
    gain1, gain2 = attn_gain[None, :], ffn_gain[None, :]
    m_out, m_down = magnitude_out[None, :], magnitude_down[None, :]
    at_qkv, at_gu = adapt_a_qkv.transpose(0, 2, 1), adapt_a_gu.transpose(0, 2, 1)
    at_out, at_down = adapt_a_out.T, adapt_a_down.T

    h1, pre, q, k, v, inverse_one, low, norm_qkv, v_qkv, norms, v_out, v_down, norm_gu, v_gu = front(
        sizes, x, gain1, cos, sin, (base_qkv, at_qkv, adapt_b_qkv, magnitude_qkv), (base_out, at_out, adapt_b_out),
        (base_down, at_down, adapt_b_down), (base_gu, at_gu, adapt_b_gu),
    )
    q, k, v = q.reshape(-1, HD), k.reshape(length, HD), v.reshape(length, HD)
    o, lse, start, place = attend(sizes, doc_lengths, q, k, v)
    dx2, x2, down_part, do, gm_down, ga_gu, gb_gu, gm_gu, g_gain2, ga_down, gb_down, ga_out, gb_out, gm_out = core(
        sizes, o.reshape(-1, group, HD), x, dy, gain2, norms, (base_out, at_out, adapt_b_out, m_out, v_out),
        (base_down, at_down, adapt_b_down, m_down, v_down), (base_gu, at_gu, adapt_b_gu, magnitude_gu, norm_gu, v_gu),
    )
    dx, mixed, wide, narrow, hid = last(
        sizes,
        (
            lse, start, place, cos, sin, low, gain1, at_qkv, adapt_b_qkv, magnitude_qkv, norm_qkv, v_qkv, ga_gu, gb_out,
            gb_down, g_gain2, gm_out, gm_down, ga_out, gb_gu, gm_gu, ga_down, inverse_one, norms, m_down,
        ),
        (down_part, q, k, v, o, do.reshape(-1, HD), h1, pre, base_qkv, x2, dx2),
        base_down.shape[0],
    )
    *g, dx, mixed = outputs(wide, narrow, hid, dx, mixed)
    return (
        mixed.reshape(rows_n, group, width),
        dx.reshape(rows_n, group, width),
        g[0][0], g[1].transpose(0, 2, 1), g[2], g[3], g[4].T, g[5], g[6][0], g[7][0], g[8].transpose(0, 2, 1), g[9],
        g[10], g[11].T, g[12], g[13][0],
    )


def solution(mesh):
    in_specs = (
        P(None, "seq", None), P(), P(None, None, "heads"), P(), P(None, None, "heads"), P(None, "heads"),
        P("heads", None), P("heads", None), P(), P(), P(), P(None, None, "heads"), P(),
        P(None, None, "heads"), P(None, "heads"), P("heads", None), P("heads", None), P(), P(), P(),
        P(None, "seq", None),
    )
    out_specs = (
        P(None, "seq", None), P(None, "seq", None), P(), P(), P(None, None, "heads"), P(None, "heads"),
        P("heads", None), P(), P(), P(), P(), P(None, None, "heads"), P(None, "heads"),
        P("heads", None), P(), P(),
    )
    return jax.shard_map(
        per_device, mesh=mesh, in_specs=in_specs, out_specs=out_specs, check_vma=False
    )
```

```python
import functools

import jax
import jax.numpy as jnp
from jax import lax
from jax.experimental import pallas as pl
from jax.experimental.pallas import tpu as pltpu
from jax.sharding import PartitionSpec as P

HD = 128
RANK = 16
ADAPT_SCALE = 2.0
NORM_EPS = 1e-05
COLUMN_EPS = 1e-06
ROPE_BASE = 10000.0
NEG_LARGE = -1e30
LOG2E = 1.4426950408889634
F32 = jnp.float32
BF16 = jnp.bfloat16
MESH = pl.DeviceIdType.MESH
NN = (((1,), (0,)), ((), ()))
NT = (((1,), (1,)), ((), ()))
TN = (((0,), (0,)), ((), ()))
OWNERS = 8
CHUNK = 16
PIECES = 1
LAG = 2
LEAD = 4
NEAR_LATE = 1
IN_A, IN_B = 4, 5
LAST_LEAD = 4
FIRST, SECOND = 7, 13
GATHER, GIVE = 10, 14
WIDE = 512
IN_VMEM = pl.BlockSpec(memory_space=pltpu.VMEM)
IN_SMEM = pl.BlockSpec(memory_space=pltpu.SMEM)
ANYWHERE = pl.BlockSpec(memory_space=pl.ANY)


def dot(a, b, dims=NN):
    return lax.dot_general(a.astype(BF16), b.astype(BF16), dims, preferred_element_type=F32)


def shape(*dims, dtype=BF16):
    return jax.ShapeDtypeStruct(dims, dtype)


def dma(*dims):
    return pltpu.SemaphoreType.DMA(dims)


def params(mib, collective_id=None):
    more = {} if collective_id is None else {"collective_id": collective_id, "has_side_effects": True}
    return pltpu.CompilerParams(vmem_limit_bytes=mib * 2**20, **more)


def tiles(count, size, body, tick=lambda t: None):
    whole = count // size
    if whole:

        def step(t, carry):
            body(pl.ds(pl.multiple_of(t * size, 128), size), t)
            tick(t)
            return carry

        lax.fori_loop(0, whole, step, 0)
    if count - whole * size:
        body(pl.ds(whole * size, count - whole * size), whole)
        tick(whole)


def row_loop(count, size, body, init=0):
    def step(t, carry):
        return body(pl.ds(pl.multiple_of(t * size, size), size), carry)

    return lax.fori_loop(0, count // size, step, init)


def fold(v):
    return jnp.sum(v.reshape(v.shape[0] // 8, 8, v.shape[1]), axis=0)


def total(v):
    return jnp.sum(v, axis=0, keepdims=True)


def greet(seq, heads):
    barrier = pltpu.get_barrier_semaphore()
    me, h = lax.axis_index("seq"), lax.axis_index("heads")
    peers = 0
    for d in range(1, seq):
        pl.semaphore_signal(barrier, inc=1, device_id={"seq": lax.rem(me + d, seq)}, device_id_type=MESH)
        peers = peers + 1
    for d in range(1, heads):
        pl.semaphore_signal(
            barrier, inc=1, device_id={"heads": lax.rem(h + d, heads)}, device_id_type=MESH
        )
        peers = peers + 1
    return lambda: pl.semaphore_wait(barrier, peers)


def remote(src, dst, send_sem, recv_sem, **where):
    return pltpu.make_async_remote_copy(
        src_ref=src, dst_ref=dst, send_sem=send_sem, recv_sem=recv_sem, device_id=where, device_id_type=MESH
    )


class Exchange:
    def __init__(self, kind, seq_n, pairs, src, dst, send_sem, recv_sem):
        fan = seq_n // pairs
        me = lax.axis_index("seq")
        self.me, self.src, self.dst, self.send_sem, self.recv_sem = me, src, dst, send_sem, recv_sem
        self.count = self.slots(kind, seq_n, pairs)
        self.target, self.block, self.slot = {
            "queries": (lambda p: p * fan + lax.rem(me, fan), lambda p: p, me // fan),
            "keys": (lambda e: e, lambda e: e // fan, me),
            "queries_back": (lambda i: lax.rem(me, fan) + fan * i, lambda i: i, me // fan),
            "keys_back": (lambda e: e, lambda e: e, me),
        }[kind]

    @staticmethod
    def slots(kind, seq_n, pairs):
        return pairs if kind.startswith("queries") else seq_n

    def copy(self, j):
        return remote(
            self.src(self.block(j)),
            self.dst(self.slot),
            self.send_sem.at[j],
            self.recv_sem.at[self.slot],
            seq=self.target(j),
        )

    def start(self, low=0, high=None):
        number = (self.count if high is None else high) - low

        def one(d, carry):
            j = low + lax.rem(self.me + d, number)

            @pl.when(self.target(j) != self.me)
            def _():
                self.copy(j).start()

            @pl.when(self.target(j) == self.me)
            def _():
                pltpu.make_async_copy(
                    self.src(self.block(j)), self.dst(self.slot), self.recv_sem.at[self.slot]
                ).start()

            return carry

        lax.fori_loop(0, number, one, 0)

    def wait_recv(self):
        def one(j, carry):
            pltpu.make_async_copy(self.dst(j), self.dst(j), self.recv_sem.at[j]).wait()
            return carry

        lax.fori_loop(0, self.count, one, 0)

    def wait_send(self):
        def one(j, carry):
            @pl.when(self.target(j) != self.me)
            def _():
                self.copy(j).wait_send()

            return carry

        lax.fori_loop(0, self.count, one, 0)


class Line:
    def __init__(self, x, out, got, near, held, *sems, per=None, base=0, lead=None):
        self.x, self.out, self.got, self.near, self.held = x, out, got, near, held
        self.far_send, self.far_recv, self.near_send, self.near_recv, self.down_send, self.down_recv = sems
        self.chunks, self.rows = got.shape[1], got.shape[2]
        self.per, self.base = per or self.chunks, base
        self.lead = self.chunks if lead is None else lead
        self.steps = self.done(self.chunks)
        self.h = lax.axis_index("heads")

    @staticmethod
    def done(chunks):
        return chunks + 3 * LAG

    @staticmethod
    def scratch(count, width, rows):
        chunks = count // (2 * rows) * PIECES
        one = pltpu.VMEM((chunks, rows, width // PIECES), BF16)
        return [
            pltpu.VMEM((2, chunks, rows, width // PIECES), BF16), one, one,
            dma(2, chunks), dma(2, chunks), dma(chunks), dma(chunks), dma(2, 2, chunks), dma(2, chunks),
        ]

    def ends(self, stream):
        if stream == 0:
            return self.h, self.h + 1, self.h - 1
        return 3 - self.h, self.h - 1, self.h + 1

    def place(self, stream, c):
        rows, per, width = self.rows, self.per // PIECES, self.got.shape[3]
        r, piece = c // PIECES, lax.rem(c, PIECES)
        first = self.base + ((r // per) * 2 + (1 - stream)) * (per * rows) + lax.rem(r, per) * rows
        return pl.ds(pl.multiple_of(first, rows), rows), pl.ds(pl.multiple_of(piece * width, width), width)

    def far(self, stream, c, src, to):
        return remote(
            src, self.got.at[stream, c], self.far_send.at[stream, c], self.far_recv.at[stream, c], heads=to
        )

    def close(self, stream, c, to):
        return remote(
            self.x.at[*self.place(stream, c)], self.near.at[c], self.near_send.at[c], self.near_recv.at[c], heads=to
        )

    def down(self, stream, way, c, to):
        part = self.out.at[*self.place(stream, c)]
        return remote(part, part, self.down_send.at[stream, way, c], self.down_recv.at[stream, c], heads=to)

    def give(self, c):
        for stream in range(2):
            pos, ahead, behind = self.ends(stream)

            @pl.when((pos == 0) & (c < self.chunks))
            def _():
                self.far(stream, c, self.x.at[*self.place(stream, c)], ahead).start()

        c = c - NEAR_LATE
        for stream in range(2):
            pos, ahead, behind = self.ends(stream)

            @pl.when((pos == 3) & (c >= 0) & (c < self.chunks))
            def _():
                self.close(stream, c, behind).start()

    def first(self):
        def one(c, carry):
            self.give(c)
            return carry

        lax.fori_loop(0, self.lead, one, 0)

    def step(self, t):
        self.give(t + self.lead)
        for stream in range(2):
            pos, ahead, behind = self.ends(stream)

            @pl.when((pos == 1) & (t < self.chunks))
            def _():
                self.far(stream, t, self.held.at[t], self.h).wait_recv()
                at = self.place(stream, t)
                self.held[t] = (self.got[stream, t].astype(F32) + self.x[*at].astype(F32)).astype(BF16)
                self.far(stream, t, self.held.at[t], ahead).start()

        for stream in range(2):
            pos, ahead, behind = self.ends(stream)
            c = t - LAG

            @pl.when((pos == 2) & (c >= 0) & (c < self.chunks))
            def _():
                self.far(stream, c, self.held.at[c], self.h).wait_recv()
                self.close(stream, c, self.h).wait_recv()
                at = self.place(stream, c)
                value = self.got[stream, c].astype(F32) + self.near[c].astype(F32) + self.x[*at].astype(F32)
                self.out[*at] = value.astype(BF16)
                self.down(stream, 0, c, behind).start()
                self.down(stream, 1, c, ahead).start()

        for stream in range(2):
            pos, ahead, behind = self.ends(stream)
            b = t - jnp.where(pos == 0, 3 * LAG, 2 * LAG)

            @pl.when((pos != 2) & (b >= 0) & (b < self.chunks))
            def _():
                self.down(stream, 0, b, self.h).wait_recv()

                @pl.when(pos == 1)
                def _():
                    self.down(stream, 0, b, behind).start()

    def run(self, start, stop):
        def one(t, carry):
            self.step(t)
            return carry

        lax.fori_loop(start, stop, one, 0)

    def spread(self, start, stop, ticks):
        def tick(k):
            now, then = (k * (stop - start)) // ticks, ((k + 1) * (stop - start)) // ticks
            self.run(start + now, start + then)

        return tick

    def drain(self):
        def one(c, carry):
            for stream in range(2):
                pos, ahead, behind = self.ends(stream)

                @pl.when(pos <= 1)
                def _():
                    self.far(stream, c, self.held.at[c], self.h).wait_send()

                @pl.when(pos == 3)
                def _():
                    self.close(stream, c, self.h).wait_send()

                @pl.when((pos == 1) | (pos == 2))
                def _():
                    self.down(stream, 0, c, self.h).wait_send()

                @pl.when(pos == 2)
                def _():
                    self.down(stream, 1, c, self.h).wait_send()

            return carry

        lax.fori_loop(0, self.chunks, one, 0)


class Across:
    def __init__(self, depth, part, others, send_sem, recv_sem):
        self.depth, self.part, self.others, self.sems = depth, part, others, (send_sem, recv_sem)
        self.h = lax.axis_index("heads")

    def copy(self, d):
        to = lax.rem(self.h + d, self.depth)
        return remote(
            self.part, self.others.at[self.h], self.sems[0].at[d], self.sems[1].at[self.h], heads=to
        )

    def start(self):
        for d in range(1, self.depth):
            self.copy(d).start()

    def finish(self):
        value = self.part[...].astype(F32)
        for d in range(1, self.depth):
            came = self.others.at[lax.rem(self.h + d, self.depth)]
            pltpu.make_async_copy(came, came, self.sems[1].at[lax.rem(self.h + d, self.depth)]).wait()
            value = value + came[...].astype(F32)
        for d in range(1, self.depth):
            self.copy(d).wait_send()
        return value


def column_stats(w, at, b, aw):
    ab = dot(dot(at, at, NT), b)
    bf = b.astype(F32)

    acc = jnp.zeros((8, w.shape[1]), F32)
    for first in range(0, w.shape[0], 64):
        v = w[first : first + 64, :].astype(F32)
        acc = acc + fold(v * v)
    squares = total(acc) + 2.0 * ADAPT_SCALE * total(bf * aw) + ADAPT_SCALE**2 * total(bf * ab)
    return squares, aw + ADAPT_SCALE * ab


def widen_tables(cos_half, sin_half, cos, sin):
    cos[...] = jnp.concatenate([cos_half[...], cos_half[...]], axis=1)
    sin[...] = jnp.concatenate([-sin_half[...], sin_half[...]], axis=1)


def front_kernel(
    seq_n, depth, rows_n, group, heads,
    x, gain, cos_half, sin_half, at_qkv, b_qkv, m_qkv, at_out, b_out, at_down, b_down,
    w_qkv, w_out, w_down,
    h1_far, pre_far, q, k, v, inverse_one, low, norm_qkv, v_qkv, norms, v_out, v_down,
    cos, sin, h1, pre, wq, wo, wd, turned, part, others, q_send, q_recv, k_send, k_recv, v_send, v_recv, z_send, z_recv, load, leave,
):
    count, pairs = rows_n * group, rows_n * heads
    leaving = [pltpu.make_async_copy(pre.at[i], pre_far.at[i], leave.at[i]) for i in range(3)]
    leaving.append(pltpu.make_async_copy(h1, h1_far, leave.at[3]))
    loads = [pltpu.make_async_copy(w_qkv.at[i], wq.at[i], load.at[i]) for i in range(3)]
    loads += [
        pltpu.make_async_copy(w_out, wo, load.at[3]),
        pltpu.make_async_copy(w_down, wd, load.at[4]),
    ]
    for one in loads[:3]:
        one.start()
    all_here = greet(seq=seq_n, heads=depth)
    widen_tables(cos_half, sin_half, cos, sin)

    def norm(rows, carry):
        v = x[rows, :].astype(F32)
        inverse = lax.rsqrt(jnp.mean(v * v, axis=-1, keepdims=True) + NORM_EPS)
        h1[rows, :] = (v * inverse * gain[...]).astype(BF16)
        inverse_one[rows, :] = jnp.broadcast_to(inverse, (rows.size, HD))
        return carry

    row_loop(count, 32, norm)
    for i in range(3):
        h1[count + i * RANK : count + (i + 1) * RANK, :] = at_qkv[i]
    leaving[3].start()
    low[...] = dot(h1[:count, :], h1[count:, :], NT).astype(BF16)
    exchanges = [
        Exchange(kind, seq_n, pairs, lambda j, i=i: turned.at[i, j], lambda j, to=to: to.at[j], *sems)
        for i, (kind, to, sems) in enumerate(
            (("queries", q, (q_send, q_recv)), ("keys", k, (k_send, k_recv)), ("keys", v, (v_send, v_recv)))
        )
    ]
    for i in range(3):
        loads[i].wait()
        if i < 2:
            loads[3 + i].start()

        def project(over, t, i=i):
            width = over.size
            r = dot(h1[...], wq[i, :, over])
            b = b_qkv[i, :, over]
            value = r[:count] + ADAPT_SCALE * dot(low[:, i * RANK : (i + 1) * RANK], b)
            aw = r[count + i * RANK : count + (i + 1) * RANK]
            squares, av = column_stats(wq.at[i, :, over], at_qkv[i], b, aw)
            n = jnp.sqrt(squares + COLUMN_EPS)
            norm_qkv[i : i + 1, over] = n
            v_qkv[i, :, over] = av
            pre[i, :, over] = value.astype(BF16)
            scaled = value * (m_qkv[i : i + 1, over] / n)
            for row in range(rows_n):
                rows = slice(row * group, (row + 1) * group)
                for hh in range(width // HD):
                    part_ = scaled[rows, hh * HD : (hh + 1) * HD]
                    if i < 2:
                        part_ = part_ * cos[rows, :] + pltpu.roll(part_, HD // 2, 1) * sin[rows, :]
                    turned[i, row * heads + t * (width // HD) + hh] = part_.astype(BF16)

        tiles(heads * HD, WIDE, project)
        if i == 0:
            all_here()
        exchanges[i].start()
        leaving[i].start()

    part[...] = jnp.zeros_like(part)
    for row, (w, at, b, av, loaded) in enumerate(
        ((wo, at_out, b_out, v_out, loads[3]), (wd, at_down, b_down, v_down, loads[4]))
    ):
        loaded.wait()

        def stats(over, t, row=row, w=w, at=at, b=b, av=av):
            squares, value = column_stats(w.at[:, over], at[...], b[:, over], dot(at[...], w[:, over]))
            part[row : row + 1, over] = squares
            av[:, over] = value

        tiles(w.shape[1], WIDE, stats)
    across = Across(depth, part, others, z_send, z_recv)
    across.start()
    norms[...] = jnp.sqrt(across.finish() + COLUMN_EPS)
    for one in exchanges:
        one.wait_recv()
    for one in exchanges:
        one.wait_send()
    for one in leaving:
        one.wait()


def front(sizes, x, gain, cos, sin, qkv, out, down):
    seq_n, depth, rows_n, group, heads = sizes
    count, pairs, width = rows_n * group, rows_n * heads, x.shape[1]
    local = qkv[0].shape[2]
    return pl.pallas_call(
        functools.partial(front_kernel, *sizes),
        out_shape=[
            shape(count + 3 * RANK, width), shape(3, count, local),
            shape(pairs, group, HD), shape(seq_n, group, HD), shape(seq_n, group, HD),
            shape(count, HD, dtype=F32), shape(count, 3 * RANK),
            shape(3, local, dtype=F32), shape(3, RANK, local, dtype=F32), shape(8, width, dtype=F32),
            shape(RANK, width, dtype=F32), shape(RANK, width, dtype=F32),
        ],
        in_specs=[IN_VMEM] * 11 + [ANYWHERE] * 3,
        out_specs=[ANYWHERE] * 2 + [IN_VMEM] * 10,
        scratch_shapes=[
            pltpu.VMEM((count, HD), F32), pltpu.VMEM((count, HD), F32),
            pltpu.VMEM((count + 3 * RANK, width), BF16), pltpu.VMEM((3, count, local), BF16),
            pltpu.VMEM(qkv[0].shape, BF16), pltpu.VMEM(out[0].shape, BF16), pltpu.VMEM(down[0].shape, BF16),
            pltpu.VMEM((3, pairs, group, HD), BF16),
            pltpu.VMEM((8, width), F32), pltpu.VMEM((depth, 8, width), F32),
            dma(pairs), dma(pairs), dma(seq_n), dma(seq_n), dma(seq_n), dma(seq_n), dma(depth), dma(depth), dma(6), dma(4),
        ],
        compiler_params=params(60, 1),
    )(
        x, gain, cos, sin, qkv[1], qkv[2], qkv[3], out[1], out[2], down[1], down[2], qkv[0], out[0], down[0],
    )


def attend_kernel(block, fan, heads, group, docs, q_ref, k_ref, v_ref, o_ref, lse_ref, start_ref, place_ref, vt):
    scale = HD**-0.5 * LOG2E
    vt[...] = v_ref[...].T
    me = lax.axis_index("seq")
    mine, row, split = lax.rem(me, fan), me // fan // heads, block // group
    lengths = [docs[row, d] for d in range(docs.shape[1])]

    def starts_of(places):
        end, begin = 0, 0
        for n in lengths:
            end = end + n
            begin = begin + jnp.where(places >= end, n, 0)
        return begin

    for b in range(q_ref.shape[0] // group):
        over = slice(b * group, (b + 1) * group)
        places = (mine + fan * b) * group + lax.broadcasted_iota(jnp.int32, (1, group), 1)
        place_ref[:, over] = places
        start_ref[:, over] = starts_of(places)

    def per_query(i, carry):
        at = pl.ds(pl.multiple_of(i * block, block), block)
        q = q_ref[at, :]
        start, place = start_ref[:, at], place_ref[:, at]

        def per_key(j, state):
            top, count, acc = state
            over = pl.ds(pl.multiple_of(j * block, block), block)
            s = dot(k_ref[over, :], q, NT) * scale
            key = j * block + lax.broadcasted_iota(jnp.int32, (block, block), 0)
            s = jnp.where((key >= start) & (key <= place), s, NEG_LARGE)
            new_top = jnp.maximum(top, jnp.max(s, axis=0, keepdims=True))
            p = jnp.exp2(s - new_top)
            fade = jnp.exp2(top - new_top)
            count = count * fade + total(p)
            acc = acc * fade + dot(vt[:, over], p)
            return new_top, count, acc

        low = starts_of((mine + fan * (i * split)) * group) // block
        high = ((mine + fan * ((i + 1) * split - 1) + 1) * group - 1) // block + 1
        begin = (
            jnp.full((1, block), -1e29, F32),
            jnp.zeros((1, block), F32),
            jnp.zeros((HD, block), F32),
        )
        top, count, acc = lax.fori_loop(low, high, per_key, begin)
        o_ref[at, :] = (acc / count).T.astype(BF16)
        lse_ref[:, at] = top + jnp.log2(count)
        return carry

    lax.fori_loop(0, q_ref.shape[0] // block, per_query, 0)


def attend(sizes, docs, q, k, v):
    seq_n, depth, rows_n, group, heads = sizes
    count, fan = q.shape[0], seq_n // (rows_n * heads)
    return pl.pallas_call(
        functools.partial(attend_kernel, 2 * group, fan, heads, group),
        out_shape=[
            shape(*q.shape), shape(1, count, dtype=F32), shape(1, count, dtype=jnp.int32),
            shape(1, count, dtype=jnp.int32),
        ],
        in_specs=[IN_SMEM] + [IN_VMEM] * 3,
        out_specs=[IN_VMEM] * 4,
        scratch_shapes=[pltpu.VMEM((HD, k.shape[0]), BF16)],
        compiler_params=params(62),
    )(docs, q, k, v)


def attend_back(block, fan, q_ref, k_ref, v_ref, o_ref, do_ref, lse_ref, start_ref, place_ref, dq, dk, dv, kt, dk_acc, dv_acc, spread):
    scale = HD**-0.5
    mine = lax.rem(lax.axis_index("seq"), fan)
    group = dq.shape[1]
    split = block // group
    blocks = q_ref.shape[0] // block

    def reach(i):
        return ((mine + fan * ((i + 1) * split - 1) + 1) * group - 1) // block + 1

    tick = spread(sum(reach(i) for i in range(blocks)))
    kt[...] = k_ref[...].T
    dk_acc[...] = jnp.zeros_like(dk_acc)
    dv_acc[...] = jnp.zeros_like(dv_acc)

    def per_query(i, before):
        at = pl.ds(pl.multiple_of(i * block, block), block)
        q, do = q_ref[at, :], do_ref[at, :]
        start, place, lse = start_ref[:, at], place_ref[:, at], lse_ref[:, at]
        delta = total((do.astype(F32) * o_ref[at, :].astype(F32)).T)

        def per_key(j, acc):
            over = pl.ds(pl.multiple_of(j * block, block), block)
            k = k_ref[over, :]
            s = dot(k, q, NT) * (scale * LOG2E)
            key = j * block + lax.broadcasted_iota(jnp.int32, (block, block), 0)
            p = jnp.exp2(jnp.where((key >= start) & (key <= place), s - lse, NEG_LARGE))
            dp = dot(v_ref[over, :], do, NT)
            ds = (p * (dp - delta)).astype(BF16)
            dv_acc[over, :] += dot(p, do)
            dk_acc[over, :] += dot(ds, q)
            tick(before + j)
            return acc + dot(kt[:, over], ds)

        acc = lax.fori_loop(0, reach(i), per_key, jnp.zeros((HD, block), F32))
        acc = (acc * scale).T.astype(BF16)
        for n in range(split):
            dq[i * split + n] = acc[n * group : (n + 1) * group]
        return before + reach(i)

    lax.fori_loop(0, blocks, per_query, 0)

    def store(j, carry):
        over = pl.ds(pl.multiple_of(j * group, group), group)
        dk[j] = (dk_acc[over, :] * scale).astype(BF16)
        dv[j] = dv_acc[over, :].astype(BF16)
        return carry

    lax.fori_loop(0, k_ref.shape[0] // group, store, 0)


def core_kernel(
    seq_n, depth, rows_n, group, heads,
    o, gain, m_out, norms, at_out, b_out, v_out, at_gu, b_gu, m_gu, at_down, b_down, m_down, v_down,
    x_far, cotangent_far, w_out, w_gu, w_down,
    dx2_far, x2_far, down_far, do, gm_down, ga_gu, gb_gu, gm_gu, g_gain, ga_down, gb_down, ga_out, gb_out, gm_out,
    dx2, x2_out, down_part, out_pre, x, cotangent, wo, wg, wd, attn, low_out, part, part2, dh2, h2, z, dz, dp, dpd, tmp, low, mix, norm_gu, v_gu, dpo, blocks,
    s_part, others, row_sums, load, send, recv, back_send, back_recv, z_send, z_recv, away, *line_refs,
):
    count, pairs = rows_n * group, rows_n * heads
    half = count // 2
    hidden, width = wd.shape
    loads = [
        pltpu.make_async_copy(far, near, load.at[i])
        for i, (far, near) in enumerate(
            ((w_out, wo), (x_far, x), (w_gu.at[0], wg.at[0]), (w_gu.at[1], wg.at[1]), (cotangent_far, cotangent), (w_down, wd))
        )
    ]
    for one in loads:
        one.start()
    greet(seq=seq_n, heads=depth)()

    def landing(pair):
        row, head = pair // heads, lax.rem(pair, heads)
        return attn.at[
            pl.ds(pl.multiple_of(row * group, group), group), pl.ds(pl.multiple_of(head * HD, HD), HD)
        ]

    def leaving(i, r):
        near, far = ((dx2, dx2_far), (x2_out, x2_far), (down_part, down_far))[i]
        return pltpu.make_async_copy(
            near.at[r * half : (r + 1) * half], far.at[r * half : (r + 1) * half], away.at[i, r]
        )

    come = Exchange("queries_back", seq_n, pairs, lambda i: o.at[i], landing, send, recv)
    leave = Exchange("queries", seq_n, pairs, lambda p: blocks.at[p], lambda s_: do.at[s_], back_send, back_recv)
    come.start()
    for ref in (s_part, ga_gu, gb_gu, gm_gu, g_gain, ga_down, gb_down, ga_out, gb_out, gm_out):
        ref[...] = jnp.zeros_like(ref)
    one_out = Line(part, out_pre, *line_refs[:9], per=half // (2 * CHUNK) * PIECES, lead=LEAD)
    two = [
        Line(part2, dh2, *line_refs[9 + 9 * r : 18 + 9 * r], base=r * half, lead=LEAD) for r in range(2)
    ]
    loads[0].wait()
    come.wait_recv()
    low_out[...] = dot(attn[...], at_out[...], NT).astype(BF16)

    def project(over, t):
        part[:, over] = (dot(attn[...], wo[:, over]) + ADAPT_SCALE * dot(low_out[...], b_out[:, over])).astype(BF16)

    tiles(width, WIDE, project)
    one_out.first()
    for one in loads[1:]:
        one.wait()
    n_out, n_down = 1.0 / norms[0:1, :], 1.0 / norms[1:2, :]
    c_out, c_down = m_out[...] * n_out, m_down[...] * n_down

    n_hidden, n_width = -(-hidden // WIDE), -(-width // WIDE)
    half_done = one_out.done(one_out.per)
    tick_first = one_out.spread(0, half_done, count // 64 + 3 * n_hidden)

    def scaled_gradient(rows, carry):
        dpd[rows, :] = (cotangent[rows, :].astype(F32) * c_down).astype(BF16)
        tick_first(rows.start // rows.size)
        return carry

    row_loop(count, 64, scaled_gradient)
    dlow_down = (ADAPT_SCALE * dot(dpd[...], b_down[...], NT)).astype(BF16)

    def hidden_gradient(over, t):
        dz[:, over] = (dot(dpd[...], wd[over, :], NT) + dot(dlow_down, at_down[:, over])).astype(BF16)

    tiles(hidden, WIDE, hidden_gradient, lambda t: tick_first(count // 64 + t))
    for i in range(2):

        def stats_gu(over, t, i=i):
            b = b_gu[i, :, over]
            squares, value = column_stats(wg.at[i, :, over], at_gu[i], b, dot(at_gu[i], wg[i, :, over]))
            norm_gu[i : i + 1, over] = jnp.sqrt(squares + COLUMN_EPS)
            v_gu[i, :, over] = value

        tiles(hidden, WIDE, stats_gu, lambda t, i=i: tick_first(count // 64 + (1 + i) * n_hidden + t))

    def feed_forward(r, tick):
        mine = slice(r * half, (r + 1) * half)
        base = r * half

        def there(rows):
            return pl.ds(pl.multiple_of(base + rows.start, rows.size), rows.size)

        def norm(rows, carry):
            x2 = x[there(rows), :].astype(F32) + out_pre[there(rows), :].astype(F32) * c_out
            inverse = lax.rsqrt(jnp.mean(x2 * x2, axis=-1, keepdims=True) + NORM_EPS)
            h2[rows, :] = (x2 * inverse * gain[...]).astype(BF16)
            tick(rows.start // rows.size)
            return carry

        row_loop(half, 32, norm)
        low[...] = dot(h2[...], at_gu[...].reshape(2 * RANK, width), NT).astype(BF16)

        def there_and_back(over, t):
            n = over.size
            for i in range(2):
                tmp[i, :, :n] = dot(h2[...], wg[i, :, over]) + ADAPT_SCALE * dot(
                    low[:, i * RANK : (i + 1) * RANK], b_gu[i, :, over]
                )
            scale = [m_gu[i : i + 1, over] / norm_gu[i : i + 1, over] for i in range(2)]

            def gated(rows, sums):
                pg, pu = tmp[0, rows, :n], tmp[1, rows, :n]
                g, u = pg * scale[0], pu * scale[1]
                sigma = jax.nn.sigmoid(g)
                silu = g * sigma
                z[there(rows), over] = (silu * u).astype(BF16)
                d = dz[there(rows), over].astype(F32)
                e_g = d * u * (sigma + silu * (1.0 - sigma))
                e_u = d * silu
                dp[0, rows, over] = (e_g * scale[0]).astype(BF16)
                dp[1, rows, over] = (e_u * scale[1]).astype(BF16)
                return sums[0] + fold(e_g * pg), sums[1] + fold(e_u * pu)

            zero = jnp.zeros((8, n), F32)
            sums = row_loop(half, 32, gated, (zero, zero))
            for i in range(2):
                s, inverse = total(sums[i]), 1.0 / norm_gu[i : i + 1, over]
                gm_gu[i : i + 1, over] += s * inverse
                turn = m_gu[i : i + 1, over] * s * inverse * inverse * inverse
                dp[i, half : half + RANK, over] = (b_gu[i, :, over].astype(F32) * turn).astype(BF16)
                gb_gu[i, :, over] += ADAPT_SCALE * (
                    dot(low[:, i * RANK : (i + 1) * RANK], dp[i, :half, over], TN) - v_gu[i, :, over] * turn
                )

        tiles(hidden, WIDE, there_and_back, lambda t: tick(half // 32 + t))
        for i in range(2):
            both = ADAPT_SCALE * dot(dp[i], b_gu[i], NT)
            mix[:half, i * RANK : (i + 1) * RANK] = both[:half].astype(BF16)
            for k in range(2):
                mix[half + k * RANK : half + (k + 1) * RANK, i * RANK : (i + 1) * RANK] = (
                    both[half:] if i == k else jnp.zeros((RANK, RANK), F32)
                ).astype(BF16)

        def inputs(over, t):
            products = [dot(dp[i], wg[i, over, :], NT) for i in range(2)]
            through = dot(mix[...], at_gu[:, :, over].reshape(2 * RANK, over.size))
            value = products[0][:half] + products[1][:half] + through[:half]
            straight = dot(mix[:half, :], h2[:, over], TN)
            for i in range(2):
                v_tb = products[i][half:] + through[half + i * RANK : half + (i + 1) * RANK]
                ga_gu[i, :, over] += straight[i * RANK : (i + 1) * RANK] - ADAPT_SCALE * v_tb
            part2[mine, over] = value.astype(BF16)
            g_gain[:, over] += total(value * h2[:, over].astype(F32)) / gain[:, over]

        tiles(width, WIDE, inputs, lambda t: tick(half // 32 + n_hidden + t))

    def norm_back(r, first):
        rows = pl.ds(pl.multiple_of(first, 16), 16)
        there = pl.ds(pl.multiple_of(r * half + first, 16), 16)
        value = out_pre[there, :].astype(F32)
        x2 = x[there, :].astype(F32) + value * c_out
        inverse = lax.rsqrt(jnp.mean(x2 * x2, axis=-1, keepdims=True) + NORM_EPS)
        scaled = dh2[there, :].astype(F32) * gain[...]
        mean = jnp.mean(scaled * x2, axis=-1, keepdims=True)
        e = cotangent[there, :].astype(F32) + inverse * scaled - x2 * (inverse**3 * mean)
        dx2[there, :] = e.astype(BF16)
        x2_out[there, :] = x2.astype(BF16)
        dpo[rows, :] = (e * c_out).astype(BF16)
        row_sums[...] += fold(e * value)

    def out_back(r):
        mine = slice(r * half, (r + 1) * half)
        rows_here = rows_n // 2

        s = total(row_sums[...])
        turn = m_out[...] * s * n_out * n_out * n_out
        gm_out[...] += s * n_out
        dpo[half : half + RANK, :] = (b_out[...].astype(F32) * turn).astype(BF16)
        both = dot(dpo[...], b_out[...], NT)
        dlow, turned = (ADAPT_SCALE * both[:half]).astype(BF16), both[half:]

        def inputs(over, t):
            product = dot(dpo[...], wo[over, :], NT)
            value = (product[:half] + dot(dlow, at_out[:, over])).astype(BF16)
            for row in range(rows_here):
                for hh in range(over.size // HD):
                    blocks[(r * rows_here + row) * heads + t * (over.size // HD) + hh] = value[
                        row * group : (row + 1) * group, hh * HD : (hh + 1) * HD
                    ]
            ga_out[:, over] += dot(dlow, attn[mine, over], TN) - ADAPT_SCALE * (
                product[half:] + ADAPT_SCALE * dot(turned, at_out[:, over])
            )

        tiles(heads * HD, WIDE, inputs)
        leave.start(r * rows_here * heads, (r + 1) * rows_here * heads)
        leaving(0, r).start()
        leaving(1, r).start()
        gb_out[...] += ADAPT_SCALE * (dot(low_out[mine, :], dpo[:half, :], TN) - v_out[...] * turn)

    ticks = half // 32 + n_hidden + n_width
    feed_forward(0, one_out.spread(half_done, half_done + IN_A, ticks))
    two[0].first()
    left = one_out.steps - half_done - IN_A

    def between(k, carry):
        one_out.step(half_done + IN_A + k)
        two[0].step(k)
        return carry

    lax.fori_loop(0, left, between, 0)
    feed_forward(1, two[0].spread(left, left + IN_B, ticks))
    two[1].first()
    rest = two[0].steps - left - IN_B

    def together(k, carry):
        two[0].step(left + IN_B + k)
        two[1].step(k)
        return carry

    lax.fori_loop(0, rest, together, 0)

    low_down = dot(z[...], at_down[...], NT).astype(BF16)

    def down(over, t):
        value = dot(z[...], wd[:, over]) + ADAPT_SCALE * dot(low_down, b_down[:, over])
        down_part[:, over] = value.astype(BF16)
        s_part[0:1, over] = total(value * cotangent[:, over].astype(F32))
        gb_down[:, over] = ADAPT_SCALE * dot(low_down, dpd[:, over], TN)

    tiles(width, WIDE, down, two[1].spread(rest, rest + 2, n_width))
    leaving(2, 0).start()
    leaving(2, 1).start()
    across = Across(depth, s_part, others, z_send, z_recv)
    across.start()

    def down_factor(over, t):
        ga_down[:, over] = dot(dlow_down, z[:, over], TN)

    tiles(hidden, WIDE, down_factor)
    row_sums[...] = jnp.zeros_like(row_sums)
    taken = rest + 4
    tick_two = two[1].spread(rest + 2, taken, half // 16)

    def first_half(k, carry):
        norm_back(0, k * 16)
        tick_two(k)
        return carry

    lax.fori_loop(0, half // 16, first_half, 0)
    out_back(0)
    row_sums[...] = jnp.zeros_like(row_sums)

    def second_half(t, carry):
        @pl.when(t >= taken)
        def _():
            two[1].step(t)

        for stream in range(2):
            norm_back(1, ((1 - stream) * two[1].chunks + t - 3 * LAG) * CHUNK)
        return carry

    lax.fori_loop(3 * LAG, two[1].steps, second_half, 0)
    out_back(1)
    for line in [one_out] + two:
        line.drain()
    s = across.finish()[0:1, :]
    turn = m_down[...] * s * n_down * n_down * n_down
    tb = (b_down[...].astype(F32) * turn).astype(BF16)
    v_tb = dot(tb, wd[...], NT) + ADAPT_SCALE * dot(dot(tb, b_down[...], NT), at_down[...])
    ga_down[...] -= ADAPT_SCALE * v_tb
    gb_down[...] -= ADAPT_SCALE * v_down[...] * turn
    gm_down[...] = s * n_down
    come.wait_send()
    for i in range(3):
        for r in range(2):
            leaving(i, r).wait()
    leave.wait_recv()
    leave.wait_send()


def core(sizes, o, x, cotangent, gain, norms, out, down, gu):
    seq_n, depth, rows_n, group, heads = sizes
    count, pairs, width = rows_n * group, rows_n * heads, x.shape[1]
    hidden, half = down[0].shape[0], rows_n * group // 2
    return pl.pallas_call(
        functools.partial(core_kernel, *sizes),
        out_shape=[
            shape(count, width), shape(count, width), shape(count, width), shape(pairs, group, HD),
            shape(1, width, dtype=F32), shape(2, RANK, width, dtype=F32), shape(2, RANK, hidden, dtype=F32),
            shape(2, hidden, dtype=F32), shape(1, width, dtype=F32), shape(RANK, hidden, dtype=F32),
            shape(RANK, width, dtype=F32), shape(RANK, heads * HD, dtype=F32), shape(RANK, width, dtype=F32),
            shape(1, width, dtype=F32),
        ],
        in_specs=[IN_VMEM] * 14 + [ANYWHERE] * 5,
        out_specs=[ANYWHERE] * 3 + [IN_VMEM] * 11,
        scratch_shapes=[pltpu.VMEM((count, width), BF16)] * 3
        + [
            pltpu.VMEM((count, width), BF16), pltpu.VMEM((count, width), BF16), pltpu.VMEM((count, width), BF16),
            pltpu.VMEM(out[0].shape, BF16),
            pltpu.VMEM(gu[0].shape, BF16), pltpu.VMEM(down[0].shape, BF16), pltpu.VMEM((count, heads * HD), BF16),
            pltpu.VMEM((count, RANK), BF16), pltpu.VMEM((count, width), BF16), pltpu.VMEM((count, width), BF16),
            pltpu.VMEM((count, width), BF16), pltpu.VMEM((half, width), BF16), pltpu.VMEM((count, hidden), BF16),
            pltpu.VMEM((count, hidden), BF16), pltpu.VMEM((2, half + RANK, hidden), BF16),
            pltpu.VMEM((count, width), BF16), pltpu.VMEM((2, half, WIDE), F32), pltpu.VMEM((half, 2 * RANK), BF16),
            pltpu.VMEM((half + 2 * RANK, 2 * RANK), BF16),
            pltpu.VMEM((2, hidden), F32), pltpu.VMEM((2, RANK, hidden), F32),
            pltpu.VMEM((half + RANK, width), BF16), pltpu.VMEM((pairs, group, HD), BF16),
            pltpu.VMEM((8, width), F32), pltpu.VMEM((depth, 8, width), F32), pltpu.VMEM((8, width), F32),
            dma(6), dma(pairs), dma(pairs), dma(pairs), dma(pairs), dma(depth), dma(depth), dma(3, 2),
        ]
        + Line.scratch(count, width, CHUNK)
        + Line.scratch(half, width, CHUNK) * 2,
        compiler_params=params(62, 2),
    )(o, gain, out[3], norms, *out[1:3], out[4], *gu[1:], *down[1:], x, cotangent, out[0], gu[0], down[0])


def last_kernel(
    seq_n, depth, rows_n, group, heads,
    lse, start, place, cos_half, sin_half, low, gain, at, b, m, norm, v_qkv,
    ga_gu, gb_out, gb_down, g_gain2, gm_out, gm_down, ga_out, gb_gu, gm_gu, ga_down, inverse_one, norms, m_down,
    down_far, q_far, k_far, v_far, o_far, do_far, h1_far, pre_far, w_qkv, x2_far, dx2_far,
    dx_far, mixed_far, wide, local, hid,
    mixed, cos, sin, dh1, dx, x2, down_part, q, k, v, o, do, h1, pre, kt, dk_acc, dv_acc, dq, dk, dv,
    wq, gq, gk, gv, dp, mix, part, wide_in, local_in, hid_in, wide_got, local_got, hid_got,
    piece, pieces, done, q_send, q_recv, k_send, k_recv, v_send, v_recv, load,
    r_send, r_recv, g_send, g_recv, z_send, z_recv, leave, *line_refs,
):
    count, pairs, width = rows_n * group, rows_n * heads, h1.shape[1]
    fan, me = seq_n // pairs, lax.axis_index("seq")
    loads = [
        pltpu.make_async_copy(far, near, load.at[i])
        for i, (far, near) in enumerate(
            (
                (down_far, down_part), (q_far, q), (k_far, k), (v_far, v), (o_far, o), (do_far, do), (h1_far, h1),
                (pre_far, pre), (w_qkv, wq), (x2_far, x2), (dx2_far, dx),
            )
        )
    ]
    for one in loads[:6]:
        one.start()
    greet(seq=seq_n, heads=depth)()
    line_down = Line(down_part, mixed, *line_refs[:9], lead=LAST_LEAD)
    loads[0].wait()
    line_down.first()
    for one in loads[1:6]:
        one.wait()
    for one in loads[6:]:
        one.start()
    exchanges = [
        Exchange(kind, seq_n, pairs, lambda j, a=a: a.at[j], lambda j, to=to: to.at[j], *sems)
        for kind, a, to, sems in (
            ("queries_back", dq, gq, (q_send, q_recv)),
            ("keys_back", dk, gk, (k_send, k_recv)),
            ("keys_back", dv, gv, (v_send, v_recv)),
        )
    ]
    first, second = FIRST, SECOND
    attend_back(
        2 * group if fan == 1 else group, fan, q, k, v, o, do, lse, start, place, dq, dk, dv, kt, dk_acc, dv_acc,
        lambda ticks: line_down.spread(0, first, ticks),
    )
    for one in exchanges:
        one.start()

    widen_tables(cos_half, sin_half, cos, sin)
    wide_in[...] = jnp.zeros_like(wide_in)
    local_in[...] = jnp.zeros_like(local_in)
    hid_in[...] = jnp.zeros_like(hid_in)
    share = 1.0 / depth
    for i in range(2):
        wide_in[(3 + i) * RANK : (4 + i) * RANK, :] = ga_gu[i].astype(BF16)
        hid_in[i * RANK : (i + 1) * RANK, :] = gb_gu[i].astype(BF16)
    wide_in[5 * RANK : 6 * RANK, :] = gb_out[...].astype(BF16)
    wide_in[6 * RANK : 7 * RANK, :] = gb_down[...].astype(BF16)
    hid_in[3 * RANK : 4 * RANK, :] = ga_down[...].astype(BF16)
    local_in[4 * RANK : 5 * RANK, :] = ga_out[...].astype(BF16)
    hid_in[2 * RANK : 3 * RANK, :] = jnp.concatenate(
        [gm_gu[...], jnp.zeros((RANK - 2, hid_in.shape[1]), F32)], axis=0
    ).astype(BF16)

    sums = [None] * 3
    line_down.run(first, second)
    for one in loads[6:9]:
        one.wait()
    for i in range(3):
        exchanges[i].wait_recv()
        came = (gq, gk, gv)[i]
        for head in range(heads):
            cols = slice(head * HD, (head + 1) * HD)
            n = norm[i : i + 1, cols]
            c = m[i : i + 1, cols] / n
            s = jnp.zeros((1, HD), F32)
            for row in range(rows_n):
                rows = slice(row * group, (row + 1) * group)
                if i == 0:
                    e = came[row * heads + head].astype(F32)
                else:
                    e = came[(row * heads + head) * fan].astype(F32)
                    for g in range(1, fan):
                        e = e + came[(row * heads + head) * fan + g].astype(F32)
                if i < 2:
                    e = e * cos[rows, :] - pltpu.roll(e, HD // 2, 1) * sin[rows, :]
                s = s + total(e * pre[i, rows, cols].astype(F32))
                dp[i, rows, cols] = (e * c).astype(BF16)
            turn = m[i : i + 1, cols] * s / (n * n * n)
            dp[i, count : count + RANK, cols] = (b[i, :, cols].astype(F32) * turn).astype(BF16)
            local_in[i * RANK : (i + 1) * RANK, cols] = (
                ADAPT_SCALE * (dot(low[:, i * RANK : (i + 1) * RANK], dp[i, :count, cols], TN) - v_qkv[i, :, cols] * turn)
            ).astype(BF16)
            sums[i] = [s / n] if head == 0 else sums[i] + [s / n]
        line_down.run(second + i, second + i + 1)
    local_in[3 * RANK : 4 * RANK, :] = jnp.concatenate(
        [jnp.concatenate(one, axis=1) for one in sums]
        + [jnp.zeros((RANK - 3, heads * HD), F32)], axis=0
    ).astype(BF16)
    mix[...] = jnp.zeros_like(mix)
    for i in range(3):
        both = (ADAPT_SCALE * dot(dp[i], b[i], NT)).astype(BF16)
        cols = slice(i * RANK, (i + 1) * RANK)
        mix[:count, cols] = both[:count]
        mix[count + i * RANK : count + (i + 1) * RANK, cols] = both[count:]

    def inputs(over, t):
        through = dot(mix[...], at[:, :, over].reshape(3 * RANK, over.size))
        straight = dot(mix[:count, :], h1[:count, over], TN)
        value = through[:count]
        for i in range(3):
            product = dot(dp[i], wq[i, over, :], NT)
            value = value + product[:count]
            rows = slice(i * RANK, (i + 1) * RANK)
            v_tb = product[count:] + through[count + i * RANK : count + (i + 1) * RANK]
            wide_in[rows, over] = (straight[rows] - ADAPT_SCALE * v_tb).astype(BF16)
        part[:, over] = value.astype(BF16)
        g_gain1 = total(value * h1[:count, over].astype(F32)) / gain[:, over]
        wide_in[7 * RANK : 8 * RANK, over] = jnp.concatenate(
            [
                g_gain1, g_gain2[:, over], gm_out[:, over] * share,
                gm_down[:, over] * share,
                jnp.zeros((RANK - 4, over.size), F32),
            ], axis=0,
        ).astype(BF16)

    tiles(width, WIDE, inputs, line_down.spread(second + 3, line_down.steps, -(-width // WIDE)))
    line_down.drain()
    line = Line(part, dh1, *line_refs[:3], *line_refs[9:], lead=LAST_LEAD)
    line.first()
    for one in loads[9:]:
        one.wait()
    c_down = m_down[...] / norms[1:2, :]

    over_gain = 1.0 / gain[...]

    def sent(stream, r):
        at_ = line.place(stream, r * PIECES)[0]
        return pltpu.make_async_copy(dx.at[at_], dx_far.at[at_], leave.at[stream, r])

    mixed_leaves = pltpu.make_async_copy(mixed, mixed_far, load.at[0])

    def advance(t, carry):
        line.step(t)

        @pl.when(t < count // (2 * CHUNK))
        def _():
            rows = pl.ds(pl.multiple_of(t * (2 * CHUNK), 2 * CHUNK), 2 * CHUNK)
            mixed[rows, :] = (x2[rows, :].astype(F32) + mixed[rows, :].astype(F32) * c_down).astype(BF16)

        @pl.when(t == count // (2 * CHUNK))
        def _():
            mixed_leaves.start()

        c = t - 3 * LAG
        r = c // PIECES

        @pl.when((c >= 0) & (lax.rem(c, PIECES) == PIECES - 1))
        def _():
            for stream in range(2):
                at_ = line.place(stream, c)[0]
                unit = h1[at_, :].astype(F32) * over_gain
                scaled = dh1[at_, :].astype(F32) * gain[...]
                mean = jnp.mean(scaled * unit, axis=-1, keepdims=True)
                change = inverse_one[at_, :1] * (scaled - unit * mean)
                dx[at_, :] = (dx[at_, :].astype(F32) + change).astype(BF16)
                sent(stream, r).start()

        return carry


    spread = seq_n // OWNERS
    slabs = (
        (wide_in, wide_got, wide, lambda j: j), (local_in, local_got, local, lambda j: j),
        (hid_in, hid_got, hid, lambda j: OWNERS - 1 - j),
    )
    own = me // spread
    chosen = lax.rem(me, spread) == 0

    def rows_of(j):
        return pl.ds(pl.multiple_of(j * RANK, RANK), RANK)

    def to_owner(i, j):
        src, got, _, owner = slabs[i]
        return remote(
            src.at[rows_of(j)], got.at[me], r_send.at[i, j], r_recv.at[i, me], seq=owner(j) * spread
        )

    def from_owner(i, j, target):
        result = slabs[i][2]
        return remote(
            done.at[i, :, : result.shape[1]], result.at[rows_of(j)], g_send.at[i, target], g_recv.at[i, j], seq=target
        )

    for i, (src, got, result, owner) in enumerate(slabs):
        for j in range(src.shape[0] // RANK):

            @pl.when(me != owner(j) * spread)
            def _(i=i, j=j):
                to_owner(i, j).start()

            @pl.when(me == owner(j) * spread)
            def _(src=src, got=got, i=i, j=j):
                pltpu.make_async_copy(src.at[rows_of(j)], got.at[me], r_recv.at[i, me]).start()

    lax.fori_loop(0, GATHER, advance, 0)
    across = Across(depth, piece, pieces, z_send, z_recv)
    blocks_n = [slab[0].shape[0] // RANK for slab in slabs]
    owns = [chosen & (slab[3](own) < n) for slab, n in zip(slabs, blocks_n)]
    for i, (src, got, result, owner) in enumerate(slabs):

        @pl.when(owns[i])
        def _(i=i, got=got, result=result):
            def add(s_, acc):
                pltpu.make_async_copy(got.at[s_], got.at[s_], r_recv.at[i, s_]).wait()
                return acc + got[s_].astype(F32)

            value = lax.fori_loop(0, seq_n, add, jnp.zeros((RANK, result.shape[1]), F32))
            if i == 0:
                piece[...] = value.astype(BF16)
                across.start()
            else:
                done[i, :, : result.shape[1]] = value.astype(BF16)

    lax.fori_loop(GATHER, GIVE, advance, 0)

    @pl.when(owns[0])
    def _():
        done[0, :, :] = across.finish().astype(BF16)

    for i, (src, got, result, owner) in enumerate(slabs):

        @pl.when(owns[i])
        def _(i=i, result=result, owner=owner):
            mine = owner(own)

            def give(d, carry):
                from_owner(i, mine, lax.rem(me + d, seq_n)).start()
                return carry

            lax.fori_loop(1, seq_n, give, 0)
            pltpu.make_async_copy(
                done.at[i, :, : result.shape[1]], result.at[rows_of(mine)], g_recv.at[i, mine]
            ).start()

    lax.fori_loop(GIVE, line.steps, advance, 0)
    line.drain()

    def gone(c, carry):
        for stream in range(2):
            sent(stream, c).wait()
        return carry

    lax.fori_loop(0, line.chunks // PIECES, gone, 0)
    mixed_leaves.wait()
    for one in exchanges:
        one.wait_send()
    for i, (src, got, result, owner) in enumerate(slabs):
        for j in range(blocks_n[i]):

            @pl.when(me != owner(j) * spread)
            def _(i=i, j=j):
                to_owner(i, j).wait_send()

            pltpu.make_async_copy(result.at[rows_of(j)], result.at[rows_of(j)], g_recv.at[i, j]).wait()

        @pl.when(owns[i])
        def _(i=i, owner=owner):
            def given(d, carry):
                from_owner(i, owner(own), lax.rem(me + d, seq_n)).wait_send()
                return carry

            lax.fori_loop(1, seq_n, given, 0)


def last(sizes, ins, far, hidden):
    seq_n, depth, rows_n, group, heads = sizes
    qkv_w = far[8]
    count, pairs, width = rows_n * group, rows_n * heads, qkv_w.shape[1]
    local, length = qkv_w.shape[2], seq_n * group
    blocks = {width: 8, local: 5, hidden: 4}
    slabs = [(n * RANK, w) for w, n in blocks.items()]
    some, every = pltpu.VMEM((pairs, group, HD), BF16), pltpu.VMEM((seq_n, group, HD), BF16)
    return pl.pallas_call(
        functools.partial(last_kernel, *sizes),
        out_shape=[shape(count, width)] * 2 + [shape(*s) for s in slabs],
        in_specs=[IN_VMEM] * len(ins) + [ANYWHERE] * len(far),
        out_specs=[ANYWHERE] * 2 + [IN_VMEM] * 3,
        scratch_shapes=[pltpu.VMEM((count, width), BF16), pltpu.VMEM((count, HD), F32), pltpu.VMEM((count, HD), F32)]
        + [pltpu.VMEM((count, width), BF16)] * 3
        + [pltpu.VMEM(a.shape, BF16) for a in far[:8]]
        + [
            pltpu.VMEM((HD, length), BF16), pltpu.VMEM((length, HD), F32), pltpu.VMEM((length, HD), F32),
            some, every, every,
            pltpu.VMEM(qkv_w.shape, BF16), some, every, every,
            pltpu.VMEM((3, count + RANK, local), BF16), pltpu.VMEM((count + 3 * RANK, 3 * RANK), BF16),
            pltpu.VMEM((count, width), BF16),
        ]
        + [pltpu.VMEM(s, BF16) for s in slabs]
        + [pltpu.VMEM((seq_n, RANK, s[1]), BF16) for s in slabs]
        + [
            pltpu.VMEM((RANK, width), BF16), pltpu.VMEM((depth, RANK, width), BF16), pltpu.VMEM((3, RANK, width), BF16),
            dma(pairs), dma(pairs), dma(seq_n), dma(seq_n), dma(seq_n), dma(seq_n), dma(11),
            dma(3, 8), dma(3, seq_n), dma(3, seq_n), dma(3, 8), dma(depth), dma(depth), dma(2, count // (2 * CHUNK)),
        ]
        + Line.scratch(count, width, CHUNK)
        + Line.scratch(count, width, CHUNK)[3:],
        compiler_params=params(62, 5),
    )(*ins, *far)


PARTS = 4


def leave_kernel(wide_far, local_far, hid_far, dx_far, mixed_far, *refs):
    outs, (dx_out, mixed_out, wide, local, hid, dx, dx_wide, mixed, sems, slab_sems) = refs[:14], refs[14:]
    slabs = [
        pltpu.make_async_copy(far, near, slab_sems.at[i])
        for i, (far, near) in enumerate(((wide_far, wide), (local_far, local), (hid_far, hid)))
    ]
    rows = dx.shape[0] // PARTS
    parts = [slice(i * rows, (i + 1) * rows) for i in range(PARTS)]
    moves = [
        [pltpu.make_async_copy(src.at[p], dst.at[p], sems.at[k, i]) for i, p in enumerate(parts)]
        for k, (src, dst) in enumerate(
            ((dx_far, dx), (dx_wide, dx_out), (mixed_far, mixed), (mixed, mixed_out))
        )
    ]
    for one in moves[0] + slabs + moves[2]:
        one.start()
    for i, p in enumerate(parts):
        moves[0][i].wait()
        dx_wide[p, :] = dx[p, :].astype(F32)
        moves[1][i].start()
    for one in slabs:
        one.wait()
    for i in range(PARTS):
        moves[2][i].wait()
        moves[3][i].start()
    places = (
        (wide, 112, 1), (wide, 0, 48), (local, 0, 48), (local, 48, 3), (local, 64, 16), (wide, 80, 16), (wide, 114, 1),
        (wide, 113, 1), (wide, 48, 32), (hid, 0, 32), (hid, 32, 2), (hid, 48, 16), (wide, 96, 16), (wide, 115, 1),
    )
    for out, (slab, first, n) in zip(outs, places):
        begin = first // RANK * RANK
        value = slab[begin : begin + -(-n // RANK) * RANK, :].astype(F32)
        out[...] = value[first - begin : first - begin + n].reshape(out.shape)
    for k in (1, 3):
        for one in moves[k]:
            one.wait()


def outputs(wide, local, hid, dx, mixed):
    w, n, f = wide.shape[1], local.shape[1], hid.shape[1]
    dims = (
        (1, w), (3, RANK, w), (3, RANK, n), (3, n), (RANK, n), (RANK, w), (1, w), (1, w), (2, RANK, w), (2, RANK, f),
        (2, f), (RANK, f), (RANK, w), (1, w),
    )
    return pl.pallas_call(
        leave_kernel,
        out_shape=[shape(*d, dtype=F32) for d in dims] + [shape(*dx.shape, dtype=F32), shape(*mixed.shape)],
        in_specs=[ANYWHERE] * 5,
        out_specs=[IN_VMEM] * len(dims) + [ANYWHERE] * 2,
        scratch_shapes=[pltpu.VMEM(a.shape, BF16) for a in (wide, local, hid)]
        + [
            pltpu.VMEM(dx.shape, BF16), pltpu.VMEM(dx.shape, F32), pltpu.VMEM(mixed.shape, BF16), dma(4, PARTS), dma(3),
        ],
        compiler_params=params(62),
    )(wide, local, hid, dx, mixed)


def per_device(
    tokens, attn_gain, base_qkv, adapt_a_qkv, adapt_b_qkv, magnitude_qkv, base_out, adapt_a_out,
    adapt_b_out, magnitude_out, ffn_gain, base_gu, adapt_a_gu, adapt_b_gu, magnitude_gu, base_down,
    adapt_a_down, adapt_b_down, magnitude_down, doc_lengths, cotangent,
):
    rows_n, group, width = tokens.shape
    count = rows_n * group
    local = base_qkv.shape[2]
    heads = local // HD
    pairs = rows_n * heads
    seq_n, depth = lax.axis_size("seq"), lax.axis_size("heads")
    sizes = (seq_n, depth, rows_n, group, heads)
    length = group * seq_n
    me = lax.axis_index("seq")

    order = jnp.arange(doc_lengths.shape[1])
    doc_ends = jnp.sum(
        jnp.where(order[None, :, None] <= order[None, None, :], doc_lengths[:, :, None], 0), axis=1
    )
    doc_starts = doc_ends - doc_lengths

    def starts_of(places, ends, starts):
        inside = (places[..., None] >= starts) & (places[..., None] < ends)
        return jnp.sum(jnp.where(inside, starts, 0), axis=-1)

    mine = me * group + jnp.arange(group, dtype=jnp.int32)
    position = mine[None, :] - starts_of(
        jnp.broadcast_to(mine[None, :], (rows_n, group)), doc_ends[:, None], doc_starts[:, None]
    )
    frequency = ROPE_BASE ** (jnp.arange(HD // 2, dtype=F32) * (-2.0 / HD))
    angles = position.reshape(count, 1).astype(F32) * frequency
    cos, sin = jnp.cos(angles), jnp.sin(angles)

    x = tokens.reshape(count, width)
    dy = cotangent.reshape(count, width)
    gain1, gain2 = attn_gain[None, :], ffn_gain[None, :]
    m_out, m_down = magnitude_out[None, :], magnitude_down[None, :]
    at_qkv, at_gu = adapt_a_qkv.transpose(0, 2, 1), adapt_a_gu.transpose(0, 2, 1)
    at_out, at_down = adapt_a_out.T, adapt_a_down.T

    h1, pre, q, k, v, inverse_one, low, norm_qkv, v_qkv, norms, v_out, v_down = front(
        sizes, x, gain1, cos, sin, (base_qkv, at_qkv, adapt_b_qkv, magnitude_qkv), (base_out, at_out, adapt_b_out),
        (base_down, at_down, adapt_b_down),
    )
    q, k, v = q.reshape(-1, HD), k.reshape(length, HD), v.reshape(length, HD)
    o, lse, start, place = attend(sizes, doc_lengths, q, k, v)
    dx2, x2, down_part, do, gm_down, ga_gu, gb_gu, gm_gu, g_gain2, ga_down, gb_down, ga_out, gb_out, gm_out = core(
        sizes, o.reshape(-1, group, HD), x, dy, gain2, norms, (base_out, at_out, adapt_b_out, m_out, v_out),
        (base_down, at_down, adapt_b_down, m_down, v_down), (base_gu, at_gu, adapt_b_gu, magnitude_gu),
    )
    dx, mixed, wide, narrow, hid = last(
        sizes,
        (
            lse, start, place, cos, sin, low, gain1, at_qkv, adapt_b_qkv, magnitude_qkv, norm_qkv, v_qkv, ga_gu, gb_out,
            gb_down, g_gain2, gm_out, gm_down, ga_out, gb_gu, gm_gu, ga_down, inverse_one, norms, m_down,
        ),
        (down_part, q, k, v, o, do.reshape(-1, HD), h1, pre, base_qkv, x2, dx2),
        base_down.shape[0],
    )
    *g, dx, mixed = outputs(wide, narrow, hid, dx, mixed)
    return (
        mixed.reshape(rows_n, group, width),
        dx.reshape(rows_n, group, width),
        g[0][0], g[1].transpose(0, 2, 1), g[2], g[3], g[4].T, g[5], g[6][0], g[7][0], g[8].transpose(0, 2, 1), g[9],
        g[10], g[11].T, g[12], g[13][0],
    )


def solution(mesh):
    in_specs = (
        P(None, "seq", None), P(), P(None, None, "heads"), P(), P(None, None, "heads"), P(None, "heads"),
        P("heads", None), P("heads", None), P(), P(), P(), P(None, None, "heads"), P(),
        P(None, None, "heads"), P(None, "heads"), P("heads", None), P("heads", None), P(), P(), P(),
        P(None, "seq", None),
    )
    out_specs = (
        P(None, "seq", None), P(None, "seq", None), P(), P(), P(None, None, "heads"), P(None, "heads"),
        P("heads", None), P(), P(), P(), P(), P(None, None, "heads"), P(None, "heads"),
        P("heads", None), P(), P(),
    )
    return jax.shard_map(
        per_device, mesh=mesh, in_specs=in_specs, out_specs=out_specs, check_vma=False
    )
```

```python
import functools

import jax
import jax.numpy as jnp
from jax import lax
from jax.experimental import pallas as pl
from jax.experimental.pallas import tpu as pltpu
from jax.sharding import PartitionSpec as P

HD = 128
RANK = 16
ADAPT_SCALE = 2.0
NORM_EPS = 1e-05
COLUMN_EPS = 1e-06
ROPE_BASE = 10000.0
NEG_LARGE = -1e30
LOG2E = 1.4426950408889634
F32 = jnp.float32
BF16 = jnp.bfloat16
MESH = pl.DeviceIdType.MESH
NN = (((1,), (0,)), ((), ()))
NT = (((1,), (1,)), ((), ()))
TN = (((0,), (0,)), ((), ()))
OWNERS = 8
CHUNK = 16
PIECES = 1
LAG = 2
LEAD = 4
NEAR_LATE = 1
IN_A, IN_B = 4, 5
LAST_LEAD = 4
FIRST, SECOND = 7, 13
GATHER, GIVE = 10, 14
WIDE = 512
IN_VMEM = pl.BlockSpec(memory_space=pltpu.VMEM)
IN_SMEM = pl.BlockSpec(memory_space=pltpu.SMEM)
ANYWHERE = pl.BlockSpec(memory_space=pl.ANY)


def dot(a, b, dims=NN):
    return lax.dot_general(a.astype(BF16), b.astype(BF16), dims, preferred_element_type=F32)


def shape(*dims, dtype=BF16):
    return jax.ShapeDtypeStruct(dims, dtype)


def dma(*dims):
    return pltpu.SemaphoreType.DMA(dims)


def params(mib, collective_id=None):
    more = {} if collective_id is None else {"collective_id": collective_id, "has_side_effects": True}
    return pltpu.CompilerParams(vmem_limit_bytes=mib * 2**20, **more)


def tiles(count, size, body, tick=lambda t: None):
    whole = count // size
    if whole:

        def step(t, carry):
            body(pl.ds(pl.multiple_of(t * size, 128), size), t)
            tick(t)
            return carry

        lax.fori_loop(0, whole, step, 0)
    if count - whole * size:
        body(pl.ds(whole * size, count - whole * size), whole)
        tick(whole)


def row_loop(count, size, body, init=0):
    def step(t, carry):
        return body(pl.ds(pl.multiple_of(t * size, size), size), carry)

    return lax.fori_loop(0, count // size, step, init)


def fold(v):
    return jnp.sum(v.reshape(v.shape[0] // 8, 8, v.shape[1]), axis=0)


def total(v):
    return jnp.sum(v, axis=0, keepdims=True)


def greet(seq, heads):
    barrier = pltpu.get_barrier_semaphore()
    me, h = lax.axis_index("seq"), lax.axis_index("heads")
    peers = 0
    for d in range(1, seq):
        pl.semaphore_signal(barrier, inc=1, device_id={"seq": lax.rem(me + d, seq)}, device_id_type=MESH)
        peers = peers + 1
    for d in range(1, heads):
        pl.semaphore_signal(
            barrier, inc=1, device_id={"heads": lax.rem(h + d, heads)}, device_id_type=MESH
        )
        peers = peers + 1
    return lambda: pl.semaphore_wait(barrier, peers)


def remote(src, dst, send_sem, recv_sem, **where):
    return pltpu.make_async_remote_copy(
        src_ref=src, dst_ref=dst, send_sem=send_sem, recv_sem=recv_sem, device_id=where, device_id_type=MESH
    )


class Exchange:
    def __init__(self, kind, seq_n, pairs, src, dst, send_sem, recv_sem):
        fan = seq_n // pairs
        me = lax.axis_index("seq")
        self.me, self.src, self.dst, self.send_sem, self.recv_sem = me, src, dst, send_sem, recv_sem
        self.count = self.slots(kind, seq_n, pairs)
        self.target, self.block, self.slot = {
            "queries": (lambda p: p * fan + lax.rem(me, fan), lambda p: p, me // fan),
            "keys": (lambda e: e, lambda e: e // fan, me),
            "queries_back": (lambda i: lax.rem(me, fan) + fan * i, lambda i: i, me // fan),
            "keys_back": (lambda e: e, lambda e: e, me),
        }[kind]

    @staticmethod
    def slots(kind, seq_n, pairs):
        return pairs if kind.startswith("queries") else seq_n

    def copy(self, j):
        return remote(
            self.src(self.block(j)),
            self.dst(self.slot),
            self.send_sem.at[j],
            self.recv_sem.at[self.slot],
            seq=self.target(j),
        )

    def start(self, low=0, high=None):
        number = (self.count if high is None else high) - low

        def one(d, carry):
            j = low + lax.rem(self.me + d, number)

            @pl.when(self.target(j) != self.me)
            def _():
                self.copy(j).start()

            @pl.when(self.target(j) == self.me)
            def _():
                pltpu.make_async_copy(
                    self.src(self.block(j)), self.dst(self.slot), self.recv_sem.at[self.slot]
                ).start()

            return carry

        lax.fori_loop(0, number, one, 0)

    def wait_recv(self):
        def one(j, carry):
            pltpu.make_async_copy(self.dst(j), self.dst(j), self.recv_sem.at[j]).wait()
            return carry

        lax.fori_loop(0, self.count, one, 0)

    def wait_send(self):
        def one(j, carry):
            @pl.when(self.target(j) != self.me)
            def _():
                self.copy(j).wait_send()

            return carry

        lax.fori_loop(0, self.count, one, 0)


class Line:
    def __init__(self, x, out, got, near, held, *sems, per=None, base=0, lead=None):
        self.x, self.out, self.got, self.near, self.held = x, out, got, near, held
        self.far_send, self.far_recv, self.near_send, self.near_recv, self.down_send, self.down_recv = sems
        self.chunks, self.rows = got.shape[1], got.shape[2]
        self.per, self.base = per or self.chunks, base
        self.lead = self.chunks if lead is None else lead
        self.steps = self.done(self.chunks)
        self.h = lax.axis_index("heads")

    @staticmethod
    def done(chunks):
        return chunks + 3 * LAG

    @staticmethod
    def scratch(count, width, rows):
        chunks = count // (2 * rows) * PIECES
        one = pltpu.VMEM((chunks, rows, width // PIECES), BF16)
        return [
            pltpu.VMEM((2, chunks, rows, width // PIECES), BF16), one, one,
            dma(2, chunks), dma(2, chunks), dma(chunks), dma(chunks), dma(2, 2, chunks), dma(2, chunks),
        ]

    def ends(self, stream):
        if stream == 0:
            return self.h, self.h + 1, self.h - 1
        return 3 - self.h, self.h - 1, self.h + 1

    def place(self, stream, c):
        rows, per, width = self.rows, self.per // PIECES, self.got.shape[3]
        r, piece = c // PIECES, lax.rem(c, PIECES)
        first = self.base + ((r // per) * 2 + (1 - stream)) * (per * rows) + lax.rem(r, per) * rows
        return pl.ds(pl.multiple_of(first, rows), rows), pl.ds(pl.multiple_of(piece * width, width), width)

    def far(self, stream, c, src, to):
        return remote(
            src, self.got.at[stream, c], self.far_send.at[stream, c], self.far_recv.at[stream, c], heads=to
        )

    def close(self, stream, c, to):
        return remote(
            self.x.at[*self.place(stream, c)], self.near.at[c], self.near_send.at[c], self.near_recv.at[c], heads=to
        )

    def down(self, stream, way, c, to):
        part = self.out.at[*self.place(stream, c)]
        return remote(part, part, self.down_send.at[stream, way, c], self.down_recv.at[stream, c], heads=to)

    def give(self, c):
        for stream in range(2):
            pos, ahead, behind = self.ends(stream)

            @pl.when((pos == 0) & (c < self.chunks))
            def _():
                self.far(stream, c, self.x.at[*self.place(stream, c)], ahead).start()

        c = c - NEAR_LATE
        for stream in range(2):
            pos, ahead, behind = self.ends(stream)

            @pl.when((pos == 3) & (c >= 0) & (c < self.chunks))
            def _():
                self.close(stream, c, behind).start()

    def first(self):
        def one(c, carry):
            self.give(c)
            return carry

        lax.fori_loop(0, self.lead, one, 0)

    def step(self, t):
        self.give(t + self.lead)
        for stream in range(2):
            pos, ahead, behind = self.ends(stream)

            @pl.when((pos == 1) & (t < self.chunks))
            def _():
                self.far(stream, t, self.held.at[t], self.h).wait_recv()
                at = self.place(stream, t)
                self.held[t] = (self.got[stream, t].astype(F32) + self.x[*at].astype(F32)).astype(BF16)
                self.far(stream, t, self.held.at[t], ahead).start()

        for stream in range(2):
            pos, ahead, behind = self.ends(stream)
            c = t - LAG

            @pl.when((pos == 2) & (c >= 0) & (c < self.chunks))
            def _():
                self.far(stream, c, self.held.at[c], self.h).wait_recv()
                self.close(stream, c, self.h).wait_recv()
                at = self.place(stream, c)
                value = self.got[stream, c].astype(F32) + self.near[c].astype(F32) + self.x[*at].astype(F32)
                self.out[*at] = value.astype(BF16)
                self.down(stream, 0, c, behind).start()
                self.down(stream, 1, c, ahead).start()

        for stream in range(2):
            pos, ahead, behind = self.ends(stream)
            b = t - jnp.where(pos == 0, 3 * LAG, 2 * LAG)

            @pl.when((pos != 2) & (b >= 0) & (b < self.chunks))
            def _():
                self.down(stream, 0, b, self.h).wait_recv()

                @pl.when(pos == 1)
                def _():
                    self.down(stream, 0, b, behind).start()

    def run(self, start, stop):
        def one(t, carry):
            self.step(t)
            return carry

        lax.fori_loop(start, stop, one, 0)

    def spread(self, start, stop, ticks):
        def tick(k):
            now, then = (k * (stop - start)) // ticks, ((k + 1) * (stop - start)) // ticks
            self.run(start + now, start + then)

        return tick

    def drain(self):
        def one(c, carry):
            for stream in range(2):
                pos, ahead, behind = self.ends(stream)

                @pl.when(pos <= 1)
                def _():
                    self.far(stream, c, self.held.at[c], self.h).wait_send()

                @pl.when(pos == 3)
                def _():
                    self.close(stream, c, self.h).wait_send()

                @pl.when((pos == 1) | (pos == 2))
                def _():
                    self.down(stream, 0, c, self.h).wait_send()

                @pl.when(pos == 2)
                def _():
                    self.down(stream, 1, c, self.h).wait_send()

            return carry

        lax.fori_loop(0, self.chunks, one, 0)


class Across:
    def __init__(self, depth, part, others, send_sem, recv_sem):
        self.depth, self.part, self.others, self.sems = depth, part, others, (send_sem, recv_sem)
        self.h = lax.axis_index("heads")

    def copy(self, d):
        to = lax.rem(self.h + d, self.depth)
        return remote(
            self.part, self.others.at[self.h], self.sems[0].at[d], self.sems[1].at[self.h], heads=to
        )

    def start(self):
        for d in range(1, self.depth):
            self.copy(d).start()

    def finish(self):
        value = self.part[...].astype(F32)
        for d in range(1, self.depth):
            came = self.others.at[lax.rem(self.h + d, self.depth)]
            pltpu.make_async_copy(came, came, self.sems[1].at[lax.rem(self.h + d, self.depth)]).wait()
            value = value + came[...].astype(F32)
        for d in range(1, self.depth):
            self.copy(d).wait_send()
        return value


def column_stats(w, at, b, aw):
    ab = dot(dot(at, at, NT), b)
    bf = b.astype(F32)

    acc = jnp.zeros((8, w.shape[1]), F32)
    for first in range(0, w.shape[0], 64):
        v = w[first : first + 64, :].astype(F32)
        acc = acc + fold(v * v)
    squares = total(acc) + 2.0 * ADAPT_SCALE * total(bf * aw) + ADAPT_SCALE**2 * total(bf * ab)
    return squares, aw + ADAPT_SCALE * ab


def widen_tables(cos_half, sin_half, cos, sin):
    cos[...] = jnp.concatenate([cos_half[...], cos_half[...]], axis=1)
    sin[...] = jnp.concatenate([-sin_half[...], sin_half[...]], axis=1)


def front_kernel(
    seq_n, depth, rows_n, group, heads,
    x, gain, cos_half, sin_half, at_qkv, b_qkv, m_qkv, at_out, b_out, at_down, b_down,
    w_qkv, w_out, w_down,
    h1_far, pre_far, q, k, v, inverse_one, low, norm_qkv, v_qkv, norms, v_out, v_down,
    cos, sin, h1, pre, wq, wo, wd, turned, part, others, q_send, q_recv, k_send, k_recv, v_send, v_recv, z_send, z_recv, load, leave,
):
    count, pairs = rows_n * group, rows_n * heads
    leaving = [pltpu.make_async_copy(pre.at[i], pre_far.at[i], leave.at[i]) for i in range(3)]
    leaving.append(pltpu.make_async_copy(h1, h1_far, leave.at[3]))
    loads = [pltpu.make_async_copy(w_qkv.at[i], wq.at[i], load.at[i]) for i in range(3)]
    loads += [
        pltpu.make_async_copy(w_out, wo, load.at[3]),
        pltpu.make_async_copy(w_down, wd, load.at[4]),
    ]
    for one in loads[:3]:
        one.start()
    all_here = greet(seq=seq_n, heads=depth)
    widen_tables(cos_half, sin_half, cos, sin)

    def norm(rows, carry):
        v = x[rows, :].astype(F32)
        inverse = lax.rsqrt(jnp.mean(v * v, axis=-1, keepdims=True) + NORM_EPS)
        h1[rows, :] = (v * inverse * gain[...]).astype(BF16)
        inverse_one[rows, :] = jnp.broadcast_to(inverse, (rows.size, HD))
        return carry

    row_loop(count, 32, norm)
    for i in range(3):
        h1[count + i * RANK : count + (i + 1) * RANK, :] = at_qkv[i]
    leaving[3].start()
    low[...] = dot(h1[:count, :], h1[count:, :], NT).astype(BF16)
    exchanges = [
        Exchange(kind, seq_n, pairs, lambda j, i=i: turned.at[i, j], lambda j, to=to: to.at[j], *sems)
        for i, (kind, to, sems) in enumerate(
            (("queries", q, (q_send, q_recv)), ("keys", k, (k_send, k_recv)), ("keys", v, (v_send, v_recv)))
        )
    ]
    for i in range(3):
        loads[i].wait()
        if i < 2:
            loads[3 + i].start()

        def project(over, t, i=i):
            width = over.size
            r = dot(h1[...], wq[i, :, over])
            b = b_qkv[i, :, over]
            value = r[:count] + ADAPT_SCALE * dot(low[:, i * RANK : (i + 1) * RANK], b)
            aw = r[count + i * RANK : count + (i + 1) * RANK]
            squares, av = column_stats(wq.at[i, :, over], at_qkv[i], b, aw)
            n = jnp.sqrt(squares + COLUMN_EPS)
            norm_qkv[i : i + 1, over] = n
            v_qkv[i, :, over] = av
            pre[i, :, over] = value.astype(BF16)
            scaled = value * (m_qkv[i : i + 1, over] / n)
            for row in range(rows_n):
                rows = slice(row * group, (row + 1) * group)
                for hh in range(width // HD):
                    part_ = scaled[rows, hh * HD : (hh + 1) * HD]
                    if i < 2:
                        part_ = part_ * cos[rows, :] + pltpu.roll(part_, HD // 2, 1) * sin[rows, :]
                    turned[i, row * heads + t * (width // HD) + hh] = part_.astype(BF16)

        tiles(heads * HD, WIDE, project)
        if i == 0:
            all_here()
        exchanges[i].start()
        leaving[i].start()

    part[...] = jnp.zeros_like(part)
    for row, (w, at, b, av, loaded) in enumerate(
        ((wo, at_out, b_out, v_out, loads[3]), (wd, at_down, b_down, v_down, loads[4]))
    ):
        loaded.wait()

        def stats(over, t, row=row, w=w, at=at, b=b, av=av):
            squares, value = column_stats(w.at[:, over], at[...], b[:, over], dot(at[...], w[:, over]))
            part[row : row + 1, over] = squares
            av[:, over] = value

        tiles(w.shape[1], WIDE, stats)
    across = Across(depth, part, others, z_send, z_recv)
    across.start()
    norms[...] = jnp.sqrt(across.finish() + COLUMN_EPS)
    for one in exchanges:
        one.wait_recv()
    for one in exchanges:
        one.wait_send()
    for one in leaving:
        one.wait()


def front(sizes, x, gain, cos, sin, qkv, out, down):
    seq_n, depth, rows_n, group, heads = sizes
    count, pairs, width = rows_n * group, rows_n * heads, x.shape[1]
    local = qkv[0].shape[2]
    return pl.pallas_call(
        functools.partial(front_kernel, *sizes),
        out_shape=[
            shape(count + 3 * RANK, width), shape(3, count, local),
            shape(pairs, group, HD), shape(seq_n, group, HD), shape(seq_n, group, HD),
            shape(count, HD, dtype=F32), shape(count, 3 * RANK),
            shape(3, local, dtype=F32), shape(3, RANK, local, dtype=F32), shape(8, width, dtype=F32),
            shape(RANK, width, dtype=F32), shape(RANK, width, dtype=F32),
        ],
        in_specs=[IN_VMEM] * 11 + [ANYWHERE] * 3,
        out_specs=[ANYWHERE] * 2 + [IN_VMEM] * 10,
        scratch_shapes=[
            pltpu.VMEM((count, HD), F32), pltpu.VMEM((count, HD), F32),
            pltpu.VMEM((count + 3 * RANK, width), BF16), pltpu.VMEM((3, count, local), BF16),
            pltpu.VMEM(qkv[0].shape, BF16), pltpu.VMEM(out[0].shape, BF16), pltpu.VMEM(down[0].shape, BF16),
            pltpu.VMEM((3, pairs, group, HD), BF16),
            pltpu.VMEM((8, width), F32), pltpu.VMEM((depth, 8, width), F32),
            dma(pairs), dma(pairs), dma(seq_n), dma(seq_n), dma(seq_n), dma(seq_n), dma(depth), dma(depth), dma(6), dma(4),
        ],
        compiler_params=params(60, 1),
    )(
        x, gain, cos, sin, qkv[1], qkv[2], qkv[3], out[1], out[2], down[1], down[2], qkv[0], out[0], down[0],
    )


def attend_kernel(block, fan, heads, group, docs, q_ref, k_ref, v_ref, o_ref, lse_ref, start_ref, place_ref, vt):
    scale = HD**-0.5 * LOG2E
    vt[...] = v_ref[...].T
    me = lax.axis_index("seq")
    mine, row, split = lax.rem(me, fan), me // fan // heads, block // group
    lengths = [docs[row, d] for d in range(docs.shape[1])]

    def starts_of(places):
        end, begin = 0, 0
        for n in lengths:
            end = end + n
            begin = begin + jnp.where(places >= end, n, 0)
        return begin

    for b in range(q_ref.shape[0] // group):
        over = slice(b * group, (b + 1) * group)
        places = (mine + fan * b) * group + lax.broadcasted_iota(jnp.int32, (1, group), 1)
        place_ref[:, over] = places
        start_ref[:, over] = starts_of(places)

    def per_query(i, carry):
        at = pl.ds(pl.multiple_of(i * block, block), block)
        q = q_ref[at, :]
        start, place = start_ref[:, at], place_ref[:, at]

        def per_key(j, state):
            top, count, acc = state
            over = pl.ds(pl.multiple_of(j * block, block), block)
            s = dot(k_ref[over, :], q, NT) * scale
            key = j * block + lax.broadcasted_iota(jnp.int32, (block, block), 0)
            s = jnp.where((key >= start) & (key <= place), s, NEG_LARGE)
            new_top = jnp.maximum(top, jnp.max(s, axis=0, keepdims=True))
            p = jnp.exp2(s - new_top)
            fade = jnp.exp2(top - new_top)
            count = count * fade + total(p)
            acc = acc * fade + dot(vt[:, over], p)
            return new_top, count, acc

        low = starts_of((mine + fan * (i * split)) * group) // block
        high = ((mine + fan * ((i + 1) * split - 1) + 1) * group - 1) // block + 1
        begin = (
            jnp.full((1, block), -1e29, F32),
            jnp.zeros((1, block), F32),
            jnp.zeros((HD, block), F32),
        )
        top, count, acc = lax.fori_loop(low, high, per_key, begin)
        o_ref[at, :] = (acc / count).T.astype(BF16)
        lse_ref[:, at] = top + jnp.log2(count)
        return carry

    lax.fori_loop(0, q_ref.shape[0] // block, per_query, 0)


def attend(sizes, docs, q, k, v):
    seq_n, depth, rows_n, group, heads = sizes
    count, fan = q.shape[0], seq_n // (rows_n * heads)
    return pl.pallas_call(
        functools.partial(attend_kernel, 2 * group, fan, heads, group),
        out_shape=[
            shape(*q.shape), shape(1, count, dtype=F32), shape(1, count, dtype=jnp.int32),
            shape(1, count, dtype=jnp.int32),
        ],
        in_specs=[IN_SMEM] + [IN_VMEM] * 3,
        out_specs=[IN_VMEM] * 4,
        scratch_shapes=[pltpu.VMEM((HD, k.shape[0]), BF16)],
        compiler_params=params(62),
    )(docs, q, k, v)


def attend_back(block, fan, q_ref, k_ref, v_ref, o_ref, do_ref, lse_ref, start_ref, place_ref, dq, dk, dv, kt, dk_acc, dv_acc, spread):
    scale = HD**-0.5
    mine = lax.rem(lax.axis_index("seq"), fan)
    group = dq.shape[1]
    split = block // group
    blocks = q_ref.shape[0] // block

    def reach(i):
        return ((mine + fan * ((i + 1) * split - 1) + 1) * group - 1) // block + 1

    tick = spread(sum(reach(i) for i in range(blocks)))
    kt[...] = k_ref[...].T
    dk_acc[...] = jnp.zeros_like(dk_acc)
    dv_acc[...] = jnp.zeros_like(dv_acc)

    def per_query(i, before):
        at = pl.ds(pl.multiple_of(i * block, block), block)
        q, do = q_ref[at, :], do_ref[at, :]
        start, place, lse = start_ref[:, at], place_ref[:, at], lse_ref[:, at]
        delta = total((do.astype(F32) * o_ref[at, :].astype(F32)).T)

        def per_key(j, acc):
            over = pl.ds(pl.multiple_of(j * block, block), block)
            k = k_ref[over, :]
            s = dot(k, q, NT) * (scale * LOG2E)
            key = j * block + lax.broadcasted_iota(jnp.int32, (block, block), 0)
            p = jnp.exp2(jnp.where((key >= start) & (key <= place), s - lse, NEG_LARGE))
            dp = dot(v_ref[over, :], do, NT)
            ds = (p * (dp - delta)).astype(BF16)
            dv_acc[over, :] += dot(p, do)
            dk_acc[over, :] += dot(ds, q)
            tick(before + j)
            return acc + dot(kt[:, over], ds)

        acc = lax.fori_loop(0, reach(i), per_key, jnp.zeros((HD, block), F32))
        acc = (acc * scale).T.astype(BF16)
        for n in range(split):
            dq[i * split + n] = acc[n * group : (n + 1) * group]
        return before + reach(i)

    lax.fori_loop(0, blocks, per_query, 0)

    def store(j, carry):
        over = pl.ds(pl.multiple_of(j * group, group), group)
        dk[j] = (dk_acc[over, :] * scale).astype(BF16)
        dv[j] = dv_acc[over, :].astype(BF16)
        return carry

    lax.fori_loop(0, k_ref.shape[0] // group, store, 0)


def core_kernel(
    seq_n, depth, rows_n, group, heads,
    o, gain, m_out, norms, at_out, b_out, v_out, at_gu, b_gu, m_gu, at_down, b_down, m_down, v_down,
    x_far, cotangent_far, w_out, w_gu, w_down,
    dx2_far, x2_far, down_far, do, gm_down, ga_gu, gb_gu, gm_gu, g_gain, ga_down, gb_down, ga_out, gb_out, gm_out,
    dx2, x2_out, down_part, out_pre, x, cotangent, wo, wg, wd, attn, low_out, part, part2, dh2, h2, z, dz, dp, dpd, tmp, low, mix, norm_gu, v_gu, dpo, blocks,
    s_part, others, row_sums, load, send, recv, back_send, back_recv, z_send, z_recv, away, *line_refs,
):
    count, pairs = rows_n * group, rows_n * heads
    half = count // 2
    hidden, width = wd.shape
    loads = [
        pltpu.make_async_copy(far, near, load.at[i])
        for i, (far, near) in enumerate(
            ((w_out, wo), (x_far, x), (w_gu.at[0], wg.at[0]), (w_gu.at[1], wg.at[1]), (cotangent_far, cotangent), (w_down, wd))
        )
    ]
    for one in loads:
        one.start()
    greet(seq=seq_n, heads=depth)()

    def landing(pair):
        row, head = pair // heads, lax.rem(pair, heads)
        return attn.at[
            pl.ds(pl.multiple_of(row * group, group), group), pl.ds(pl.multiple_of(head * HD, HD), HD)
        ]

    def leaving(i, r):
        near, far = ((dx2, dx2_far), (x2_out, x2_far), (down_part, down_far))[i]
        return pltpu.make_async_copy(
            near.at[r * half : (r + 1) * half], far.at[r * half : (r + 1) * half], away.at[i, r]
        )

    come = Exchange("queries_back", seq_n, pairs, lambda i: o.at[i], landing, send, recv)
    leave = Exchange("queries", seq_n, pairs, lambda p: blocks.at[p], lambda s_: do.at[s_], back_send, back_recv)
    come.start()
    for ref in (s_part, ga_gu, gb_gu, gm_gu, g_gain, ga_down, gb_down, ga_out, gb_out, gm_out):
        ref[...] = jnp.zeros_like(ref)
    one_out = Line(part, out_pre, *line_refs[:9], per=half // (2 * CHUNK) * PIECES, lead=LEAD)
    two = [
        Line(part2, dh2, *line_refs[9 + 9 * r : 18 + 9 * r], base=r * half, lead=LEAD) for r in range(2)
    ]
    loads[0].wait()
    come.wait_recv()
    low_out[...] = dot(attn[...], at_out[...], NT).astype(BF16)

    def project(over, t):
        part[:, over] = (dot(attn[...], wo[:, over]) + ADAPT_SCALE * dot(low_out[...], b_out[:, over])).astype(BF16)

    tiles(width, WIDE, project)
    one_out.first()
    for one in loads[1:]:
        one.wait()
    n_out, n_down = 1.0 / norms[0:1, :], 1.0 / norms[1:2, :]
    c_out, c_down = m_out[...] * n_out, m_down[...] * n_down

    n_hidden, n_width = -(-hidden // WIDE), -(-width // WIDE)
    half_done = one_out.done(one_out.per)
    tick_first = one_out.spread(0, half_done, count // 64 + 3 * n_hidden)

    def scaled_gradient(rows, carry):
        dpd[rows, :] = (cotangent[rows, :].astype(F32) * c_down).astype(BF16)
        tick_first(rows.start // rows.size)
        return carry

    row_loop(count, 64, scaled_gradient)
    dlow_down = (ADAPT_SCALE * dot(dpd[...], b_down[...], NT)).astype(BF16)

    def hidden_gradient(over, t):
        dz[:, over] = (dot(dpd[...], wd[over, :], NT) + dot(dlow_down, at_down[:, over])).astype(BF16)

    tiles(hidden, WIDE, hidden_gradient, lambda t: tick_first(count // 64 + t))
    for i in range(2):

        def stats_gu(over, t, i=i):
            b = b_gu[i, :, over]
            squares, value = column_stats(wg.at[i, :, over], at_gu[i], b, dot(at_gu[i], wg[i, :, over]))
            norm_gu[i : i + 1, over] = jnp.sqrt(squares + COLUMN_EPS)
            v_gu[i, :, over] = value

        tiles(hidden, WIDE, stats_gu, lambda t, i=i: tick_first(count // 64 + (1 + i) * n_hidden + t))

    def feed_forward(r, tick):
        mine = slice(r * half, (r + 1) * half)
        base = r * half

        def there(rows):
            return pl.ds(pl.multiple_of(base + rows.start, rows.size), rows.size)

        def norm(rows, carry):
            x2 = x[there(rows), :].astype(F32) + out_pre[there(rows), :].astype(F32) * c_out
            inverse = lax.rsqrt(jnp.mean(x2 * x2, axis=-1, keepdims=True) + NORM_EPS)
            h2[rows, :] = (x2 * inverse * gain[...]).astype(BF16)
            tick(rows.start // rows.size)
            return carry

        row_loop(half, 32, norm)
        low[...] = dot(h2[...], at_gu[...].reshape(2 * RANK, width), NT).astype(BF16)

        def there_and_back(over, t):
            n = over.size
            for i in range(2):
                tmp[i, :, :n] = dot(h2[...], wg[i, :, over]) + ADAPT_SCALE * dot(
                    low[:, i * RANK : (i + 1) * RANK], b_gu[i, :, over]
                )
            scale = [m_gu[i : i + 1, over] / norm_gu[i : i + 1, over] for i in range(2)]

            def gated(rows, sums):
                pg, pu = tmp[0, rows, :n], tmp[1, rows, :n]
                g, u = pg * scale[0], pu * scale[1]
                sigma = jax.nn.sigmoid(g)
                silu = g * sigma
                z[there(rows), over] = (silu * u).astype(BF16)
                d = dz[there(rows), over].astype(F32)
                e_g = d * u * (sigma + silu * (1.0 - sigma))
                e_u = d * silu
                dp[0, rows, over] = (e_g * scale[0]).astype(BF16)
                dp[1, rows, over] = (e_u * scale[1]).astype(BF16)
                return sums[0] + fold(e_g * pg), sums[1] + fold(e_u * pu)

            zero = jnp.zeros((8, n), F32)
            sums = row_loop(half, 32, gated, (zero, zero))
            for i in range(2):
                s, inverse = total(sums[i]), 1.0 / norm_gu[i : i + 1, over]
                gm_gu[i : i + 1, over] += s * inverse
                turn = m_gu[i : i + 1, over] * s * inverse * inverse * inverse
                dp[i, half : half + RANK, over] = (b_gu[i, :, over].astype(F32) * turn).astype(BF16)
                gb_gu[i, :, over] += ADAPT_SCALE * (
                    dot(low[:, i * RANK : (i + 1) * RANK], dp[i, :half, over], TN) - v_gu[i, :, over] * turn
                )

        tiles(hidden, WIDE, there_and_back, lambda t: tick(half // 32 + t))
        for i in range(2):
            both = ADAPT_SCALE * dot(dp[i], b_gu[i], NT)
            mix[:half, i * RANK : (i + 1) * RANK] = both[:half].astype(BF16)
            for k in range(2):
                mix[half + k * RANK : half + (k + 1) * RANK, i * RANK : (i + 1) * RANK] = (
                    both[half:] if i == k else jnp.zeros((RANK, RANK), F32)
                ).astype(BF16)

        def inputs(over, t):
            products = [dot(dp[i], wg[i, over, :], NT) for i in range(2)]
            through = dot(mix[...], at_gu[:, :, over].reshape(2 * RANK, over.size))
            value = products[0][:half] + products[1][:half] + through[:half]
            straight = dot(mix[:half, :], h2[:, over], TN)
            for i in range(2):
                v_tb = products[i][half:] + through[half + i * RANK : half + (i + 1) * RANK]
                ga_gu[i, :, over] += straight[i * RANK : (i + 1) * RANK] - ADAPT_SCALE * v_tb
            part2[mine, over] = value.astype(BF16)
            g_gain[:, over] += total(value * h2[:, over].astype(F32)) / gain[:, over]

        tiles(width, WIDE, inputs, lambda t: tick(half // 32 + n_hidden + t))

    def norm_back(r, first):
        rows = pl.ds(pl.multiple_of(first, 16), 16)
        there = pl.ds(pl.multiple_of(r * half + first, 16), 16)
        value = out_pre[there, :].astype(F32)
        x2 = x[there, :].astype(F32) + value * c_out
        inverse = lax.rsqrt(jnp.mean(x2 * x2, axis=-1, keepdims=True) + NORM_EPS)
        scaled = dh2[there, :].astype(F32) * gain[...]
        mean = jnp.mean(scaled * x2, axis=-1, keepdims=True)
        e = cotangent[there, :].astype(F32) + inverse * scaled - x2 * (inverse**3 * mean)
        dx2[there, :] = e.astype(BF16)
        x2_out[there, :] = x2.astype(BF16)
        dpo[rows, :] = (e * c_out).astype(BF16)
        row_sums[...] += fold(e * value)

    def out_back(r):
        mine = slice(r * half, (r + 1) * half)
        rows_here = rows_n // 2

        s = total(row_sums[...])
        turn = m_out[...] * s * n_out * n_out * n_out
        gm_out[...] += s * n_out
        dpo[half : half + RANK, :] = (b_out[...].astype(F32) * turn).astype(BF16)
        both = dot(dpo[...], b_out[...], NT)
        dlow, turned = (ADAPT_SCALE * both[:half]).astype(BF16), both[half:]

        def inputs(over, t):
            product = dot(dpo[...], wo[over, :], NT)
            value = (product[:half] + dot(dlow, at_out[:, over])).astype(BF16)
            for row in range(rows_here):
                for hh in range(over.size // HD):
                    blocks[(r * rows_here + row) * heads + t * (over.size // HD) + hh] = value[
                        row * group : (row + 1) * group, hh * HD : (hh + 1) * HD
                    ]
            ga_out[:, over] += dot(dlow, attn[mine, over], TN) - ADAPT_SCALE * (
                product[half:] + ADAPT_SCALE * dot(turned, at_out[:, over])
            )

        tiles(heads * HD, WIDE, inputs)
        leave.start(r * rows_here * heads, (r + 1) * rows_here * heads)
        leaving(0, r).start()
        leaving(1, r).start()
        gb_out[...] += ADAPT_SCALE * (dot(low_out[mine, :], dpo[:half, :], TN) - v_out[...] * turn)

    ticks = half // 32 + n_hidden + n_width
    feed_forward(0, one_out.spread(half_done, half_done + IN_A, ticks))
    two[0].first()
    left = one_out.steps - half_done - IN_A

    def between(k, carry):
        one_out.step(half_done + IN_A + k)
        two[0].step(k)
        return carry

    lax.fori_loop(0, left, between, 0)
    feed_forward(1, two[0].spread(left, left + IN_B, ticks))
    two[1].first()
    rest = two[0].steps - left - IN_B

    def together(k, carry):
        two[0].step(left + IN_B + k)
        two[1].step(k)
        return carry

    lax.fori_loop(0, rest, together, 0)

    low_down = dot(z[...], at_down[...], NT).astype(BF16)

    def down(over, t):
        value = dot(z[...], wd[:, over]) + ADAPT_SCALE * dot(low_down, b_down[:, over])
        down_part[:, over] = value.astype(BF16)
        s_part[0:1, over] = total(value * cotangent[:, over].astype(F32))
        gb_down[:, over] = ADAPT_SCALE * dot(low_down, dpd[:, over], TN)

    tiles(width, WIDE, down, two[1].spread(rest, rest + 2, n_width))
    leaving(2, 0).start()
    leaving(2, 1).start()
    across = Across(depth, s_part, others, z_send, z_recv)
    across.start()

    def down_factor(over, t):
        ga_down[:, over] = dot(dlow_down, z[:, over], TN)

    tiles(hidden, WIDE, down_factor)
    row_sums[...] = jnp.zeros_like(row_sums)
    taken = rest + 4
    tick_two = two[1].spread(rest + 2, taken, half // 16)

    def first_half(k, carry):
        norm_back(0, k * 16)
        tick_two(k)
        return carry

    lax.fori_loop(0, half // 16, first_half, 0)
    out_back(0)
    row_sums[...] = jnp.zeros_like(row_sums)

    def second_half(t, carry):
        @pl.when(t >= taken)
        def _():
            two[1].step(t)

        for stream in range(2):
            norm_back(1, ((1 - stream) * two[1].chunks + t - 3 * LAG) * CHUNK)
        return carry

    lax.fori_loop(3 * LAG, two[1].steps, second_half, 0)
    out_back(1)
    for line in [one_out] + two:
        line.drain()
    s = across.finish()[0:1, :]
    turn = m_down[...] * s * n_down * n_down * n_down
    tb = (b_down[...].astype(F32) * turn).astype(BF16)
    v_tb = dot(tb, wd[...], NT) + ADAPT_SCALE * dot(dot(tb, b_down[...], NT), at_down[...])
    ga_down[...] -= ADAPT_SCALE * v_tb
    gb_down[...] -= ADAPT_SCALE * v_down[...] * turn
    gm_down[...] = s * n_down
    come.wait_send()
    for i in range(3):
        for r in range(2):
            leaving(i, r).wait()
    leave.wait_recv()
    leave.wait_send()


def core(sizes, o, x, cotangent, gain, norms, out, down, gu):
    seq_n, depth, rows_n, group, heads = sizes
    count, pairs, width = rows_n * group, rows_n * heads, x.shape[1]
    hidden, half = down[0].shape[0], rows_n * group // 2
    return pl.pallas_call(
        functools.partial(core_kernel, *sizes),
        out_shape=[
            shape(count, width), shape(count, width), shape(count, width), shape(pairs, group, HD),
            shape(1, width, dtype=F32), shape(2, RANK, width, dtype=F32), shape(2, RANK, hidden, dtype=F32),
            shape(2, hidden, dtype=F32), shape(1, width, dtype=F32), shape(RANK, hidden, dtype=F32),
            shape(RANK, width, dtype=F32), shape(RANK, heads * HD, dtype=F32), shape(RANK, width, dtype=F32),
            shape(1, width, dtype=F32),
        ],
        in_specs=[IN_VMEM] * 14 + [ANYWHERE] * 5,
        out_specs=[ANYWHERE] * 3 + [IN_VMEM] * 11,
        scratch_shapes=[pltpu.VMEM((count, width), BF16)] * 3
        + [
            pltpu.VMEM((count, width), BF16), pltpu.VMEM((count, width), BF16), pltpu.VMEM((count, width), BF16),
            pltpu.VMEM(out[0].shape, BF16),
            pltpu.VMEM(gu[0].shape, BF16), pltpu.VMEM(down[0].shape, BF16), pltpu.VMEM((count, heads * HD), BF16),
            pltpu.VMEM((count, RANK), BF16), pltpu.VMEM((count, width), BF16), pltpu.VMEM((count, width), BF16),
            pltpu.VMEM((count, width), BF16), pltpu.VMEM((half, width), BF16), pltpu.VMEM((count, hidden), BF16),
            pltpu.VMEM((count, hidden), BF16), pltpu.VMEM((2, half + RANK, hidden), BF16),
            pltpu.VMEM((count, width), BF16), pltpu.VMEM((2, half, WIDE), F32), pltpu.VMEM((half, 2 * RANK), BF16),
            pltpu.VMEM((half + 2 * RANK, 2 * RANK), BF16),
            pltpu.VMEM((2, hidden), F32), pltpu.VMEM((2, RANK, hidden), F32),
            pltpu.VMEM((half + RANK, width), BF16), pltpu.VMEM((pairs, group, HD), BF16),
            pltpu.VMEM((8, width), F32), pltpu.VMEM((depth, 8, width), F32), pltpu.VMEM((8, width), F32),
            dma(6), dma(pairs), dma(pairs), dma(pairs), dma(pairs), dma(depth), dma(depth), dma(3, 2),
        ]
        + Line.scratch(count, width, CHUNK)
        + Line.scratch(half, width, CHUNK) * 2,
        compiler_params=params(62, 2),
    )(o, gain, out[3], norms, *out[1:3], out[4], *gu[1:], *down[1:], x, cotangent, out[0], gu[0], down[0])


def last_kernel(
    seq_n, depth, rows_n, group, heads,
    lse, start, place, cos_half, sin_half, low, gain, at, b, m, norm, v_qkv,
    ga_gu, gb_out, gb_down, g_gain2, gm_out, gm_down, ga_out, gb_gu, gm_gu, ga_down, inverse_one, norms, m_down,
    down_far, q_far, k_far, v_far, o_far, do_far, h1_far, pre_far, w_qkv, x2_far, dx2_far,
    dx_far, mixed_far, wide, local, hid,
    mixed, cos, sin, dh1, dx, x2, down_part, q, k, v, o, do, h1, pre, kt, dk_acc, dv_acc, dq, dk, dv,
    wq, gq, gk, gv, dp, mix, part, wide_in, local_in, hid_in, wide_got, local_got, hid_got,
    piece, pieces, done, q_send, q_recv, k_send, k_recv, v_send, v_recv, load,
    r_send, r_recv, g_send, g_recv, z_send, z_recv, leave, *line_refs,
):
    count, pairs, width = rows_n * group, rows_n * heads, h1.shape[1]
    fan, me = seq_n // pairs, lax.axis_index("seq")
    loads = [
        pltpu.make_async_copy(far, near, load.at[i])
        for i, (far, near) in enumerate(
            (
                (down_far, down_part), (q_far, q), (k_far, k), (v_far, v), (o_far, o), (do_far, do), (h1_far, h1),
                (pre_far, pre), (w_qkv, wq), (x2_far, x2), (dx2_far, dx),
            )
        )
    ]
    for one in loads[:6]:
        one.start()
    greet(seq=seq_n, heads=depth)()
    line_down = Line(down_part, mixed, *line_refs[:9], lead=LAST_LEAD)
    loads[0].wait()
    line_down.first()
    for one in loads[1:6]:
        one.wait()
    for one in loads[6:]:
        one.start()
    exchanges = [
        Exchange(kind, seq_n, pairs, lambda j, a=a: a.at[j], lambda j, to=to: to.at[j], *sems)
        for kind, a, to, sems in (
            ("queries_back", dq, gq, (q_send, q_recv)),
            ("keys_back", dk, gk, (k_send, k_recv)),
            ("keys_back", dv, gv, (v_send, v_recv)),
        )
    ]
    first, second = FIRST, SECOND
    attend_back(
        2 * group if fan == 1 else group, fan, q, k, v, o, do, lse, start, place, dq, dk, dv, kt, dk_acc, dv_acc,
        lambda ticks: line_down.spread(0, first, ticks),
    )
    for one in exchanges:
        one.start()

    widen_tables(cos_half, sin_half, cos, sin)
    wide_in[...] = jnp.zeros_like(wide_in)
    local_in[...] = jnp.zeros_like(local_in)
    hid_in[...] = jnp.zeros_like(hid_in)
    share = 1.0 / depth
    for i in range(2):
        wide_in[(3 + i) * RANK : (4 + i) * RANK, :] = ga_gu[i].astype(BF16)
        hid_in[i * RANK : (i + 1) * RANK, :] = gb_gu[i].astype(BF16)
    wide_in[5 * RANK : 6 * RANK, :] = gb_out[...].astype(BF16)
    wide_in[6 * RANK : 7 * RANK, :] = gb_down[...].astype(BF16)
    hid_in[3 * RANK : 4 * RANK, :] = ga_down[...].astype(BF16)
    local_in[4 * RANK : 5 * RANK, :] = ga_out[...].astype(BF16)
    hid_in[2 * RANK : 3 * RANK, :] = jnp.concatenate(
        [gm_gu[...], jnp.zeros((RANK - 2, hid_in.shape[1]), F32)], axis=0
    ).astype(BF16)

    sums = [None] * 3
    line_down.run(first, second)
    for one in loads[6:9]:
        one.wait()
    for i in range(3):
        exchanges[i].wait_recv()
        came = (gq, gk, gv)[i]
        for head in range(heads):
            cols = slice(head * HD, (head + 1) * HD)
            n = norm[i : i + 1, cols]
            c = m[i : i + 1, cols] / n
            s = jnp.zeros((1, HD), F32)
            for row in range(rows_n):
                rows = slice(row * group, (row + 1) * group)
                if i == 0:
                    e = came[row * heads + head].astype(F32)
                else:
                    e = came[(row * heads + head) * fan].astype(F32)
                    for g in range(1, fan):
                        e = e + came[(row * heads + head) * fan + g].astype(F32)
                if i < 2:
                    e = e * cos[rows, :] - pltpu.roll(e, HD // 2, 1) * sin[rows, :]
                s = s + total(e * pre[i, rows, cols].astype(F32))
                dp[i, rows, cols] = (e * c).astype(BF16)
            turn = m[i : i + 1, cols] * s / (n * n * n)
            dp[i, count : count + RANK, cols] = (b[i, :, cols].astype(F32) * turn).astype(BF16)
            local_in[i * RANK : (i + 1) * RANK, cols] = (
                ADAPT_SCALE * (dot(low[:, i * RANK : (i + 1) * RANK], dp[i, :count, cols], TN) - v_qkv[i, :, cols] * turn)
            ).astype(BF16)
            sums[i] = [s / n] if head == 0 else sums[i] + [s / n]
        line_down.run(second + i, second + i + 1)
    local_in[3 * RANK : 4 * RANK, :] = jnp.concatenate(
        [jnp.concatenate(one, axis=1) for one in sums]
        + [jnp.zeros((RANK - 3, heads * HD), F32)], axis=0
    ).astype(BF16)
    mix[...] = jnp.zeros_like(mix)
    for i in range(3):
        both = (ADAPT_SCALE * dot(dp[i], b[i], NT)).astype(BF16)
        cols = slice(i * RANK, (i + 1) * RANK)
        mix[:count, cols] = both[:count]
        mix[count + i * RANK : count + (i + 1) * RANK, cols] = both[count:]

    def inputs(over, t):
        through = dot(mix[...], at[:, :, over].reshape(3 * RANK, over.size))
        straight = dot(mix[:count, :], h1[:count, over], TN)
        value = through[:count]
        for i in range(3):
            product = dot(dp[i], wq[i, over, :], NT)
            value = value + product[:count]
            rows = slice(i * RANK, (i + 1) * RANK)
            v_tb = product[count:] + through[count + i * RANK : count + (i + 1) * RANK]
            wide_in[rows, over] = (straight[rows] - ADAPT_SCALE * v_tb).astype(BF16)
        part[:, over] = value.astype(BF16)
        g_gain1 = total(value * h1[:count, over].astype(F32)) / gain[:, over]
        wide_in[7 * RANK : 8 * RANK, over] = jnp.concatenate(
            [
                g_gain1, g_gain2[:, over], gm_out[:, over] * share,
                gm_down[:, over] * share,
                jnp.zeros((RANK - 4, over.size), F32),
            ], axis=0,
        ).astype(BF16)

    tiles(width, WIDE, inputs, line_down.spread(second + 3, line_down.steps, -(-width // WIDE)))
    line_down.drain()
    line = Line(part, dh1, *line_refs[:3], *line_refs[9:], lead=LAST_LEAD)
    line.first()
    for one in loads[9:]:
        one.wait()
    c_down = m_down[...] / norms[1:2, :]

    over_gain = 1.0 / gain[...]

    def sent(stream, r):
        at_ = line.place(stream, r * PIECES)[0]
        return pltpu.make_async_copy(dx.at[at_], dx_far.at[at_], leave.at[stream, r])

    mixed_leaves = pltpu.make_async_copy(mixed, mixed_far, load.at[0])

    def advance(t, carry):
        line.step(t)

        @pl.when(t < count // (2 * CHUNK))
        def _():
            rows = pl.ds(pl.multiple_of(t * (2 * CHUNK), 2 * CHUNK), 2 * CHUNK)
            mixed[rows, :] = (x2[rows, :].astype(F32) + mixed[rows, :].astype(F32) * c_down).astype(BF16)

        @pl.when(t == count // (2 * CHUNK))
        def _():
            mixed_leaves.start()

        c = t - 3 * LAG
        r = c // PIECES

        @pl.when((c >= 0) & (lax.rem(c, PIECES) == PIECES - 1))
        def _():
            for stream in range(2):
                at_ = line.place(stream, c)[0]
                unit = h1[at_, :].astype(F32) * over_gain
                scaled = dh1[at_, :].astype(F32) * gain[...]
                mean = jnp.mean(scaled * unit, axis=-1, keepdims=True)
                change = inverse_one[at_, :1] * (scaled - unit * mean)
                dx[at_, :] = (dx[at_, :].astype(F32) + change).astype(BF16)
                sent(stream, r).start()

        return carry


    spread = seq_n // OWNERS
    slabs = (
        (wide_in, wide_got, wide, lambda j: j), (local_in, local_got, local, lambda j: j),
        (hid_in, hid_got, hid, lambda j: OWNERS - 1 - j),
    )
    own = me // spread
    chosen = lax.rem(me, spread) == 0

    def rows_of(j):
        return pl.ds(pl.multiple_of(j * RANK, RANK), RANK)

    def to_owner(i, j):
        src, got, _, owner = slabs[i]
        return remote(
            src.at[rows_of(j)], got.at[me], r_send.at[i, j], r_recv.at[i, me], seq=owner(j) * spread
        )

    def from_owner(i, j, target):
        result = slabs[i][2]
        return remote(
            done.at[i, :, : result.shape[1]], result.at[rows_of(j)], g_send.at[i, target], g_recv.at[i, j], seq=target
        )

    for i, (src, got, result, owner) in enumerate(slabs):
        for j in range(src.shape[0] // RANK):

            @pl.when(me != owner(j) * spread)
            def _(i=i, j=j):
                to_owner(i, j).start()

            @pl.when(me == owner(j) * spread)
            def _(src=src, got=got, i=i, j=j):
                pltpu.make_async_copy(src.at[rows_of(j)], got.at[me], r_recv.at[i, me]).start()

    lax.fori_loop(0, GATHER, advance, 0)
    across = Across(depth, piece, pieces, z_send, z_recv)
    blocks_n = [slab[0].shape[0] // RANK for slab in slabs]
    owns = [chosen & (slab[3](own) < n) for slab, n in zip(slabs, blocks_n)]
    for i, (src, got, result, owner) in enumerate(slabs):

        @pl.when(owns[i])
        def _(i=i, got=got, result=result):
            def add(s_, acc):
                pltpu.make_async_copy(got.at[s_], got.at[s_], r_recv.at[i, s_]).wait()
                return acc + got[s_].astype(F32)

            value = lax.fori_loop(0, seq_n, add, jnp.zeros((RANK, result.shape[1]), F32))
            if i == 0:
                piece[...] = value.astype(BF16)
                across.start()
            else:
                done[i, :, : result.shape[1]] = value.astype(BF16)

    lax.fori_loop(GATHER, GIVE, advance, 0)

    @pl.when(owns[0])
    def _():
        done[0, :, :] = across.finish().astype(BF16)

    for i, (src, got, result, owner) in enumerate(slabs):

        @pl.when(owns[i])
        def _(i=i, result=result, owner=owner):
            mine = owner(own)

            def give(d, carry):
                from_owner(i, mine, lax.rem(me + d, seq_n)).start()
                return carry

            lax.fori_loop(1, seq_n, give, 0)
            pltpu.make_async_copy(
                done.at[i, :, : result.shape[1]], result.at[rows_of(mine)], g_recv.at[i, mine]
            ).start()

    lax.fori_loop(GIVE, line.steps, advance, 0)
    line.drain()

    def gone(c, carry):
        for stream in range(2):
            sent(stream, c).wait()
        return carry

    lax.fori_loop(0, line.chunks // PIECES, gone, 0)
    mixed_leaves.wait()
    for one in exchanges:
        one.wait_send()
    for i, (src, got, result, owner) in enumerate(slabs):
        for j in range(blocks_n[i]):

            @pl.when(me != owner(j) * spread)
            def _(i=i, j=j):
                to_owner(i, j).wait_send()

            pltpu.make_async_copy(result.at[rows_of(j)], result.at[rows_of(j)], g_recv.at[i, j]).wait()

        @pl.when(owns[i])
        def _(i=i, owner=owner):
            def given(d, carry):
                from_owner(i, owner(own), lax.rem(me + d, seq_n)).wait_send()
                return carry

            lax.fori_loop(1, seq_n, given, 0)


def last(sizes, ins, far, hidden):
    seq_n, depth, rows_n, group, heads = sizes
    qkv_w = far[8]
    count, pairs, width = rows_n * group, rows_n * heads, qkv_w.shape[1]
    local, length = qkv_w.shape[2], seq_n * group
    blocks = {width: 8, local: 5, hidden: 4}
    slabs = [(n * RANK, w) for w, n in blocks.items()]
    some, every = pltpu.VMEM((pairs, group, HD), BF16), pltpu.VMEM((seq_n, group, HD), BF16)
    return pl.pallas_call(
        functools.partial(last_kernel, *sizes),
        out_shape=[shape(count, width)] * 2 + [shape(*s) for s in slabs],
        in_specs=[IN_VMEM] * len(ins) + [ANYWHERE] * len(far),
        out_specs=[ANYWHERE] * 2 + [IN_VMEM] * 3,
        scratch_shapes=[pltpu.VMEM((count, width), BF16), pltpu.VMEM((count, HD), F32), pltpu.VMEM((count, HD), F32)]
        + [pltpu.VMEM((count, width), BF16)] * 3
        + [pltpu.VMEM(a.shape, BF16) for a in far[:8]]
        + [
            pltpu.VMEM((HD, length), BF16), pltpu.VMEM((length, HD), F32), pltpu.VMEM((length, HD), F32),
            some, every, every,
            pltpu.VMEM(qkv_w.shape, BF16), some, every, every,
            pltpu.VMEM((3, count + RANK, local), BF16), pltpu.VMEM((count + 3 * RANK, 3 * RANK), BF16),
            pltpu.VMEM((count, width), BF16),
        ]
        + [pltpu.VMEM(s, BF16) for s in slabs]
        + [pltpu.VMEM((seq_n, RANK, s[1]), BF16) for s in slabs]
        + [
            pltpu.VMEM((RANK, width), BF16), pltpu.VMEM((depth, RANK, width), BF16), pltpu.VMEM((3, RANK, width), BF16),
            dma(pairs), dma(pairs), dma(seq_n), dma(seq_n), dma(seq_n), dma(seq_n), dma(11),
            dma(3, 8), dma(3, seq_n), dma(3, seq_n), dma(3, 8), dma(depth), dma(depth), dma(2, count // (2 * CHUNK)),
        ]
        + Line.scratch(count, width, CHUNK)
        + Line.scratch(count, width, CHUNK)[3:],
        compiler_params=params(62, 5),
    )(*ins, *far)


PARTS = 4


def leave_kernel(wide_far, local_far, hid_far, dx_far, mixed_far, *refs):
    outs, (dx_out, mixed_out, wide, local, hid, dx, dx_wide, mixed, sems, slab_sems) = refs[:14], refs[14:]
    slabs = [
        pltpu.make_async_copy(far, near, slab_sems.at[i])
        for i, (far, near) in enumerate(((wide_far, wide), (local_far, local), (hid_far, hid)))
    ]
    rows = dx.shape[0] // PARTS
    parts = [slice(i * rows, (i + 1) * rows) for i in range(PARTS)]
    moves = [
        [pltpu.make_async_copy(src.at[p], dst.at[p], sems.at[k, i]) for i, p in enumerate(parts)]
        for k, (src, dst) in enumerate(
            ((dx_far, dx), (dx_wide, dx_out), (mixed_far, mixed), (mixed, mixed_out))
        )
    ]
    for one in moves[0] + slabs + moves[2]:
        one.start()
    for i, p in enumerate(parts):
        moves[0][i].wait()
        dx_wide[p, :] = dx[p, :].astype(F32)
        moves[1][i].start()
    for one in slabs:
        one.wait()
    for i in range(PARTS):
        moves[2][i].wait()
        moves[3][i].start()
    places = (
        (wide, 112, 1), (wide, 0, 48), (local, 0, 48), (local, 48, 3), (local, 64, 16), (wide, 80, 16), (wide, 114, 1),
        (wide, 113, 1), (wide, 48, 32), (hid, 0, 32), (hid, 32, 2), (hid, 48, 16), (wide, 96, 16), (wide, 115, 1),
    )
    for out, (slab, first, n) in zip(outs, places):
        begin = first // RANK * RANK
        value = slab[begin : begin + -(-n // RANK) * RANK, :].astype(F32)
        out[...] = value[first - begin : first - begin + n].reshape(out.shape)
    for k in (1, 3):
        for one in moves[k]:
            one.wait()


def outputs(wide, local, hid, dx, mixed):
    w, n, f = wide.shape[1], local.shape[1], hid.shape[1]
    dims = (
        (1, w), (3, RANK, w), (3, RANK, n), (3, n), (RANK, n), (RANK, w), (1, w), (1, w), (2, RANK, w), (2, RANK, f),
        (2, f), (RANK, f), (RANK, w), (1, w),
    )
    return pl.pallas_call(
        leave_kernel,
        out_shape=[shape(*d, dtype=F32) for d in dims] + [shape(*dx.shape, dtype=F32), shape(*mixed.shape)],
        in_specs=[ANYWHERE] * 5,
        out_specs=[IN_VMEM] * len(dims) + [ANYWHERE] * 2,
        scratch_shapes=[pltpu.VMEM(a.shape, BF16) for a in (wide, local, hid)]
        + [
            pltpu.VMEM(dx.shape, BF16), pltpu.VMEM(dx.shape, F32), pltpu.VMEM(mixed.shape, BF16), dma(4, PARTS), dma(3),
        ],
        compiler_params=params(62),
    )(wide, local, hid, dx, mixed)


def per_device(
    tokens, attn_gain, base_qkv, adapt_a_qkv, adapt_b_qkv, magnitude_qkv, base_out, adapt_a_out,
    adapt_b_out, magnitude_out, ffn_gain, base_gu, adapt_a_gu, adapt_b_gu, magnitude_gu, base_down,
    adapt_a_down, adapt_b_down, magnitude_down, doc_lengths, cotangent,
):
    rows_n, group, width = tokens.shape
    count = rows_n * group
    local = base_qkv.shape[2]
    heads = local // HD
    pairs = rows_n * heads
    seq_n, depth = lax.axis_size("seq"), lax.axis_size("heads")
    sizes = (seq_n, depth, rows_n, group, heads)
    length = group * seq_n
    me = lax.axis_index("seq")

    order = jnp.arange(doc_lengths.shape[1])
    doc_ends = jnp.sum(
        jnp.where(order[None, :, None] <= order[None, None, :], doc_lengths[:, :, None], 0), axis=1
    )
    mine = me * group + jnp.arange(group, dtype=jnp.int32)
    ended = mine[None, :, None] >= doc_ends[:, None, :]
    position = mine[None, :] - jnp.sum(jnp.where(ended, doc_lengths[:, None, :], 0), axis=-1)
    frequency = ROPE_BASE ** (jnp.arange(HD // 2, dtype=F32) * (-2.0 / HD))
    angles = position.reshape(count, 1).astype(F32) * frequency
    cos, sin = jnp.cos(angles), jnp.sin(angles)

    x = tokens.reshape(count, width)
    dy = cotangent.reshape(count, width)
    gain1, gain2 = attn_gain[None, :], ffn_gain[None, :]
    m_out, m_down = magnitude_out[None, :], magnitude_down[None, :]
    at_qkv, at_gu = adapt_a_qkv.transpose(0, 2, 1), adapt_a_gu.transpose(0, 2, 1)
    at_out, at_down = adapt_a_out.T, adapt_a_down.T

    h1, pre, q, k, v, inverse_one, low, norm_qkv, v_qkv, norms, v_out, v_down = front(
        sizes, x, gain1, cos, sin, (base_qkv, at_qkv, adapt_b_qkv, magnitude_qkv), (base_out, at_out, adapt_b_out),
        (base_down, at_down, adapt_b_down),
    )
    q, k, v = q.reshape(-1, HD), k.reshape(length, HD), v.reshape(length, HD)
    o, lse, start, place = attend(sizes, doc_lengths, q, k, v)
    dx2, x2, down_part, do, gm_down, ga_gu, gb_gu, gm_gu, g_gain2, ga_down, gb_down, ga_out, gb_out, gm_out = core(
        sizes, o.reshape(-1, group, HD), x, dy, gain2, norms, (base_out, at_out, adapt_b_out, m_out, v_out),
        (base_down, at_down, adapt_b_down, m_down, v_down), (base_gu, at_gu, adapt_b_gu, magnitude_gu),
    )
    dx, mixed, wide, narrow, hid = last(
        sizes,
        (
            lse, start, place, cos, sin, low, gain1, at_qkv, adapt_b_qkv, magnitude_qkv, norm_qkv, v_qkv, ga_gu, gb_out,
            gb_down, g_gain2, gm_out, gm_down, ga_out, gb_gu, gm_gu, ga_down, inverse_one, norms, m_down,
        ),
        (down_part, q, k, v, o, do.reshape(-1, HD), h1, pre, base_qkv, x2, dx2),
        base_down.shape[0],
    )
    *g, dx, mixed = outputs(wide, narrow, hid, dx, mixed)
    return (
        mixed.reshape(rows_n, group, width),
        dx.reshape(rows_n, group, width),
        g[0][0], g[1].transpose(0, 2, 1), g[2], g[3], g[4].T, g[5], g[6][0], g[7][0], g[8].transpose(0, 2, 1), g[9],
        g[10], g[11].T, g[12], g[13][0],
    )


def solution(mesh):
    in_specs = (
        P(None, "seq", None), P(), P(None, None, "heads"), P(), P(None, None, "heads"), P(None, "heads"),
        P("heads", None), P("heads", None), P(), P(), P(), P(None, None, "heads"), P(),
        P(None, None, "heads"), P(None, "heads"), P("heads", None), P("heads", None), P(), P(), P(),
        P(None, "seq", None),
    )
    out_specs = (
        P(None, "seq", None), P(None, "seq", None), P(), P(), P(None, None, "heads"), P(None, "heads"),
        P("heads", None), P(), P(), P(), P(), P(None, None, "heads"), P(None, "heads"),
        P("heads", None), P(), P(),
    )
    return jax.shard_map(
        per_device, mesh=mesh, in_specs=in_specs, out_specs=out_specs, check_vma=False
    )
```
